32 devices in a mesh: seq: 4 (over z), rows: 8 (over y, x, core).
Axes of the slice: x: 2, y: 2, z: 4, core: 2. Of those that a mesh axis runs over, the one named last changes fastest.
Arguments:
- tokens: bfloat16 [8, 1024, 1536], P('rows', 'seq'), may hold values from -6 to 6
- resets: int32 [8, 1024], P('rows', 'seq'), may hold values from 0 to 1, as said below
- norm_gain: bfloat16 [1536], P('rows'), may hold values from 0.5 to 1.5
- in_proj: bfloat16 [1536, 6144], P('rows'), may hold values from -0.15625 to 0.15625
- x_proj: bfloat16 [3072, 128], P('rows'), may hold values from -0.3125 to 0.3125
- dt_proj: bfloat16 [96, 3072], P(None, 'rows'), may hold values from -0.625 to 0.625
- conv_weight: bfloat16 [4, 3072], P(None, 'rows'), may hold values from -3 to 3
- conv_bias: bfloat16 [3072], P('rows'), may hold values from -3 to 3
- dt_bias: bfloat16 [3072], P('rows'), may hold values from -6 to -2
- a_log: bfloat16 [16, 3072], P(None, 'rows'), may hold values from -4.59375 to 2.796875
- out_proj: bfloat16 [3072, 1536], P('rows'), may hold values from -0.109375 to 0.109375
- cotangent: bfloat16 [8, 1024, 1536], P('rows', 'seq'), may hold values from -6 to 6
Outputs:
- block_out: bfloat16 [8, 1024, 1536], P('rows', 'seq')
- d_tokens: bfloat16 [8, 1024, 1536], P('rows', 'seq')
- d_norm_gain: float32 [1536], P('rows')
- d_in_proj: float32 [1536, 6144], P('rows')
- d_x_proj: float32 [3072, 128], P('rows')
- d_dt_proj: float32 [96, 3072], P(None, 'rows')
- d_conv_weight: float32 [4, 3072], P(None, 'rows')
- d_conv_bias: float32 [3072], P('rows')
- d_dt_bias: float32 [3072], P('rows')
- d_a_log: float32 [16, 3072], P(None, 'rows')
- d_out_proj: float32 [3072, 1536], P('rows')
The draws below stay inside these ranges and needn't reach their ends.
Inputs may be any that keep to these rules, and one draw needn't show every extreme that they name: `resets`: each packed row holds either one item of 1024 tokens or four items of 256 tokens; a 1 marks an item's first token, so every row starts with 1, and some row holds a single item in every draw.
All inputs are finite; a program needn't handle non-finite values.
Results may differ from the reference program's by a relative error of at most 0.019.
Values may be sent and summed in bfloat16 or wider, within the bound.
A program may use at most 256 MiB of HBM per device.

```python
import math
import jax
import jax.numpy as jnp
from jax import lax

D = 1536
E = 3072
R = 96
NS = 16
KC = 4
LEN = 1024
NROWS = 8


def draw_resets(key, part):
    first_key, second_key = jax.random.split(jax.random.fold_in(key, 17))
    quartered = jax.random.randint(first_key, (NROWS,), 0, 2)
    forced = jax.random.randint(second_key, (), 0, NROWS)
    quartered = jnp.where(jnp.arange(NROWS) == forced, 0, quartered)
    position = jnp.arange(LEN)
    quarter_starts = position % (LEN // 4) == 0
    row_start = position == 0
    marks = jnp.where(quartered[:, None] == 1, quarter_starts[None, :], row_start[None, :])
    return marks.astype(jnp.int32)


def block_levels(stream_key, extent, cuts, smallest, high):
    def one(dim, blocks):
        steps = jax.random.uniform(jax.random.fold_in(jax.random.fold_in(stream_key, 6), dim), (blocks,), jnp.float32, smallest / len(cuts), high / len(cuts))
        return jnp.repeat(jnp.exp(steps), extent[dim] // blocks).reshape((-1,) + (1,) * (len(extent) - dim - 1))

    gain = one(*cuts[0])
    for cut in cuts[1:]:
        gain = gain * one(*cut)
    return gain


def gaussian(own_key, extent, scale, reach, cuts=(), kind=jnp.bfloat16):
    factor_of = block_levels(own_key, extent, cuts, -0.22, 0.18) if cuts else 1.0
    values = jax.random.normal(own_key, extent, jnp.float32) * scale * factor_of
    return jnp.minimum(jnp.maximum(values, -reach), reach).astype(kind)


def setup_inputs(seed: int = 0) -> dict:
    seeds = jax.random.split(jax.random.key(seed), 13)
    return {
        "tokens": gaussian(seeds[0], (NROWS, LEN, D), 1.0, 6.0, ((0, 8), (1, 4))),
        "resets": draw_resets(jax.random.fold_in(seeds[12], 71), 0),
        "norm_gain": jnp.clip(1.0 + 0.1 * jax.random.normal(seeds[2], (D,), jnp.float32), 0.5, 1.5).astype(jnp.bfloat16),
        "in_proj": gaussian(seeds[3], (D, 2 * E), D ** -0.5, 0.15625, ((0, 8),)),
        "x_proj": gaussian(seeds[4], (E, R + 2 * NS), (E // 8) ** -0.5, 0.3125, ((0, 8),)),
        "dt_proj": gaussian(seeds[5], (R, E), R ** -0.5, 0.625, ((1, 8),)),
        "conv_weight": gaussian(seeds[6], (KC, E), KC ** -0.5, 3.0, ((1, 8),)),
        "conv_bias": gaussian(seeds[7], (E,), 0.5, 3.0, ((0, 8),)),
        "dt_bias": jnp.clip(-6.0 + 4.0 * jax.random.uniform(seeds[8], (E,), jnp.float32) ** block_levels(seeds[8], (E,), ((0, 8),), -0.2, 0.2), -6.0, -2.0).astype(jnp.bfloat16),
        "a_log": jnp.clip(-4.59375 + 7.390625 * jax.random.uniform(seeds[9], (NS, E), jnp.float32) ** block_levels(seeds[9], (NS, E), ((1, 8),), -0.2, 0.2), -4.59375, 2.796875).astype(jnp.bfloat16),
        "out_proj": gaussian(seeds[10], (E, D), E ** -0.5, 0.109375, ((0, 8),)),
        "cotangent": gaussian(seeds[11], (NROWS, LEN, D), 1.0, 6.0, ((0, 8), (1, 4))),
    }


epsilon = 1e-05

@jax.custom_vjp
def low(v):
    return lax.optimization_barrier(v.astype(jnp.bfloat16)).astype(jnp.float32)

@jax.custom_vjp
def low_back(v):
    return v

def low_keep(v):
    return (low(v), None)

def low_pass(kept, grad):
    return (grad,)

def back_keep(v):
    return (v, None)

def back_low(kept, grad):
    return (low(grad),)
low.defvjp(low_keep, low_pass)
low_back.defvjp(back_keep, back_low)

def matmul(left, right):
    return jnp.dot(left, right, precision=lax.Precision.HIGHEST, preferred_element_type=jnp.float32)

def selective_scan(step_size, inputs, b_coef, c_coef, alive, decay_rate):
    group = alive.shape[0]
    length = alive.shape[1]
    block_len = math.gcd(length, 64)
    count = length // block_len

    def to_steps(values):
        moved = jnp.moveaxis(values, 1, 0)
        return moved.reshape((count, block_len) + moved.shape[1:])

    def one_step(carried, pieces):
        step_delta, step_input, step_b, step_c, step_alive = pieces
        decay_now = jnp.exp(step_delta[:, None, :] * decay_rate[None]) * step_alive[:, None, None]
        carried = decay_now * carried + (step_delta * step_input)[:, None, :] * step_b[:, :, None]
        return (carried, lax.optimization_barrier(jnp.sum(carried * step_c[:, :, None], axis=1)))

    def one_block(carried, pieces):
        return lax.scan(one_step, carried, pieces)
    initial = jnp.zeros((group, NS, E), jnp.float32)
    pieces = (to_steps(step_size), to_steps(inputs), to_steps(b_coef), to_steps(c_coef), to_steps(alive))
    final_state, outputs = lax.scan(jax.checkpoint(one_block), initial, pieces)
    return jnp.moveaxis(outputs.reshape((length, group, E)), 0, 1)

def forward(group_in, weights, alive):
    norm_gain, in_proj, x_proj, dt_proj, conv_weight, conv_bias, dt_bias, a_log, out_proj = weights
    group = alive.shape[0]
    length = alive.shape[1]
    flat_in = group_in.reshape(group * length, D)
    inv_rms = lax.rsqrt(lax.optimization_barrier(jnp.mean(flat_in * flat_in, axis=1, keepdims=True)) + epsilon)
    normed = low(flat_in * inv_rms * norm_gain)
    mixed = low_back(matmul(normed, in_proj))
    conv_in = low(mixed[:, :E]).reshape(group, length, E)
    gate_pre = mixed[:, E:].reshape(group, length, E)
    padded = jnp.pad(conv_in, ((0, 0), (KC - 1, 0), (0, 0)))
    conv_pre = conv_bias + sum((conv_weight[offset] * padded[:, offset:offset + length] for offset in range(KC)))
    conv_out = low(jax.nn.silu(conv_pre))
    projected = low_back(matmul(conv_out.reshape(group * length, E), x_proj))
    rank_part = low(projected[:, :R])
    b_coef = projected[:, R:R + NS].reshape(group, length, NS)
    c_coef = projected[:, R + NS:].reshape(group, length, NS)
    step_size = jax.nn.softplus(low_back(matmul(rank_part, dt_proj)) + dt_bias).reshape(group, length, E)
    decay_rate = -jnp.exp(a_log)
    scan_y = selective_scan(step_size, conv_out, b_coef, c_coef, alive, decay_rate)
    gated = low(scan_y * jax.nn.silu(gate_pre))
    result = flat_in + matmul(gated.reshape(group * length, E), out_proj)
    return result.reshape(group, length, D)

def reference(tokens, resets, norm_gain, in_proj, x_proj, dt_proj, conv_weight, conv_bias, dt_bias, a_log, out_proj, cotangent):
    weights = tuple((argument.astype(jnp.float32) for argument in (norm_gain, in_proj, x_proj, dt_proj, conv_weight, conv_bias, dt_bias, a_log, out_proj)))
    rows_total = tokens.shape[0]
    group = math.gcd(rows_total, max(1, 4096 // LEN))
    count = rows_total // group
    grouped_in = tokens.astype(jnp.float32).reshape(count, group, LEN, D)
    grouped_alive = (1 - resets).astype(jnp.float32).reshape(count, group, LEN)
    grouped_cot = cotangent.astype(jnp.float32).reshape(count, group, LEN, D)

    def one_group(totals, pieces):
        group_in, group_alive, group_cot = pieces
        result, pullback = jax.vjp(lambda values, params: forward(values, params, group_alive), group_in, weights)
        grad_in, grad_weights = pullback(group_cot)
        totals = jax.tree.map(lambda left, right: left + right, totals, grad_weights)
        return (totals, (result.astype(jnp.bfloat16), grad_in.astype(jnp.bfloat16)))
    zero_totals = tuple((jnp.zeros_like(argument) for argument in weights))
    totals, (outputs, grads_in) = lax.scan(one_group, zero_totals, (grouped_in, grouped_alive, grouped_cot))
    return (outputs.reshape(rows_total, LEN, D), grads_in.reshape(rows_total, LEN, D), totals[0], totals[1], totals[2], totals[3], totals[4], totals[5], totals[6], totals[7], totals[8])
```

```python
import functools
import math

import jax
import jax.numpy as jnp
from jax import lax
from jax.experimental import pallas as pl
from jax.experimental.pallas import tpu as pltpu
from jax.sharding import PartitionSpec as P

D = 1536
E = 3072
R = 96
NS = 16
KC = 4
ITEM = 256

epsilon = 1e-05
LOG2E = 1.4426950408889634
LN2 = 0.6931471805599453
MIB = 2**20


LANES = 128


def pad_lanes(lanes):
    return -(-lanes // LANES) * LANES


def selector(wide):
    row = lax.broadcasted_iota(jnp.int32, (256, 2 * NS * wide), 0) % 128
    col = lax.broadcasted_iota(jnp.int32, (256, 2 * NS * wide), 1) // wide
    return (row == col + R).astype(jnp.bfloat16)


def spread(proj, sel_ref):
    high = proj.astype(jnp.bfloat16)
    low = (proj - high.astype(jnp.float32)).astype(jnp.bfloat16)
    return jnp.dot(
        jnp.concatenate([high, low], axis=1), sel_ref[...], preferred_element_type=jnp.float32
    )


def load_blocks(sources, targets, sems):
    copies = []
    for i, (source, target) in enumerate(zip(sources, targets)):
        for b in range(target.shape[0]):
            lanes = pl.ds(b * LANES, LANES)
            copies.append(pltpu.make_async_copy(source.at[:, lanes], target.at[b], sems.at[i, b]))
    for copy in copies:
        copy.start()
    return copies


def store_blocks(sources, targets, sems):
    copies = []
    for i, (source, target) in enumerate(zip(sources, targets)):
        for b in range(source.shape[0]):
            lanes = pl.ds(b * LANES, LANES)
            copies.append(pltpu.make_async_copy(source.at[b], target.at[:, lanes], sems.at[i, b]))
    for copy in copies:
        copy.start()
    return copies


def ends_kernel(
    nr, tt, ct, uu, delta_in, x_in, gy_in, proj_ref, a_ref, out_ref, sel, bc, delta_ref, x_ref, gy_ref, sems
):
    el = a_ref.shape[1]
    half = NS // 2
    copies = load_blocks((delta_in, x_in, gy_in), (delta_ref, x_ref, gy_ref), sems)
    sel[...] = selector(LANES)
    out_ref[0] = jnp.zeros((NS, nr, el), jnp.float32)
    out_ref[1] = jnp.ones((NS, nr, el), jnp.float32)
    out_ref[2] = jnp.zeros((NS, nr, el), jnp.float32)
    for copy in copies:
        copy.wait()

    def chunk(c, none):
        rows = pl.multiple_of(c * (ct * nr), ct * nr)
        bc[...] = spread(proj_ref[pl.ds(rows, ct * nr), :], sel)
        for b in range(el // LANES):
            lanes = slice(b * LANES, (b + 1) * LANES)
            for n0 in range(0, NS, half):
                ns = range(n0, n0 + half)
                rate = [jnp.broadcast_to(a_ref[n : n + 1, lanes], (nr, LANES)) for n in ns]

                def steps(s, carried):
                    state, through, back = (list(v) for v in carried)
                    for u in range(uu):
                        at = s * uu + u
                        here = pl.ds(c * ct + at, nr, stride=tt)
                        delta = delta_ref[b, here, :]
                        gy = gy_ref[b, here, :]
                        du = delta * x_ref[b, here, :]
                        near = pl.ds(pl.multiple_of(at * nr, nr), nr)
                        for i, n in enumerate(ns):
                            b_at, c_at = n * LANES, (NS + n) * LANES
                            decay = jnp.exp2(delta * rate[i])
                            state[i] = decay * state[i] + du * bc[near, b_at : b_at + LANES]
                            through[i] = through[i] * decay
                            back[i] = back[i] + through[i] * (gy * bc[near, c_at : c_at + LANES])
                    return tuple(state), tuple(through), tuple(back)

                start = tuple(tuple(out_ref[k, n, :, lanes] for n in ns) for k in range(3))
                last = lax.fori_loop(0, ct // uu, steps, start)
                for k in range(3):
                    for i, n in enumerate(ns):
                        out_ref[k, n, :, lanes] = last[k][i]
        return none

    lax.fori_loop(0, tt // ct, chunk, 0)


def scan_ends(delta, x, gy, proj, rate, nr, tt):
    el = rate.shape[1]
    ct = math.gcd(tt, 32)
    here = pl.BlockSpec(memory_space=pltpu.VMEM)
    away = pl.BlockSpec(memory_space=pl.ANY)
    blocks = pltpu.VMEM((el // LANES, nr * tt, LANES), jnp.float32)
    return pl.pallas_call(
        functools.partial(ends_kernel, nr, tt, ct, min(8, ct)),
        in_specs=[away] * 3 + [here] * 2,
        out_specs=here,
        out_shape=jax.ShapeDtypeStruct((3, NS, nr, el), jnp.float32),
        scratch_shapes=[
            pltpu.VMEM((256, 2 * NS * LANES), jnp.bfloat16),
            pltpu.VMEM((ct * nr, 2 * NS * LANES), jnp.float32),
            blocks,
            blocks,
            blocks,
            pltpu.SemaphoreType.DMA((3, el // LANES)),
        ],
        compiler_params=pltpu.CompilerParams(vmem_limit_bytes=56 * MIB),
        name="scan_ends",
    )(delta, x, gy, proj, rate)


def main_kernel(
    nr, tt, ct, uu,
    delta_in, x_in, gy_in, proj_ref, a_ref, carry_ref,
    y_out, gdelta_out, gx_out, gbc_ref, grate_ref,
    sel, bc, hist, prod, state_ref, fold, delta_ref, x_ref, gy_ref, y_ref, gdelta_ref, gx_ref, sems, out_sems,
):
    el = a_ref.shape[1]
    blocks = el // LANES
    copies = load_blocks((delta_in, x_in, gy_in), (delta_ref, x_ref, gy_ref), sems)
    sel[...] = selector(LANES)
    fold_row = lax.broadcasted_iota(jnp.int32, fold.shape, 0) // LANES
    fold_col = lax.broadcasted_iota(jnp.int32, fold.shape, 1)
    fold[...] = (fold_row + R == fold_col).astype(jnp.bfloat16)
    state_ref[...] = carry_ref[0]

    def enter(p):
        return pl.ds(2 * p * nr, 2 * nr)

    def keep(b, t, state):
        for p in range(NS // 2):
            both = jnp.concatenate([state[2 * p], state[2 * p + 1]], axis=0)
            hist[b, t, enter(p), :] = both.astype(jnp.bfloat16)

    for b in range(blocks):
        keep(b, 0, [carry_ref[0, n, :, b * LANES : (b + 1) * LANES] for n in range(NS)])
    for copy in copies:
        copy.wait()

    def forward(c, none):
        rows = pl.multiple_of(c * (ct * nr), ct * nr)
        bc[...] = spread(proj_ref[pl.ds(rows, ct * nr), :], sel)
        for b in range(blocks):
            lanes = slice(b * LANES, (b + 1) * LANES)
            rate = [jnp.broadcast_to(a_ref[n : n + 1, lanes], (nr, LANES)) for n in range(NS)]

            def steps(s, carried):
                state = list(carried)
                for u in range(uu):
                    at = s * uu + u
                    t = c * ct + at
                    here = pl.ds(t, nr, stride=tt)
                    delta = delta_ref[b, here, :]
                    du = delta * x_ref[b, here, :]
                    near = pl.ds(pl.multiple_of(at * nr, nr), nr)
                    y = None
                    for n in range(NS):
                        b_at, c_at = n * LANES, (NS + n) * LANES
                        decay = jnp.exp2(delta * rate[n])
                        state[n] = decay * state[n] + du * bc[near, b_at : b_at + LANES]
                        term = state[n] * bc[near, c_at : c_at + LANES]
                        y = term if y is None else y + term
                    keep(b, t + 1, state)
                    y_ref[b, here, :] = y
                return tuple(state)

            start = tuple(state_ref[n, :, lanes] for n in range(NS))
            last = lax.fori_loop(0, ct // uu, steps, start)
            for n in range(NS):
                state_ref[n, :, lanes] = last[n]
        return none

    lax.fori_loop(0, tt // ct, forward, 0)
    y_copies = store_blocks((y_ref,), (y_out,), out_sems.at[pl.ds(0, 1)])

    state_ref[...] = carry_ref[1]
    grate_ref[...] = jnp.zeros_like(grate_ref)

    def backward(k, none):
        c = tt // ct - 1 - k
        rows = pl.multiple_of(c * (ct * nr), ct * nr)
        bc[...] = spread(proj_ref[pl.ds(rows, ct * nr), :], sel)
        for b in range(blocks):
            lanes = slice(b * LANES, (b + 1) * LANES)
            for first in (True, False):
                ns = range(0, NS // 2) if first else range(NS // 2, NS)
                pairs = range(ns[0] // 2, ns[-1] // 2 + 1)
                rate = [jnp.broadcast_to(a_ref[n : n + 1, lanes], (nr, LANES)) for n in ns]

                def steps(s, carried):
                    grad, total, after = (list(v) for v in carried)
                    for u in reversed(range(uu)):
                        at = (ct // uu - 1 - s) * uu + u
                        t = c * ct + at
                        here = pl.ds(t, nr, stride=tt)
                        delta = delta_ref[b, here, :]
                        x = x_ref[b, here, :]
                        gy = gy_ref[b, here, :]
                        du = delta * x
                        near = pl.ds(pl.multiple_of(at * nr, nr), nr)
                        along_rate = along_b = None
                        for p in pairs:
                            pair = hist[b, t, enter(p), :].astype(jnp.float32)
                            for n, before in ((2 * p, pair[:nr]), (2 * p + 1, pair[nr:])):
                                i = n - ns[0]
                                to_b_at = slice(n * LANES, (n + 1) * LANES)
                                to_c_at = slice((NS + n) * LANES, (NS + n + 1) * LANES)
                                decay = jnp.exp2(delta * rate[i])
                                grad[i] = grad[i] + gy * bc[near, to_c_at]
                                to_c = after[i] * gy
                                to_b = grad[i] * du
                                if b > 0:
                                    to_c = to_c + prod[near, to_c_at]
                                    to_b = to_b + prod[near, to_b_at]
                                prod[near, to_c_at] = to_c
                                prod[near, to_b_at] = to_b
                                term_b = grad[i] * bc[near, to_b_at]
                                along_b = term_b if along_b is None else along_b + term_b
                                grad[i] = grad[i] * decay
                                weighted = grad[i] * before
                                total[i] = total[i] + weighted * delta
                                term = weighted * rate[i]
                                along_rate = term if along_rate is None else along_rate + term
                                after[i] = before
                        gdelta = along_rate * LN2 + along_b * x
                        gx = along_b * delta
                        if not first:
                            gdelta = gdelta + gdelta_ref[b, here, :]
                            gx = gx + gx_ref[b, here, :]
                        gdelta_ref[b, here, :] = gdelta
                        gx_ref[b, here, :] = gx
                    return tuple(grad), tuple(total), tuple(after)

                after = []
                for p in pairs:
                    pair = hist[b, (c + 1) * ct, enter(p), :].astype(jnp.float32)
                    after += [pair[:nr], pair[nr:]]
                start = (
                    tuple(state_ref[n, :, lanes] for n in ns),
                    tuple(grate_ref[n, :, lanes] for n in ns),
                    tuple(after),
                )
                grad, total, unused = lax.fori_loop(0, ct // uu, steps, start)
                for i, n in enumerate(ns):
                    state_ref[n, :, lanes] = grad[i]
                    grate_ref[n, :, lanes] = total[i]
        gbc_ref[pl.ds(rows, ct * nr), :] = jnp.dot(
            prod[...].astype(jnp.bfloat16), fold[...], preferred_element_type=jnp.float32
        )
        return none

    lax.fori_loop(0, tt // ct, backward, 0)
    late = store_blocks((gdelta_ref, gx_ref), (gdelta_out, gx_out), out_sems.at[pl.ds(1, 2)])
    for copy in y_copies + late:
        copy.wait()


def scan_main(delta, x, gy, proj, rate, carry, nr, tt):
    el = rate.shape[1]
    ct = math.gcd(tt, 32)
    here = pl.BlockSpec(memory_space=pltpu.VMEM)
    away = pl.BlockSpec(memory_space=pl.ANY)
    full = jax.ShapeDtypeStruct((nr * tt, el), jnp.float32)
    blocks = pltpu.VMEM((el // LANES, nr * tt, LANES), jnp.float32)
    return pl.pallas_call(
        functools.partial(main_kernel, nr, tt, ct, min(8, ct)),
        in_specs=[away] * 3 + [here] * 3,
        out_specs=[away] * 3 + [here] * 2,
        out_shape=[
            full,
            full,
            full,
            jax.ShapeDtypeStruct((tt * nr, LANES), jnp.float32),
            jax.ShapeDtypeStruct((NS, nr, el), jnp.float32),
        ],
        scratch_shapes=[
            pltpu.VMEM((256, 2 * NS * LANES), jnp.bfloat16),
            pltpu.VMEM((ct * nr, 2 * NS * LANES), jnp.float32),
            pltpu.VMEM((el // LANES, tt + 1, NS * nr, LANES), jnp.bfloat16),
            pltpu.VMEM((ct * nr, 2 * NS * LANES), jnp.float32),
            pltpu.VMEM((NS, nr, el), jnp.float32),
            pltpu.VMEM((2 * NS * LANES, LANES), jnp.bfloat16),
        ]
        + [blocks] * 6
        + [
            pltpu.SemaphoreType.DMA((3, el // LANES)),
            pltpu.SemaphoreType.DMA((3, el // LANES)),
        ],
        compiler_params=pltpu.CompilerParams(vmem_limit_bytes=63 * MIB),
        name="scan_main",
    )(delta, x, gy, proj, rate, carry)


MESH = pl.DeviceIdType.MESH


def greet(devices):
    barrier = pltpu.get_barrier_semaphore()
    for device in devices:
        pl.semaphore_signal(barrier, inc=1, device_id=device, device_id_type=MESH)
    pl.semaphore_wait(barrier, len(devices))


def remote(source, target, send, recv, device):
    copy = pltpu.make_async_remote_copy(
        src_ref=source, dst_ref=target, send_sem=send, recv_sem=recv, device_id=device, device_id_type=MESH
    )
    copy.start()
    return copy


def row_peers(size):
    me = lax.axis_index("rows")
    half = size // 2
    mine = me // 2
    return me, me % 2, me + 1 - 2 * (me % 2), [lax.rem(mine + k, half) for k in range(half)]


def sum_rows(size, part_of, part, near, total, mail, far, out, sems, use):
    me, parity, partner, others = row_peers(size)
    place = lax.axis_index("seq")
    half = size // 2
    greet([(place, partner)] + [(place, 2 * j + parity) for j in others[1:]])
    first = []
    for j in range(half):
        block = 2 * j + 1 - parity
        part[block] = part_of(block).astype(jnp.bfloat16)
        first.append(
            remote(part.at[block], near.at[j], sems.at[0, j], sems.at[1, j], (place, partner))
        )
    for j in range(half):
        total[j] = part_of(2 * j + parity)
    for copy in first:
        copy.wait()
    second = []
    for k in list(range(1, half)) + [0]:
        j = others[k]
        total[j] = total[j] + near[j].astype(jnp.float32)
        if k:
            mail[j] = total[j].astype(jnp.bfloat16)
            target = (place, 2 * j + parity)
            second.append(remote(mail.at[j], far.at[k], sems.at[2, k], sems.at[3, k], target))
    mine = others[0]
    done = total[mine]
    for k in range(1, half):
        second[k - 1].wait()
        done = done + far[k].astype(jnp.float32)
    out[me] = done.astype(jnp.bfloat16)
    third = []
    for k in range(1, half):
        target = (place, 2 * others[k] + parity)
        third.append(remote(out.at[me], out.at[me], sems.at[4, k], sems.at[5, k], target))
    fourth = [remote(out.at[me], out.at[me], sems.at[6, 0], sems.at[7, 0], (place, partner))]
    use(me)
    for k in range(1, half):
        block = 2 * others[half - k] + parity
        here = pltpu.make_async_remote_copy(
            src_ref=out.at[me], dst_ref=out.at[block], send_sem=sems.at[4, k], recv_sem=sems.at[5, k],
            device_id=(place, partner), device_id_type=MESH,
        )
        here.wait_recv()
        fourth.append(
            remote(out.at[block], out.at[block], sems.at[6, k], sems.at[7, k], (place, partner))
        )
        use(block)
    for k in range(half):
        block = 2 * others[(half - k) % half] + 1 - parity
        here = pltpu.make_async_remote_copy(
            src_ref=out.at[me], dst_ref=out.at[block], send_sem=sems.at[6, k], recv_sem=sems.at[7, k],
            device_id=(place, partner), device_id_type=MESH,
        )
        here.wait_recv()
        use(block)
    for copy in third + fourth:
        copy.wait_send()


def sum_scratch(size, tt):
    half = size // 2
    return [
        pltpu.VMEM((size, tt, LANES), jnp.bfloat16),
        pltpu.VMEM((half, tt, LANES), jnp.bfloat16),
        pltpu.VMEM((half, tt, LANES), jnp.float32),
        pltpu.VMEM((half, tt, LANES), jnp.bfloat16),
        pltpu.VMEM((half, tt, LANES), jnp.bfloat16),
        pltpu.VMEM((size, tt, LANES), jnp.bfloat16),
        pltpu.SemaphoreType.DMA((8, half)),
    ]


def project_kernel(
    size, conv_ref, x_proj_ref, dt_ref, bias_ref, proj_ref, delta_ref, rank_ref,
    part, near, total, mail, far, out, sems,
):
    tt = conv_ref.shape[1]

    def part_of(p):
        return jnp.dot(conv_ref[p], x_proj_ref[...], preferred_element_type=jnp.float32)

    def use(p):
        block = out[p]
        rank_ref[p] = block
        proj_ref[pl.ds(p, tt, stride=size), :] = block.astype(jnp.float32)
        step = jnp.dot(block, dt_ref[...], preferred_element_type=jnp.float32) + bias_ref[...]
        delta_ref[p] = jnp.maximum(step, 0.0) + jnp.log1p(jnp.exp(-jnp.abs(step)))

    sum_rows(size, part_of, part, near, total, mail, far, out, sems, use)


def project(conv_out, x_proj, dt_pad, bias):
    size, tt, el = conv_out.shape
    here = pl.BlockSpec(memory_space=pltpu.VMEM)
    return pl.pallas_call(
        functools.partial(project_kernel, size),
        in_specs=[here] * 4,
        out_specs=[here] * 3,
        out_shape=[
            jax.ShapeDtypeStruct((tt * size, LANES), jnp.float32),
            jax.ShapeDtypeStruct((size, tt, el), jnp.float32),
            jax.ShapeDtypeStruct((size, tt, LANES), jnp.bfloat16),
        ],
        scratch_shapes=sum_scratch(size, tt),
        compiler_params=pltpu.CompilerParams(
            vmem_limit_bytes=40 * MIB, collective_id=0, has_side_effects=True
        ),
        name="project",
    )(conv_out, x_proj, dt_pad, bias)


def back_project_kernel(
    size, low_ref, dt_ref, gbc_ref, out_ref, part, near, total, mail, far, out, sems
):
    tt = low_ref.shape[1]

    def part_of(p):
        ranks = lax.dot_general(
            low_ref[p], dt_ref[...], (((1,), (1,)), ((), ())), preferred_element_type=jnp.float32
        )
        return ranks + gbc_ref[pl.ds(p, tt, stride=size), :]

    def use(p):
        out_ref[p] = out[p]

    sum_rows(size, part_of, part, near, total, mail, far, out, sems, use)


def back_project(low_step, dt_pad, gbc):
    size, tt, unused_el = low_step.shape
    here = pl.BlockSpec(memory_space=pltpu.VMEM)
    return pl.pallas_call(
        functools.partial(back_project_kernel, size),
        in_specs=[here] * 3,
        out_specs=here,
        out_shape=jax.ShapeDtypeStruct((size, tt, LANES), jnp.bfloat16),
        scratch_shapes=sum_scratch(size, tt),
        compiler_params=pltpu.CompilerParams(
            vmem_limit_bytes=40 * MIB, collective_id=1, has_side_effects=True
        ),
        name="back_project",
    )(low_step, dt_pad, gbc)


def carry_kernel(seq, ends_ref, alive_ref, out_ref, mail, land, sems):
    place = lax.axis_index("seq")
    me = lax.axis_index("rows")
    barrier = pltpu.get_barrier_semaphore()
    alive = alive_ref[...][None]

    for step, there in ((-1, place > 0), (1, place < seq - 1)):

        @pl.when(there)
        def _(step=step):
            pl.semaphore_signal(barrier, inc=1, device_id=(place + step, me), device_id_type=MESH)

    pl.semaphore_wait(barrier, (place > 0).astype(jnp.int32) + (place < seq - 1).astype(jnp.int32))

    def hop(way):
        first, last, step = ((0, seq - 1, 1), (seq - 1, 0, -1))[way]
        target = (jnp.clip(place + step, 0, seq - 1), me)
        copy = pltpu.make_async_remote_copy(
            src_ref=mail.at[way], dst_ref=land.at[way], send_sem=sems.at[way, 0], recv_sem=sems.at[way, 1],
            device_id=target, device_id_type=MESH,
        )

        @pl.when(place == first)
        def _():
            out_ref[way] = jnp.zeros_like(out_ref[way])

        @pl.when(place != first)
        def _():
            copy.wait_recv()
            entering = land[way].astype(jnp.float32)
            out_ref[way] = entering * alive if way == 0 else entering

        @pl.when(place != last)
        def _():
            if way == 0:
                leaving = ends_ref[0] + ends_ref[1] * out_ref[0]
            else:
                leaving = (ends_ref[2] + ends_ref[1] * out_ref[1]) * alive
            mail[way] = leaving.astype(jnp.bfloat16)
            copy.start()

    def finish(way):
        last, step = ((seq - 1, 1), (0, -1))[way]
        target = (jnp.clip(place + step, 0, seq - 1), me)

        @pl.when(place != last)
        def _():
            pltpu.make_async_remote_copy(
                src_ref=mail.at[way], dst_ref=land.at[way], send_sem=sems.at[way, 0],
                recv_sem=sems.at[way, 1], device_id=target, device_id_type=MESH,
            ).wait_send()

    @pl.when(place < seq // 2)
    def _():
        hop(0)
        hop(1)

    @pl.when(place >= seq // 2)
    def _():
        hop(1)
        hop(0)

    finish(0)
    finish(1)


def exchange_carry(ends, alive, seq):
    here = pl.BlockSpec(memory_space=pltpu.VMEM)
    shape = ends.shape[1:]
    return pl.pallas_call(
        functools.partial(carry_kernel, seq),
        in_specs=[here] * 2,
        out_specs=here,
        out_shape=jax.ShapeDtypeStruct((2,) + shape, jnp.float32),
        scratch_shapes=[
            pltpu.VMEM((2,) + shape, jnp.bfloat16),
            pltpu.VMEM((2,) + shape, jnp.bfloat16),
            pltpu.SemaphoreType.DMA((2, 2)),
        ],
        compiler_params=pltpu.CompilerParams(
            vmem_limit_bytes=40 * MIB, collective_id=2, has_side_effects=True
        ),
        name="exchange_carry",
    )(ends, alive)


def flip(place, mask):
    for k in range(mask.bit_length()):
        bit = 1 << k
        if mask & bit:
            place = place + bit * (1 - 2 * (lax.div(place, bit) % 2))
    return place


def bit_orders(size):
    rest = [1 << k for k in range(1, size.bit_length() - 1)]
    cut = max(1, len(rest) // 2)
    return [1] + rest, [1] + rest[cut:] + rest[:cut]


def masks_of(bits):
    masks = [0]
    for bit in bits:
        masks = masks + [m | bit for m in masks]
    return masks


def gather_kernel(size, count, *refs):
    sources, outs, (local_sem, send, recv) = refs[:count], refs[count : 2 * count], refs[2 * count :]
    me, place = lax.axis_index("rows"), lax.axis_index("seq")
    greet([(place, flip(me, 1 << k)) for k in range(size.bit_length() - 1)])
    started = []
    kept = []
    for i in range(count):
        copy = pltpu.make_async_copy(sources[i], outs[i].at[me], local_sem.at[i])
        copy.start()
        kept.append(copy)

    def cut(i, h, ref):
        width = outs[i].shape[-1] // 2
        return ref.at[:, pl.ds(h * width, width)]

    def slot(i, h, m):
        return (i, h, m)

    def push(i, h, m, bit):
        source = sources[i] if m == 0 else outs[i].at[flip(me, m)]
        key = slot(i, h, m | bit)
        started.append(
            remote(
                cut(i, h, source), cut(i, h, outs[i].at[flip(me, m)]), send.at[key], recv.at[key],
                (place, flip(me, bit)),
            )
        )

    def arrived(i, h, m):
        key = slot(i, h, m)
        block = cut(i, h, outs[i].at[flip(me, m)])
        pltpu.make_async_remote_copy(
            src_ref=block, dst_ref=block, send_sem=send.at[key], recv_sem=recv.at[key],
            device_id=(place, flip(me, 1)), device_id_type=MESH,
        ).wait_recv()

    orders = [order[1:] + order[:1] for order in bit_orders(size)]
    steps = len(orders[0])
    for i in range(count):
        for h in range(2):
            push(i, h, 0, orders[h][0])
    for i in range(count):
        for h in range(2):
            push(i, h, 0, 1)
    for i in range(count):
        for k in range(1, steps):
            for h in range(2):
                order = orders[h]
                old = masks_of(order[: k - 1])
                if k < steps - 1:
                    for m in old:
                        push(i, h, m, order[k])
                for m in old:
                    fresh = m | order[k - 1]
                    arrived(i, h, fresh)
                    if k < steps - 1:
                        push(i, h, fresh, order[k])
                    push(i, h, fresh, 1)
    for i in range(count):
        for h in range(2):
            for m in masks_of(orders[h][:-1]):
                arrived(i, h, m | 1)
    for copy in started:
        copy.wait_send()
    for copy in kept:
        copy.wait()


def gather_rows(arrays, size):
    count = len(arrays)
    away = pl.BlockSpec(memory_space=pl.ANY)
    return pl.pallas_call(
        functools.partial(gather_kernel, size, count),
        in_specs=[away] * count,
        out_specs=[away] * count,
        out_shape=[jax.ShapeDtypeStruct((size,) + v.shape, v.dtype) for v in arrays],
        scratch_shapes=[
            pltpu.SemaphoreType.DMA((count,)),
            pltpu.SemaphoreType.DMA((count, 2, size)),
            pltpu.SemaphoreType.DMA((count, 2, size)),
        ],
        compiler_params=pltpu.CompilerParams(collective_id=3, has_side_effects=True),
        name="gather_rows",
    )(*arrays)


def by_tiles(rows, tile, body):
    def step(i, none):
        body(pl.ds(pl.multiple_of(i * tile, tile), tile))
        return none

    lax.fori_loop(0, rows // tile, step, 0)


def wait_for(ref, sem):
    pltpu.make_async_copy(ref, ref, sem).wait()


def greet_rows_and_seq(size, seq):
    me, place = lax.axis_index("rows"), lax.axis_index("seq")
    barrier = pltpu.get_barrier_semaphore()
    for mask in range(1, size):
        pl.semaphore_signal(barrier, inc=1, device_id=(place, flip(me, mask)), device_id_type=MESH)
    for step, there in ((-1, place > 0), (1, place < seq - 1)):

        @pl.when(there)
        def _(step=step):
            pl.semaphore_signal(barrier, inc=1, device_id=(place + step, me), device_id_type=MESH)

    near = (place > 0).astype(jnp.int32) + (place < seq - 1).astype(jnp.int32)
    pl.semaphore_wait(barrier, near + size - 1)


class RowScatter:
    def __init__(self, size, part, keep, land, mail, keep_sem, send, recv):
        self.size, self.part, self.keep, self.land, self.mail = size, part, keep, land, mail
        self.keep_sem, self.send, self.recv = keep_sem, send, recv
        self.me, self.place = lax.axis_index("rows"), lax.axis_index("seq")
        self.tt, self.width = part.shape[1], part.shape[2] // 2
        self.orders = bit_orders(size)
        self.steps = len(self.orders[0])
        self.started, self.local = [], []

    @staticmethod
    def scratch(size, tt, width):
        return [
            pltpu.VMEM((size // 2, tt, width), jnp.bfloat16),
            pltpu.VMEM((size - 1, tt, width), jnp.bfloat16),
            pltpu.VMEM((size // 2 - 1, tt, width), jnp.bfloat16),
            pltpu.SemaphoreType.DMA((size // 2,)),
            pltpu.SemaphoreType.DMA((2, size - 1)),
            pltpu.SemaphoreType.DMA((2, size - 1)),
        ]

    def free(self, h, k):
        return masks_of(self.orders[h][k + 1 :])

    def at(self, h, k, m):
        return sum(len(self.free(h, j)) for j in range(k)) + self.free(h, k).index(m)

    def cols(self, h):
        return pl.ds(h * self.width, self.width)

    def receive(self, h, k, m):
        slot = self.at(h, k, m)
        wait_for(self.land.at[slot, :, self.cols(h)], self.recv.at[h, slot])

    def partial_sum(self, h, k, m, rows):
        value = self.keep[m >> 1, rows, self.cols(h)].astype(jnp.float32)
        for j in range(k):
            value = value + self.land[self.at(h, j, m), rows, self.cols(h)].astype(jnp.float32)
        return value

    def start(self):
        for h in range(2):
            self.scatter(h, 0)
        for m in self.free(0, 0):
            copy = pltpu.make_async_copy(
                self.part.at[flip(self.me, m)], self.keep.at[m >> 1], self.keep_sem.at[m >> 1]
            )
            copy.start()
            self.local.append(copy)

    def step(self, k):
        if k == 1:
            for copy in self.local:
                copy.wait()
        for h in range(2):
            self.scatter(h, k)

    def scatter(self, h, k):
        bit = self.orders[h][k]
        for m in self.free(h, k):
            slot = self.at(h, k, m)
            if k == 0:
                source = self.part.at[flip(self.me, m | bit), :, self.cols(h)]
            else:
                for j in range(k):
                    self.receive(h, j, m | bit)
                box = slot - self.size // 2

                def fill(rows, m=m, box=box):
                    value = self.partial_sum(h, k, m | bit, rows)
                    self.mail[box, rows, self.cols(h)] = value.astype(jnp.bfloat16)

                by_tiles(self.tt, 32, fill)
                source = self.mail.at[box, :, self.cols(h)]
            self.started.append(
                remote(
                    source, self.land.at[slot, :, self.cols(h)], self.send.at[h, slot], self.recv.at[h, slot],
                    (self.place, flip(self.me, bit)),
                )
            )

    def finish(self, own):
        for h in range(2):
            for j in range(self.steps):
                self.receive(h, j, 0)

            def fill(rows, h=h):
                own[rows, self.cols(h)] = self.partial_sum(h, self.steps, 0, rows).astype(jnp.bfloat16)

            by_tiles(self.tt, 32, fill)

    def drain(self):
        for copy in self.started:
            copy.wait_send()


class SeqSum:
    def __init__(self, seq, held, land, mail, fill_sem, send, recv):
        self.seq, self.held, self.land, self.mail = seq, held, land, mail
        self.fill_sem, self.send, self.recv = fill_sem, send, recv
        self.me, self.place = lax.axis_index("rows"), lax.axis_index("seq")
        self.behind = (self.place, seq - 1 - self.place)
        self.chunks = held.shape[0]
        self.last_step = self.chunks + seq - 1

    @staticmethod
    def scratch(chunks, block):
        return [
            pltpu.VMEM((chunks,) + block, jnp.bfloat16),
            pltpu.VMEM((2, chunks) + block, jnp.bfloat16),
            pltpu.VMEM((2, chunks) + block, jnp.bfloat16),
            pltpu.SemaphoreType.DMA((chunks,)),
            pltpu.SemaphoreType.DMA((2, chunks)),
            pltpu.SemaphoreType.DMA((2, chunks)),
        ]

    def copy(self, n, way, source):
        target = (jnp.clip(self.place + 1 - 2 * way, 0, self.seq - 1), self.me)
        return pltpu.make_async_remote_copy(
            src_ref=source, dst_ref=self.land.at[way, n], send_sem=self.send.at[way, n],
            recv_sem=self.recv.at[way, n], device_id=target, device_id_type=MESH,
        )

    def hop(self, step, way):
        n = step - self.behind[way]

        @pl.when((n >= 0) & (n < self.chunks))
        def _():
            @pl.when(self.behind[way] == 0)
            def _():
                self.copy(n, way, self.held.at[n]).start()

            @pl.when(self.behind[way] > 0)
            def _():
                self.copy(n, way, self.held.at[n]).wait_recv()

                @pl.when(self.behind[way] < self.seq - 1)
                def _():
                    value = self.held[n].astype(jnp.float32) + self.land[way, n].astype(jnp.float32)
                    self.mail[way, n] = value.astype(jnp.bfloat16)
                    self.copy(n, way, self.mail.at[way, n]).start()

    def advance(self, step, total):
        first = step - jnp.minimum(self.behind[0], self.behind[1])

        @pl.when((first >= 0) & (first < self.chunks))
        def _():
            wait_for(self.held.at[first], self.fill_sem.at[first])

        self.hop(step, 0)
        self.hop(step, 1)
        n = step - jnp.maximum(self.behind[0], self.behind[1])

        @pl.when((n >= 0) & (n < self.chunks))
        def _():
            for ways, there in (
                ((1,), self.behind[0] == 0),
                ((0,), self.behind[1] == 0),
                ((0, 1), (self.behind[0] > 0) & (self.behind[1] > 0)),
            ):

                @pl.when(there)
                def _(ways=ways):
                    value = self.held[n].astype(jnp.float32)
                    for way in ways:
                        value = value + self.land[way, n].astype(jnp.float32)
                    total[n] = value.astype(jnp.bfloat16)

    def run(self, first, last, total):
        def body(step, none):
            self.advance(step, total)
            return none

        lax.fori_loop(first, last, body, 0)

    def drain(self):
        for way in range(2):

            @pl.when(self.behind[way] < self.seq - 1)
            def _(way=way):
                def sent(n, none):
                    self.copy(n, way, self.held.at[n]).wait_send()
                    return none

                lax.fori_loop(0, self.chunks, sent, 0)


def chunk_order(size):
    return sorted(range(size), key=lambda m: (m > 1, (m >> 1).bit_count(), m))


def tail_kernel(size, seq, *refs):
    branch, normed, weight, out_w, small = refs[:5]
    branch_own, normed_own, total = refs[5:8]
    scatter_a = RowScatter(size, branch, *refs[8:14])
    scatter_b = RowScatter(size, normed, *refs[14:20])
    held, land, mail, fill_sem, zsend, zrecv, swap_send = refs[20:]
    chain = SeqSum(seq, held, land, mail, fill_sem, zsend, zrecv)
    me, place = lax.axis_index("rows"), lax.axis_index("seq")
    rows, cols = held.shape[1:]
    greet_rows_and_seq(size, seq)
    scatter_a.start()
    n = 0
    for source in (out_w, small):
        for i in range(source.shape[0] // rows):
            for j in range(source.shape[1] // cols):
                piece = source.at[pl.ds(i * rows, rows), pl.ds(j * cols, cols)]
                pltpu.make_async_copy(piece, held.at[n], fill_sem.at[n]).start()
                n += 1
    sent = []
    for m in chunk_order(size):
        for i in range(weight.shape[1] // rows):
            piece = weight.at[flip(me, m), pl.ds(i * rows, rows), :]
            if m == 0:
                pltpu.make_async_copy(piece, held.at[n], fill_sem.at[n]).start()
            else:
                target = (place, flip(me, m))
                sent.append(remote(piece, held.at[n], swap_send.at[n], fill_sem.at[n], target))
            n += 1
    scatter_b.start()
    jobs = []
    for k in range(1, scatter_a.steps):
        jobs += [functools.partial(scatter_a.step, k), functools.partial(scatter_b.step, k)]
    jobs += [functools.partial(scatter_a.finish, branch_own), functools.partial(scatter_b.finish, normed_own)]
    done = 0
    for i, job in enumerate(jobs):
        upto = chain.last_step * (i + 1) // (len(jobs) + 1)
        chain.run(done, upto, total)
        done = upto
        job()
    chain.run(done, chain.last_step, total)
    scatter_a.drain()
    scatter_b.drain()
    for copy in sent:
        copy.wait_send()
    chain.drain()


def reduce_all(branch, normed, weight, out_w, small, size, seq):
    away = pl.BlockSpec(memory_space=pl.ANY)
    here = pl.BlockSpec(memory_space=pltpu.VMEM)
    tt, width = branch.shape[1:]
    share, cols = weight.shape[1:]
    rows = share // 2
    chunks = (weight.size + out_w.size + small.size) // (rows * cols)
    return pl.pallas_call(
        functools.partial(tail_kernel, size, seq),
        in_specs=[away] * 5,
        out_specs=[here] * 3,
        out_shape=[jax.ShapeDtypeStruct((tt, width), jnp.bfloat16)] * 2
        + [jax.ShapeDtypeStruct((chunks, rows, cols), jnp.bfloat16)],
        scratch_shapes=RowScatter.scratch(size, tt, width) * 2
        + SeqSum.scratch(chunks, (rows, cols))
        + [pltpu.SemaphoreType.DMA((chunks,))],
        compiler_params=pltpu.CompilerParams(
            vmem_limit_bytes=60 * MIB, collective_id=4, has_side_effects=True
        ),
        name="reduce_all",
    )(branch, normed, weight, out_w, small)


def from_behind(value, axis, steps):
    count = lax.axis_size(axis)
    first, last = (max(0, -steps), min(count, count - steps))
    return lax.ppermute(value, axis, [(source, source + steps) for source in range(first, last)])


def shortened(x):
    return x.astype(jnp.bfloat16)


def contract_rows(left, right):
    return lax.dot_general(left, right, (((0,), (0,)), ((), ())), preferred_element_type=jnp.float32)


def contract_cols(left, right):
    return lax.dot_general(left, right, (((1,), (1,)), ((), ())), preferred_element_type=jnp.float32)


def local(
    tokens, resets, norm_gain, in_proj, x_proj, dt_proj, conv_weight, conv_bias, dt_bias, a_log, out_proj,
    cotangent,
):
    size = lax.axis_size("rows")
    seq = lax.axis_size("seq")
    rd, tt, unused_d = tokens.shape
    nr = rd * size
    el = E // size
    count = nr * tt
    assert rd == 1 and ITEM % tt == 0 and nr % 8 == 0

    w_in = lax.all_to_all(
        in_proj.reshape(D // size, 2, size, el), "rows", split_axis=2, concat_axis=0, tiled=True
    ).reshape(D, 2 * el)
    share = D // size
    notes = jnp.zeros((16, -(-share // 256) * 256), jnp.bfloat16)
    notes = notes.at[0, :share].set(norm_gain).at[1, 0].set(1.0 - resets[0, 0].astype(jnp.bfloat16))
    all_tokens, all_cot, all_notes = gather_rows([tokens[0], cotangent[0], notes], size)
    all_tokens, all_cot = all_tokens.reshape(count, D), all_cot.reshape(count, D)
    gain = all_notes[:, 0, :share].reshape(D).astype(jnp.float32)
    alive = all_notes[:, 1, :1].astype(jnp.float32)

    flat = all_tokens.astype(jnp.float32)
    inv_all = lax.rsqrt(jnp.mean(flat * flat, axis=1, keepdims=True) + epsilon)
    normed = (flat * inv_all * gain).astype(jnp.bfloat16)
    mixed = jnp.dot(normed, w_in, preferred_element_type=jnp.float32)
    conv_in = mixed[:, :el].astype(jnp.bfloat16).reshape(nr, tt, el)
    gate_pre = mixed[:, el:]
    left_rim = from_behind(conv_in[:, tt - (KC - 1) :], "seq", 1)
    extended = jnp.concatenate([left_rim, conv_in], axis=1)
    taps = conv_weight.astype(jnp.float32)
    conv_pre = conv_bias.astype(jnp.float32) + sum(
        taps[k] * extended[:, k : k + tt].astype(jnp.float32) for k in range(KC)
    )
    conv_out = jax.nn.silu(conv_pre).astype(jnp.bfloat16).reshape(count, el)
    dt_pad = jnp.pad(dt_proj, ((0, LANES - R), (0, 0)))
    proj_t, step_size, rank_all = project(
        conv_out.reshape(nr, tt, el), x_proj, dt_pad, dt_bias.astype(jnp.float32)[None]
    )
    step_size = step_size.reshape(count, el)
    rank_part = rank_all.reshape(count, LANES)[:, :R]
    decay_rate = -jnp.exp(a_log.astype(jnp.float32))
    rate2 = decay_rate * LOG2E
    conv_float = conv_out.astype(jnp.float32)

    grad_gated = contract_cols(all_cot, out_proj)
    gate_sig = jax.nn.sigmoid(gate_pre)
    gate_act = gate_pre * gate_sig
    grad_y = grad_gated * gate_act

    wide = -(-el // LANES) * LANES
    extra = [(0, 0), (0, wide - el)]
    scanned = [jnp.pad(v, extra) for v in (step_size, conv_float, grad_y)]
    rate2 = jnp.pad(rate2, extra)
    ends = scan_ends(*scanned, proj_t, rate2, nr, tt)
    carry = exchange_carry(ends, alive, seq)
    scan_y, grad_delta, grad_input, grad_bc, grate = scan_main(
        *scanned, proj_t, rate2, carry, nr, tt
    )
    scan_y, grad_delta, grad_input = scan_y[:, :el], grad_delta[:, :el], grad_input[:, :el]
    grate = grate[:, :, :el]
    grad_a_log = jnp.sum(grate, axis=1) * decay_rate

    gated = (scan_y * gate_act).astype(jnp.bfloat16)
    branch = jnp.dot(gated, out_proj, preferred_element_type=jnp.float32).astype(jnp.bfloat16)
    grad_out_proj = contract_rows(gated, all_cot)
    grad_gate_pre = grad_gated * scan_y * gate_sig * (1.0 + gate_pre * (1.0 - gate_sig))

    grad_step_pre = grad_delta * -jnp.expm1(-step_size)
    grad_dt_bias = jnp.sum(grad_step_pre, axis=0)
    low_step = grad_step_pre.astype(jnp.bfloat16)
    grad_dt_proj = contract_rows(rank_part, low_step)
    grad_projected = back_project(low_step.reshape(nr, tt, el), dt_pad, grad_bc).reshape(count, LANES)
    grad_x_proj = contract_rows(conv_out, grad_projected)
    grad_conv_out = contract_cols(grad_projected, x_proj) + grad_input
    conv_sig = jax.nn.sigmoid(conv_pre).reshape(count, el)
    conv_flat = conv_pre.reshape(count, el)
    grad_conv_pre = (grad_conv_out * conv_sig * (1.0 + conv_flat * (1.0 - conv_sig))).reshape(nr, tt, el)
    grad_conv_bias = jnp.sum(grad_conv_pre, axis=(0, 1))
    grad_taps = jnp.stack(
        [
            jnp.sum(grad_conv_pre * extended[:, k : k + tt].astype(jnp.float32), axis=(0, 1))
            for k in range(KC)
        ]
    )
    grad_ext = sum(
        jnp.pad(taps[k] * grad_conv_pre, ((0, 0), (k, KC - 1 - k), (0, 0))) for k in range(KC)
    )
    right_rim = from_behind(shortened(grad_ext[:, : KC - 1]), "seq", -1)
    grad_conv_in = grad_ext[:, KC - 1 :] + jnp.pad(
        right_rim.astype(jnp.float32), ((0, 0), (tt - (KC - 1), 0), (0, 0))
    )
    grad_mixed = jnp.concatenate([grad_conv_in.reshape(count, el), grad_gate_pre], axis=1).astype(
        jnp.bfloat16
    )
    grad_in_proj = contract_rows(normed, grad_mixed).astype(jnp.bfloat16)
    grad_normed_part = contract_cols(grad_mixed, w_in).astype(jnp.bfloat16)
    small = jnp.concatenate(
        [grad_x_proj.T, grad_dt_proj, grad_taps, grad_conv_bias[None], grad_dt_bias[None], grad_a_log],
        axis=0,
    )
    piece = (share // 2, 2 * el)
    folded = shortened(small)
    folded = jnp.pad(folded, ((0, -folded.shape[0] % 2), (0, 0)))
    high = folded.shape[0] // 2
    folded = jnp.concatenate([folded[:high], folded[high:]], axis=1)
    folded = jnp.pad(folded, ((0, -high % piece[0]), (0, 0)))
    branch_own, grad_normed, summed = reduce_all(
        branch.reshape(nr, tt, D), grad_normed_part.reshape(nr, tt, D),
        grad_in_proj.reshape(size, share, 2 * el), shortened(grad_out_proj), folded, size, seq,
    )
    summed = summed.astype(jnp.float32)
    out_rows, out_cols = el // piece[0], D // piece[1]
    at = out_rows * out_cols
    sum_out = jnp.swapaxes(summed[:at].reshape(out_rows, out_cols, *piece), 1, 2).reshape(el, D)
    folded = summed[at : at + folded.shape[0] // piece[0]].reshape(folded.shape)
    small = jnp.concatenate([folded[:high, :el], folded[:high, el:]], axis=0)
    blocks = summed[-2 * size :].reshape(size, share, 2, el)
    me = lax.axis_index("rows")
    places = [chunk_order(size).index(m) for m in range(size)]
    order = jnp.array(places)[jnp.array(range(size)) ^ me]
    sum_in = jnp.moveaxis(blocks[order], 0, 2).reshape(share, 2 * E)
    block_out = (tokens.astype(jnp.float32) + branch_own[None].astype(jnp.float32)).astype(jnp.bfloat16)
    grad_normed = grad_normed[None].astype(jnp.float32)

    own = tokens.astype(jnp.float32)
    inv = lax.rsqrt(jnp.mean(own * own, axis=2, keepdims=True) + epsilon)
    gain_own = jnp.sum(in_proj.astype(jnp.float32) * sum_in, axis=1) / norm_gain.astype(jnp.float32)
    grad_hat = grad_normed * gain
    grad_norm_in = inv * (
        grad_hat - own * (inv * inv) * jnp.mean(grad_hat * own, axis=2, keepdims=True)
    )
    d_tokens = (cotangent.astype(jnp.float32) + grad_norm_in).astype(jnp.bfloat16)

    cuts = [128, R, KC, 1, 1, NS]
    parts = []
    at = 0
    for cut in cuts:
        parts.append(small[at : at + cut])
        at += cut
    return (
        block_out,
        d_tokens,
        gain_own,
        sum_in,
        parts[0].T,
        parts[1],
        parts[2],
        parts[3][0],
        parts[4][0],
        parts[5],
        sum_out,
    )


def solution(mesh):
    in_specs = (
        P("rows", "seq", None),
        P("rows", "seq"),
        P("rows"),
        P("rows", None),
        P("rows", None),
        P(None, "rows"),
        P(None, "rows"),
        P("rows"),
        P("rows"),
        P(None, "rows"),
        P("rows", None),
        P("rows", "seq", None),
    )
    out_specs = (
        P("rows", "seq", None),
        P("rows", "seq", None),
        P("rows"),
        P("rows", None),
        P("rows", None),
        P(None, "rows"),
        P(None, "rows"),
        P("rows"),
        P("rows"),
        P(None, "rows"),
        P("rows", None),
    )
    return jax.shard_map(local, mesh=mesh, in_specs=in_specs, out_specs=out_specs, check_vma=False)
```

```python
import functools
import math

import jax
import jax.numpy as jnp
from jax import lax
from jax.experimental import pallas as pl
from jax.experimental.pallas import tpu as pltpu
from jax.sharding import PartitionSpec as P

D = 1536
E = 3072
R = 96
NS = 16
KC = 4
ITEM = 256

epsilon = 1e-05
LOG2E = 1.4426950408889634
LN2 = 0.6931471805599453
MIB = 2**20


LANES = 128


def pad_lanes(lanes):
    return -(-lanes // LANES) * LANES


def selector(wide):
    row = lax.broadcasted_iota(jnp.int32, (LANES, 2 * NS * wide), 0)
    col = lax.broadcasted_iota(jnp.int32, (LANES, 2 * NS * wide), 1) // wide
    return (row == col + R).astype(jnp.bfloat16)


def spread(proj, sel_ref):
    return jnp.dot(proj.astype(jnp.bfloat16), sel_ref[...], preferred_element_type=jnp.float32)


def copy_all(sources, targets, sems):
    copies = []
    for i, (source, target) in enumerate(zip(sources, targets)):
        copies.append(pltpu.make_async_copy(source, target, sems.at[i]))
        copies[-1].start()
    return copies


def ends_kernel(
    seq, nr, tt, ct, uu, delta_in, x_in, gy_in, proj_ref, a_ref, alive_ref, carry_ref,
    out_ref, mail, land, carry_sems, sel, bc, delta_ref, x_ref, gy_ref, sems,
):
    el = a_ref.shape[1]
    carry = Carry(seq, out_ref, alive_ref, carry_ref, mail, land, carry_sems)
    greet_seq(seq)
    half = NS // 2
    copies = copy_all((delta_in, x_in, gy_in), (delta_ref, x_ref, gy_ref), sems)
    sel[...] = selector(LANES)
    out_ref[0] = jnp.zeros((NS, nr, el), jnp.float32)
    out_ref[1] = jnp.ones((NS, nr, el), jnp.float32)
    out_ref[2] = jnp.zeros((NS, nr, el), jnp.float32)
    for copy in copies:
        copy.wait()

    def chunk(c, none):
        rows = pl.multiple_of(c * (ct * nr), ct * nr)
        bc[...] = spread(proj_ref[pl.ds(rows, ct * nr), :], sel)
        for b in range(el // LANES):
            lanes = slice(b * LANES, (b + 1) * LANES)
            for n0 in range(0, NS, half):
                ns = range(n0, n0 + half)
                rate = [jnp.broadcast_to(a_ref[n : n + 1, lanes], (nr, LANES)) for n in ns]

                def steps(s, carried):
                    state, through, back = (list(v) for v in carried)
                    for u in range(uu):
                        at = s * uu + u
                        here = pl.ds(pl.multiple_of((c * ct + at) * nr, nr), nr)
                        delta = delta_ref[b, here, :]
                        gy = gy_ref[b, here, :]
                        du = delta * x_ref[b, here, :]
                        near = pl.ds(pl.multiple_of(at * nr, nr), nr)
                        for i, n in enumerate(ns):
                            b_at, c_at = n * LANES, (NS + n) * LANES
                            decay = jnp.exp2(delta * rate[i])
                            state[i] = decay * state[i] + du * bc[near, b_at : b_at + LANES]
                            through[i] = through[i] * decay
                            back[i] = back[i] + through[i] * (gy * bc[near, c_at : c_at + LANES])
                    return tuple(state), tuple(through), tuple(back)

                start = tuple(tuple(out_ref[k, n, :, lanes] for n in ns) for k in range(3))
                last = lax.fori_loop(0, ct // uu, steps, start)
                for k in range(3):
                    for i, n in enumerate(ns):
                        out_ref[k, n, :, lanes] = last[k][i]
        return none

    lax.fori_loop(0, tt // ct, chunk, 0)
    carry.both()
    carry.drain()


def scan_ends(delta, x, gy, proj, rate, alive, nr, tt, seq):
    el = rate.shape[1]
    ct = math.gcd(tt, 32)
    here = pl.BlockSpec(memory_space=pltpu.VMEM)
    away = pl.BlockSpec(memory_space=pl.ANY)
    blocks = pltpu.VMEM((el // LANES, nr * tt, LANES), jnp.float32)
    return pl.pallas_call(
        functools.partial(ends_kernel, seq, nr, tt, ct, min(8, ct)),
        in_specs=[away] * 3 + [here] * 3,
        out_specs=here,
        out_shape=jax.ShapeDtypeStruct((2, NS, nr, el), jnp.float32),
        scratch_shapes=[pltpu.VMEM((3, NS, nr, el), jnp.float32)]
        + Carry.scratch((NS, nr, el))
        + [
            pltpu.VMEM((LANES, 2 * NS * LANES), jnp.bfloat16),
            pltpu.VMEM((ct * nr, 2 * NS * LANES), jnp.float32),
            blocks,
            blocks,
            blocks,
            pltpu.SemaphoreType.DMA((3,)),
        ],
        compiler_params=pltpu.CompilerParams(
            vmem_limit_bytes=56 * MIB, collective_id=2, has_side_effects=True
        ),
        name="scan_ends",
    )(delta, x, gy, proj, rate, alive)


def main_kernel(
    nr, tt, ct, uu,
    delta_in, x_in, gy_in, proj_ref, a_ref, carry_ref,
    y_out, gdelta_out, gx_out, gbc_ref, grate_ref,
    sel, bc, hist, prod, state_ref, fold, delta_ref, x_ref, gy_ref, y_ref, gdelta_ref, gx_ref, sems, out_sems,
):
    el = a_ref.shape[1]
    blocks = el // LANES
    copies = copy_all((delta_in, x_in, gy_in), (delta_ref, x_ref, gy_ref), sems)
    sel[...] = selector(LANES)
    fold_row = lax.broadcasted_iota(jnp.int32, fold.shape, 0) // LANES
    fold_col = lax.broadcasted_iota(jnp.int32, fold.shape, 1)
    fold[...] = (fold_row + R == fold_col).astype(jnp.bfloat16)
    state_ref[...] = carry_ref[0]

    def enter(p):
        return pl.ds(2 * p * nr, 2 * nr)

    def keep(b, t, state):
        for p in range(NS // 2):
            both = jnp.concatenate([state[2 * p], state[2 * p + 1]], axis=0)
            hist[b, t, enter(p), :] = both.astype(jnp.bfloat16)

    for b in range(blocks):
        keep(b, 0, [carry_ref[0, n, :, b * LANES : (b + 1) * LANES] for n in range(NS)])
    for copy in copies:
        copy.wait()

    def forward(c, none):
        rows = pl.multiple_of(c * (ct * nr), ct * nr)
        bc[...] = spread(proj_ref[pl.ds(rows, ct * nr), :], sel)
        for b in range(blocks):
            lanes = slice(b * LANES, (b + 1) * LANES)
            rate = [jnp.broadcast_to(a_ref[n : n + 1, lanes], (nr, LANES)) for n in range(NS)]

            def steps(s, carried):
                state = list(carried)
                for u in range(uu):
                    at = s * uu + u
                    t = c * ct + at
                    here = pl.ds(pl.multiple_of(t * nr, nr), nr)
                    delta = delta_ref[b, here, :]
                    du = delta * x_ref[b, here, :]
                    near = pl.ds(pl.multiple_of(at * nr, nr), nr)
                    y = None
                    for n in range(NS):
                        b_at, c_at = n * LANES, (NS + n) * LANES
                        decay = jnp.exp2(delta * rate[n])
                        state[n] = decay * state[n] + du * bc[near, b_at : b_at + LANES]
                        term = state[n] * bc[near, c_at : c_at + LANES]
                        y = term if y is None else y + term
                    keep(b, t + 1, state)
                    y_ref[b, here, :] = y
                return tuple(state)

            start = tuple(state_ref[n, :, lanes] for n in range(NS))
            last = lax.fori_loop(0, ct // uu, steps, start)
            for n in range(NS):
                state_ref[n, :, lanes] = last[n]
        return none

    lax.fori_loop(0, tt // ct, forward, 0)
    y_copies = copy_all((y_ref,), (y_out,), out_sems.at[pl.ds(0, 1)])

    state_ref[...] = carry_ref[1]
    grate_ref[...] = jnp.zeros_like(grate_ref)

    def backward(k, none):
        c = tt // ct - 1 - k
        rows = pl.multiple_of(c * (ct * nr), ct * nr)
        bc[...] = spread(proj_ref[pl.ds(rows, ct * nr), :], sel)
        for b in range(blocks):
            lanes = slice(b * LANES, (b + 1) * LANES)
            for first in (True, False):
                ns = range(0, NS // 2) if first else range(NS // 2, NS)
                pairs = range(ns[0] // 2, ns[-1] // 2 + 1)
                rate = [jnp.broadcast_to(a_ref[n : n + 1, lanes], (nr, LANES)) for n in ns]

                def steps(s, carried):
                    grad, total, after = (list(v) for v in carried)
                    for u in reversed(range(uu)):
                        at = (ct // uu - 1 - s) * uu + u
                        t = c * ct + at
                        here = pl.ds(pl.multiple_of(t * nr, nr), nr)
                        delta = delta_ref[b, here, :]
                        x = x_ref[b, here, :]
                        gy = gy_ref[b, here, :]
                        du = delta * x
                        near = pl.ds(pl.multiple_of(at * nr, nr), nr)
                        along_rate = along_b = None
                        for p in pairs:
                            pair = hist[b, t, enter(p), :].astype(jnp.float32)
                            for n, before in ((2 * p, pair[:nr]), (2 * p + 1, pair[nr:])):
                                i = n - ns[0]
                                to_b_at = slice(n * LANES, (n + 1) * LANES)
                                to_c_at = slice((NS + n) * LANES, (NS + n + 1) * LANES)
                                decay = jnp.exp2(delta * rate[i])
                                grad[i] = grad[i] + gy * bc[near, to_c_at]
                                to_c = after[i] * gy
                                to_b = grad[i] * du
                                if b > 0:
                                    to_c = to_c + prod[near, to_c_at]
                                    to_b = to_b + prod[near, to_b_at]
                                prod[near, to_c_at] = to_c
                                prod[near, to_b_at] = to_b
                                term_b = grad[i] * bc[near, to_b_at]
                                along_b = term_b if along_b is None else along_b + term_b
                                grad[i] = grad[i] * decay
                                weighted = grad[i] * before
                                total[i] = total[i] + weighted * delta
                                term = weighted * rate[i]
                                along_rate = term if along_rate is None else along_rate + term
                                after[i] = before
                        gdelta = along_rate * LN2 + along_b * x
                        gx = along_b * delta
                        if not first:
                            gdelta = gdelta + gdelta_ref[b, here, :]
                            gx = gx + gx_ref[b, here, :]
                        gdelta_ref[b, here, :] = gdelta
                        gx_ref[b, here, :] = gx
                    return tuple(grad), tuple(total), tuple(after)

                after = []
                for p in pairs:
                    pair = hist[b, (c + 1) * ct, enter(p), :].astype(jnp.float32)
                    after += [pair[:nr], pair[nr:]]
                start = (
                    tuple(state_ref[n, :, lanes] for n in ns),
                    tuple(grate_ref[n, :, lanes] for n in ns),
                    tuple(after),
                )
                grad, total, unused = lax.fori_loop(0, ct // uu, steps, start)
                for i, n in enumerate(ns):
                    state_ref[n, :, lanes] = grad[i]
                    grate_ref[n, :, lanes] = total[i]
        gbc_ref[pl.ds(rows, ct * nr), :] = jnp.dot(
            prod[...].astype(jnp.bfloat16), fold[...], preferred_element_type=jnp.float32
        )
        return none

    lax.fori_loop(0, tt // ct, backward, 0)
    late = copy_all((gdelta_ref, gx_ref), (gdelta_out, gx_out), out_sems.at[pl.ds(1, 2)])
    for copy in y_copies + late:
        copy.wait()


def scan_main(delta, x, gy, proj, rate, carry, nr, tt):
    el = rate.shape[1]
    ct = math.gcd(tt, 32)
    here = pl.BlockSpec(memory_space=pltpu.VMEM)
    away = pl.BlockSpec(memory_space=pl.ANY)
    full = jax.ShapeDtypeStruct((el // LANES, tt * nr, LANES), jnp.float32)
    blocks = pltpu.VMEM((el // LANES, nr * tt, LANES), jnp.float32)
    return pl.pallas_call(
        functools.partial(main_kernel, nr, tt, ct, min(8, ct)),
        in_specs=[away] * 3 + [here] * 3,
        out_specs=[away] * 3 + [here] * 2,
        out_shape=[
            full,
            full,
            full,
            jax.ShapeDtypeStruct((tt * nr, LANES), jnp.float32),
            jax.ShapeDtypeStruct((NS, nr, el), jnp.float32),
        ],
        scratch_shapes=[
            pltpu.VMEM((LANES, 2 * NS * LANES), jnp.bfloat16),
            pltpu.VMEM((ct * nr, 2 * NS * LANES), jnp.float32),
            pltpu.VMEM((el // LANES, tt + 1, NS * nr, LANES), jnp.bfloat16),
            pltpu.VMEM((ct * nr, 2 * NS * LANES), jnp.float32),
            pltpu.VMEM((NS, nr, el), jnp.float32),
            pltpu.VMEM((2 * NS * LANES, LANES), jnp.bfloat16),
        ]
        + [blocks] * 6
        + [
            pltpu.SemaphoreType.DMA((3,)),
            pltpu.SemaphoreType.DMA((3,)),
        ],
        compiler_params=pltpu.CompilerParams(vmem_limit_bytes=63 * MIB),
        name="scan_main",
    )(delta, x, gy, proj, rate, carry)


MESH = pl.DeviceIdType.MESH


def greet(devices):
    barrier = pltpu.get_barrier_semaphore()
    for device in devices:
        pl.semaphore_signal(barrier, inc=1, device_id=device, device_id_type=MESH)
    pl.semaphore_wait(barrier, len(devices))


def remote(source, target, send, recv, device):
    copy = pltpu.make_async_remote_copy(
        src_ref=source, dst_ref=target, send_sem=send, recv_sem=recv, device_id=device, device_id_type=MESH
    )
    copy.start()
    return copy


def row_peers(size):
    me = lax.axis_index("rows")
    half = size // 2
    mine = me // 2
    return me, me % 2, me + 1 - 2 * (me % 2), [lax.rem(mine + k, half) for k in range(half)]


def sum_rows(size, part_of, part, near, total, mail, far, out, sems, use):
    me, parity, partner, others = row_peers(size)
    place = lax.axis_index("seq")
    half = size // 2
    greet([(place, partner)] + [(place, 2 * j + parity) for j in others[1:]])
    first = []
    for j in range(half):
        block = 2 * j + 1 - parity
        part[block] = part_of(block).astype(jnp.bfloat16)
        first.append(
            remote(part.at[block], near.at[j], sems.at[0, j], sems.at[1, j], (place, partner))
        )
    for j in range(half):
        total[j] = part_of(2 * j + parity)
    exchange_sums(size, near, total, mail, far, out, sems, use)
    for copy in first:
        copy.wait_send()


def exchange_sums(size, near, total, mail, far, out, sems, use, between=None):
    me, parity, partner, others = row_peers(size)
    place = lax.axis_index("seq")
    half = size // 2
    second = []
    for k in list(range(1, half)) + [0]:
        j = others[k]
        wait_for(near.at[j], sems.at[1, j])
        total[j] = total[j] + near[j].astype(jnp.float32)
        if k:
            mail[j] = total[j].astype(jnp.bfloat16)
            target = (place, 2 * j + parity)
            second.append(remote(mail.at[j], far.at[k], sems.at[2, k], sems.at[3, k], target))
    mine = others[0]
    done = total[mine]
    for k in range(1, half):
        wait_for(far.at[k], sems.at[3, k])
        done = done + far[k].astype(jnp.float32)
    out[me] = done.astype(jnp.bfloat16)
    third = []
    for k in range(1, half):
        target = (place, 2 * others[k] + parity)
        third.append(remote(out.at[me], out.at[me], sems.at[4, k], sems.at[5, k], target))
    fourth = [remote(out.at[me], out.at[me], sems.at[6, 0], sems.at[7, 0], (place, partner))]
    use(me)
    for k in range(1, half):
        block = 2 * others[half - k] + parity
        wait_for(out.at[block], sems.at[5, k])
        fourth.append(
            remote(out.at[block], out.at[block], sems.at[6, k], sems.at[7, k], (place, partner))
        )
        use(block)
    for k in range(half):
        block = 2 * others[(half - k) % half] + 1 - parity
        wait_for(out.at[block], sems.at[7, k])
        use(block)
    if between:
        between()
    for copy in second + third + fourth:
        copy.wait_send()


def sum_scratch(size, tt):
    half = size // 2
    return [
        pltpu.VMEM((size, tt, LANES), jnp.bfloat16),
        pltpu.VMEM((half, tt, LANES), jnp.bfloat16),
        pltpu.VMEM((half, tt, LANES), jnp.float32),
        pltpu.VMEM((half, tt, LANES), jnp.bfloat16),
        pltpu.VMEM((half, tt, LANES), jnp.bfloat16),
        pltpu.VMEM((size, tt, LANES), jnp.bfloat16),
        pltpu.SemaphoreType.DMA((8, half)),
    ]


def back_project_kernel(
    size, low_ref, dt_ref, gbc_ref, out_ref, part, near, total, mail, far, out, sems
):
    tt = low_ref.shape[1]

    def part_of(p):
        ranks = lax.dot_general(
            low_ref[p], dt_ref[...], (((1,), (1,)), ((), ())), preferred_element_type=jnp.float32
        )
        return ranks + gbc_ref[pl.ds(p, tt, stride=size), :]

    def use(p):
        out_ref[p] = out[p]

    sum_rows(size, part_of, part, near, total, mail, far, out, sems, use)


def back_project(low_step, dt_pad, gbc):
    size, tt, unused_el = low_step.shape
    here = pl.BlockSpec(memory_space=pltpu.VMEM)
    return pl.pallas_call(
        functools.partial(back_project_kernel, size),
        in_specs=[here] * 3,
        out_specs=here,
        out_shape=jax.ShapeDtypeStruct((size, tt, LANES), jnp.bfloat16),
        scratch_shapes=sum_scratch(size, tt),
        compiler_params=pltpu.CompilerParams(
            vmem_limit_bytes=40 * MIB, collective_id=1, has_side_effects=True
        ),
        name="back_project",
    )(low_step, dt_pad, gbc)


class Carry:
    def __init__(self, seq, ends, alive, out, mail, land, sems):
        self.seq, self.ends, self.alive, self.out = seq, ends, alive, out
        self.mail, self.land, self.sems = mail, land, sems
        self.me, self.place = lax.axis_index("rows"), lax.axis_index("seq")

    @staticmethod
    def scratch(shape):
        return [
            pltpu.VMEM((2,) + shape, jnp.bfloat16),
            pltpu.VMEM((2,) + shape, jnp.bfloat16),
            pltpu.SemaphoreType.DMA((2, 2)),
        ]

    def copy(self, way):
        target = (jnp.clip(self.place + 1 - 2 * way, 0, self.seq - 1), self.me)
        return pltpu.make_async_remote_copy(
            src_ref=self.mail.at[way], dst_ref=self.land.at[way], send_sem=self.sems.at[way, 0],
            recv_sem=self.sems.at[way, 1], device_id=target, device_id_type=MESH,
        )

    def hop(self, way):
        first, last = ((0, self.seq - 1), (self.seq - 1, 0))[way]
        alive = self.alive[...][None]

        @pl.when(self.place == first)
        def _():
            self.out[way] = jnp.zeros_like(self.out[way])

        @pl.when(self.place != first)
        def _():
            self.copy(way).wait_recv()
            entering = self.land[way].astype(jnp.float32)
            self.out[way] = entering * alive if way == 0 else entering

        @pl.when(self.place != last)
        def _():
            if way == 0:
                leaving = self.ends[0] + self.ends[1] * self.out[0]
            else:
                leaving = (self.ends[2] + self.ends[1] * self.out[1]) * alive
            self.mail[way] = leaving.astype(jnp.bfloat16)
            self.copy(way).start()

    def both(self):
        @pl.when(self.place < self.seq // 2)
        def _():
            self.hop(0)
            self.hop(1)

        @pl.when(self.place >= self.seq // 2)
        def _():
            self.hop(1)
            self.hop(0)

    def drain(self):
        for way, last in ((0, self.seq - 1), (1, 0)):

            @pl.when(self.place != last)
            def _(way=way):
                self.copy(way).wait_send()


def flip(place, mask):
    for k in range(mask.bit_length()):
        bit = 1 << k
        if mask & bit:
            place = place + bit * (1 - 2 * (lax.div(place, bit) % 2))
    return place


def bit_orders(size):
    rest = [1 << k for k in range(1, size.bit_length() - 1)]
    cut = max(1, len(rest) // 2)
    return [1] + rest, [1] + rest[cut:] + rest[:cut]


def masks_of(bits):
    masks = [0]
    for bit in bits:
        masks = masks + [m | bit for m in masks]
    return masks


def by_tiles(rows, tile, body):
    def step(i, none):
        body(pl.ds(pl.multiple_of(i * tile, tile), tile))
        return none

    lax.fori_loop(0, rows // tile, step, 0)


def wait_for(ref, sem):
    pltpu.make_async_copy(ref, ref, sem).wait()


def greet_seq(seq):
    me, place = lax.axis_index("rows"), lax.axis_index("seq")
    barrier = pltpu.get_barrier_semaphore()
    for step, there in ((-1, place > 0), (1, place < seq - 1)):

        @pl.when(there)
        def _(step=step):
            pl.semaphore_signal(barrier, inc=1, device_id=(place + step, me), device_id_type=MESH)

    pl.semaphore_wait(barrier, (place > 0).astype(jnp.int32) + (place < seq - 1).astype(jnp.int32))


def greet_rows_and_seq(size, seq):
    me, place = lax.axis_index("rows"), lax.axis_index("seq")
    barrier = pltpu.get_barrier_semaphore()
    for mask in range(1, size):
        pl.semaphore_signal(barrier, inc=1, device_id=(place, flip(me, mask)), device_id_type=MESH)
    for step, there in ((-1, place > 0), (1, place < seq - 1)):

        @pl.when(there)
        def _(step=step):
            pl.semaphore_signal(barrier, inc=1, device_id=(place + step, me), device_id_type=MESH)

    near = (place > 0).astype(jnp.int32) + (place < seq - 1).astype(jnp.int32)
    pl.semaphore_wait(barrier, near + size - 1)


def crossed(place, mask, size):
    out = 0
    for k in range(size.bit_length() - 1):
        bit = 1 << k
        out = out + bit * lax.rem(lax.div(place, bit) + lax.div(mask, bit), 2)
    return out


class RowGather:
    def __init__(self, size, source, out, own_sem, send, recv):
        self.size, self.source, self.out, self.own_sem, self.send, self.recv = size, source, out, own_sem, send, recv
        self.me, self.place = lax.axis_index("rows"), lax.axis_index("seq")
        self.rows = source.shape[0] // 2
        self.orders = [order[1:] for order in bit_orders(size)]
        self.steps = len(self.orders[0])
        self.started = []

    @staticmethod
    def sems(size):
        return [pltpu.SemaphoreType.DMA((1,))] + [pltpu.SemaphoreType.DMA((2, size))] * 2

    def half(self, h, m, ref=None):
        ref = self.out.at[flip(self.me, m)] if ref is None else ref
        return ref.at[pl.ds(h * self.rows, self.rows), :]

    def push(self, h, m, bit):
        source = self.half(h, m, self.source if m == 0 else None)
        key = (h, m | bit)
        self.started.append(
            remote(
                source, self.half(h, m), self.send.at[key], self.recv.at[key],
                (self.place, flip(self.me, bit)),
            )
        )

    def arrived(self, h, m):
        wait_for(self.half(h, m), self.recv.at[h, m])

    def start(self):
        pltpu.make_async_copy(self.source, self.out.at[self.me], self.own_sem.at[0]).start()
        for h in range(2):
            self.push(h, 0, self.orders[h][0])
        for h in range(2):
            self.push(h, 0, 1)

    def own(self):
        wait_for(self.out.at[self.me], self.own_sem.at[0])

    def step(self, k, use=None):
        for h in range(2):
            order = self.orders[h]
            old = masks_of(order[:k])
            if k + 1 < self.steps:
                for m in old:
                    self.push(h, m, order[k + 1])
            for m in old:
                fresh = m | order[k]
                self.arrived(h, fresh)
                if k + 1 < self.steps:
                    self.push(h, fresh, order[k + 1])
                self.push(h, fresh, 1)
                if use:
                    use(h, fresh)

    def paired(self, use=None):
        for m in masks_of(self.orders[0]):
            for h in range(2):
                self.arrived(h, m | 1)
                if use:
                    use(h, m | 1)

    def drain(self):
        for copy in self.started:
            copy.wait_send()


def front_kernel(size, seq, direct, *refs):
    (tokens, cot, notes, w_local, out_w, x_w, dt_w, taps_ref, bias_ref, dt_bias_ref) = refs[:10]
    (
        normed_out, cot_out, w_out, x_out, delta_out, gy_out, pre_out, gate_out, gg_out, cext_out,
        proj_ref, rank_ref, all_notes,
    ) = refs[10:23]
    (
        tok, normed, cot_s, wc, wg, cext, pre, xb, x_s, delta_s, gy_s, gate_s, gg_s, gain_ref,
    ) = refs[23:37]
    token_sems, cot_sems = refs[37:40], refs[40:43]
    part, near, total, mail, far, out, sems = refs[43:50]
    note_send, note_recv, wc_send, wc_recv, wg_send, wg_recv, halo_send, halo_recv, out_sems = refs[50:]
    me, parity, partner, others = row_peers(size)
    place = lax.axis_index("seq")
    tt, width = tokens.shape
    share, el = wc.shape[1:]
    blocks = el // LANES
    half = size // 2
    f32, bf16 = jnp.float32, jnp.bfloat16
    tile = 32
    stores = []

    def put(source, target):
        copy = pltpu.make_async_copy(source, target, out_sems.at[len(stores)])
        copy.start()
        stores.append(copy)

    def piece(q, gate):
        if direct:
            at = pl.multiple_of(q * el, LANES) + gate * size * el
            return w_local.at[:, pl.ds(at, el)]
        return w_local.at[q, :, pl.ds(gate * el, el)]

    def swap(gate, target, send, recv):
        copies = []
        for m in range(1, size):
            q = flip(me, m)
            copies.append(remote(piece(q, gate), target.at[me], send.at[m], recv.at[m], (place, q)))
        pltpu.make_async_copy(piece(me, gate), target.at[me], recv.at[0]).start()
        return copies

    def swapped(target, recv):
        for m in range(size):
            wait_for(target.at[flip(me, m)], recv.at[m])

    greet_rows_and_seq(size, seq)

    sent = []
    for m in range(1, size):
        sent.append(remote(notes, all_notes.at[me], note_send.at[m], note_recv.at[m], (place, flip(me, m))))
    pltpu.make_async_copy(notes, all_notes.at[me], note_recv.at[0]).start()
    token_rows = RowGather(size, tokens, tok, *token_sems)
    cot_rows = RowGather(size, cot, cot_s, *cot_sems)
    token_rows.start()
    sent += swap(0, wc, wc_send, wc_recv)

    for m in range(size):
        wait_for(all_notes.at[flip(me, m)], note_recv.at[m])
    for p in range(size):
        gain_ref[:, p * share : (p + 1) * share] = all_notes[p, 0:1, :share].astype(f32)

    def norm(p, base, rows):
        def body(span):
            there = pl.ds(base + span.start, span.size)
            x = tok[p, there, :].astype(f32)
            inv = lax.rsqrt(jnp.mean(x * x, axis=1, keepdims=True) + epsilon)
            normed[p, there, :] = (x * inv * gain_ref[...]).astype(bf16)

        by_tiles(rows, 16, body)

    def norm_half(h, m):
        norm(flip(me, m), h * (tt // 2), tt // 2)

    token_rows.own()
    norm(me, 0, tt)
    for k in range(token_rows.steps):
        token_rows.step(k, norm_half)
    cot_rows.start()
    sent += swap(1, wg, wg_send, wg_recv)
    token_rows.paired(norm_half)
    swapped(wc, wc_recv)

    @pl.when(place == 0)
    def _():
        cext[:, 0:16, :] = jnp.zeros((size, 16, el), bf16)

    def halo(p, i):
        there = cext.at[p, pl.ds(0, 16), :]
        return pltpu.make_async_remote_copy(
            src_ref=cext.at[p, pl.ds(tt, 16), :], dst_ref=there, send_sem=halo_send.at[i],
            recv_sem=halo_recv.at[i], device_id=(jnp.minimum(place + 1, seq - 1), me), device_id_type=MESH,
        )

    def block_at(i):
        return 2 * lax.rem(me // 2 + lax.rem(i, half), half) + lax.rem(parity + 1 + lax.div(i, half), 2)

    def mix(i, none):
        p = block_at(i)
        weight = wc[...].reshape(size * share, el)
        cext[p, 16:, :] = jnp.dot(normed[p], weight, preferred_element_type=f32).astype(bf16)

        @pl.when(place < seq - 1)
        def _():
            halo(p, i).start()

        return none

    lax.fori_loop(0, size, mix, 0)
    for p in range(size):
        put(normed.at[p], normed_out.at[p])

    def conv(i, none):
        p = block_at(i)

        @pl.when(place > 0)
        def _():
            halo(p, i).wait_recv()

        def body(span):
            ext = cext[p, pl.ds(span.start, tile + 16), :].astype(f32)
            value = bias_ref[...]
            for k in range(KC):
                value = value + taps_ref[k : k + 1, :] * ext[16 - KC + 1 + k : 16 - KC + 1 + k + tile]
            pre[p, span, :] = value
            x = (value / (1.0 + jnp.exp(-value))).astype(bf16)
            xb[p, span, :] = x
            for b in range(blocks):
                there = pl.ds(p + span.start * size, tile, stride=size)
                x_s[b, there, :] = x[:, b * LANES : (b + 1) * LANES].astype(f32)

        by_tiles(tt, tile, body)
        value = jnp.dot(xb[p], x_w[...], preferred_element_type=f32)

        @pl.when(i < half)
        def _():
            part[p] = value.astype(bf16)
            pltpu.make_async_remote_copy(
                src_ref=part.at[p], dst_ref=near.at[lax.div(p, 2)], send_sem=sems.at[0, lax.div(p, 2)],
                recv_sem=sems.at[1, lax.div(p, 2)], device_id=(place, partner), device_id_type=MESH,
            ).start()

        @pl.when(i >= half)
        def _():
            total[lax.div(p, 2)] = value

        return none

    lax.fori_loop(0, size, conv, 0)
    put(cext, cext_out)
    put(pre, pre_out)
    put(x_s, x_out)

    def use(p):
        block = out[p]
        rank_ref[p] = block
        proj_ref[pl.ds(p, tt, stride=size), :] = block.astype(f32)

        def body(span):
            step = jnp.dot(out[p, span, :], dt_w[...], preferred_element_type=f32) + dt_bias_ref[...]
            delta = jnp.maximum(step, 0.0) + jnp.log1p(jnp.exp(-jnp.abs(step)))
            for b in range(blocks):
                there = pl.ds(p + span.start * size, 64, stride=size)
                delta_s[b, there, :] = delta[:, b * LANES : (b + 1) * LANES]

        by_tiles(tt, 64, body)

    def between():
        for k in range(cot_rows.steps):
            cot_rows.step(k)

    exchange_sums(size, near, total, mail, far, out, sems, use, between)
    for j in range(half):
        pltpu.make_async_remote_copy(
            src_ref=part.at[j], dst_ref=near.at[j], send_sem=sems.at[0, j], recv_sem=sems.at[1, j],
            device_id=(place, partner), device_id_type=MESH,
        ).wait_send()
    put(delta_s, delta_out)
    put(wc, w_out.at[:, :, pl.ds(0, el)])

    cot_rows.own()
    cot_rows.paired()
    put(cot_s, cot_out)
    swapped(wg, wg_recv)
    put(wg, w_out.at[:, :, pl.ds(el, el)])

    def gates(p, none):
        weight = wg[...].reshape(size * share, el)
        gate_s[p] = jnp.dot(normed[p], weight, preferred_element_type=f32)
        gg_s[p] = lax.dot_general(
            cot_s[p], out_w[...], (((1,), (1,)), ((), ())), preferred_element_type=f32
        )

        def body(span):
            gate = gate_s[p, span, :]
            gy = gg_s[p, span, :] * gate / (1.0 + jnp.exp(-gate))
            for b in range(blocks):
                there = pl.ds(p + span.start * size, tile, stride=size)
                gy_s[b, there, :] = gy[:, b * LANES : (b + 1) * LANES]

        by_tiles(tt, tile, body)
        return none

    lax.fori_loop(0, size, gates, 0)
    put(gy_s, gy_out)
    put(gate_s, gate_out)
    put(gg_s, gg_out)

    for i in range(size):

        @pl.when(place < seq - 1)
        def _(i=i):
            halo(i, i).wait_send()

    token_rows.drain()
    cot_rows.drain()
    for copy in sent:
        copy.wait_send()
    for copy in stores:
        copy.wait()


def front(tokens, cot, notes, w_local, out_w, x_w, dt_w, taps, bias, dt_bias, size, seq, direct):
    tt, width = tokens.shape
    el = out_w.shape[0]
    share = width // size
    blocks = el // LANES
    away = pl.BlockSpec(memory_space=pl.ANY)
    here = pl.BlockSpec(memory_space=pltpu.VMEM)
    f32, bf16 = jnp.float32, jnp.bfloat16
    rows, scan = (size, tt, width), (blocks, tt * size, LANES)
    channels, ext = (size, tt, el), (size, tt + 16, el)
    shapes = [
        (rows, bf16), (rows, bf16), ((size, share, 2 * el), bf16), (scan, f32), (scan, f32), (scan, f32),
        (channels, f32), (channels, f32), (channels, f32), (ext, bf16),
        ((tt * size, LANES), f32), ((size, tt, LANES), bf16), ((size,) + notes.shape, bf16),
    ]
    weights = (size, share, el)
    scratch = [
        (rows, bf16), (rows, bf16), (rows, bf16), (weights, bf16), (weights, bf16), (ext, bf16),
        (channels, f32), (channels, bf16), (scan, f32), (scan, f32), (scan, f32),
        (channels, f32), (channels, f32), ((1, width), f32),
    ]
    one = pltpu.SemaphoreType.DMA((size,))
    return pl.pallas_call(
        functools.partial(front_kernel, size, seq, direct),
        in_specs=[away] * 4 + [here] * 6,
        out_specs=[away] * 10 + [here] * 3,
        out_shape=[jax.ShapeDtypeStruct(*v) for v in shapes],
        scratch_shapes=[pltpu.VMEM(*v) for v in scratch]
        + RowGather.sems(size) * 2
        + sum_scratch(size, tt)
        + [one] * 8
        + [pltpu.SemaphoreType.DMA((size + 10,))],
        compiler_params=pltpu.CompilerParams(
            vmem_limit_bytes=62 * MIB, collective_id=0, has_side_effects=True
        ),
        name="front",
    )(tokens, cot, notes, w_local, out_w, x_w, dt_w, taps, bias, dt_bias)


class RowScatter:
    def __init__(self, size, part, keep, land, mail, keep_sem, send, recv):
        self.size, self.part, self.keep, self.land, self.mail = size, part, keep, land, mail
        self.keep_sem, self.send, self.recv = keep_sem, send, recv
        self.me, self.place = lax.axis_index("rows"), lax.axis_index("seq")
        self.tt, self.width = part.shape[1], part.shape[2] // 2
        self.orders = bit_orders(size)
        self.steps = len(self.orders[0])
        self.started, self.local = [], []

    @staticmethod
    def scratch(size, tt, width):
        return [
            pltpu.VMEM((size // 2, tt, width), jnp.bfloat16),
            pltpu.VMEM((size - 1, tt, width), jnp.bfloat16),
            pltpu.VMEM((size // 2 - 1, tt, width), jnp.bfloat16),
            pltpu.SemaphoreType.DMA((size // 2,)),
            pltpu.SemaphoreType.DMA((2, size - 1)),
            pltpu.SemaphoreType.DMA((2, size - 1)),
        ]

    def free(self, h, k):
        return masks_of(self.orders[h][k + 1 :])

    def at(self, h, k, m):
        return sum(len(self.free(h, j)) for j in range(k)) + self.free(h, k).index(m)

    def cols(self, h):
        return pl.ds(h * self.width, self.width)

    def receive(self, h, k, m):
        slot = self.at(h, k, m)
        wait_for(self.land.at[slot, :, self.cols(h)], self.recv.at[h, slot])

    def partial_sum(self, h, k, m, rows):
        value = self.keep[m >> 1, rows, self.cols(h)].astype(jnp.float32)
        for j in range(k):
            value = value + self.land[self.at(h, j, m), rows, self.cols(h)].astype(jnp.float32)
        return value

    def start(self):
        for h in range(2):
            self.scatter(h, 0)
        for m in self.free(0, 0):
            copy = pltpu.make_async_copy(
                self.part.at[flip(self.me, m)], self.keep.at[m >> 1], self.keep_sem.at[m >> 1]
            )
            copy.start()
            self.local.append(copy)

    def step(self, k):
        if k == 1:
            for copy in self.local:
                copy.wait()
        for h in range(2):
            self.scatter(h, k)

    def scatter(self, h, k):
        bit = self.orders[h][k]
        for m in self.free(h, k):
            slot = self.at(h, k, m)
            if k == 0:
                source = self.part.at[flip(self.me, m | bit), :, self.cols(h)]
            else:
                for j in range(k):
                    self.receive(h, j, m | bit)
                box = slot - self.size // 2

                def fill(rows, m=m, box=box):
                    value = self.partial_sum(h, k, m | bit, rows)
                    self.mail[box, rows, self.cols(h)] = value.astype(jnp.bfloat16)

                by_tiles(self.tt, 32, fill)
                source = self.mail.at[box, :, self.cols(h)]
            self.started.append(
                remote(
                    source, self.land.at[slot, :, self.cols(h)], self.send.at[h, slot], self.recv.at[h, slot],
                    (self.place, flip(self.me, bit)),
                )
            )

    def finish(self, own):
        for h in range(2):
            for j in range(self.steps):
                self.receive(h, j, 0)

            def fill(rows, h=h):
                own[rows, self.cols(h)] = self.partial_sum(h, self.steps, 0, rows).astype(jnp.bfloat16)

            by_tiles(self.tt, 32, fill)

    def drain(self):
        for copy in self.started:
            copy.wait_send()


class SeqSum:
    def __init__(self, seq, held, land, mail, fill_sem, send, recv):
        self.seq, self.held, self.land, self.mail = seq, held, land, mail
        self.fill_sem, self.send, self.recv = fill_sem, send, recv
        self.me, self.place = lax.axis_index("rows"), lax.axis_index("seq")
        self.behind = (self.place, seq - 1 - self.place)
        self.chunks = held.shape[0]
        self.last_step = self.chunks + seq - 1

    @staticmethod
    def scratch(chunks, block):
        return [
            pltpu.VMEM((chunks,) + block, jnp.bfloat16),
            pltpu.VMEM((2, chunks) + block, jnp.bfloat16),
            pltpu.VMEM((2, chunks) + block, jnp.bfloat16),
            pltpu.SemaphoreType.DMA((chunks,)),
            pltpu.SemaphoreType.DMA((2, chunks)),
            pltpu.SemaphoreType.DMA((2, chunks)),
        ]

    def copy(self, n, way, source):
        target = (jnp.clip(self.place + 1 - 2 * way, 0, self.seq - 1), self.me)
        return pltpu.make_async_remote_copy(
            src_ref=source, dst_ref=self.land.at[way, n], send_sem=self.send.at[way, n],
            recv_sem=self.recv.at[way, n], device_id=target, device_id_type=MESH,
        )

    def hop(self, step, way):
        n = step - self.behind[way]

        @pl.when((n >= 0) & (n < self.chunks))
        def _():
            @pl.when(self.behind[way] == 0)
            def _():
                self.copy(n, way, self.held.at[n]).start()

            @pl.when(self.behind[way] > 0)
            def _():
                self.copy(n, way, self.held.at[n]).wait_recv()

                @pl.when(self.behind[way] < self.seq - 1)
                def _():
                    value = self.held[n].astype(jnp.float32) + self.land[way, n].astype(jnp.float32)
                    self.mail[way, n] = value.astype(jnp.bfloat16)
                    self.copy(n, way, self.mail.at[way, n]).start()

    def advance(self, step, total):
        first = step - jnp.minimum(self.behind[0], self.behind[1])

        @pl.when((first >= 0) & (first < self.chunks))
        def _():
            wait_for(self.held.at[first], self.fill_sem.at[first])

        self.hop(step, 0)
        self.hop(step, 1)
        n = step - jnp.maximum(self.behind[0], self.behind[1])

        @pl.when((n >= 0) & (n < self.chunks))
        def _():
            for ways, there in (
                ((1,), self.behind[0] == 0),
                ((0,), self.behind[1] == 0),
                ((0, 1), (self.behind[0] > 0) & (self.behind[1] > 0)),
            ):

                @pl.when(there)
                def _(ways=ways):
                    value = self.held[n].astype(jnp.float32)
                    for way in ways:
                        value = value + self.land[way, n].astype(jnp.float32)
                    total[n] = value.astype(jnp.bfloat16)

    def run(self, first, last, total):
        def body(step, none):
            self.advance(step, total)
            return none

        lax.fori_loop(first, last, body, 0)

    def drain(self):
        for way in range(2):

            @pl.when(self.behind[way] < self.seq - 1)
            def _(way=way):
                def sent(n, none):
                    self.copy(n, way, self.held.at[n]).wait_send()
                    return none

                lax.fori_loop(0, self.chunks, sent, 0)


def chunk_order(size):
    return sorted(range(size), key=lambda m: (m > 1, (m >> 1).bit_count(), m))


def tail_kernel(size, seq, *refs):
    branch, normed, weight, out_w, small = refs[:5]
    branch_own, normed_own, total = refs[5:8]
    scatter_a = RowScatter(size, branch, *refs[8:14])
    scatter_b = RowScatter(size, normed, *refs[14:20])
    held, land, mail, fill_sem, zsend, zrecv, swap_send = refs[20:]
    chain = SeqSum(seq, held, land, mail, fill_sem, zsend, zrecv)
    me, place = lax.axis_index("rows"), lax.axis_index("seq")
    rows, cols = held.shape[1:]
    greet_rows_and_seq(size, seq)
    scatter_a.start()
    n = 0
    for source in (out_w, small):
        for i in range(source.shape[0] // rows):
            for j in range(source.shape[1] // cols):
                piece = source.at[pl.ds(i * rows, rows), pl.ds(j * cols, cols)]
                pltpu.make_async_copy(piece, held.at[n], fill_sem.at[n]).start()
                n += 1
    sent = []
    for m in chunk_order(size):
        for i in range(weight.shape[1] // rows):
            piece = weight.at[flip(me, m), pl.ds(i * rows, rows), :]
            if m == 0:
                pltpu.make_async_copy(piece, held.at[n], fill_sem.at[n]).start()
            else:
                target = (place, flip(me, m))
                sent.append(remote(piece, held.at[n], swap_send.at[n], fill_sem.at[n], target))
            n += 1
    scatter_b.start()
    jobs = []
    for k in range(1, scatter_a.steps):
        jobs += [functools.partial(scatter_a.step, k), functools.partial(scatter_b.step, k)]
    jobs += [functools.partial(scatter_a.finish, branch_own), functools.partial(scatter_b.finish, normed_own)]
    done = 0
    for i, job in enumerate(jobs):
        upto = chain.last_step * (i + 1) // (len(jobs) + 1)
        chain.run(done, upto, total)
        done = upto
        job()
    chain.run(done, chain.last_step, total)
    scatter_a.drain()
    scatter_b.drain()
    for copy in sent:
        copy.wait_send()
    chain.drain()


def reduce_all(branch, normed, weight, out_w, small, size, seq):
    away = pl.BlockSpec(memory_space=pl.ANY)
    here = pl.BlockSpec(memory_space=pltpu.VMEM)
    tt, width = branch.shape[1:]
    share, cols = weight.shape[1:]
    rows = share // 2
    chunks = (weight.size + out_w.size + small.size) // (rows * cols)
    return pl.pallas_call(
        functools.partial(tail_kernel, size, seq),
        in_specs=[away] * 5,
        out_specs=[here] * 3,
        out_shape=[jax.ShapeDtypeStruct((tt, width), jnp.bfloat16)] * 2
        + [jax.ShapeDtypeStruct((chunks, rows, cols), jnp.bfloat16)],
        scratch_shapes=RowScatter.scratch(size, tt, width) * 2
        + SeqSum.scratch(chunks, (rows, cols))
        + [pltpu.SemaphoreType.DMA((chunks,))],
        compiler_params=pltpu.CompilerParams(
            vmem_limit_bytes=60 * MIB, collective_id=4, has_side_effects=True
        ),
        name="reduce_all",
    )(branch, normed, weight, out_w, small)


def from_behind(value, axis, steps):
    count = lax.axis_size(axis)
    first, last = (max(0, -steps), min(count, count - steps))
    return lax.ppermute(value, axis, [(source, source + steps) for source in range(first, last)])


def shortened(x):
    return x.astype(jnp.bfloat16)


def contract_rows(left, right):
    return lax.dot_general(left, right, (((0,), (0,)), ((), ())), preferred_element_type=jnp.float32)


def contract_cols(left, right):
    return lax.dot_general(left, right, (((1,), (1,)), ((), ())), preferred_element_type=jnp.float32)


def local(
    tokens, resets, norm_gain, in_proj, x_proj, dt_proj, conv_weight, conv_bias, dt_bias, a_log, out_proj,
    cotangent,
):
    size = lax.axis_size("rows")
    seq = lax.axis_size("seq")
    rd, tt, unused_d = tokens.shape
    nr = rd * size
    el = E // size
    count = nr * tt
    assert rd == 1 and ITEM % tt == 0 and nr % 8 == 0

    elp = pad_lanes(el)
    share = D // size
    direct = elp == el
    f32, bf16 = jnp.float32, jnp.bfloat16

    def widen(value, axis):
        pad = [(0, 0)] * value.ndim
        pad[axis] = (0, elp - el)
        return jnp.pad(value, pad)

    if direct:
        w_local = in_proj
    else:
        w_local = jnp.moveaxis(in_proj.reshape(share, 2, size, el), 2, 0)
        w_local = widen(w_local, 3).reshape(size, share, 2 * elp)
    out_proj, x_proj = widen(out_proj, 0), widen(x_proj, 0)
    dt_pad = widen(jnp.pad(dt_proj, ((0, LANES - R), (0, 0))), 1)
    taps = widen(conv_weight.astype(f32), 1)
    bias = widen(conv_bias.astype(f32), 0)[None]
    rate = widen(-jnp.exp(a_log.astype(f32)), 1)
    notes = jnp.zeros((16, -(-share // 256) * 256), bf16)
    notes = notes.at[0, :share].set(norm_gain).at[1, 0].set(1.0 - resets[0, 0].astype(bf16))
    (
        normed, all_cot, w_in, x_t, delta_t, gy_t, conv_pre, gate_pre, grad_gated, conv_ext, proj_t, rank_all,
        all_notes,
    ) = front(
        tokens[0], cotangent[0], notes, w_local, out_proj, x_proj, dt_pad, taps, bias,
        widen(dt_bias.astype(f32), 0)[None], size, seq, direct,
    )
    normed, all_cot = normed.reshape(count, D), all_cot.reshape(count, D)
    w_in = w_in.reshape(D, 2 * elp)
    gate_pre, grad_gated = gate_pre.reshape(count, elp), grad_gated.reshape(count, elp)
    gain = all_notes[:, 0, :share].reshape(D).astype(f32)
    alive = all_notes[:, 1, :1].astype(f32)
    rank_part = rank_all.reshape(count, LANES)[:, :R]
    extended = conv_ext[:, 16 - KC + 1 :]

    def by_row(value):
        value = value.reshape(elp // LANES, tt, nr, LANES)
        return jnp.transpose(value, (2, 1, 0, 3)).reshape(count, elp)

    rate2 = rate * LOG2E
    scanned = (delta_t, x_t, gy_t)
    carry = scan_ends(*scanned, proj_t, rate2, alive, nr, tt, seq)
    scan_y, grad_delta, grad_input, grad_bc, grate = scan_main(
        *scanned, proj_t, rate2, carry, nr, tt
    )
    scan_y, grad_delta, grad_input, step_size = (by_row(v) for v in (scan_y, grad_delta, grad_input, delta_t))
    conv_out = jax.nn.silu(conv_pre).astype(bf16).reshape(count, elp)
    gate_sig = jax.nn.sigmoid(gate_pre)
    gate_act = gate_pre * gate_sig
    grad_a_log = jnp.sum(grate, axis=1) * rate

    gated = (scan_y * gate_act).astype(jnp.bfloat16)
    branch = jnp.dot(gated, out_proj, preferred_element_type=jnp.float32).astype(jnp.bfloat16)
    grad_out_proj = contract_rows(gated, all_cot)
    grad_gate_pre = grad_gated * scan_y * gate_sig * (1.0 + gate_pre * (1.0 - gate_sig))

    grad_step_pre = grad_delta * -jnp.expm1(-step_size)
    grad_dt_bias = jnp.sum(grad_step_pre, axis=0)
    low_step = grad_step_pre.astype(jnp.bfloat16)
    grad_dt_proj = contract_rows(rank_part, low_step)
    grad_projected = back_project(low_step.reshape(nr, tt, elp), dt_pad, grad_bc).reshape(count, LANES)
    grad_x_proj = contract_rows(conv_out, grad_projected)
    grad_conv_out = contract_cols(grad_projected, x_proj) + grad_input
    conv_sig = jax.nn.sigmoid(conv_pre).reshape(count, elp)
    conv_flat = conv_pre.reshape(count, elp)
    grad_conv_pre = (grad_conv_out * conv_sig * (1.0 + conv_flat * (1.0 - conv_sig))).reshape(nr, tt, elp)
    grad_conv_bias = jnp.sum(grad_conv_pre, axis=(0, 1))
    grad_taps = jnp.stack(
        [
            jnp.sum(grad_conv_pre * extended[:, k : k + tt].astype(jnp.float32), axis=(0, 1))
            for k in range(KC)
        ]
    )
    grad_ext = sum(
        jnp.pad(taps[k] * grad_conv_pre, ((0, 0), (k, KC - 1 - k), (0, 0))) for k in range(KC)
    )
    right_rim = from_behind(shortened(grad_ext[:, : KC - 1]), "seq", -1)
    grad_conv_in = grad_ext[:, KC - 1 :] + jnp.pad(
        right_rim.astype(jnp.float32), ((0, 0), (tt - (KC - 1), 0), (0, 0))
    )
    grad_mixed = jnp.concatenate([grad_conv_in.reshape(count, elp), grad_gate_pre], axis=1).astype(
        jnp.bfloat16
    )
    grad_in_proj = contract_rows(normed, grad_mixed).astype(jnp.bfloat16)
    grad_normed_part = contract_cols(grad_mixed, w_in).astype(jnp.bfloat16)
    small = jnp.concatenate(
        [grad_x_proj.T, grad_dt_proj, grad_taps, grad_conv_bias[None], grad_dt_bias[None], grad_a_log],
        axis=0,
    )
    piece = (share // 2, 2 * elp)
    folded = shortened(small)
    folded = jnp.pad(folded, ((0, -folded.shape[0] % 2), (0, 0)))
    high = folded.shape[0] // 2
    folded = jnp.concatenate([folded[:high], folded[high:]], axis=1)
    folded = jnp.pad(folded, ((0, -high % piece[0]), (0, 0)))
    branch_own, grad_normed, summed = reduce_all(
        branch.reshape(nr, tt, D), grad_normed_part.reshape(nr, tt, D),
        grad_in_proj.reshape(size, share, 2 * elp), shortened(grad_out_proj)[:el], folded, size, seq,
    )
    summed = summed.astype(jnp.float32)
    out_rows, out_cols = el // piece[0], D // piece[1]
    at = out_rows * out_cols
    sum_out = jnp.swapaxes(summed[:at].reshape(out_rows, out_cols, *piece), 1, 2).reshape(el, D)
    folded = summed[at : at + folded.shape[0] // piece[0]].reshape(folded.shape)
    small = jnp.concatenate([folded[:high, :elp], folded[:high, elp:]], axis=0)[:, :el]
    blocks = summed[-2 * size :].reshape(size, share, 2, elp)[..., :el]
    me = lax.axis_index("rows")
    places = [chunk_order(size).index(m) for m in range(size)]
    order = jnp.array(places)[jnp.array(range(size)) ^ me]
    sum_in = jnp.moveaxis(blocks[order], 0, 2).reshape(share, 2 * E)
    block_out = (tokens.astype(jnp.float32) + branch_own[None].astype(jnp.float32)).astype(jnp.bfloat16)
    grad_normed = grad_normed[None].astype(jnp.float32)

    own = tokens.astype(jnp.float32)
    inv = lax.rsqrt(jnp.mean(own * own, axis=2, keepdims=True) + epsilon)
    gain_own = jnp.sum(in_proj.astype(jnp.float32) * sum_in, axis=1) / norm_gain.astype(jnp.float32)
    grad_hat = grad_normed * gain
    grad_norm_in = inv * (
        grad_hat - own * (inv * inv) * jnp.mean(grad_hat * own, axis=2, keepdims=True)
    )
    d_tokens = (cotangent.astype(jnp.float32) + grad_norm_in).astype(jnp.bfloat16)

    cuts = [128, R, KC, 1, 1, NS]
    parts = []
    at = 0
    for cut in cuts:
        parts.append(small[at : at + cut])
        at += cut
    return (
        block_out,
        d_tokens,
        gain_own,
        sum_in,
        parts[0].T,
        parts[1],
        parts[2],
        parts[3][0],
        parts[4][0],
        parts[5],
        sum_out,
    )


def solution(mesh):
    in_specs = (
        P("rows", "seq", None),
        P("rows", "seq"),
        P("rows"),
        P("rows", None),
        P("rows", None),
        P(None, "rows"),
        P(None, "rows"),
        P("rows"),
        P("rows"),
        P(None, "rows"),
        P("rows", None),
        P("rows", "seq", None),
    )
    out_specs = (
        P("rows", "seq", None),
        P("rows", "seq", None),
        P("rows"),
        P("rows", None),
        P("rows", None),
        P(None, "rows"),
        P(None, "rows"),
        P("rows"),
        P("rows"),
        P(None, "rows"),
        P("rows", None),
    )
    return jax.shard_map(local, mesh=mesh, in_specs=in_specs, out_specs=out_specs, check_vma=False)
```

```python
import functools
import math

import jax
import jax.numpy as jnp
from jax import lax
from jax.experimental import pallas as pl
from jax.experimental.pallas import tpu as pltpu
from jax.sharding import PartitionSpec as P

D = 1536
E = 3072
R = 96
NS = 16
KC = 4
ITEM = 256

epsilon = 1e-05
LOG2E = 1.4426950408889634
LN2 = 0.6931471805599453
MIB = 2**20


LANES = 128


def pad_lanes(lanes):
    return -(-lanes // LANES) * LANES


def selector(wide):
    row = lax.broadcasted_iota(jnp.int32, (LANES, 2 * NS * wide), 0)
    col = lax.broadcasted_iota(jnp.int32, (LANES, 2 * NS * wide), 1) // wide
    return (row == col + R).astype(jnp.bfloat16)


def spread(proj, sel_ref):
    return jnp.dot(proj.astype(jnp.bfloat16), sel_ref[...], preferred_element_type=jnp.float32)


def copy_all(sources, targets, sems):
    copies = []
    for i, (source, target) in enumerate(zip(sources, targets)):
        copies.append(pltpu.make_async_copy(source, target, sems.at[i]))
        copies[-1].start()
    return copies


def ends_kernel(
    seq, nr, tt, ct, uu, delta_in, x_in, gy_in, proj_ref, a_ref, alive_ref, carry_ref,
    out_ref, mail, land, carry_sems, sel, bc, delta_ref, x_ref, gy_ref, sems,
):
    el = a_ref.shape[1]
    carry = Carry(seq, out_ref, alive_ref, carry_ref, mail, land, carry_sems)
    greet_seq(seq)
    half = NS // 2
    copies = copy_all((delta_in, x_in, gy_in), (delta_ref, x_ref, gy_ref), sems)
    sel[...] = selector(LANES)
    out_ref[0] = jnp.zeros((NS, nr, el), jnp.float32)
    out_ref[1] = jnp.ones((NS, nr, el), jnp.float32)
    out_ref[2] = jnp.zeros((NS, nr, el), jnp.float32)
    for copy in copies:
        copy.wait()

    def chunk(c, none):
        rows = pl.multiple_of(c * (ct * nr), ct * nr)
        bc[...] = spread(proj_ref[pl.ds(rows, ct * nr), :], sel)
        for b in range(el // LANES):
            lanes = slice(b * LANES, (b + 1) * LANES)
            for n0 in range(0, NS, half):
                ns = range(n0, n0 + half)
                rate = [jnp.broadcast_to(a_ref[n : n + 1, lanes], (nr, LANES)) for n in ns]

                def steps(s, carried):
                    state, through, back = (list(v) for v in carried)
                    for u in range(uu):
                        at = s * uu + u
                        here = pl.ds(pl.multiple_of((c * ct + at) * nr, nr), nr)
                        delta = delta_ref[b, here, :]
                        gy = gy_ref[b, here, :]
                        du = delta * x_ref[b, here, :]
                        near = pl.ds(pl.multiple_of(at * nr, nr), nr)
                        for i, n in enumerate(ns):
                            b_at, c_at = n * LANES, (NS + n) * LANES
                            decay = jnp.exp2(delta * rate[i])
                            state[i] = decay * state[i] + du * bc[near, b_at : b_at + LANES]
                            through[i] = through[i] * decay
                            back[i] = back[i] + through[i] * (gy * bc[near, c_at : c_at + LANES])
                    return tuple(state), tuple(through), tuple(back)

                start = tuple(tuple(out_ref[k, n, :, lanes] for n in ns) for k in range(3))
                last = lax.fori_loop(0, ct // uu, steps, start)
                for k in range(3):
                    for i, n in enumerate(ns):
                        out_ref[k, n, :, lanes] = last[k][i]
        return none

    lax.fori_loop(0, tt // ct, chunk, 0)
    carry.both()
    carry.drain()


def scan_ends(delta, x, gy, proj, rate, alive, nr, tt, seq):
    el = rate.shape[1]
    ct = math.gcd(tt, 32)
    here = pl.BlockSpec(memory_space=pltpu.VMEM)
    away = pl.BlockSpec(memory_space=pl.ANY)
    blocks = pltpu.VMEM((el // LANES, nr * tt, LANES), jnp.float32)
    return pl.pallas_call(
        functools.partial(ends_kernel, seq, nr, tt, ct, min(8, ct)),
        in_specs=[away] * 3 + [here] * 3,
        out_specs=here,
        out_shape=jax.ShapeDtypeStruct((2, NS, nr, el), jnp.float32),
        scratch_shapes=[pltpu.VMEM((3, NS, nr, el), jnp.float32)]
        + Carry.scratch((NS, nr, el))
        + [
            pltpu.VMEM((LANES, 2 * NS * LANES), jnp.bfloat16),
            pltpu.VMEM((ct * nr, 2 * NS * LANES), jnp.float32),
            blocks,
            blocks,
            blocks,
            pltpu.SemaphoreType.DMA((3,)),
        ],
        compiler_params=pltpu.CompilerParams(
            vmem_limit_bytes=56 * MIB, collective_id=2, has_side_effects=True
        ),
        name="scan_ends",
    )(delta, x, gy, proj, rate, alive)


def forward_kernel(
    nr, tt, ct, uu, delta_in, x_in, proj_ref, a_ref, carry_ref,
    y_out, hist_out, last_ref, sel, bc, hist, delta_ref, x_ref, y_ref, sems, out_sem, hist_sems,
):
    el = a_ref.shape[1]
    blocks = el // LANES
    copies = copy_all((delta_in, x_in), (delta_ref, x_ref), sems)
    sel[...] = selector(LANES)
    last_ref[...] = carry_ref[0]
    for copy in copies:
        copy.wait()

    def store(c):
        slot = lax.rem(c, 2)
        return pltpu.make_async_copy(hist.at[slot], hist_out.at[pl.ds(c * ct, ct)], hist_sems.at[slot])

    def forward(c, none):
        slot = lax.rem(c, 2)

        @pl.when(c >= 2)
        def _():
            store(c - 2).wait()

        rows = pl.multiple_of(c * (ct * nr), ct * nr)
        bc[...] = spread(proj_ref[pl.ds(rows, ct * nr), :], sel)
        for b in range(blocks):
            lanes = slice(b * LANES, (b + 1) * LANES)
            rate = [jnp.broadcast_to(a_ref[n : n + 1, lanes], (nr, LANES)) for n in range(NS)]

            def steps(s, carried):
                state = list(carried)
                for u in range(uu):
                    at = s * uu + u
                    here = pl.ds(pl.multiple_of((c * ct + at) * nr, nr), nr)
                    delta = delta_ref[b, here, :]
                    du = delta * x_ref[b, here, :]
                    near = pl.ds(pl.multiple_of(at * nr, nr), nr)
                    y = None
                    for n in range(NS):
                        if n % 2 == 0:
                            both = jnp.concatenate([state[n], state[n + 1]], axis=0)
                            hist[slot, at, b, pl.ds(n * nr, 2 * nr), :] = both.astype(jnp.bfloat16)
                        b_at, c_at = n * LANES, (NS + n) * LANES
                        decay = jnp.exp2(delta * rate[n])
                        state[n] = decay * state[n] + du * bc[near, b_at : b_at + LANES]
                        term = state[n] * bc[near, c_at : c_at + LANES]
                        y = term if y is None else y + term
                    y_ref[b, here, :] = y
                return tuple(state)

            start = tuple(last_ref[n, :, lanes] for n in range(NS))
            last = lax.fori_loop(0, ct // uu, steps, start)
            for n in range(NS):
                last_ref[n, :, lanes] = last[n]
        store(c).start()
        return none

    count = tt // ct
    lax.fori_loop(0, count, forward, 0)
    copies = copy_all((y_ref,), (y_out,), out_sem)
    for c in range(max(0, count - 2), count):
        store(c).wait()
    for copy in copies:
        copy.wait()


def scan_forward(delta, x, proj, rate, carry, nr, tt):
    el = rate.shape[1]
    blocks = el // LANES
    ct = math.gcd(tt, 32)
    here = pl.BlockSpec(memory_space=pltpu.VMEM)
    away = pl.BlockSpec(memory_space=pl.ANY)
    f32, bf16 = jnp.float32, jnp.bfloat16
    scan = (blocks, nr * tt, LANES)
    return pl.pallas_call(
        functools.partial(forward_kernel, nr, tt, ct, min(8, ct)),
        in_specs=[away] * 2 + [here] * 3,
        out_specs=[away] * 2 + [here],
        out_shape=[
            jax.ShapeDtypeStruct(scan, f32),
            jax.ShapeDtypeStruct((tt, blocks, NS * nr, LANES), bf16),
            jax.ShapeDtypeStruct((NS, nr, el), f32),
        ],
        scratch_shapes=[
            pltpu.VMEM((LANES, 2 * NS * LANES), bf16),
            pltpu.VMEM((ct * nr, 2 * NS * LANES), f32),
            pltpu.VMEM((2, ct, blocks, NS * nr, LANES), bf16),
            pltpu.VMEM(scan, f32),
            pltpu.VMEM(scan, f32),
            pltpu.VMEM(scan, f32),
            pltpu.SemaphoreType.DMA((2,)),
            pltpu.SemaphoreType.DMA((1,)),
            pltpu.SemaphoreType.DMA((2,)),
        ],
        compiler_params=pltpu.CompilerParams(vmem_limit_bytes=56 * MIB),
        name="scan_forward",
    )(delta, x, proj, rate, carry)


MESH = pl.DeviceIdType.MESH


def greet(devices):
    barrier = pltpu.get_barrier_semaphore()
    for device in devices:
        pl.semaphore_signal(barrier, inc=1, device_id=device, device_id_type=MESH)
    pl.semaphore_wait(barrier, len(devices))


def remote(source, target, send, recv, device):
    copy = pltpu.make_async_remote_copy(
        src_ref=source, dst_ref=target, send_sem=send, recv_sem=recv, device_id=device, device_id_type=MESH
    )
    copy.start()
    return copy


def row_peers(size):
    me = lax.axis_index("rows")
    half = size // 2
    mine = me // 2
    return me, me % 2, me + 1 - 2 * (me % 2), [lax.rem(mine + k, half) for k in range(half)]


def exchange_sums(size, near, total, mail, far, out, sems, use, between=None):
    me, parity, partner, others = row_peers(size)
    place = lax.axis_index("seq")
    half = size // 2
    second = []
    for k in list(range(1, half)) + [0]:
        j = others[k]
        wait_for(near.at[j], sems.at[1, j])
        total[j] = total[j] + near[j].astype(jnp.float32)
        if k:
            mail[j] = total[j].astype(jnp.bfloat16)
            target = (place, 2 * j + parity)
            second.append(remote(mail.at[j], far.at[k], sems.at[2, k], sems.at[3, k], target))
    mine = others[0]
    done = total[mine]
    for k in range(1, half):
        wait_for(far.at[k], sems.at[3, k])
        done = done + far[k].astype(jnp.float32)
    out[me] = done.astype(jnp.bfloat16)
    third = []
    for k in range(1, half):
        target = (place, 2 * others[k] + parity)
        third.append(remote(out.at[me], out.at[me], sems.at[4, k], sems.at[5, k], target))
    fourth = [remote(out.at[me], out.at[me], sems.at[6, 0], sems.at[7, 0], (place, partner))]
    use(me)
    for k in range(1, half):
        block = 2 * others[half - k] + parity
        wait_for(out.at[block], sems.at[5, k])
        fourth.append(
            remote(out.at[block], out.at[block], sems.at[6, k], sems.at[7, k], (place, partner))
        )
        use(block)
    for k in range(half):
        block = 2 * others[(half - k) % half] + 1 - parity
        wait_for(out.at[block], sems.at[7, k])
        use(block)
    if between:
        between()
    for copy in second + third + fourth:
        copy.wait_send()


def sum_scratch(size, tt):
    half = size // 2
    return [
        pltpu.VMEM((size, tt, LANES), jnp.bfloat16),
        pltpu.VMEM((half, tt, LANES), jnp.bfloat16),
        pltpu.VMEM((half, tt, LANES), jnp.float32),
        pltpu.VMEM((half, tt, LANES), jnp.bfloat16),
        pltpu.VMEM((half, tt, LANES), jnp.bfloat16),
        pltpu.VMEM((size, tt, LANES), jnp.bfloat16),
        pltpu.SemaphoreType.DMA((8, half)),
    ]


class Carry:
    def __init__(self, seq, ends, alive, out, mail, land, sems):
        self.seq, self.ends, self.alive, self.out = seq, ends, alive, out
        self.mail, self.land, self.sems = mail, land, sems
        self.me, self.place = lax.axis_index("rows"), lax.axis_index("seq")

    @staticmethod
    def scratch(shape):
        return [
            pltpu.VMEM((2,) + shape, jnp.bfloat16),
            pltpu.VMEM((2,) + shape, jnp.bfloat16),
            pltpu.SemaphoreType.DMA((2, 2)),
        ]

    def copy(self, way):
        target = (jnp.clip(self.place + 1 - 2 * way, 0, self.seq - 1), self.me)
        return pltpu.make_async_remote_copy(
            src_ref=self.mail.at[way], dst_ref=self.land.at[way], send_sem=self.sems.at[way, 0],
            recv_sem=self.sems.at[way, 1], device_id=target, device_id_type=MESH,
        )

    def hop(self, way):
        first, last = ((0, self.seq - 1), (self.seq - 1, 0))[way]
        alive = self.alive[...][None]

        @pl.when(self.place == first)
        def _():
            self.out[way] = jnp.zeros_like(self.out[way])

        @pl.when(self.place != first)
        def _():
            self.copy(way).wait_recv()
            entering = self.land[way].astype(jnp.float32)
            self.out[way] = entering * alive if way == 0 else entering

        @pl.when(self.place != last)
        def _():
            if way == 0:
                leaving = self.ends[0] + self.ends[1] * self.out[0]
            else:
                leaving = (self.ends[2] + self.ends[1] * self.out[1]) * alive
            self.mail[way] = leaving.astype(jnp.bfloat16)
            self.copy(way).start()

    def both(self):
        @pl.when(self.place < self.seq // 2)
        def _():
            self.hop(0)
            self.hop(1)

        @pl.when(self.place >= self.seq // 2)
        def _():
            self.hop(1)
            self.hop(0)

    def drain(self):
        for way, last in ((0, self.seq - 1), (1, 0)):

            @pl.when(self.place != last)
            def _(way=way):
                self.copy(way).wait_send()


def flip(place, mask):
    for k in range(mask.bit_length()):
        bit = 1 << k
        if mask & bit:
            place = place + bit * (1 - 2 * (lax.div(place, bit) % 2))
    return place


def bit_orders(size):
    rest = [1 << k for k in range(1, size.bit_length() - 1)]
    cut = max(1, len(rest) // 2)
    return [1] + rest, [1] + rest[cut:] + rest[:cut]


def masks_of(bits):
    masks = [0]
    for bit in bits:
        masks = masks + [m | bit for m in masks]
    return masks


def by_tiles(rows, tile, body):
    def step(i, none):
        body(pl.ds(pl.multiple_of(i * tile, tile), tile))
        return none

    lax.fori_loop(0, rows // tile, step, 0)


def wait_for(ref, sem):
    pltpu.make_async_copy(ref, ref, sem).wait()


def greet_seq(seq):
    me, place = lax.axis_index("rows"), lax.axis_index("seq")
    barrier = pltpu.get_barrier_semaphore()
    for step, there in ((-1, place > 0), (1, place < seq - 1)):

        @pl.when(there)
        def _(step=step):
            pl.semaphore_signal(barrier, inc=1, device_id=(place + step, me), device_id_type=MESH)

    pl.semaphore_wait(barrier, (place > 0).astype(jnp.int32) + (place < seq - 1).astype(jnp.int32))


def greet_rows_and_seq(size, seq):
    me, place = lax.axis_index("rows"), lax.axis_index("seq")
    barrier = pltpu.get_barrier_semaphore()
    for mask in range(1, size):
        pl.semaphore_signal(barrier, inc=1, device_id=(place, flip(me, mask)), device_id_type=MESH)
    for step, there in ((-1, place > 0), (1, place < seq - 1)):

        @pl.when(there)
        def _(step=step):
            pl.semaphore_signal(barrier, inc=1, device_id=(place + step, me), device_id_type=MESH)

    near = (place > 0).astype(jnp.int32) + (place < seq - 1).astype(jnp.int32)
    pl.semaphore_wait(barrier, near + size - 1)


def crossed(place, mask, size):
    out = 0
    for k in range(size.bit_length() - 1):
        bit = 1 << k
        out = out + bit * lax.rem(lax.div(place, bit) + lax.div(mask, bit), 2)
    return out


class RowGather:
    def __init__(self, size, source, out, own_sem, send, recv):
        self.size, self.source, self.out, self.own_sem, self.send, self.recv = size, source, out, own_sem, send, recv
        self.me, self.place = lax.axis_index("rows"), lax.axis_index("seq")
        self.rows = source.shape[0] // 2
        self.orders = [order[1:] for order in bit_orders(size)]
        self.steps = len(self.orders[0])
        self.started = []

    @staticmethod
    def sems(size):
        return [pltpu.SemaphoreType.DMA((1,))] + [pltpu.SemaphoreType.DMA((2, size))] * 2

    def half(self, h, m, ref=None):
        ref = self.out.at[flip(self.me, m)] if ref is None else ref
        return ref.at[pl.ds(h * self.rows, self.rows), :]

    def push(self, h, m, bit):
        source = self.half(h, m, self.source if m == 0 else None)
        key = (h, m | bit)
        self.started.append(
            remote(
                source, self.half(h, m), self.send.at[key], self.recv.at[key],
                (self.place, flip(self.me, bit)),
            )
        )

    def arrived(self, h, m):
        wait_for(self.half(h, m), self.recv.at[h, m])

    def start(self):
        pltpu.make_async_copy(self.source, self.out.at[self.me], self.own_sem.at[0]).start()
        for h in range(2):
            self.push(h, 0, self.orders[h][0])
        for h in range(2):
            self.push(h, 0, 1)

    def own(self):
        wait_for(self.out.at[self.me], self.own_sem.at[0])

    def step(self, k, use=None):
        for h in range(2):
            order = self.orders[h]
            old = masks_of(order[:k])
            if k + 1 < self.steps:
                for m in old:
                    self.push(h, m, order[k + 1])
            for m in old:
                fresh = m | order[k]
                self.arrived(h, fresh)
                if k + 1 < self.steps:
                    self.push(h, fresh, order[k + 1])
                self.push(h, fresh, 1)
                if use:
                    use(h, fresh)

    def paired(self, use=None):
        for m in masks_of(self.orders[0]):
            for h in range(2):
                self.arrived(h, m | 1)
                if use:
                    use(h, m | 1)

    def drain(self):
        for copy in self.started:
            copy.wait_send()


def front_kernel(size, seq, direct, *refs):
    (tokens, cot, notes, w_local, out_w, x_w, dt_w, taps_ref, bias_ref, dt_bias_ref) = refs[:10]
    (
        normed_out, cot_out, w_out, x_out, delta_out, gy_out, pre_out, gate_out, gg_out, cext_out,
        proj_ref, rank_ref, all_notes,
    ) = refs[10:23]
    (
        tok, normed, cot_s, wc, wg, cext, pre, xb, x_s, delta_s, gy_s, gate_s, gg_s, gain_ref,
    ) = refs[23:37]
    token_sems, cot_sems = refs[37:40], refs[40:43]
    part, near, total, mail, far, out, sems = refs[43:50]
    note_send, note_recv, wc_send, wc_recv, wg_send, wg_recv, halo_send, halo_recv, out_sems = refs[50:]
    me, parity, partner, others = row_peers(size)
    place = lax.axis_index("seq")
    tt, width = tokens.shape
    share, el = wc.shape[1:]
    blocks = el // LANES
    half = size // 2
    f32, bf16 = jnp.float32, jnp.bfloat16
    tile = 32
    stores = []

    def put(source, target):
        copy = pltpu.make_async_copy(source, target, out_sems.at[len(stores)])
        copy.start()
        stores.append(copy)

    def piece(q, gate):
        if direct:
            at = pl.multiple_of(q * el, LANES) + gate * size * el
            return w_local.at[:, pl.ds(at, el)]
        return w_local.at[q, :, pl.ds(gate * el, el)]

    def swap(gate, target, send, recv):
        copies = []
        for m in range(1, size):
            q = flip(me, m)
            copies.append(remote(piece(q, gate), target.at[me], send.at[m], recv.at[m], (place, q)))
        pltpu.make_async_copy(piece(me, gate), target.at[me], recv.at[0]).start()
        return copies

    def swapped(target, recv):
        for m in range(size):
            wait_for(target.at[flip(me, m)], recv.at[m])

    greet_rows_and_seq(size, seq)

    sent = []
    for m in range(1, size):
        sent.append(remote(notes, all_notes.at[me], note_send.at[m], note_recv.at[m], (place, flip(me, m))))
    pltpu.make_async_copy(notes, all_notes.at[me], note_recv.at[0]).start()
    token_rows = RowGather(size, tokens, tok, *token_sems)
    cot_rows = RowGather(size, cot, cot_s, *cot_sems)
    token_rows.start()
    sent += swap(0, wc, wc_send, wc_recv)

    for m in range(size):
        wait_for(all_notes.at[flip(me, m)], note_recv.at[m])
    for p in range(size):
        gain_ref[:, p * share : (p + 1) * share] = all_notes[p, 0:1, :share].astype(f32)

    def norm(p, base, rows):
        def body(span):
            there = pl.ds(base + span.start, span.size)
            x = tok[p, there, :].astype(f32)
            inv = lax.rsqrt(jnp.mean(x * x, axis=1, keepdims=True) + epsilon)
            normed[p, there, :] = (x * inv * gain_ref[...]).astype(bf16)

        by_tiles(rows, 16, body)

    def norm_half(h, m):
        norm(flip(me, m), h * (tt // 2), tt // 2)

    token_rows.own()
    norm(me, 0, tt)
    for k in range(token_rows.steps):
        token_rows.step(k, norm_half)
    cot_rows.start()
    sent += swap(1, wg, wg_send, wg_recv)
    token_rows.paired(norm_half)
    swapped(wc, wc_recv)

    @pl.when(place == 0)
    def _():
        cext[:, 0:16, :] = jnp.zeros((size, 16, el), bf16)

    def halo(p, i):
        there = cext.at[p, pl.ds(0, 16), :]
        return pltpu.make_async_remote_copy(
            src_ref=cext.at[p, pl.ds(tt, 16), :], dst_ref=there, send_sem=halo_send.at[i],
            recv_sem=halo_recv.at[i], device_id=(jnp.minimum(place + 1, seq - 1), me), device_id_type=MESH,
        )

    def block_at(i):
        return 2 * lax.rem(me // 2 + lax.rem(i, half), half) + lax.rem(parity + 1 + lax.div(i, half), 2)

    def mix(i, none):
        p = block_at(i)
        weight = wc[...].reshape(size * share, el)
        cext[p, 16:, :] = jnp.dot(normed[p], weight, preferred_element_type=f32).astype(bf16)

        @pl.when(place < seq - 1)
        def _():
            halo(p, i).start()

        return none

    lax.fori_loop(0, size, mix, 0)
    for p in range(size):
        put(normed.at[p], normed_out.at[p])

    def conv(i, none):
        p = block_at(i)

        @pl.when(place > 0)
        def _():
            halo(p, i).wait_recv()

        def body(span):
            ext = cext[p, pl.ds(span.start, tile + 16), :].astype(f32)
            value = bias_ref[...]
            for k in range(KC):
                value = value + taps_ref[k : k + 1, :] * ext[16 - KC + 1 + k : 16 - KC + 1 + k + tile]
            pre[p, span, :] = value
            x = (value / (1.0 + jnp.exp(-value))).astype(bf16)
            xb[p, span, :] = x
            for b in range(blocks):
                there = pl.ds(p + span.start * size, tile, stride=size)
                x_s[b, there, :] = x[:, b * LANES : (b + 1) * LANES].astype(f32)

        by_tiles(tt, tile, body)
        value = jnp.dot(xb[p], x_w[...], preferred_element_type=f32)

        @pl.when(i < half)
        def _():
            part[p] = value.astype(bf16)
            pltpu.make_async_remote_copy(
                src_ref=part.at[p], dst_ref=near.at[lax.div(p, 2)], send_sem=sems.at[0, lax.div(p, 2)],
                recv_sem=sems.at[1, lax.div(p, 2)], device_id=(place, partner), device_id_type=MESH,
            ).start()

        @pl.when(i >= half)
        def _():
            total[lax.div(p, 2)] = value

        return none

    lax.fori_loop(0, size, conv, 0)
    put(cext, cext_out)
    put(pre, pre_out)
    put(x_s, x_out)

    def use(p):
        block = out[p]
        rank_ref[p] = block
        proj_ref[pl.ds(p, tt, stride=size), :] = block.astype(f32)

        def body(span):
            step = jnp.dot(out[p, span, :], dt_w[...], preferred_element_type=f32) + dt_bias_ref[...]
            delta = jnp.maximum(step, 0.0) + jnp.log1p(jnp.exp(-jnp.abs(step)))
            for b in range(blocks):
                there = pl.ds(p + span.start * size, 64, stride=size)
                delta_s[b, there, :] = delta[:, b * LANES : (b + 1) * LANES]

        by_tiles(tt, 64, body)

    def between():
        for k in range(cot_rows.steps):
            cot_rows.step(k)

    exchange_sums(size, near, total, mail, far, out, sems, use, between)
    for j in range(half):
        pltpu.make_async_remote_copy(
            src_ref=part.at[j], dst_ref=near.at[j], send_sem=sems.at[0, j], recv_sem=sems.at[1, j],
            device_id=(place, partner), device_id_type=MESH,
        ).wait_send()
    put(delta_s, delta_out)
    put(wc, w_out.at[:, :, pl.ds(0, el)])

    cot_rows.own()
    cot_rows.paired()
    put(cot_s, cot_out)
    swapped(wg, wg_recv)
    put(wg, w_out.at[:, :, pl.ds(el, el)])

    def gates(p, none):
        weight = wg[...].reshape(size * share, el)
        gate_s[p] = jnp.dot(normed[p], weight, preferred_element_type=f32)
        gg_s[p] = lax.dot_general(
            cot_s[p], out_w[...], (((1,), (1,)), ((), ())), preferred_element_type=f32
        )

        def body(span):
            gate = gate_s[p, span, :]
            gy = gg_s[p, span, :] * gate / (1.0 + jnp.exp(-gate))
            for b in range(blocks):
                there = pl.ds(p + span.start * size, tile, stride=size)
                gy_s[b, there, :] = gy[:, b * LANES : (b + 1) * LANES]

        by_tiles(tt, tile, body)
        return none

    lax.fori_loop(0, size, gates, 0)
    put(gy_s, gy_out)
    put(gate_s, gate_out)
    put(gg_s, gg_out)

    for i in range(size):

        @pl.when(place < seq - 1)
        def _(i=i):
            halo(i, i).wait_send()

    token_rows.drain()
    cot_rows.drain()
    for copy in sent:
        copy.wait_send()
    for copy in stores:
        copy.wait()


def front(tokens, cot, notes, w_local, out_w, x_w, dt_w, taps, bias, dt_bias, size, seq, direct):
    tt, width = tokens.shape
    el = out_w.shape[0]
    share = width // size
    blocks = el // LANES
    away = pl.BlockSpec(memory_space=pl.ANY)
    here = pl.BlockSpec(memory_space=pltpu.VMEM)
    f32, bf16 = jnp.float32, jnp.bfloat16
    rows, scan = (size, tt, width), (blocks, tt * size, LANES)
    channels, ext = (size, tt, el), (size, tt + 16, el)
    shapes = [
        (rows, bf16), (rows, bf16), ((size, share, 2 * el), bf16), (scan, f32), (scan, f32), (scan, f32),
        (channels, f32), (channels, f32), (channels, f32), (ext, bf16),
        ((tt * size, LANES), f32), ((size, tt, LANES), bf16), ((size,) + notes.shape, bf16),
    ]
    weights = (size, share, el)
    scratch = [
        (rows, bf16), (rows, bf16), (rows, bf16), (weights, bf16), (weights, bf16), (ext, bf16),
        (channels, f32), (channels, bf16), (scan, f32), (scan, f32), (scan, f32),
        (channels, f32), (channels, f32), ((1, width), f32),
    ]
    one = pltpu.SemaphoreType.DMA((size,))
    return pl.pallas_call(
        functools.partial(front_kernel, size, seq, direct),
        in_specs=[away] * 4 + [here] * 6,
        out_specs=[away] * 10 + [here] * 3,
        out_shape=[jax.ShapeDtypeStruct(*v) for v in shapes],
        scratch_shapes=[pltpu.VMEM(*v) for v in scratch]
        + RowGather.sems(size) * 2
        + sum_scratch(size, tt)
        + [one] * 8
        + [pltpu.SemaphoreType.DMA((size + 10,))],
        compiler_params=pltpu.CompilerParams(
            vmem_limit_bytes=62 * MIB, collective_id=0, has_side_effects=True
        ),
        name="front",
    )(tokens, cot, notes, w_local, out_w, x_w, dt_w, taps, bias, dt_bias)


class RowScatter:
    def __init__(self, size, part, keep, land, mail, keep_sem, send, recv):
        self.size, self.part, self.keep, self.land, self.mail = size, part, keep, land, mail
        self.keep_sem, self.send, self.recv = keep_sem, send, recv
        self.me, self.place = lax.axis_index("rows"), lax.axis_index("seq")
        self.tt, self.width = keep.shape[1], keep.shape[2] // 2
        self.orders = bit_orders(size)
        self.steps = len(self.orders[0])

    @staticmethod
    def scratch(size, tt, width):
        return [
            pltpu.VMEM((size // 2, tt, width), jnp.bfloat16),
            pltpu.VMEM((size - 1, tt, width), jnp.bfloat16),
            pltpu.VMEM((size // 2 - 1, tt, width), jnp.bfloat16),
            pltpu.SemaphoreType.DMA((size // 2,)),
            pltpu.SemaphoreType.DMA((2, size - 1)),
            pltpu.SemaphoreType.DMA((2, size - 1)),
        ]

    def free(self, h, k):
        return masks_of(self.orders[h][k + 1 :])

    def at(self, h, k, m):
        if k == 0:
            return m >> 1
        return sum(len(self.free(h, j)) for j in range(k)) + self.free(h, k).index(m)

    def cols(self, h):
        return pl.ds(h * self.width, self.width)

    def receive(self, h, k, m):
        slot = self.at(h, k, m)
        wait_for(self.land.at[slot, :, self.cols(h)], self.recv.at[h, slot])

    def partial_sum(self, h, k, m, rows):
        value = self.keep[m >> 1, rows, self.cols(h)].astype(jnp.float32)
        for j in range(k):
            value = value + self.land[self.at(h, j, m), rows, self.cols(h)].astype(jnp.float32)
        return value

    def staged(self, i, stage):
        for h in range(2):
            remote(
                stage.at[i, :, self.cols(h)], self.land.at[i, :, self.cols(h)], self.send.at[h, i],
                self.recv.at[h, i], (self.place, flip(self.me, 1)),
            )

    def start(self):
        for h in range(2):
            self.scatter(h, 0)
        for m in self.free(0, 0):
            pltpu.make_async_copy(
                self.part.at[flip(self.me, m)], self.keep.at[m >> 1], self.keep_sem.at[m >> 1]
            ).start()

    def step(self, k):
        if k == 1 and self.part is not None:
            for j in range(self.size // 2):
                wait_for(self.keep.at[j], self.keep_sem.at[j])
        for h in range(2):
            self.scatter(h, k)

    def scatter(self, h, k):
        bit = self.orders[h][k]
        for m in self.free(h, k):
            slot = self.at(h, k, m)
            if k == 0:
                source = self.part.at[flip(self.me, m | bit), :, self.cols(h)]
            else:
                for j in range(k):
                    self.receive(h, j, m | bit)
                box = slot - self.size // 2

                def fill(rows, m=m, box=box):
                    value = self.partial_sum(h, k, m | bit, rows)
                    self.mail[box, rows, self.cols(h)] = value.astype(jnp.bfloat16)

                by_tiles(self.tt, 32, fill)
                source = self.mail.at[box, :, self.cols(h)]
            remote(
                source, self.land.at[slot, :, self.cols(h)], self.send.at[h, slot], self.recv.at[h, slot],
                (self.place, flip(self.me, bit)),
            )

    def later(self, first):
        for k in range(first, self.steps):
            self.step(k)

    def finish(self, own):
        for h in range(2):
            for j in range(self.steps):
                self.receive(h, j, 0)

            def fill(rows, h=h):
                own[rows, self.cols(h)] = self.partial_sum(h, self.steps, 0, rows).astype(jnp.bfloat16)

            by_tiles(self.tt, 32, fill)

    def drain(self):
        for h in range(2):
            for slot in range(self.size - 1):
                wait_for(self.land.at[slot, :, self.cols(h)], self.send.at[h, slot])


class SeqSum:
    def __init__(self, seq, lag, held, land, mail, fill_sem, send, recv):
        self.seq, self.lag, self.held, self.land, self.mail = seq, lag, held, land, mail
        self.fill_sem, self.send, self.recv = fill_sem, send, recv
        self.me, self.place = lax.axis_index("rows"), lax.axis_index("seq")
        self.behind = (self.place, seq - 1 - self.place)
        self.chunks = held.shape[0]
        self.last_step = self.chunks + lag * (seq - 1)

    @staticmethod
    def scratch(chunks, block):
        return [
            pltpu.VMEM((chunks,) + block, jnp.bfloat16),
            pltpu.VMEM((2, chunks) + block, jnp.bfloat16),
            pltpu.VMEM((2, chunks) + block, jnp.bfloat16),
            pltpu.SemaphoreType.DMA((chunks,)),
            pltpu.SemaphoreType.DMA((2, chunks)),
            pltpu.SemaphoreType.DMA((2, chunks)),
        ]

    def copy(self, n, way, source):
        target = (jnp.clip(self.place + 1 - 2 * way, 0, self.seq - 1), self.me)
        return pltpu.make_async_remote_copy(
            src_ref=source, dst_ref=self.land.at[way, n], send_sem=self.send.at[way, n],
            recv_sem=self.recv.at[way, n], device_id=target, device_id_type=MESH,
        )

    def hop(self, step, way):
        n = step - self.lag * self.behind[way]

        @pl.when((n >= 0) & (n < self.chunks))
        def _():
            @pl.when(self.behind[way] == 0)
            def _():
                self.copy(n, way, self.held.at[n]).start()

            @pl.when(self.behind[way] > 0)
            def _():
                self.copy(n, way, self.held.at[n]).wait_recv()

                @pl.when(self.behind[way] < self.seq - 1)
                def _():
                    value = self.held[n].astype(jnp.float32) + self.land[way, n].astype(jnp.float32)
                    self.mail[way, n] = value.astype(jnp.bfloat16)
                    self.copy(n, way, self.mail.at[way, n]).start()

    def advance(self, step, total):
        first = step - self.lag * jnp.minimum(self.behind[0], self.behind[1])

        @pl.when((first >= 0) & (first < self.chunks))
        def _():
            wait_for(self.held.at[first], self.fill_sem.at[first])

        self.hop(step, 0)
        self.hop(step, 1)
        n = step - self.lag * jnp.maximum(self.behind[0], self.behind[1])

        @pl.when((n >= 0) & (n < self.chunks))
        def _():
            for ways, there in (
                ((1,), self.behind[0] == 0),
                ((0,), self.behind[1] == 0),
                ((0, 1), (self.behind[0] > 0) & (self.behind[1] > 0)),
            ):

                @pl.when(there)
                def _(ways=ways):
                    value = self.held[n].astype(jnp.float32)
                    for way in ways:
                        value = value + self.land[way, n].astype(jnp.float32)
                    total[n] = value.astype(jnp.bfloat16)

    def run(self, first, last, total):
        def body(step, none):
            self.advance(step, total)
            return none

        lax.fori_loop(first, last, body, 0)

    def drain(self):
        for way in range(2):

            @pl.when(self.behind[way] < self.seq - 1)
            def _(way=way):
                def sent(n, none):
                    self.copy(n, way, self.held.at[n]).wait_send()
                    return none

                lax.fori_loop(0, self.chunks, sent, 0)


def fill_chunks(size, held, fill_sem, swap_send, sources, weight):
    me, place = lax.axis_index("rows"), lax.axis_index("seq")
    rows, cols = held.shape[1:]
    n = 0
    for source in sources:
        for i in range(source.shape[0] // rows):
            for j in range(source.shape[1] // cols):
                piece = source.at[pl.ds(i * rows, rows), pl.ds(j * cols, cols)]
                pltpu.make_async_copy(piece, held.at[n], fill_sem.at[n]).start()
                n += 1
    for m in range(size):
        q = flip(me, m)
        for i in range(weight.shape[1] // rows):
            piece = weight.at[q, pl.ds(i * rows, rows), :]
            if m == 0:
                pltpu.make_async_copy(piece, held.at[n], fill_sem.at[n]).start()
            else:
                remote(piece, held.at[n], swap_send.at[n], fill_sem.at[n], (place, q))
            n += 1


def drain_swap(size, held, swap_send, weight):
    parts = weight.shape[1] // held.shape[1]
    first = held.shape[0] - (size - 1) * parts
    for n in range(first, held.shape[0]):
        wait_for(held.at[n], swap_send.at[n])


def backward_kernel(size, seq, nr, tt, ct, uu, *refs):
    delta_in, x_in, gy_in, hist_in, proj_ref, a_ref, carry_ref, last_ref, branch, out_w, gate_w = refs[:11]
    gdelta_out, gx_out, gbc_ref, grate_ref, branch_own, total = refs[11:17]
    sel, bc, hist, prod, state_ref, after_ref, fold, delta_ref, x_ref, gy_ref, gdelta_ref, gx_ref = refs[17:29]
    sems, out_sems, hist_sems = refs[29:32]
    scatter = RowScatter(size, branch, *refs[32:38])
    held, land, mail, fill_sem, zsend, zrecv, swap_send = refs[38:]
    chain = SeqSum(seq, 3, held, land, mail, fill_sem, zsend, zrecv)
    el = a_ref.shape[1]
    blocks = el // LANES
    count = tt // ct

    def fetch(c):
        slot = lax.rem(c, 2)
        return pltpu.make_async_copy(hist_in.at[pl.ds(c * ct, ct)], hist.at[slot], hist_sems.at[slot])

    copies = copy_all((delta_in, x_in, gy_in), (delta_ref, x_ref, gy_ref), sems)
    fetch(count - 1).start()
    greet_rows_and_seq(size, seq)
    scatter.start()
    fill_chunks(size, held, fill_sem, swap_send, (out_w,), gate_w)
    sel[...] = selector(LANES)
    fold_row = lax.broadcasted_iota(jnp.int32, fold.shape, 0) // LANES
    fold_col = lax.broadcasted_iota(jnp.int32, fold.shape, 1)
    fold[...] = (fold_row + R == fold_col).astype(jnp.bfloat16)
    state_ref[...] = carry_ref[1]
    after_ref[...] = last_ref[...]
    grate_ref[...] = jnp.zeros_like(grate_ref)
    for copy in copies:
        copy.wait()

    def backward(k, none):
        c = count - 1 - k
        slot = lax.rem(c, 2)

        @pl.when(c > 0)
        def _():
            fetch(c - 1).start()

        for at_k, job in (
            (1, functools.partial(scatter.step, 1)),
            (count // 2, functools.partial(scatter.later, 2)),
            (count - 2, functools.partial(scatter.finish, branch_own)),
        ):
            pl.when(k == at_k)(job)

        rows = pl.multiple_of(c * (ct * nr), ct * nr)
        bc[...] = spread(proj_ref[pl.ds(rows, ct * nr), :], sel)
        fetch(c).wait()
        for b in range(blocks):
            lanes = slice(b * LANES, (b + 1) * LANES)
            for first in (True, False):
                ns = range(0, NS // 2) if first else range(NS // 2, NS)
                pairs = range(ns[0] // 2, ns[-1] // 2 + 1)
                rate = [jnp.broadcast_to(a_ref[n : n + 1, lanes], (nr, LANES)) for n in ns]

                def steps(s, carried):
                    grad, total_rate, after = (list(v) for v in carried)
                    for u in reversed(range(uu)):
                        at = (ct // uu - 1 - s) * uu + u
                        here = pl.ds(pl.multiple_of((c * ct + at) * nr, nr), nr)
                        delta = delta_ref[b, here, :]
                        x = x_ref[b, here, :]
                        gy = gy_ref[b, here, :]
                        du = delta * x
                        near = pl.ds(pl.multiple_of(at * nr, nr), nr)
                        along_rate = along_b = None
                        for p in pairs:
                            pair = hist[slot, at, b, pl.ds(2 * p * nr, 2 * nr), :].astype(jnp.float32)
                            for n, before in ((2 * p, pair[:nr]), (2 * p + 1, pair[nr:])):
                                i = n - ns[0]
                                to_b_at = slice(n * LANES, (n + 1) * LANES)
                                to_c_at = slice((NS + n) * LANES, (NS + n + 1) * LANES)
                                decay = jnp.exp2(delta * rate[i])
                                grad[i] = grad[i] + gy * bc[near, to_c_at]
                                to_c = after[i] * gy
                                to_b = grad[i] * du
                                if b > 0:
                                    to_c = to_c + prod[near, to_c_at]
                                    to_b = to_b + prod[near, to_b_at]
                                prod[near, to_c_at] = to_c
                                prod[near, to_b_at] = to_b
                                term_b = grad[i] * bc[near, to_b_at]
                                along_b = term_b if along_b is None else along_b + term_b
                                grad[i] = grad[i] * decay
                                weighted = grad[i] * before
                                total_rate[i] = total_rate[i] + weighted * delta
                                term = weighted * rate[i]
                                along_rate = term if along_rate is None else along_rate + term
                                after[i] = before
                        gdelta = along_rate * LN2 + along_b * x
                        gx = along_b * delta
                        if not first:
                            gdelta = gdelta + gdelta_ref[b, here, :]
                            gx = gx + gx_ref[b, here, :]
                        gdelta_ref[b, here, :] = gdelta
                        gx_ref[b, here, :] = gx
                    return tuple(grad), tuple(total_rate), tuple(after)

                start = tuple(tuple(ref[n, :, lanes] for n in ns) for ref in (state_ref, grate_ref, after_ref))
                ends = lax.fori_loop(0, ct // uu, steps, start)
                for i, n in enumerate(ns):
                    for ref, end in zip((state_ref, grate_ref, after_ref), ends):
                        ref[n, :, lanes] = end[i]
            if b < 2:
                chain.advance(2 * k + b, total)
        gbc_ref[pl.ds(rows, ct * nr), :] = jnp.dot(
            prod[...].astype(jnp.bfloat16), fold[...], preferred_element_type=jnp.float32
        )
        return none

    lax.fori_loop(0, count, backward, 0)
    late = copy_all((gdelta_ref, gx_ref), (gdelta_out, gx_out), out_sems)
    done = min(2, blocks) * count if blocks > 1 else count
    chain.run(2 * count, max(2 * count, chain.last_step), total)
    scatter.drain()
    chain.drain()
    drain_swap(size, held, swap_send, gate_w)
    for copy in late:
        copy.wait()


def scan_backward(delta, x, gy, hist, proj, rate, carry, last, branch, out_w, gate_w, size, seq):
    nr, tt, width = branch.shape
    el = rate.shape[1]
    blocks = el // LANES
    ct = math.gcd(tt, 16)
    here = pl.BlockSpec(memory_space=pltpu.VMEM)
    away = pl.BlockSpec(memory_space=pl.ANY)
    f32, bf16 = jnp.float32, jnp.bfloat16
    scan = (blocks, nr * tt, LANES)
    piece = gate_w.shape[1:]
    chunks = (out_w.size + gate_w.size) // math.prod(piece)
    return pl.pallas_call(
        functools.partial(backward_kernel, size, seq, nr, tt, ct, min(8, ct)),
        in_specs=[away] * 4 + [here] * 4 + [away] * 3,
        out_specs=[away] * 2 + [here] * 4,
        out_shape=[
            jax.ShapeDtypeStruct(scan, f32),
            jax.ShapeDtypeStruct(scan, f32),
            jax.ShapeDtypeStruct((tt * nr, LANES), f32),
            jax.ShapeDtypeStruct((NS, nr, el), f32),
            jax.ShapeDtypeStruct((tt, width), bf16),
            jax.ShapeDtypeStruct((chunks,) + piece, bf16),
        ],
        scratch_shapes=[
            pltpu.VMEM((LANES, 2 * NS * LANES), bf16),
            pltpu.VMEM((ct * nr, 2 * NS * LANES), f32),
            pltpu.VMEM((2, ct, blocks, NS * nr, LANES), bf16),
            pltpu.VMEM((ct * nr, 2 * NS * LANES), f32),
            pltpu.VMEM((NS, nr, el), f32),
            pltpu.VMEM((NS, nr, el), f32),
            pltpu.VMEM((2 * NS * LANES, LANES), bf16),
        ]
        + [pltpu.VMEM(scan, f32)] * 5
        + [
            pltpu.SemaphoreType.DMA((3,)),
            pltpu.SemaphoreType.DMA((2,)),
            pltpu.SemaphoreType.DMA((2,)),
        ]
        + RowScatter.scratch(size, tt, width)
        + SeqSum.scratch(chunks, piece)
        + [pltpu.SemaphoreType.DMA((chunks,))],
        compiler_params=pltpu.CompilerParams(
            vmem_limit_bytes=62 * MIB, collective_id=3, has_side_effects=True
        ),
        name="scan_backward",
    )(delta, x, gy, hist, proj, rate, carry, last, branch, out_w, gate_w)


def small_rows(piece_rows):
    rows = 2 * LANES + 32
    return rows + -rows % piece_rows


def back_kernel(size, seq, *refs):
    gdelta_in, gx_in, delta_in, normed_in, w_in, pre_in, cext_in, ggp_in, gbc_in = refs[:9]
    rank_ref, dt_w, x_w, taps_ref, rate_ref, grate_ref = refs[9:15]
    own, sums = refs[15:17]
    (
        gdelta, gx, delta, normed, wv, pre, cext, gmix, gbc, low, gcp, turned, w_stage, acc_x, acc_dt, acc,
        small, hmail, hland, stage,
    ) = refs[17:37]
    part, near, total, mail, far, out, sems = refs[37:44]
    scatter = RowScatter(size, None, *refs[44:50])
    held, zland, zmail, fill_sem, zsend, zrecv = refs[50:56]
    swap_send, in_sems, halo_send, halo_recv = refs[56:]
    chain = SeqSum(seq, 2, held, zland, zmail, fill_sem, zsend, zrecv)
    me, parity, partner, others = row_peers(size)
    place = lax.axis_index("seq")
    share, el = w_stage.shape[1:]
    tt = low.shape[0]
    width = normed.shape[1]
    blocks = el // LANES
    half = size // 2
    f32, bf16 = jnp.float32, jnp.bfloat16
    nt = (((1,), (1,)), ((), ()))
    tn = (((0,), (0,)), ((), ()))
    copies = copy_all(
        (gdelta_in, delta_in, gbc_in, pre_in, cext_in, gx_in, ggp_in, w_in, normed_in),
        (gdelta, delta, gbc, pre, cext, gx, gmix.at[:, :, pl.ds(el, el)], wv, normed),
        in_sems,
    )
    greet_rows_and_seq(size, seq)
    for ref in (acc_x, acc_dt, acc, small):
        ref[...] = jnp.zeros_like(ref)
    for copy in copies[:3]:
        copy.wait()

    def fold8(value):
        return jnp.sum(value.reshape(value.shape[0] // 8, 8, value.shape[1]), axis=0)

    def block_at(i):
        return 2 * lax.rem(me // 2 + lax.rem(i, half), half) + lax.rem(parity + 1 + lax.div(i, half), 2)

    def steps_back(i, none):
        p = block_at(i)

        def body(span):
            for b in range(blocks):
                lanes = slice(b * LANES, (b + 1) * LANES)
                there = pl.ds(p + span.start * size, 32, stride=size)
                dl = delta[b, there, :]
                near_zero = dl * (1.0 - dl * (0.5 - dl * (1.0 / 6.0)))
                value = gdelta[b, there, :] * jnp.where(dl < 0.01, near_zero, 1.0 - jnp.exp(-dl))
                low[span, lanes] = value.astype(bf16)
                acc[KC + 1, :, lanes] = acc[KC + 1, :, lanes] + fold8(value)

        by_tiles(tt, 32, body)
        value = lax.dot_general(low[...], dt_w[...], nt, preferred_element_type=f32)
        value = value + gbc[pl.ds(p, tt, stride=size), :]
        acc_dt[...] += lax.dot_general(rank_ref[p], low[...], tn, preferred_element_type=f32)

        @pl.when(i < half)
        def _():
            part[p] = value.astype(bf16)
            remote(
                part.at[p], near.at[lax.div(p, 2)], sems.at[0, lax.div(p, 2)], sems.at[1, lax.div(p, 2)],
                (place, partner),
            )

        @pl.when(i >= half)
        def _():
            total[lax.div(p, 2)] = value

        return none

    lax.fori_loop(0, size, steps_back, 0)
    for copy in copies[3:]:
        copy.wait()
    exchange_sums(size, near, total, mail, far, out, sems, lambda p: None)
    for j in range(half):
        wait_for(near.at[j], sems.at[0, j])

    def halo(p):
        return pltpu.make_async_remote_copy(
            src_ref=hmail.at[p], dst_ref=hland.at[p], send_sem=halo_send.at[p], recv_sem=halo_recv.at[p],
            device_id=(jnp.maximum(place - 1, 0), me), device_id_type=MESH,
        )

    def conv_back(p, none):
        def body(span):
            value = lax.dot_general(out[p, span, :], x_w[...], nt, preferred_element_type=f32)
            there = pl.ds(p + span.start * size, 32, stride=size)
            value = value + jnp.concatenate([gx[b, there, :] for b in range(blocks)], axis=1)
            here = pre[p, span, :]
            sig = 1.0 / (1.0 + jnp.exp(-here))
            low[span, :] = (here * sig).astype(bf16)
            value = value * sig * (1.0 + here * (1.0 - sig))
            gcp[p, span, :] = value
            ext = cext[p, pl.ds(span.start, 48), :].astype(f32)
            acc[KC] = acc[KC] + fold8(value)
            for k in range(KC):
                acc[k] = acc[k] + fold8(value * ext[16 - KC + 1 + k : 16 - KC + 1 + k + 32])

        by_tiles(tt, 32, body)
        acc_x[...] += lax.dot_general(out[p], low[...], tn, preferred_element_type=f32)
        hmail[p] = gcp[p, 0:16, :].astype(bf16)

        @pl.when(place > 0)
        def _():
            halo(p).start()

        return none

    lax.fori_loop(0, size, conv_back, 0)

    def turn(p, none):
        @pl.when(place < seq - 1)
        def _():
            halo(p).wait_recv()
            gcp[p, tt : tt + 8, :] = hland[p, 0:8, :].astype(f32)

        @pl.when(place == seq - 1)
        def _():
            gcp[p, tt : tt + 8, :] = jnp.zeros((8, el), f32)

        def body(span):
            ext = gcp[p, pl.ds(span.start, 40), :]
            value = taps_ref[KC - 1 : KC, :] * ext[0:32]
            for k in range(KC - 1):
                value = value + taps_ref[k : k + 1, :] * ext[KC - 1 - k : KC - 1 - k + 32]
            gmix[p, span, 0:el] = value.astype(bf16)

        by_tiles(tt, 32, body)
        columns = pl.ds(pl.multiple_of(p * tt, tt), tt)
        turned[:, columns] = jnp.transpose(gmix[p, :, 0:el].astype(f32)).astype(bf16)
        return none

    lax.fori_loop(0, size, turn, 0)

    group = 384 // share

    def weights(j, none):
        columns = pl.ds(pl.multiple_of(j * 384, 384), 384)
        value = jnp.dot(turned[...], normed[:, columns], preferred_element_type=f32)
        value = jnp.transpose(value).astype(bf16)
        for g in range(group):
            w_stage[j * group + g] = value[g * share : (g + 1) * share, :]
        return none

    lax.fori_loop(0, width // 384, weights, 0)
    rows = 2 * LANES
    small[0:LANES, :] = acc_x[...].astype(bf16)
    small[LANES:rows, :] = acc_dt[...].astype(bf16)
    rate_sum = jnp.sum(grate_ref[...], axis=1) * rate_ref[...]
    last = [rate_sum] + [jnp.sum(acc[k], axis=0, keepdims=True) for k in range(KC + 2)]
    last.append(jnp.zeros((16 - KC - 2, el), f32))
    small[rows : rows + 32, :] = jnp.concatenate(last, axis=0).astype(bf16)
    fill_chunks(size, held, fill_sem, swap_send, (small,), w_stage)

    def spread_back(i, none):
        p = crossed(me, jnp.where(i < half, 2 * i + 1, 2 * (i - half)), size)
        weight = wv[...].reshape(width, 2 * el)
        value = lax.dot_general(gmix[p], weight, nt, preferred_element_type=f32).astype(bf16)

        @pl.when(i < half)
        def _():
            stage[i] = value
            scatter.staged(i, stage)

        @pl.when(i >= half)
        def _():
            scatter.keep[i - half] = value

        chain.advance(i, sums)
        return none

    lax.fori_loop(0, size, spread_back, 0)
    jobs = [functools.partial(scatter.step, k) for k in range(1, scatter.steps)]
    jobs.append(functools.partial(scatter.finish, own))
    done = size
    for i, job in enumerate(jobs):
        job()
        upto = min(chain.last_step, done + chain.last_step // 4)
        chain.run(done, upto, sums)
        done = upto
    chain.run(done, max(done, chain.last_step), sums)
    scatter.drain()
    chain.drain()
    drain_swap(size, held, swap_send, w_stage)

    def halo_sent(p, none):
        halo(p).wait_send()
        return none

    @pl.when(place > 0)
    def _():
        lax.fori_loop(0, size, halo_sent, 0)


def back(gdelta, gx, delta, normed, w_in, pre, cext, ggp, gbc, rank, dt_w, x_w, taps, rate, grate, size, seq):
    away = pl.BlockSpec(memory_space=pl.ANY)
    here = pl.BlockSpec(memory_space=pltpu.VMEM)
    f32, bf16 = jnp.float32, jnp.bfloat16
    unused_size, tt, el = pre.shape
    share = w_in.shape[1]
    width = normed.shape[1]
    piece = (share // 2, el)
    low = small_rows(piece[0])
    chunks = 2 * size + low // piece[0]
    scratch = [
        (gdelta.shape, f32), (gx.shape, f32), (delta.shape, f32), (normed.shape, bf16), (w_in.shape, bf16),
        (pre.shape, f32), (cext.shape, bf16), ((size, tt, 2 * el), bf16), (gbc.shape, f32), ((tt, el), bf16),
        ((size, tt + 8, el), f32), ((el, size * tt), bf16), ((size, share, el), bf16), ((LANES, el), f32),
        ((LANES, el), f32), ((KC + 2, 8, el), f32), ((low, el), bf16), ((size, 16, el), bf16),
        ((size, 16, el), bf16), ((size // 2, tt, width), bf16),
    ]
    return pl.pallas_call(
        functools.partial(back_kernel, size, seq),
        in_specs=[away] * 9 + [here] * 6,
        out_specs=[here] * 2,
        out_shape=[
            jax.ShapeDtypeStruct((tt, width), bf16),
            jax.ShapeDtypeStruct((chunks,) + piece, bf16),
        ],
        scratch_shapes=[pltpu.VMEM(*v) for v in scratch]
        + sum_scratch(size, tt)
        + RowScatter.scratch(size, tt, width)
        + SeqSum.scratch(chunks, piece)
        + [
            pltpu.SemaphoreType.DMA((chunks,)),
            pltpu.SemaphoreType.DMA((9,)),
            pltpu.SemaphoreType.DMA((size,)),
            pltpu.SemaphoreType.DMA((size,)),
        ],
        compiler_params=pltpu.CompilerParams(
            vmem_limit_bytes=63 * MIB, collective_id=4, has_side_effects=True
        ),
        name="back",
    )(gdelta, gx, delta, normed, w_in, pre, cext, ggp, gbc, rank, dt_w, x_w, taps, rate, grate)


def contract_rows(left, right):
    return lax.dot_general(left, right, (((0,), (0,)), ((), ())), preferred_element_type=jnp.float32)


def contract_cols(left, right):
    return lax.dot_general(left, right, (((1,), (1,)), ((), ())), preferred_element_type=jnp.float32)


def local(
    tokens, resets, norm_gain, in_proj, x_proj, dt_proj, conv_weight, conv_bias, dt_bias, a_log, out_proj,
    cotangent,
):
    size = lax.axis_size("rows")
    seq = lax.axis_size("seq")
    rd, tt, unused_d = tokens.shape
    nr = rd * size
    el = E // size
    count = nr * tt
    assert rd == 1 and ITEM % tt == 0 and nr % 8 == 0

    elp = pad_lanes(el)
    share = D // size
    direct = elp == el
    f32, bf16 = jnp.float32, jnp.bfloat16

    def widen(value, axis):
        pad = [(0, 0)] * value.ndim
        pad[axis] = (0, elp - el)
        return jnp.pad(value, pad)

    if direct:
        w_local = in_proj
    else:
        w_local = jnp.moveaxis(in_proj.reshape(share, 2, size, el), 2, 0)
        w_local = widen(w_local, 3).reshape(size, share, 2 * elp)
    out_proj, x_proj = widen(out_proj, 0), widen(x_proj, 0)
    dt_pad = widen(jnp.pad(dt_proj, ((0, LANES - R), (0, 0))), 1)
    taps = widen(conv_weight.astype(f32), 1)
    bias = widen(conv_bias.astype(f32), 0)[None]
    rate = widen(-jnp.exp(a_log.astype(f32)), 1)
    notes = jnp.zeros((16, -(-share // 256) * 256), bf16)
    notes = notes.at[0, :share].set(norm_gain).at[1, 0].set(1.0 - resets[0, 0].astype(bf16))
    (
        normed, all_cot, w_in, x_t, delta_t, gy_t, conv_pre, gate_pre, grad_gated, conv_ext, proj_t, rank_all,
        all_notes,
    ) = front(
        tokens[0], cotangent[0], notes, w_local, out_proj, x_proj, dt_pad, taps, bias,
        widen(dt_bias.astype(f32), 0)[None], size, seq, direct,
    )
    normed, all_cot = normed.reshape(count, D), all_cot.reshape(count, D)
    gate_pre, grad_gated = gate_pre.reshape(count, elp), grad_gated.reshape(count, elp)
    gain = all_notes[:, 0, :share].reshape(D).astype(f32)
    alive = all_notes[:, 1, :1].astype(f32)
    def by_row(value):
        value = value.reshape(elp // LANES, tt, nr, LANES)
        return jnp.transpose(value, (2, 1, 0, 3)).reshape(count, elp)

    rate2 = rate * LOG2E
    scanned = (delta_t, x_t, gy_t)
    carry = scan_ends(*scanned, proj_t, rate2, alive, nr, tt, seq)
    scan_y, hist, last = scan_forward(delta_t, x_t, proj_t, rate2, carry, nr, tt)
    scan_y = by_row(scan_y)
    gate_sig = jax.nn.sigmoid(gate_pre)
    gated = (scan_y * gate_pre * gate_sig).astype(bf16)
    grad_gate_pre = grad_gated * scan_y * gate_sig * (1.0 + gate_pre * (1.0 - gate_sig))
    grad_gate_pre = grad_gate_pre.astype(bf16)
    branch = jnp.dot(gated, out_proj, preferred_element_type=f32).astype(bf16)
    grad_out_proj = contract_rows(gated, all_cot).astype(bf16)[:el]
    grad_in_gate = contract_rows(normed, grad_gate_pre).astype(bf16).reshape(size, share, elp)
    grad_delta, grad_input, grad_bc, grate, branch_own, summed_gate = scan_backward(
        *scanned, hist, proj_t, rate2, carry, last, branch.reshape(nr, tt, D),
        grad_out_proj, grad_in_gate, size, seq,
    )
    grad_normed, summed_conv = back(
        grad_delta, grad_input, delta_t, normed, w_in, conv_pre, conv_ext,
        grad_gate_pre.reshape(nr, tt, elp), grad_bc, rank_all, dt_pad, x_proj, taps, rate, grate, size, seq,
    )
    piece = (share, elp)
    out_rows, out_cols = el // share, D // elp
    sum_out = summed_gate[: out_rows * out_cols].reshape(out_rows, out_cols, *piece)
    sum_out = jnp.swapaxes(sum_out, 1, 2).reshape(el, D).astype(f32)
    small = summed_conv[: -2 * size].reshape(-1, elp)[:, :el].astype(f32)
    order = jnp.array(range(size)) ^ lax.axis_index("rows")
    sum_in = jnp.stack([summed_conv[-2 * size :].reshape((size,) + piece)[order], summed_gate[-size:][order]])
    sum_in = jnp.transpose(sum_in[..., :el].astype(f32), (2, 0, 1, 3)).reshape(share, 2 * E)
    block_out = (tokens.astype(jnp.float32) + branch_own[None].astype(jnp.float32)).astype(jnp.bfloat16)
    grad_normed = grad_normed[None].astype(jnp.float32)

    own = tokens.astype(jnp.float32)
    inv = lax.rsqrt(jnp.mean(own * own, axis=2, keepdims=True) + epsilon)
    gain_own = jnp.sum(in_proj.astype(jnp.float32) * sum_in, axis=1) / norm_gain.astype(jnp.float32)
    grad_hat = grad_normed * gain
    grad_norm_in = inv * (
        grad_hat - own * (inv * inv) * jnp.mean(grad_hat * own, axis=2, keepdims=True)
    )
    d_tokens = (cotangent.astype(jnp.float32) + grad_norm_in).astype(jnp.bfloat16)

    more = small[2 * LANES :]
    return (
        block_out,
        d_tokens,
        gain_own,
        sum_in,
        small[:LANES].T,
        small[LANES : LANES + R],
        more[NS : NS + KC],
        more[NS + KC],
        more[NS + KC + 1],
        more[:NS],
        sum_out,
    )


def solution(mesh):
    in_specs = (
        P("rows", "seq", None),
        P("rows", "seq"),
        P("rows"),
        P("rows", None),
        P("rows", None),
        P(None, "rows"),
        P(None, "rows"),
        P("rows"),
        P("rows"),
        P(None, "rows"),
        P("rows", None),
        P("rows", "seq", None),
    )
    out_specs = (
        P("rows", "seq", None),
        P("rows", "seq", None),
        P("rows"),
        P("rows", None),
        P("rows", None),
        P(None, "rows"),
        P(None, "rows"),
        P("rows"),
        P("rows"),
        P(None, "rows"),
        P("rows", None),
    )
    return jax.shard_map(local, mesh=mesh, in_specs=in_specs, out_specs=out_specs, check_vma=False)
```

```python
import functools
import math

import jax
import jax.numpy as jnp
from jax import lax
from jax.experimental import pallas as pl
from jax.experimental.pallas import tpu as pltpu
from jax.sharding import PartitionSpec as P

D = 1536
E = 3072
R = 96
NS = 16
KC = 4
ITEM = 256

epsilon = 1e-05
LOG2E = 1.4426950408889634
LN2 = 0.6931471805599453
MIB = 2**20


LANES = 128


def pad_lanes(lanes):
    return -(-lanes // LANES) * LANES


def selector(wide):
    row = lax.broadcasted_iota(jnp.int32, (LANES, 2 * NS * wide), 0)
    col = lax.broadcasted_iota(jnp.int32, (LANES, 2 * NS * wide), 1) // wide
    return (row == col + R).astype(jnp.bfloat16)


def spread(proj, sel_ref):
    return jnp.dot(proj.astype(jnp.bfloat16), sel_ref[...], preferred_element_type=jnp.float32)


def copy_all(sources, targets, sems):
    copies = []
    for i, (source, target) in enumerate(zip(sources, targets)):
        copies.append(pltpu.make_async_copy(source, target, sems.at[i]))
        copies[-1].start()
    return copies


MESH = pl.DeviceIdType.MESH


def greet(devices):
    barrier = pltpu.get_barrier_semaphore()
    for device in devices:
        pl.semaphore_signal(barrier, inc=1, device_id=device, device_id_type=MESH)
    pl.semaphore_wait(barrier, len(devices))


def remote(source, target, send, recv, device):
    copy = pltpu.make_async_remote_copy(
        src_ref=source, dst_ref=target, send_sem=send, recv_sem=recv, device_id=device, device_id_type=MESH
    )
    copy.start()
    return copy


def row_peers(size):
    me = lax.axis_index("rows")
    half = size // 2
    mine = me // 2
    return me, me % 2, me + 1 - 2 * (me % 2), [lax.rem(mine + k, half) for k in range(half)]


def exchange_sums(size, near, total, mail, far, out, sems, use, between=None):
    me, parity, partner, others = row_peers(size)
    place = lax.axis_index("seq")
    half = size // 2
    second = []
    for k in list(range(1, half)) + [0]:
        j = others[k]
        wait_for(near.at[j], sems.at[1, j])
        total[j] = total[j] + near[j].astype(jnp.float32)
        if k:
            mail[j] = total[j].astype(jnp.bfloat16)
            target = (place, 2 * j + parity)
            second.append(remote(mail.at[j], far.at[k], sems.at[2, k], sems.at[3, k], target))
    mine = others[0]
    done = total[mine]
    for k in range(1, half):
        wait_for(far.at[k], sems.at[3, k])
        done = done + far[k].astype(jnp.float32)
    out[me] = done.astype(jnp.bfloat16)
    third = []
    for k in range(1, half):
        target = (place, 2 * others[k] + parity)
        third.append(remote(out.at[me], out.at[me], sems.at[4, k], sems.at[5, k], target))
    fourth = [remote(out.at[me], out.at[me], sems.at[6, 0], sems.at[7, 0], (place, partner))]
    use(me)
    for k in range(1, half):
        block = 2 * others[half - k] + parity
        wait_for(out.at[block], sems.at[5, k])
        fourth.append(
            remote(out.at[block], out.at[block], sems.at[6, k], sems.at[7, k], (place, partner))
        )
        use(block)
    for k in range(half):
        block = 2 * others[(half - k) % half] + 1 - parity
        wait_for(out.at[block], sems.at[7, k])
        use(block)
    if between:
        between()
    for copy in second + third + fourth:
        copy.wait_send()


def sum_scratch(size, tt):
    half = size // 2
    return [
        pltpu.VMEM((size, tt, LANES), jnp.bfloat16),
        pltpu.VMEM((half, tt, LANES), jnp.bfloat16),
        pltpu.VMEM((half, tt, LANES), jnp.float32),
        pltpu.VMEM((half, tt, LANES), jnp.bfloat16),
        pltpu.VMEM((half, tt, LANES), jnp.bfloat16),
        pltpu.VMEM((size, tt, LANES), jnp.bfloat16),
        pltpu.SemaphoreType.DMA((8, half)),
    ]


class Carry:
    def __init__(self, seq, ends, alive, out, mail, land, sems):
        self.seq, self.ends, self.alive, self.out = seq, ends, alive, out
        self.mail, self.land, self.sems = mail, land, sems
        self.me, self.place = lax.axis_index("rows"), lax.axis_index("seq")

    @staticmethod
    def scratch(shape):
        return [
            pltpu.VMEM((2,) + shape, jnp.bfloat16),
            pltpu.VMEM((2,) + shape, jnp.bfloat16),
            pltpu.SemaphoreType.DMA((2, 2)),
        ]

    def copy(self, way):
        target = (jnp.clip(self.place + 1 - 2 * way, 0, self.seq - 1), self.me)
        return pltpu.make_async_remote_copy(
            src_ref=self.mail.at[way], dst_ref=self.land.at[way], send_sem=self.sems.at[way, 0],
            recv_sem=self.sems.at[way, 1], device_id=target, device_id_type=MESH,
        )

    def hop(self, way):
        first, last = ((0, self.seq - 1), (self.seq - 1, 0))[way]
        alive = self.alive[:, 0:1][None]

        @pl.when(self.place == first)
        def _():
            self.out[way] = jnp.zeros_like(self.out[way])

        @pl.when(self.place != first)
        def _():
            self.copy(way).wait_recv()
            entering = self.land[way].astype(jnp.float32)
            self.out[way] = entering * alive if way == 0 else entering

        @pl.when(self.place != last)
        def _():
            if way == 0:
                leaving = self.ends[0] + self.ends[1] * self.out[0]
            else:
                leaving = (self.ends[2] + self.ends[1] * self.out[1]) * alive
            self.mail[way] = leaving.astype(jnp.bfloat16)
            self.copy(way).start()

    def turn(self, way, t):
        behind = (self.place, self.seq - 1 - self.place)[way]
        pl.when(behind == t)(functools.partial(self.hop, way))

    def drain(self):
        for way, last in ((0, self.seq - 1), (1, 0)):

            @pl.when(self.place != last)
            def _(way=way):
                self.copy(way).wait_send()


def flip(place, mask):
    for k in range(mask.bit_length()):
        bit = 1 << k
        if mask & bit:
            place = place + bit * (1 - 2 * (lax.div(place, bit) % 2))
    return place


def bit_orders(size):
    rest = [1 << k for k in range(1, size.bit_length() - 1)]
    cut = max(1, len(rest) // 2)
    return [1] + rest, [1] + rest[cut:] + rest[:cut]


def masks_of(bits):
    masks = [0]
    for bit in bits:
        masks = masks + [m | bit for m in masks]
    return masks


def by_tiles(rows, tile, body):
    def step(i, none):
        body(pl.ds(pl.multiple_of(i * tile, tile), tile))
        return none

    lax.fori_loop(0, rows // tile, step, 0)


def wait_for(ref, sem):
    pltpu.make_async_copy(ref, ref, sem).wait()


def greet_seq(seq):
    me, place = lax.axis_index("rows"), lax.axis_index("seq")
    barrier = pltpu.get_barrier_semaphore()
    for step, there in ((-1, place > 0), (1, place < seq - 1)):

        @pl.when(there)
        def _(step=step):
            pl.semaphore_signal(barrier, inc=1, device_id=(place + step, me), device_id_type=MESH)

    pl.semaphore_wait(barrier, (place > 0).astype(jnp.int32) + (place < seq - 1).astype(jnp.int32))


def greet_rows_and_seq(size, seq):
    me, place = lax.axis_index("rows"), lax.axis_index("seq")
    barrier = pltpu.get_barrier_semaphore()
    for mask in range(1, size):
        pl.semaphore_signal(barrier, inc=1, device_id=(place, flip(me, mask)), device_id_type=MESH)
    for step, there in ((-1, place > 0), (1, place < seq - 1)):

        @pl.when(there)
        def _(step=step):
            pl.semaphore_signal(barrier, inc=1, device_id=(place + step, me), device_id_type=MESH)

    near = (place > 0).astype(jnp.int32) + (place < seq - 1).astype(jnp.int32)
    pl.semaphore_wait(barrier, near + size - 1)


def crossed(place, mask, size):
    out = 0
    for k in range(size.bit_length() - 1):
        bit = 1 << k
        out = out + bit * lax.rem(lax.div(place, bit) + lax.div(mask, bit), 2)
    return out


class RowGather:
    def __init__(self, size, source, out, own_sem, send, recv):
        self.size, self.source, self.out, self.own_sem, self.send, self.recv = size, source, out, own_sem, send, recv
        self.me, self.place = lax.axis_index("rows"), lax.axis_index("seq")
        self.rows = source.shape[0] // 2
        self.orders = [order[1:] for order in bit_orders(size)]
        self.steps = len(self.orders[0])
        self.started = []

    @staticmethod
    def sems(size):
        return [pltpu.SemaphoreType.DMA((1,))] + [pltpu.SemaphoreType.DMA((2, size))] * 2

    def half(self, h, m, ref=None):
        ref = self.out.at[flip(self.me, m)] if ref is None else ref
        return ref.at[pl.ds(h * self.rows, self.rows), :]

    def push(self, h, m, bit):
        source = self.half(h, m, self.source if m == 0 else None)
        key = (h, m | bit)
        self.started.append(
            remote(
                source, self.half(h, m), self.send.at[key], self.recv.at[key],
                (self.place, flip(self.me, bit)),
            )
        )

    def arrived(self, h, m):
        wait_for(self.half(h, m), self.recv.at[h, m])

    def start(self):
        pltpu.make_async_copy(self.source, self.out.at[self.me], self.own_sem.at[0]).start()
        for h in range(2):
            self.push(h, 0, self.orders[h][0])
        for h in range(2):
            self.push(h, 0, 1)

    def own(self):
        wait_for(self.out.at[self.me], self.own_sem.at[0])

    def step(self, k, use=None):
        for h in range(2):
            order = self.orders[h]
            old = masks_of(order[:k])
            if k + 1 < self.steps:
                for m in old:
                    self.push(h, m, order[k + 1])
            for m in old:
                fresh = m | order[k]
                self.arrived(h, fresh)
                if k + 1 < self.steps:
                    self.push(h, fresh, order[k + 1])
                self.push(h, fresh, 1)
                if use:
                    use(h, fresh)

    def paired(self, use=None):
        for m in masks_of(self.orders[0]):
            for h in range(2):
                self.arrived(h, m | 1)
                if use:
                    use(h, m | 1)

    def drain(self):
        for copy in self.started:
            copy.wait_send()


def front_kernel(size, seq, direct, ct, uu, *refs):
    (tokens, cot, notes, w_local, out_w, x_w, dt_w, taps_ref, bias_ref, dt_bias_ref, a_ref) = refs[:11]
    (
        normed_out, w_out, x_out, delta_out, gy_out, cext_out, hist_out, branch_out, dout_out, dwg_out, ggp_out,
        proj_ref, rank_ref, all_notes, last_ref, leaving_ref,
    ) = refs[11:27]
    (
        tok, cot_s, wc, wg, cext, xb, x_s, delta_s, gy_s, gate_s, gg_s, gain_ref, alive_ref, sel, bc, ends, entered,
        delta_sum, hist, y_s, gated, ggp, branch_s, turned, d_stage, w_stage,
    ) = refs[27:53]
    token_sems, cot_sems = refs[53:56], refs[56:59]
    part, near, total, mail, far, out, sems = refs[59:66]
    carry = Carry(seq, ends, alive_ref, entered, *refs[66:69])
    (
        note_send, note_recv, wc_send, wc_recv, wg_send, wg_recv, halo_send, halo_recv, out_sems, hist_sems, branch_sems,
    ) = refs[69:]
    normed = tok
    me, parity, partner, others = row_peers(size)
    place = lax.axis_index("seq")
    tt, width = tokens.shape
    share, el = wc.shape[1:]
    nr = size
    blocks = el // LANES
    half = size // 2
    f32, bf16 = jnp.float32, jnp.bfloat16
    tile = 32
    stores = []

    def put(source, target):
        copy = pltpu.make_async_copy(source, target, out_sems.at[len(stores)])
        copy.start()
        stores.append(copy)

    def piece(q, gate):
        if direct:
            at = pl.multiple_of(q * el, LANES) + gate * size * el
            return w_local.at[:, pl.ds(at, el)]
        return w_local.at[q, :, pl.ds(gate * el, el)]

    def swap(gate, target, send, recv):
        copies = []
        for m in range(1, size):
            q = flip(me, m)
            copies.append(remote(piece(q, gate), target.at[me], send.at[m], recv.at[m], (place, q)))
        pltpu.make_async_copy(piece(me, gate), target.at[me], recv.at[0]).start()
        return copies

    def swapped(target, recv):
        for m in range(size):
            wait_for(target.at[flip(me, m)], recv.at[m])

    greet_rows_and_seq(size, seq)

    sent = []
    for m in range(1, size):
        sent.append(remote(notes, all_notes.at[me], note_send.at[m], note_recv.at[m], (place, flip(me, m))))
    pltpu.make_async_copy(notes, all_notes.at[me], note_recv.at[0]).start()
    token_rows = RowGather(size, tokens, tok, *token_sems)
    cot_rows = RowGather(size, cot, cot_s, *cot_sems)
    token_rows.start()
    sent += swap(0, wc, wc_send, wc_recv)

    for m in range(size):
        wait_for(all_notes.at[flip(me, m)], note_recv.at[m])
    for p in range(size):
        note = all_notes[p].astype(f32)
        gain_ref[:, p * share : (p + 1) * share] = note[0:1, :share]
        alive_ref[p : p + 1, :] = note[1:2, :LANES]

    def norm(p, base, rows):
        def body(span):
            there = pl.ds(base + span.start, span.size)
            x = tok[p, there, :].astype(f32)
            inv = lax.rsqrt(jnp.mean(x * x, axis=1, keepdims=True) + epsilon)
            normed[p, there, :] = (x * inv * gain_ref[...]).astype(bf16)

        by_tiles(rows, 16, body)

    def norm_half(h, m):
        norm(flip(me, m), h * (tt // 2), tt // 2)

    token_rows.own()
    norm(me, 0, tt)
    sel[...] = selector(LANES)
    for k in range(token_rows.steps):
        token_rows.step(k)
    cot_rows.start()
    sent += swap(1, wg, wg_send, wg_recv)
    token_rows.paired(norm_half)
    token_rows.drain()
    for m in masks_of(token_rows.orders[0])[1:]:
        norm(flip(me, m), 0, tt)
    swapped(wc, wc_recv)

    @pl.when(place == 0)
    def _():
        cext[:, 0:16, :] = jnp.zeros((size, 16, el), bf16)

    def halo(p, i):
        there = cext.at[p, pl.ds(0, 16), :]
        return pltpu.make_async_remote_copy(
            src_ref=cext.at[p, pl.ds(tt, 16), :], dst_ref=there, send_sem=halo_send.at[i],
            recv_sem=halo_recv.at[i], device_id=(jnp.minimum(place + 1, seq - 1), me), device_id_type=MESH,
        )

    def block_at(i):
        return 2 * lax.rem(me // 2 + lax.rem(i, half), half) + lax.rem(parity + 1 + lax.div(i, half), 2)

    def mix(i, none):
        p = block_at(i)
        weight = wc[...].reshape(size * share, el)
        cext[p, 16:, :] = jnp.dot(normed[p], weight, preferred_element_type=f32).astype(bf16)

        @pl.when(place < seq - 1)
        def _():
            halo(p, i).start()

        return none

    lax.fori_loop(0, size, mix, 0)
    for p in range(size):
        put(normed.at[p], normed_out.at[p])

    def conv(i, none):
        p = block_at(i)

        @pl.when(place > 0)
        def _():
            halo(p, i).wait_recv()

        def body(span):
            ext = cext[p, pl.ds(span.start, tile + 16), :].astype(f32)
            value = bias_ref[...]
            for k in range(KC):
                value = value + taps_ref[k : k + 1, :] * ext[16 - KC + 1 + k : 16 - KC + 1 + k + tile]
            x = (value / (1.0 + jnp.exp(-value))).astype(bf16)
            xb[span, :] = x
            for b in range(blocks):
                there = pl.ds(p + span.start * size, tile, stride=size)
                x_s[b, there, :] = x[:, b * LANES : (b + 1) * LANES].astype(f32)

        by_tiles(tt, tile, body)
        value = jnp.dot(xb[...], x_w[...], preferred_element_type=f32)

        @pl.when(i < half)
        def _():
            part[p] = value.astype(bf16)
            pltpu.make_async_remote_copy(
                src_ref=part.at[p], dst_ref=near.at[lax.div(p, 2)], send_sem=sems.at[0, lax.div(p, 2)],
                recv_sem=sems.at[1, lax.div(p, 2)], device_id=(place, partner), device_id_type=MESH,
            ).start()

        @pl.when(i >= half)
        def _():
            total[lax.div(p, 2)] = value

        return none

    lax.fori_loop(0, size, conv, 0)
    put(cext, cext_out)
    put(x_s, x_out)

    def use(p):
        block = out[p]
        rank_ref[p] = block
        proj_ref[pl.ds(p, tt, stride=size), :] = block.astype(f32)

        def body(span):
            step = jnp.dot(out[p, span, :], dt_w[...], preferred_element_type=f32) + dt_bias_ref[...]
            delta = jnp.maximum(step, 0.0) + jnp.log1p(jnp.exp(-jnp.abs(step)))
            for b in range(blocks):
                there = pl.ds(p + span.start * size, 64, stride=size)
                delta_s[b, there, :] = delta[:, b * LANES : (b + 1) * LANES]

        by_tiles(tt, 64, body)

    def between():
        for k in range(cot_rows.steps):
            cot_rows.step(k)

    exchange_sums(size, near, total, mail, far, out, sems, use, between)
    for j in range(half):
        pltpu.make_async_remote_copy(
            src_ref=part.at[j], dst_ref=near.at[j], send_sem=sems.at[0, j], recv_sem=sems.at[1, j],
            device_id=(place, partner), device_id_type=MESH,
        ).wait_send()
    put(delta_s, delta_out)
    put(wc, w_out.at[:, :, pl.ds(0, el)])

    count = tt // ct
    ends[0] = jnp.zeros((NS, nr, el), f32)
    ends[2] = jnp.zeros((NS, nr, el), f32)
    ends[3] = jnp.ones((NS, nr, el), f32)
    delta_sum[...] = jnp.zeros_like(delta_sum)

    def spread_chunk(c):
        rows = pl.multiple_of(c * (ct * nr), ct * nr)
        bc[...] = spread(proj_ref[pl.ds(rows, ct * nr), :], sel)

    def token(c, at):
        return pl.ds(pl.multiple_of((c * ct + at) * nr, nr), nr), pl.ds(pl.multiple_of(at * nr, nr), nr)

    def rates(ns, lanes):
        return [jnp.broadcast_to(a_ref[n : n + 1, lanes], (nr, LANES)) for n in ns]

    def ends_forward(c, none):
        spread_chunk(c)
        for b in range(blocks):
            lanes = slice(b * LANES, (b + 1) * LANES)
            rate = rates(range(NS), lanes)

            def steps(s, carried):
                state, so_far = list(carried[:-1]), carried[-1]
                for u in range(uu):
                    here, close = token(c, s * uu + u)
                    delta = delta_s[b, here, :]
                    du = delta * x_s[b, here, :]
                    so_far = so_far + delta
                    for n in range(NS):
                        b_at = n * LANES
                        state[n] = jnp.exp2(delta * rate[n]) * state[n] + du * bc[close, b_at : b_at + LANES]
                return tuple(state) + (so_far,)

            start = tuple(ends[0, n, :, lanes] for n in range(NS)) + (delta_sum[b],)
            last = lax.fori_loop(0, ct // uu, steps, start)
            for n in range(NS):
                ends[0, n, :, lanes] = last[n]
            delta_sum[b] = last[NS]
        return none

    lax.fori_loop(0, count, ends_forward, 0)
    for b in range(blocks):
        lanes = slice(b * LANES, (b + 1) * LANES)
        for n in range(NS):
            ends[1, n, :, lanes] = jnp.exp2(delta_sum[b] * a_ref[n : n + 1, lanes])
    carry.turn(0, 0)

    cot_rows.own()
    cot_rows.paired()
    swapped(wg, wg_recv)
    put(wg, w_out.at[:, :, pl.ds(el, el)])

    def gates(p):
        weight = wg[...].reshape(size * share, el)
        gate_s[...] = jnp.dot(normed[p], weight, preferred_element_type=f32)
        gg_s[...] = lax.dot_general(
            cot_s[p], out_w[...], (((1,), (1,)), ((), ())), preferred_element_type=f32
        )

    def grad_y(p, none):
        gates(p)

        def body(span):
            gate = gate_s[span, :]
            gy = gg_s[span, :] * gate / (1.0 + jnp.exp(-gate))
            for b in range(blocks):
                there = pl.ds(p + span.start * size, tile, stride=size)
                gy_s[b, there, :] = gy[:, b * LANES : (b + 1) * LANES]

        by_tiles(tt, tile, body)
        return none

    lax.fori_loop(0, size, grad_y, 0)
    put(gy_s, gy_out)
    carry.turn(0, 1)

    def hops(way, c, first):
        @pl.when(lax.rem(c, 2) == 1)
        def _():
            carry.turn(way, lax.div(c, 2) + first)

    def ends_back(c, none):
        spread_chunk(c)
        for b in range(blocks):
            lanes = slice(b * LANES, (b + 1) * LANES)
            for n0 in (0, NS // 2):
                ns = range(n0, n0 + NS // 2)
                rate = rates(ns, lanes)

                def steps(s, carried):
                    through, back = (list(v) for v in carried)
                    for u in range(uu):
                        here, close = token(c, s * uu + u)
                        delta = delta_s[b, here, :]
                        gy = gy_s[b, here, :]
                        for i, n in enumerate(ns):
                            c_at = (NS + n) * LANES
                            through[i] = through[i] * jnp.exp2(delta * rate[i])
                            back[i] = back[i] + through[i] * (gy * bc[close, c_at : c_at + LANES])
                    return tuple(through), tuple(back)

                start = tuple(tuple(ends[k, n, :, lanes] for n in ns) for k in (3, 2))
                last = lax.fori_loop(0, ct // uu, steps, start)
                for i, n in enumerate(ns):
                    ends[3, n, :, lanes] = last[0][i]
                    ends[2, n, :, lanes] = last[1][i]
        hops(0, c, 2)
        return none

    lax.fori_loop(0, count, ends_back, 0)
    for t in range(count // 2 + 2, seq):
        carry.turn(0, t)
    carry.turn(1, 0)
    last_ref[...] = entered[0]

    def store_hist(c):
        slot = lax.rem(c, 2)
        return pltpu.make_async_copy(hist.at[slot], hist_out.at[pl.ds(c * ct, ct)], hist_sems.at[slot])

    def forward(c, none):
        slot = lax.rem(c, 2)

        @pl.when(c >= 2)
        def _():
            store_hist(c - 2).wait()

        spread_chunk(c)
        for b in range(blocks):
            lanes = slice(b * LANES, (b + 1) * LANES)
            rate = rates(range(NS), lanes)

            def steps(s, carried):
                state = list(carried)
                for u in range(uu):
                    at = s * uu + u
                    here, close = token(c, at)
                    delta = delta_s[b, here, :]
                    du = delta * x_s[b, here, :]
                    y = None
                    for n in range(NS):
                        if n % 2 == 0:
                            both = jnp.concatenate([state[n], state[n + 1]], axis=0)
                            hist[slot, at, b, pl.ds(n * nr, 2 * nr), :] = both.astype(bf16)
                        b_at, c_at = n * LANES, (NS + n) * LANES
                        decay = jnp.exp2(delta * rate[n])
                        state[n] = decay * state[n] + du * bc[close, b_at : b_at + LANES]
                        term = state[n] * bc[close, c_at : c_at + LANES]
                        y = term if y is None else y + term
                    y_s[b, here, :] = y
                return tuple(state)

            last = lax.fori_loop(0, ct // uu, steps, tuple(last_ref[n, :, lanes] for n in range(NS)))
            for n in range(NS):
                last_ref[n, :, lanes] = last[n]
        store_hist(c).start()
        hops(1, c, 1)
        return none

    lax.fori_loop(0, count, forward, 0)
    for t in range(count // 2 + 1, seq):
        carry.turn(1, t)
    leaving_ref[...] = entered[1]

    def store_branch(i):
        slot = lax.rem(i, 2)
        return pltpu.make_async_copy(branch_s.at[slot], branch_out.at[i], branch_sems.at[slot])

    def turn(value, p):
        columns = pl.ds(pl.multiple_of(p * tt, tt), tt)
        turned[:, columns] = jnp.transpose(value.astype(f32)).astype(bf16)

    def products(p, none):
        gates(p)

        def body(span):
            there = pl.ds(p + span.start * size, tile, stride=size)
            y = jnp.concatenate([y_s[b, there, :] for b in range(blocks)], axis=1)
            gate = gate_s[span, :]
            sig = 1.0 / (1.0 + jnp.exp(-gate))
            gated[span, :] = (y * gate * sig).astype(bf16)
            ggp[p, span, :] = (gg_s[span, :] * y * sig * (1.0 + gate * (1.0 - sig))).astype(bf16)

        by_tiles(tt, tile, body)

        @pl.when(p >= 2)
        def _():
            store_branch(p - 2).wait()

        branch = jnp.dot(gated[...], out_w[...], preferred_element_type=f32)
        branch_s[lax.rem(p, 2)] = branch.astype(bf16)
        store_branch(p).start()
        turn(gated[...], p)
        return none

    lax.fori_loop(0, size, products, 0)
    put(ggp, ggp_out)
    wide = 384
    group = wide // share

    def out_weights(j, none):
        columns = pl.ds(pl.multiple_of(j * wide, wide), wide)
        right = cot_s[:, :, columns].reshape(size * tt, wide)
        d_stage[:, columns] = jnp.dot(turned[...], right, preferred_element_type=f32).astype(bf16)
        return none

    lax.fori_loop(0, width // wide, out_weights, 0)
    put(d_stage, dout_out)

    def turn_gate(p, none):
        turn(ggp[p], p)
        return none

    lax.fori_loop(0, size, turn_gate, 0)

    def gate_weights(j, none):
        columns = pl.ds(pl.multiple_of(j * wide, wide), wide)
        right = normed[:, :, columns].reshape(size * tt, wide)
        value = jnp.transpose(jnp.dot(turned[...], right, preferred_element_type=f32)).astype(bf16)
        for g in range(group):
            w_stage[j * group + g] = value[g * share : (g + 1) * share, :]
        return none

    lax.fori_loop(0, width // wide, gate_weights, 0)
    put(w_stage, dwg_out)
    for c in range(max(0, count - 2), count):
        store_hist(c).wait()
    for p in range(size - 2, size):
        store_branch(p).wait()
    carry.drain()

    for i in range(size):

        @pl.when(place < seq - 1)
        def _(i=i):
            halo(i, i).wait_send()

    cot_rows.drain()
    for copy in sent:
        copy.wait_send()
    for copy in stores:
        copy.wait()


def front(tokens, cot, notes, w_local, out_w, x_w, dt_w, taps, bias, dt_bias, rate, size, seq, direct):
    tt, width = tokens.shape
    el = out_w.shape[0]
    share = width // size
    blocks = el // LANES
    ct = math.gcd(tt, 32)
    away = pl.BlockSpec(memory_space=pl.ANY)
    here = pl.BlockSpec(memory_space=pltpu.VMEM)
    f32, bf16 = jnp.float32, jnp.bfloat16
    rows, scan, states = (size, tt, width), (blocks, tt * size, LANES), (NS, size, el)
    channels, ext = (size, tt, el), (size, tt + 16, el)
    weights = (size, share, el)
    shapes = [
        (rows, bf16), ((size, share, 2 * el), bf16), (scan, f32), (scan, f32), (scan, f32), (ext, bf16),
        ((tt, blocks, NS * size, LANES), bf16), (rows, bf16), ((el, width), bf16), (weights, bf16), (channels, bf16),
        ((tt * size, LANES), f32), ((size, tt, LANES), bf16), ((size,) + notes.shape, bf16), (states, f32),
        (states, f32),
    ]
    scratch = [
        (rows, bf16), (rows, bf16), (weights, bf16), (weights, bf16), (ext, bf16), ((tt, el), bf16), (scan, f32),
        (scan, f32), (scan, f32), ((tt, el), f32), ((tt, el), f32), ((1, width), f32), ((size, LANES), f32),
        ((LANES, 2 * NS * LANES), bf16), ((ct * size, 2 * NS * LANES), f32), ((4,) + states, f32), ((2,) + states, f32),
        ((blocks, size, LANES), f32), ((2, ct, blocks, NS * size, LANES), bf16), (scan, f32), ((tt, el), bf16), (channels, bf16),
        ((2, tt, width), bf16), ((el, size * tt), bf16), ((el, width), bf16), (weights, bf16),
    ]
    one = pltpu.SemaphoreType.DMA((size,))
    return pl.pallas_call(
        functools.partial(front_kernel, size, seq, direct, ct, min(8, ct)),
        in_specs=[away] * 4 + [here] * 7,
        out_specs=[away] * 11 + [here] * 5,
        out_shape=[jax.ShapeDtypeStruct(*v) for v in shapes],
        scratch_shapes=[pltpu.VMEM(*v) for v in scratch]
        + RowGather.sems(size) * 2
        + sum_scratch(size, tt)
        + Carry.scratch(states)
        + [one] * 8
        + [
            pltpu.SemaphoreType.DMA((size + 9,)),
            pltpu.SemaphoreType.DMA((2,)),
            pltpu.SemaphoreType.DMA((2,)),
        ],
        compiler_params=pltpu.CompilerParams(
            vmem_limit_bytes=63 * MIB, collective_id=0, has_side_effects=True
        ),
        name="front",
    )(tokens, cot, notes, w_local, out_w, x_w, dt_w, taps, bias, dt_bias, rate)


class RowScatter:
    def __init__(self, size, part, keep, land, mail, keep_sem, send, recv):
        self.size, self.part, self.keep, self.land, self.mail = size, part, keep, land, mail
        self.keep_sem, self.send, self.recv = keep_sem, send, recv
        self.me, self.place = lax.axis_index("rows"), lax.axis_index("seq")
        self.tt, self.width = keep.shape[1], keep.shape[2] // 2
        self.orders = bit_orders(size)
        self.steps = len(self.orders[0])

    @staticmethod
    def scratch(size, tt, width):
        return [
            pltpu.VMEM((size // 2, tt, width), jnp.bfloat16),
            pltpu.VMEM((size - 1, tt, width), jnp.bfloat16),
            pltpu.VMEM((size // 2 - 1, tt, width), jnp.bfloat16),
            pltpu.SemaphoreType.DMA((size // 2,)),
            pltpu.SemaphoreType.DMA((2, size - 1)),
            pltpu.SemaphoreType.DMA((2, size - 1)),
        ]

    def free(self, h, k):
        return masks_of(self.orders[h][k + 1 :])

    def at(self, h, k, m):
        if k == 0:
            return m >> 1
        return sum(len(self.free(h, j)) for j in range(k)) + self.free(h, k).index(m)

    def cols(self, h):
        return pl.ds(h * self.width, self.width)

    def receive(self, h, k, m):
        slot = self.at(h, k, m)
        wait_for(self.land.at[slot, :, self.cols(h)], self.recv.at[h, slot])

    def partial_sum(self, h, k, m, rows):
        value = self.keep[m >> 1, rows, self.cols(h)].astype(jnp.float32)
        for j in range(k):
            value = value + self.land[self.at(h, j, m), rows, self.cols(h)].astype(jnp.float32)
        return value

    def staged(self, i, stage):
        for h in range(2):
            remote(
                stage.at[i, :, self.cols(h)], self.land.at[i, :, self.cols(h)], self.send.at[h, i],
                self.recv.at[h, i], (self.place, flip(self.me, 1)),
            )

    def start(self):
        for h in range(2):
            self.scatter(h, 0)
        for m in self.free(0, 0):
            pltpu.make_async_copy(
                self.part.at[flip(self.me, m)], self.keep.at[m >> 1], self.keep_sem.at[m >> 1]
            ).start()

    def step(self, k):
        if k == 1 and self.part is not None:
            for j in range(self.size // 2):
                wait_for(self.keep.at[j], self.keep_sem.at[j])
        for h in range(2):
            self.scatter(h, k)

    def scatter(self, h, k):
        bit = self.orders[h][k]
        for m in self.free(h, k):
            slot = self.at(h, k, m)
            if k == 0:
                source = self.part.at[flip(self.me, m | bit), :, self.cols(h)]
            else:
                for j in range(k):
                    self.receive(h, j, m | bit)
                box = slot - self.size // 2

                def fill(rows, m=m, box=box):
                    value = self.partial_sum(h, k, m | bit, rows)
                    self.mail[box, rows, self.cols(h)] = value.astype(jnp.bfloat16)

                by_tiles(self.tt, 32, fill)
                source = self.mail.at[box, :, self.cols(h)]
            remote(
                source, self.land.at[slot, :, self.cols(h)], self.send.at[h, slot], self.recv.at[h, slot],
                (self.place, flip(self.me, bit)),
            )

    def later(self, first):
        for k in range(first, self.steps):
            self.step(k)

    def finish(self, own):
        for h in range(2):
            for j in range(self.steps):
                self.receive(h, j, 0)

            def fill(rows, h=h):
                own[rows, self.cols(h)] = self.partial_sum(h, self.steps, 0, rows).astype(jnp.bfloat16)

            by_tiles(self.tt, 32, fill)

    def drain(self):
        for h in range(2):
            for slot in range(self.size - 1):
                wait_for(self.land.at[slot, :, self.cols(h)], self.send.at[h, slot])


class SeqSum:
    def __init__(self, seq, lag, held, land, mail, fill_sem, send, recv):
        self.seq, self.lag, self.held, self.land, self.mail = seq, lag, held, land, mail
        self.fill_sem, self.send, self.recv = fill_sem, send, recv
        self.me, self.place = lax.axis_index("rows"), lax.axis_index("seq")
        self.behind = (self.place, seq - 1 - self.place)
        self.chunks = held.shape[0]
        self.last_step = self.chunks + lag * (seq - 1)

    @staticmethod
    def scratch(chunks, block):
        return [
            pltpu.VMEM((chunks,) + block, jnp.bfloat16),
            pltpu.VMEM((2, chunks) + block, jnp.bfloat16),
            pltpu.VMEM((2, chunks) + block, jnp.bfloat16),
            pltpu.SemaphoreType.DMA((chunks,)),
            pltpu.SemaphoreType.DMA((2, chunks)),
            pltpu.SemaphoreType.DMA((2, chunks)),
        ]

    def copy(self, n, way, source):
        target = (jnp.clip(self.place + 1 - 2 * way, 0, self.seq - 1), self.me)
        return pltpu.make_async_remote_copy(
            src_ref=source, dst_ref=self.land.at[way, n], send_sem=self.send.at[way, n],
            recv_sem=self.recv.at[way, n], device_id=target, device_id_type=MESH,
        )

    def hop(self, step, way):
        n = step - self.lag * self.behind[way]

        @pl.when((n >= 0) & (n < self.chunks))
        def _():
            @pl.when(self.behind[way] == 0)
            def _():
                self.copy(n, way, self.held.at[n]).start()

            @pl.when(self.behind[way] > 0)
            def _():
                self.copy(n, way, self.held.at[n]).wait_recv()

                @pl.when(self.behind[way] < self.seq - 1)
                def _():
                    value = self.held[n].astype(jnp.float32) + self.land[way, n].astype(jnp.float32)
                    self.mail[way, n] = value.astype(jnp.bfloat16)
                    self.copy(n, way, self.mail.at[way, n]).start()

    def advance(self, step, total):
        first = step - self.lag * jnp.minimum(self.behind[0], self.behind[1])

        @pl.when((first >= 0) & (first < self.chunks))
        def _():
            wait_for(self.held.at[first], self.fill_sem.at[first])

        self.hop(step, 0)
        self.hop(step, 1)
        n = step - self.lag * jnp.maximum(self.behind[0], self.behind[1])

        @pl.when((n >= 0) & (n < self.chunks))
        def _():
            for ways, there in (
                ((1,), self.behind[0] == 0),
                ((0,), self.behind[1] == 0),
                ((0, 1), (self.behind[0] > 0) & (self.behind[1] > 0)),
            ):

                @pl.when(there)
                def _(ways=ways):
                    value = self.held[n].astype(jnp.float32)
                    for way in ways:
                        value = value + self.land[way, n].astype(jnp.float32)
                    total[n] = value.astype(jnp.bfloat16)

    def run(self, first, last, total):
        def body(step, none):
            self.advance(step, total)
            return none

        lax.fori_loop(first, last, body, 0)

    def drain(self):
        for way in range(2):

            @pl.when(self.behind[way] < self.seq - 1)
            def _(way=way):
                def sent(n, none):
                    self.copy(n, way, self.held.at[n]).wait_send()
                    return none

                lax.fori_loop(0, self.chunks, sent, 0)


def fill_chunks(size, held, fill_sem, swap_send, sources, weight):
    me, place = lax.axis_index("rows"), lax.axis_index("seq")
    rows, cols = held.shape[1:]
    n = 0
    for source in sources:
        for i in range(source.shape[0] // rows):
            for j in range(source.shape[1] // cols):
                piece = source.at[pl.ds(i * rows, rows), pl.ds(j * cols, cols)]
                pltpu.make_async_copy(piece, held.at[n], fill_sem.at[n]).start()
                n += 1
    for m in range(size):
        q = flip(me, m)
        for i in range(weight.shape[1] // rows):
            piece = weight.at[q, pl.ds(i * rows, rows), :]
            if m == 0:
                pltpu.make_async_copy(piece, held.at[n], fill_sem.at[n]).start()
            else:
                remote(piece, held.at[n], swap_send.at[n], fill_sem.at[n], (place, q))
            n += 1


def drain_swap(size, held, swap_send, weight):
    parts = weight.shape[1] // held.shape[1]
    first = held.shape[0] - (size - 1) * parts
    for n in range(first, held.shape[0]):
        wait_for(held.at[n], swap_send.at[n])


def backward_kernel(size, seq, nr, tt, ct, uu, *refs):
    delta_in, x_in, gy_in, hist_in, proj_ref, a_ref, carry_ref, last_ref, branch, out_w, gate_w = refs[:11]
    gdelta_out, gx_out, gbc_ref, grate_ref, branch_own, total = refs[11:17]
    sel, bc, hist, prod, state_ref, after_ref, fold, delta_ref, x_ref, gy_ref, gdelta_ref, gx_ref = refs[17:29]
    sems, out_sems, hist_sems = refs[29:32]
    scatter = RowScatter(size, branch, *refs[32:38])
    held, land, mail, fill_sem, zsend, zrecv, swap_send = refs[38:]
    chain = SeqSum(seq, 3, held, land, mail, fill_sem, zsend, zrecv)
    el = a_ref.shape[1]
    blocks = el // LANES
    count = tt // ct

    def fetch(c):
        slot = lax.rem(c, 2)
        return pltpu.make_async_copy(hist_in.at[pl.ds(c * ct, ct)], hist.at[slot], hist_sems.at[slot])

    copies = copy_all((delta_in, x_in, gy_in), (delta_ref, x_ref, gy_ref), sems)
    fetch(count - 1).start()
    greet_rows_and_seq(size, seq)
    scatter.start()
    fill_chunks(size, held, fill_sem, swap_send, (out_w,), gate_w)
    sel[...] = selector(LANES)
    fold_row = lax.broadcasted_iota(jnp.int32, fold.shape, 0) // LANES
    fold_col = lax.broadcasted_iota(jnp.int32, fold.shape, 1)
    fold[...] = (fold_row + R == fold_col).astype(jnp.bfloat16)
    state_ref[...] = carry_ref[...]
    after_ref[...] = last_ref[...]
    grate_ref[...] = jnp.zeros_like(grate_ref)
    for copy in copies:
        copy.wait()

    def backward(k, none):
        c = count - 1 - k
        slot = lax.rem(c, 2)

        @pl.when(c > 0)
        def _():
            fetch(c - 1).start()

        for at_k, job in (
            (1, functools.partial(scatter.step, 1)),
            (count // 2, functools.partial(scatter.later, 2)),
            (count - 2, functools.partial(scatter.finish, branch_own)),
        ):
            pl.when(k == at_k)(job)

        rows = pl.multiple_of(c * (ct * nr), ct * nr)
        bc[...] = spread(proj_ref[pl.ds(rows, ct * nr), :], sel)
        fetch(c).wait()
        for b in range(blocks):
            lanes = slice(b * LANES, (b + 1) * LANES)
            for first in (True, False):
                ns = range(0, NS // 2) if first else range(NS // 2, NS)
                pairs = range(ns[0] // 2, ns[-1] // 2 + 1)
                rate = [jnp.broadcast_to(a_ref[n : n + 1, lanes], (nr, LANES)) for n in ns]

                def steps(s, carried):
                    grad, total_rate, after = (list(v) for v in carried)
                    for u in reversed(range(uu)):
                        at = (ct // uu - 1 - s) * uu + u
                        here = pl.ds(pl.multiple_of((c * ct + at) * nr, nr), nr)
                        delta = delta_ref[b, here, :]
                        x = x_ref[b, here, :]
                        gy = gy_ref[b, here, :]
                        du = delta * x
                        near = pl.ds(pl.multiple_of(at * nr, nr), nr)
                        along_rate = along_b = None
                        for p in pairs:
                            pair = hist[slot, at, b, pl.ds(2 * p * nr, 2 * nr), :].astype(jnp.float32)
                            for n, before in ((2 * p, pair[:nr]), (2 * p + 1, pair[nr:])):
                                i = n - ns[0]
                                to_b_at = slice(n * LANES, (n + 1) * LANES)
                                to_c_at = slice((NS + n) * LANES, (NS + n + 1) * LANES)
                                decay = jnp.exp2(delta * rate[i])
                                grad[i] = grad[i] + gy * bc[near, to_c_at]
                                to_c = after[i] * gy
                                to_b = grad[i] * du
                                if b > 0:
                                    to_c = to_c + prod[near, to_c_at]
                                    to_b = to_b + prod[near, to_b_at]
                                prod[near, to_c_at] = to_c
                                prod[near, to_b_at] = to_b
                                term_b = grad[i] * bc[near, to_b_at]
                                along_b = term_b if along_b is None else along_b + term_b
                                grad[i] = grad[i] * decay
                                weighted = grad[i] * before
                                total_rate[i] = total_rate[i] + weighted * delta
                                term = weighted * rate[i]
                                along_rate = term if along_rate is None else along_rate + term
                                after[i] = before
                        gdelta = along_rate * LN2 + along_b * x
                        gx = along_b * delta
                        if not first:
                            gdelta = gdelta + gdelta_ref[b, here, :]
                            gx = gx + gx_ref[b, here, :]
                        gdelta_ref[b, here, :] = gdelta
                        gx_ref[b, here, :] = gx
                    return tuple(grad), tuple(total_rate), tuple(after)

                start = tuple(tuple(ref[n, :, lanes] for n in ns) for ref in (state_ref, grate_ref, after_ref))
                ends = lax.fori_loop(0, ct // uu, steps, start)
                for i, n in enumerate(ns):
                    for ref, end in zip((state_ref, grate_ref, after_ref), ends):
                        ref[n, :, lanes] = end[i]
            if b < 2:
                chain.advance(2 * k + b, total)
        gbc_ref[pl.ds(rows, ct * nr), :] = jnp.dot(
            prod[...].astype(jnp.bfloat16), fold[...], preferred_element_type=jnp.float32
        )
        return none

    lax.fori_loop(0, count, backward, 0)
    late = copy_all((gdelta_ref, gx_ref), (gdelta_out, gx_out), out_sems)
    done = min(2, blocks) * count if blocks > 1 else count
    chain.run(2 * count, max(2 * count, chain.last_step), total)
    scatter.drain()
    chain.drain()
    drain_swap(size, held, swap_send, gate_w)
    for copy in late:
        copy.wait()


def scan_backward(delta, x, gy, hist, proj, rate, carry, last, branch, out_w, gate_w, size, seq):
    nr, tt, width = branch.shape
    el = rate.shape[1]
    blocks = el // LANES
    ct = math.gcd(tt, 16)
    here = pl.BlockSpec(memory_space=pltpu.VMEM)
    away = pl.BlockSpec(memory_space=pl.ANY)
    f32, bf16 = jnp.float32, jnp.bfloat16
    scan = (blocks, nr * tt, LANES)
    piece = gate_w.shape[1:]
    chunks = (out_w.size + gate_w.size) // math.prod(piece)
    return pl.pallas_call(
        functools.partial(backward_kernel, size, seq, nr, tt, ct, min(8, ct)),
        in_specs=[away] * 4 + [here] * 4 + [away] * 3,
        out_specs=[away] * 2 + [here] * 4,
        out_shape=[
            jax.ShapeDtypeStruct(scan, f32),
            jax.ShapeDtypeStruct(scan, f32),
            jax.ShapeDtypeStruct((tt * nr, LANES), f32),
            jax.ShapeDtypeStruct((NS, nr, el), f32),
            jax.ShapeDtypeStruct((tt, width), bf16),
            jax.ShapeDtypeStruct((chunks,) + piece, bf16),
        ],
        scratch_shapes=[
            pltpu.VMEM((LANES, 2 * NS * LANES), bf16),
            pltpu.VMEM((ct * nr, 2 * NS * LANES), f32),
            pltpu.VMEM((2, ct, blocks, NS * nr, LANES), bf16),
            pltpu.VMEM((ct * nr, 2 * NS * LANES), f32),
            pltpu.VMEM((NS, nr, el), f32),
            pltpu.VMEM((NS, nr, el), f32),
            pltpu.VMEM((2 * NS * LANES, LANES), bf16),
        ]
        + [pltpu.VMEM(scan, f32)] * 5
        + [
            pltpu.SemaphoreType.DMA((3,)),
            pltpu.SemaphoreType.DMA((2,)),
            pltpu.SemaphoreType.DMA((2,)),
        ]
        + RowScatter.scratch(size, tt, width)
        + SeqSum.scratch(chunks, piece)
        + [pltpu.SemaphoreType.DMA((chunks,))],
        compiler_params=pltpu.CompilerParams(
            vmem_limit_bytes=62 * MIB, collective_id=3, has_side_effects=True
        ),
        name="scan_backward",
    )(delta, x, gy, hist, proj, rate, carry, last, branch, out_w, gate_w)


def small_rows(piece_rows):
    rows = 2 * LANES + 32
    return rows + -rows % piece_rows


def back_kernel(size, seq, *refs):
    gdelta_in, gx_in, delta_in, normed_in, w_in, cext_in, ggp_in, gbc_in = refs[:8]
    rank_ref, dt_w, x_w, taps_ref, bias_ref, rate_ref, grate_ref = refs[8:15]
    own, sums = refs[15:17]
    (
        gdelta, gx, delta, normed, wv, cext, gmix, gbc, low, gcp, turned, w_stage, acc_x, acc_dt, acc,
        small, hmail, hland, stage,
    ) = refs[17:36]
    part, near, total, mail, far, out, sems = refs[36:43]
    scatter = RowScatter(size, None, *refs[43:49])
    held, zland, zmail, fill_sem, zsend, zrecv = refs[49:55]
    swap_send, in_sems, halo_send, halo_recv = refs[55:]
    chain = SeqSum(seq, 2, held, zland, zmail, fill_sem, zsend, zrecv)
    me, parity, partner, others = row_peers(size)
    place = lax.axis_index("seq")
    share, el = w_stage.shape[1:]
    tt = low.shape[0]
    width = normed.shape[1]
    blocks = el // LANES
    half = size // 2
    f32, bf16 = jnp.float32, jnp.bfloat16
    nt = (((1,), (1,)), ((), ()))
    tn = (((0,), (0,)), ((), ()))
    copies = copy_all(
        (gdelta_in, delta_in, gbc_in, cext_in, gx_in, ggp_in, w_in, normed_in),
        (gdelta, delta, gbc, cext, gx, gmix.at[:, :, pl.ds(el, el)], wv, normed),
        in_sems,
    )
    greet_rows_and_seq(size, seq)
    for ref in (acc_x, acc_dt, acc, small):
        ref[...] = jnp.zeros_like(ref)
    for copy in copies[:3]:
        copy.wait()

    def fold8(value):
        return jnp.sum(value.reshape(value.shape[0] // 8, 8, value.shape[1]), axis=0)

    def block_at(i):
        return 2 * lax.rem(me // 2 + lax.rem(i, half), half) + lax.rem(parity + 1 + lax.div(i, half), 2)

    def steps_back(i, none):
        p = block_at(i)

        def body(span):
            for b in range(blocks):
                lanes = slice(b * LANES, (b + 1) * LANES)
                there = pl.ds(p + span.start * size, 32, stride=size)
                dl = delta[b, there, :]
                near_zero = dl * (1.0 - dl * (0.5 - dl * (1.0 / 6.0)))
                value = gdelta[b, there, :] * jnp.where(dl < 0.01, near_zero, 1.0 - jnp.exp(-dl))
                low[span, lanes] = value.astype(bf16)
                acc[KC + 1, :, lanes] = acc[KC + 1, :, lanes] + fold8(value)

        by_tiles(tt, 32, body)
        value = lax.dot_general(low[...], dt_w[...], nt, preferred_element_type=f32)
        value = value + gbc[pl.ds(p, tt, stride=size), :]
        acc_dt[...] += lax.dot_general(rank_ref[p], low[...], tn, preferred_element_type=f32)

        @pl.when(i < half)
        def _():
            part[p] = value.astype(bf16)
            remote(
                part.at[p], near.at[lax.div(p, 2)], sems.at[0, lax.div(p, 2)], sems.at[1, lax.div(p, 2)],
                (place, partner),
            )

        @pl.when(i >= half)
        def _():
            total[lax.div(p, 2)] = value

        return none

    lax.fori_loop(0, size, steps_back, 0)
    for copy in copies[3:]:
        copy.wait()
    exchange_sums(size, near, total, mail, far, out, sems, lambda p: None)
    for j in range(half):
        wait_for(near.at[j], sems.at[0, j])

    def halo(p):
        return pltpu.make_async_remote_copy(
            src_ref=hmail.at[p], dst_ref=hland.at[p], send_sem=halo_send.at[p], recv_sem=halo_recv.at[p],
            device_id=(jnp.maximum(place - 1, 0), me), device_id_type=MESH,
        )

    def conv_back(p, none):
        def body(span):
            value = lax.dot_general(out[p, span, :], x_w[...], nt, preferred_element_type=f32)
            there = pl.ds(p + span.start * size, 32, stride=size)
            value = value + jnp.concatenate([gx[b, there, :] for b in range(blocks)], axis=1)
            ext = cext[p, pl.ds(span.start, 48), :].astype(f32)
            here = bias_ref[...]
            for k in range(KC):
                here = here + taps_ref[k : k + 1, :] * ext[16 - KC + 1 + k : 16 - KC + 1 + k + 32]
            sig = 1.0 / (1.0 + jnp.exp(-here))
            low[span, :] = (here * sig).astype(bf16)
            value = value * sig * (1.0 + here * (1.0 - sig))
            gcp[p, span, :] = value
            acc[KC] = acc[KC] + fold8(value)
            for k in range(KC):
                acc[k] = acc[k] + fold8(value * ext[16 - KC + 1 + k : 16 - KC + 1 + k + 32])

        by_tiles(tt, 32, body)
        acc_x[...] += lax.dot_general(out[p], low[...], tn, preferred_element_type=f32)
        hmail[p] = gcp[p, 0:16, :].astype(bf16)

        @pl.when(place > 0)
        def _():
            halo(p).start()

        return none

    lax.fori_loop(0, size, conv_back, 0)

    def turn(p, none):
        @pl.when(place < seq - 1)
        def _():
            halo(p).wait_recv()
            gcp[p, tt : tt + 8, :] = hland[p, 0:8, :].astype(f32)

        @pl.when(place == seq - 1)
        def _():
            gcp[p, tt : tt + 8, :] = jnp.zeros((8, el), f32)

        def body(span):
            ext = gcp[p, pl.ds(span.start, 40), :]
            value = taps_ref[KC - 1 : KC, :] * ext[0:32]
            for k in range(KC - 1):
                value = value + taps_ref[k : k + 1, :] * ext[KC - 1 - k : KC - 1 - k + 32]
            gmix[p, span, 0:el] = value.astype(bf16)

        by_tiles(tt, 32, body)
        columns = pl.ds(pl.multiple_of(p * tt, tt), tt)
        turned[:, columns] = jnp.transpose(gmix[p, :, 0:el].astype(f32)).astype(bf16)
        return none

    lax.fori_loop(0, size, turn, 0)

    group = 384 // share

    def weights(j, none):
        columns = pl.ds(pl.multiple_of(j * 384, 384), 384)
        value = jnp.dot(turned[...], normed[:, columns], preferred_element_type=f32)
        value = jnp.transpose(value).astype(bf16)
        for g in range(group):
            w_stage[j * group + g] = value[g * share : (g + 1) * share, :]
        return none

    lax.fori_loop(0, width // 384, weights, 0)
    rows = 2 * LANES
    small[0:LANES, :] = acc_x[...].astype(bf16)
    small[LANES:rows, :] = acc_dt[...].astype(bf16)
    rate_sum = jnp.sum(grate_ref[...], axis=1) * rate_ref[...]
    last = [rate_sum] + [jnp.sum(acc[k], axis=0, keepdims=True) for k in range(KC + 2)]
    last.append(jnp.zeros((16 - KC - 2, el), f32))
    small[rows : rows + 32, :] = jnp.concatenate(last, axis=0).astype(bf16)
    fill_chunks(size, held, fill_sem, swap_send, (small,), w_stage)

    def spread_back(i, none):
        p = crossed(me, jnp.where(i < half, 2 * i + 1, 2 * (i - half)), size)
        weight = wv[...].reshape(width, 2 * el)
        value = lax.dot_general(gmix[p], weight, nt, preferred_element_type=f32).astype(bf16)

        @pl.when(i < half)
        def _():
            stage[i] = value
            scatter.staged(i, stage)

        @pl.when(i >= half)
        def _():
            scatter.keep[i - half] = value

        chain.advance(i, sums)
        return none

    lax.fori_loop(0, size, spread_back, 0)
    jobs = [functools.partial(scatter.step, k) for k in range(1, scatter.steps)]
    jobs.append(functools.partial(scatter.finish, own))
    done = size
    for i, job in enumerate(jobs):
        job()
        upto = min(chain.last_step, done + chain.last_step // 4)
        chain.run(done, upto, sums)
        done = upto
    chain.run(done, max(done, chain.last_step), sums)
    scatter.drain()
    chain.drain()
    drain_swap(size, held, swap_send, w_stage)

    def halo_sent(p, none):
        halo(p).wait_send()
        return none

    @pl.when(place > 0)
    def _():
        lax.fori_loop(0, size, halo_sent, 0)


def back(gdelta, gx, delta, normed, w_in, cext, ggp, gbc, rank, dt_w, x_w, taps, bias, rate, grate, size, seq):
    away = pl.BlockSpec(memory_space=pl.ANY)
    here = pl.BlockSpec(memory_space=pltpu.VMEM)
    f32, bf16 = jnp.float32, jnp.bfloat16
    unused_size, tt, el = ggp.shape
    share = w_in.shape[1]
    width = normed.shape[1]
    piece = (share // 2, el)
    low = small_rows(piece[0])
    chunks = 2 * size + low // piece[0]
    scratch = [
        (gdelta.shape, f32), (gx.shape, f32), (delta.shape, f32), (normed.shape, bf16), (w_in.shape, bf16),
        (cext.shape, bf16), ((size, tt, 2 * el), bf16), (gbc.shape, f32), ((tt, el), bf16),
        ((size, tt + 8, el), f32), ((el, size * tt), bf16), ((size, share, el), bf16), ((LANES, el), f32),
        ((LANES, el), f32), ((KC + 2, 8, el), f32), ((low, el), bf16), ((size, 16, el), bf16),
        ((size, 16, el), bf16), ((size // 2, tt, width), bf16),
    ]
    return pl.pallas_call(
        functools.partial(back_kernel, size, seq),
        in_specs=[away] * 8 + [here] * 7,
        out_specs=[here] * 2,
        out_shape=[
            jax.ShapeDtypeStruct((tt, width), bf16),
            jax.ShapeDtypeStruct((chunks,) + piece, bf16),
        ],
        scratch_shapes=[pltpu.VMEM(*v) for v in scratch]
        + sum_scratch(size, tt)
        + RowScatter.scratch(size, tt, width)
        + SeqSum.scratch(chunks, piece)
        + [
            pltpu.SemaphoreType.DMA((chunks,)),
            pltpu.SemaphoreType.DMA((8,)),
            pltpu.SemaphoreType.DMA((size,)),
            pltpu.SemaphoreType.DMA((size,)),
        ],
        compiler_params=pltpu.CompilerParams(
            vmem_limit_bytes=63 * MIB, collective_id=4, has_side_effects=True
        ),
        name="back",
    )(gdelta, gx, delta, normed, w_in, cext, ggp, gbc, rank, dt_w, x_w, taps, bias, rate, grate)


def local(
    tokens, resets, norm_gain, in_proj, x_proj, dt_proj, conv_weight, conv_bias, dt_bias, a_log, out_proj,
    cotangent,
):
    size = lax.axis_size("rows")
    seq = lax.axis_size("seq")
    rd, tt, unused_d = tokens.shape
    nr = rd * size
    el = E // size
    count = nr * tt
    assert rd == 1 and ITEM % tt == 0 and nr % 8 == 0

    elp = pad_lanes(el)
    share = D // size
    direct = elp == el
    f32, bf16 = jnp.float32, jnp.bfloat16

    def widen(value, axis):
        pad = [(0, 0)] * value.ndim
        pad[axis] = (0, elp - el)
        return jnp.pad(value, pad)

    if direct:
        w_local = in_proj
    else:
        w_local = jnp.moveaxis(in_proj.reshape(share, 2, size, el), 2, 0)
        w_local = widen(w_local, 3).reshape(size, share, 2 * elp)
    out_proj, x_proj = widen(out_proj, 0), widen(x_proj, 0)
    dt_pad = widen(jnp.pad(dt_proj, ((0, LANES - R), (0, 0))), 1)
    taps = widen(conv_weight.astype(f32), 1)
    bias = widen(conv_bias.astype(f32), 0)[None]
    rate = widen(-jnp.exp(a_log.astype(f32)), 1)
    notes = jnp.zeros((16, -(-share // 256) * 256), bf16)
    notes = notes.at[0, :share].set(norm_gain).at[1].set(1.0 - resets[0, 0].astype(bf16))
    (
        normed, w_in, x_t, delta_t, gy_t, conv_ext, hist, branch, grad_out_proj, grad_in_gate, grad_gate_pre, proj_t,
        rank_all, all_notes, last, carry_back,
    ) = front(
        tokens[0], cotangent[0], notes, w_local, out_proj, x_proj, dt_pad, taps, bias,
        widen(dt_bias.astype(f32), 0)[None], rate * LOG2E, size, seq, direct,
    )
    gain = all_notes[:, 0, :share].reshape(D).astype(f32)
    grad_delta, grad_input, grad_bc, grate, branch_own, summed_gate = scan_backward(
        delta_t, x_t, gy_t, hist, proj_t, rate * LOG2E, carry_back, last, branch,
        grad_out_proj[:el], grad_in_gate, size, seq,
    )
    grad_normed, summed_conv = back(
        grad_delta, grad_input, delta_t, normed.reshape(count, D), w_in, conv_ext, grad_gate_pre, grad_bc, rank_all,
        dt_pad, x_proj, taps, bias, rate, grate, size, seq,
    )
    piece = (share, elp)
    out_rows, out_cols = el // share, D // elp
    sum_out = summed_gate[: out_rows * out_cols].reshape(out_rows, out_cols, *piece)
    sum_out = jnp.swapaxes(sum_out, 1, 2).reshape(el, D).astype(f32)
    small = summed_conv[: -2 * size].reshape(-1, elp)[:, :el].astype(f32)
    order = jnp.array(range(size)) ^ lax.axis_index("rows")
    sum_in = jnp.stack([summed_conv[-2 * size :].reshape((size,) + piece)[order], summed_gate[-size:][order]])
    sum_in = jnp.transpose(sum_in[..., :el].astype(f32), (2, 0, 1, 3)).reshape(share, 2 * E)
    block_out = (tokens.astype(jnp.float32) + branch_own[None].astype(jnp.float32)).astype(jnp.bfloat16)
    grad_normed = grad_normed[None].astype(jnp.float32)

    own = tokens.astype(jnp.float32)
    inv = lax.rsqrt(jnp.mean(own * own, axis=2, keepdims=True) + epsilon)
    gain_own = jnp.sum(in_proj.astype(jnp.float32) * sum_in, axis=1) / norm_gain.astype(jnp.float32)
    grad_hat = grad_normed * gain
    grad_norm_in = inv * (
        grad_hat - own * (inv * inv) * jnp.mean(grad_hat * own, axis=2, keepdims=True)
    )
    d_tokens = (cotangent.astype(jnp.float32) + grad_norm_in).astype(jnp.bfloat16)

    more = small[2 * LANES :]
    return (
        block_out,
        d_tokens,
        gain_own,
        sum_in,
        small[:LANES].T,
        small[LANES : LANES + R],
        more[NS : NS + KC],
        more[NS + KC],
        more[NS + KC + 1],
        more[:NS],
        sum_out,
    )


def solution(mesh):
    in_specs = (
        P("rows", "seq", None),
        P("rows", "seq"),
        P("rows"),
        P("rows", None),
        P("rows", None),
        P(None, "rows"),
        P(None, "rows"),
        P("rows"),
        P("rows"),
        P(None, "rows"),
        P("rows", None),
        P("rows", "seq", None),
    )
    out_specs = (
        P("rows", "seq", None),
        P("rows", "seq", None),
        P("rows"),
        P("rows", None),
        P("rows", None),
        P(None, "rows"),
        P(None, "rows"),
        P("rows"),
        P("rows"),
        P(None, "rows"),
        P("rows", None),
    )
    return jax.shard_map(local, mesh=mesh, in_specs=in_specs, out_specs=out_specs, check_vma=False)
```

```python
import functools
import math

import jax
import jax.numpy as jnp
from jax import lax
from jax.experimental import pallas as pl
from jax.experimental.pallas import tpu as pltpu
from jax.sharding import PartitionSpec as P

D = 1536
E = 3072
R = 96
NS = 16
KC = 4
ITEM = 256

epsilon = 1e-05
LOG2E = 1.4426950408889634
LN2 = 0.6931471805599453
MIB = 2**20


LANES = 128


def pad_lanes(lanes):
    return -(-lanes // LANES) * LANES


def selector(wide):
    row = lax.broadcasted_iota(jnp.int32, (LANES, 2 * NS * wide), 0)
    col = lax.broadcasted_iota(jnp.int32, (LANES, 2 * NS * wide), 1) // wide
    return (row == col + R).astype(jnp.bfloat16)


def spread(proj, sel_ref):
    return jnp.dot(proj.astype(jnp.bfloat16), sel_ref[...], preferred_element_type=jnp.float32)


def copy_all(sources, targets, sems):
    copies = []
    for i, (source, target) in enumerate(zip(sources, targets)):
        copies.append(pltpu.make_async_copy(source, target, sems.at[i]))
        copies[-1].start()
    return copies


MESH = pl.DeviceIdType.MESH


def greet(devices):
    barrier = pltpu.get_barrier_semaphore()
    for device in devices:
        pl.semaphore_signal(barrier, inc=1, device_id=device, device_id_type=MESH)
    pl.semaphore_wait(barrier, len(devices))


def remote(source, target, send, recv, device):
    copy = pltpu.make_async_remote_copy(
        src_ref=source, dst_ref=target, send_sem=send, recv_sem=recv, device_id=device, device_id_type=MESH
    )
    copy.start()
    return copy


def row_peers(size):
    me = lax.axis_index("rows")
    half = size // 2
    mine = me // 2
    return me, me % 2, me + 1 - 2 * (me % 2), [lax.rem(mine + k, half) for k in range(half)]


def exchange_sums(size, near, total, mail, far, out, sems, use, between=None):
    me, parity, partner, others = row_peers(size)
    place = lax.axis_index("seq")
    half = size // 2
    second = []
    for k in list(range(1, half)) + [0]:
        j = others[k]
        wait_for(near.at[j], sems.at[1, j])
        total[j] = total[j] + near[j].astype(jnp.float32)
        if k:
            mail[j] = total[j].astype(jnp.bfloat16)
            target = (place, 2 * j + parity)
            second.append(remote(mail.at[j], far.at[k], sems.at[2, k], sems.at[3, k], target))
    mine = others[0]
    done = total[mine]
    for k in range(1, half):
        wait_for(far.at[k], sems.at[3, k])
        done = done + far[k].astype(jnp.float32)
    out[me] = done.astype(jnp.bfloat16)
    third = []
    for k in range(1, half):
        target = (place, 2 * others[k] + parity)
        third.append(remote(out.at[me], out.at[me], sems.at[4, k], sems.at[5, k], target))
    fourth = [remote(out.at[me], out.at[me], sems.at[6, 0], sems.at[7, 0], (place, partner))]
    use(me)
    for k in range(1, half):
        block = 2 * others[half - k] + parity
        wait_for(out.at[block], sems.at[5, k])
        fourth.append(
            remote(out.at[block], out.at[block], sems.at[6, k], sems.at[7, k], (place, partner))
        )
        use(block)
    for k in range(half):
        block = 2 * others[(half - k) % half] + 1 - parity
        wait_for(out.at[block], sems.at[7, k])
        use(block)
    if between:
        between()
    for copy in second + third + fourth:
        copy.wait_send()


def sum_scratch(size, tt):
    half = size // 2
    return [
        pltpu.VMEM((size, tt, LANES), jnp.bfloat16),
        pltpu.VMEM((half, tt, LANES), jnp.bfloat16),
        pltpu.VMEM((half, tt, LANES), jnp.float32),
        pltpu.VMEM((half, tt, LANES), jnp.bfloat16),
        pltpu.VMEM((half, tt, LANES), jnp.bfloat16),
        pltpu.VMEM((size, tt, LANES), jnp.bfloat16),
        pltpu.SemaphoreType.DMA((8, half)),
    ]


class Carry:
    def __init__(self, seq, ends, alive, out, mail, land, sems):
        self.seq, self.ends, self.alive, self.out = seq, ends, alive, out
        self.mail, self.land, self.sems = mail, land, sems
        self.me, self.place = lax.axis_index("rows"), lax.axis_index("seq")

    @staticmethod
    def scratch(shape):
        return [
            pltpu.VMEM((2,) + shape, jnp.bfloat16),
            pltpu.VMEM((2,) + shape, jnp.bfloat16),
            pltpu.SemaphoreType.DMA((2, 2)),
        ]

    def copy(self, way):
        target = (jnp.clip(self.place + 1 - 2 * way, 0, self.seq - 1), self.me)
        return pltpu.make_async_remote_copy(
            src_ref=self.mail.at[way], dst_ref=self.land.at[way], send_sem=self.sems.at[way, 0],
            recv_sem=self.sems.at[way, 1], device_id=target, device_id_type=MESH,
        )

    def hop(self, way):
        first, last = ((0, self.seq - 1), (self.seq - 1, 0))[way]
        alive = self.alive[:, 0:1][None]

        @pl.when(self.place == first)
        def _():
            self.out[way] = jnp.zeros_like(self.out[way])

        @pl.when(self.place != first)
        def _():
            self.copy(way).wait_recv()
            entering = self.land[way].astype(jnp.float32)
            self.out[way] = entering * alive if way == 0 else entering

        @pl.when(self.place != last)
        def _():
            if way == 0:
                leaving = self.ends[0] + self.ends[1] * self.out[0]
            else:
                leaving = (self.ends[2] + self.ends[1] * self.out[1]) * alive
            self.mail[way] = leaving.astype(jnp.bfloat16)
            self.copy(way).start()

    def turn(self, way, t):
        behind = (self.place, self.seq - 1 - self.place)[way]
        pl.when(behind == t)(functools.partial(self.hop, way))

    def drain(self):
        for way, last in ((0, self.seq - 1), (1, 0)):

            @pl.when(self.place != last)
            def _(way=way):
                self.copy(way).wait_send()


def flip(place, mask):
    for k in range(mask.bit_length()):
        bit = 1 << k
        if mask & bit:
            place = place + bit * (1 - 2 * (lax.div(place, bit) % 2))
    return place


def bit_orders(size):
    rest = [1 << k for k in range(1, size.bit_length() - 1)]
    cut = max(1, len(rest) // 2)
    return [1] + rest, [1] + rest[cut:] + rest[:cut]


def masks_of(bits):
    masks = [0]
    for bit in bits:
        masks = masks + [m | bit for m in masks]
    return masks


def by_tiles(rows, tile, body):
    def step(i, none):
        body(pl.ds(pl.multiple_of(i * tile, tile), tile))
        return none

    lax.fori_loop(0, rows // tile, step, 0)


def wait_for(ref, sem):
    pltpu.make_async_copy(ref, ref, sem).wait()


def greet_seq(seq):
    me, place = lax.axis_index("rows"), lax.axis_index("seq")
    barrier = pltpu.get_barrier_semaphore()
    for step, there in ((-1, place > 0), (1, place < seq - 1)):

        @pl.when(there)
        def _(step=step):
            pl.semaphore_signal(barrier, inc=1, device_id=(place + step, me), device_id_type=MESH)

    pl.semaphore_wait(barrier, (place > 0).astype(jnp.int32) + (place < seq - 1).astype(jnp.int32))


def greet_rows_and_seq(size, seq):
    me, place = lax.axis_index("rows"), lax.axis_index("seq")
    barrier = pltpu.get_barrier_semaphore()
    for mask in range(1, size):
        pl.semaphore_signal(barrier, inc=1, device_id=(place, flip(me, mask)), device_id_type=MESH)
    for step, there in ((-1, place > 0), (1, place < seq - 1)):

        @pl.when(there)
        def _(step=step):
            pl.semaphore_signal(barrier, inc=1, device_id=(place + step, me), device_id_type=MESH)

    near = (place > 0).astype(jnp.int32) + (place < seq - 1).astype(jnp.int32)
    pl.semaphore_wait(barrier, near + size - 1)


def crossed(place, mask, size):
    out = 0
    for k in range(size.bit_length() - 1):
        bit = 1 << k
        out = out + bit * lax.rem(lax.div(place, bit) + lax.div(mask, bit), 2)
    return out


class RowGather:
    def __init__(self, size, source, out, own_sem, send, recv):
        self.size, self.source, self.out, self.own_sem, self.send, self.recv = size, source, out, own_sem, send, recv
        self.me, self.place = lax.axis_index("rows"), lax.axis_index("seq")
        self.rows = source.shape[0] // 2
        self.orders = [order[1:] for order in bit_orders(size)]
        self.steps = len(self.orders[0])
        self.started = []

    @staticmethod
    def sems(size):
        return [pltpu.SemaphoreType.DMA((1,))] + [pltpu.SemaphoreType.DMA((2, size))] * 2

    def half(self, h, m, ref=None):
        ref = self.out.at[flip(self.me, m)] if ref is None else ref
        return ref.at[pl.ds(h * self.rows, self.rows), :]

    def push(self, h, m, bit):
        source = self.half(h, m, self.source if m == 0 else None)
        key = (h, m | bit)
        self.started.append(
            remote(
                source, self.half(h, m), self.send.at[key], self.recv.at[key],
                (self.place, flip(self.me, bit)),
            )
        )

    def arrived(self, h, m):
        wait_for(self.half(h, m), self.recv.at[h, m])

    def start(self):
        pltpu.make_async_copy(self.source, self.out.at[self.me], self.own_sem.at[0]).start()
        for h in range(2):
            self.push(h, 0, self.orders[h][0])
        for h in range(2):
            self.push(h, 0, 1)

    def own(self):
        wait_for(self.out.at[self.me], self.own_sem.at[0])

    def step(self, k, use=None):
        for h in range(2):
            order = self.orders[h]
            old = masks_of(order[:k])
            if k + 1 < self.steps:
                for m in old:
                    self.push(h, m, order[k + 1])
            for m in old:
                fresh = m | order[k]
                self.arrived(h, fresh)
                if k + 1 < self.steps:
                    self.push(h, fresh, order[k + 1])
                self.push(h, fresh, 1)
                if use:
                    use(h, fresh)

    def paired(self, use=None):
        for m in masks_of(self.orders[0]):
            for h in range(2):
                self.arrived(h, m | 1)
                if use:
                    use(h, m | 1)

    def drain(self):
        for copy in self.started:
            copy.wait_send()


def front_kernel(size, seq, direct, ct, uu, *refs):
    (tokens, cot, notes, w_local, out_w, x_w, dt_w, taps_ref, bias_ref, dt_bias_ref, a_ref) = refs[:11]
    (
        normed_out, w_out, x_out, delta_out, gy_out, cext_out, hist_out, branch_out, dout_out, dwg_out, ggp_out,
        proj_ref, rank_ref, all_notes, last_ref, leaving_ref,
    ) = refs[11:27]
    (
        tok, cot_s, wc, wg, cext, xb, x_s, delta_s, gy_s, gate_s, gg_s, gain_ref, alive_ref, sel, bc, ends, entered,
        delta_sum, hist, y_s, gated, ggp, branch_s, turned, d_stage, w_stage,
    ) = refs[27:53]
    token_sems, cot_sems = refs[53:56], refs[56:59]
    part, near, total, mail, far, out, sems = refs[59:66]
    carry = Carry(seq, ends, alive_ref, entered, *refs[66:69])
    (
        note_send, note_recv, wc_send, wc_recv, wg_send, wg_recv, halo_send, halo_recv, out_sems, hist_sems, branch_sems,
    ) = refs[69:]
    normed = tok
    me, parity, partner, others = row_peers(size)
    place = lax.axis_index("seq")
    tt, width = tokens.shape
    share, el = wc.shape[1:]
    nr = size
    blocks = el // LANES
    half = size // 2
    f32, bf16 = jnp.float32, jnp.bfloat16
    tile = 32
    stores = []

    def put(source, target):
        copy = pltpu.make_async_copy(source, target, out_sems.at[len(stores)])
        copy.start()
        stores.append(copy)

    def piece(q, gate):
        if direct:
            at = pl.multiple_of(q * el, LANES) + gate * size * el
            return w_local.at[:, pl.ds(at, el)]
        return w_local.at[q, :, pl.ds(gate * el, el)]

    cut = share // 2
    beside = (flip(place, 1), me)

    def swap(gate, target, send, recv):
        there = pl.ds(pl.multiple_of(lax.rem(place, 2) * cut, cut), cut)
        for m in range(1, size):
            q = flip(me, m)
            remote(piece(q, gate).at[there, :], target.at[me, there, :], send.at[0, m], recv.at[0, m], (place, q))
        pltpu.make_async_copy(piece(me, gate), target.at[me], recv.at[0, 0]).start()

    def swap_on(target, send, recv):
        there = pl.ds(pl.multiple_of(lax.rem(place, 2) * cut, cut), cut)
        for m in range(1, size):
            block = target.at[flip(me, m), there, :]
            wait_for(block, recv.at[0, m])
            remote(block, block, send.at[1, m], recv.at[1, m], beside)

    def swapped(target, send, recv):
        wait_for(target.at[me], recv.at[0, 0])
        for m in range(1, size):
            wait_for(target.at[flip(me, m), pl.ds(0, cut), :], recv.at[1, m])

    def swap_drain(target, send):
        for k in range(2):
            for m in range(1, size):
                wait_for(target.at[0, pl.ds(0, cut), :], send.at[k, m])

    greet_rows_and_seq(size, seq)

    sent = []
    for m in range(1, size):
        sent.append(remote(notes, all_notes.at[me], note_send.at[m], note_recv.at[m], (place, flip(me, m))))
    pltpu.make_async_copy(notes, all_notes.at[me], note_recv.at[0]).start()
    token_rows = RowGather(size, tokens, tok, *token_sems)
    cot_rows = RowGather(size, cot, cot_s, *cot_sems)
    swap(0, wc, wc_send, wc_recv)
    token_rows.start()

    for m in range(size):
        wait_for(all_notes.at[flip(me, m)], note_recv.at[m])
    for p in range(size):
        note = all_notes[p].astype(f32)
        gain_ref[:, p * share : (p + 1) * share] = note[0:1, :share]
        alive_ref[p : p + 1, :] = note[1:2, :LANES]

    def norm(p, base, rows):
        def body(span):
            there = pl.ds(base + span.start, span.size)
            x = tok[p, there, :].astype(f32)
            inv = lax.rsqrt(jnp.mean(x * x, axis=1, keepdims=True) + epsilon)
            normed[p, there, :] = (x * inv * gain_ref[...]).astype(bf16)

        by_tiles(rows, 64, body)

    def norm_half(h, m):
        norm(flip(me, m), h * (tt // 2), tt // 2)

    token_rows.own()
    norm(me, 0, tt)
    swap_on(wc, wc_send, wc_recv)
    sel[...] = selector(LANES)
    for k in range(token_rows.steps):
        token_rows.step(k)
    cot_rows.start()
    token_rows.paired(norm_half)
    token_rows.drain()
    for m in masks_of(token_rows.orders[0])[1:]:
        norm(flip(me, m), 0, tt)
    swapped(wc, wc_send, wc_recv)

    @pl.when(place == 0)
    def _():
        cext[:, 0:16, :] = jnp.zeros((size, 16, el), bf16)

    def halo(p, i):
        there = cext.at[p, pl.ds(0, 16), :]
        return pltpu.make_async_remote_copy(
            src_ref=cext.at[p, pl.ds(tt, 16), :], dst_ref=there, send_sem=halo_send.at[i],
            recv_sem=halo_recv.at[i], device_id=(jnp.minimum(place + 1, seq - 1), me), device_id_type=MESH,
        )

    def block_at(i):
        return 2 * lax.rem(me // 2 + lax.rem(i, half), half) + lax.rem(parity + 1 + lax.div(i, half), 2)

    def mix(i, none):
        p = block_at(i)
        weight = wc[...].reshape(size * share, el)
        cext[p, 16:, :] = jnp.dot(normed[p], weight, preferred_element_type=f32).astype(bf16)

        @pl.when(place < seq - 1)
        def _():
            halo(p, i).start()

        return none

    lax.fori_loop(0, size, mix, 0)
    for p in range(size):
        put(normed.at[p], normed_out.at[p])

    def conv(i, none):
        p = block_at(i)

        @pl.when(place > 0)
        def _():
            halo(p, i).wait_recv()

        def body(span):
            ext = cext[p, pl.ds(span.start, tile + 16), :].astype(f32)
            value = bias_ref[...]
            for k in range(KC):
                value = value + taps_ref[k : k + 1, :] * ext[16 - KC + 1 + k : 16 - KC + 1 + k + tile]
            x = (value / (1.0 + jnp.exp(-value))).astype(bf16)
            xb[span, :] = x
            for b in range(blocks):
                there = pl.ds(p + span.start * size, tile, stride=size)
                x_s[b, there, :] = x[:, b * LANES : (b + 1) * LANES].astype(f32)

        by_tiles(tt, tile, body)
        value = jnp.dot(xb[...], x_w[...], preferred_element_type=f32)

        @pl.when(i < half)
        def _():
            part[p] = value.astype(bf16)
            pltpu.make_async_remote_copy(
                src_ref=part.at[p], dst_ref=near.at[lax.div(p, 2)], send_sem=sems.at[0, lax.div(p, 2)],
                recv_sem=sems.at[1, lax.div(p, 2)], device_id=(place, partner), device_id_type=MESH,
            ).start()

        @pl.when(i >= half)
        def _():
            total[lax.div(p, 2)] = value

        return none

    lax.fori_loop(0, size, conv, 0)
    put(cext, cext_out)
    put(x_s, x_out)

    def use(p):
        block = out[p]
        rank_ref[p] = block
        proj_ref[pl.ds(p, tt, stride=size), :] = block.astype(f32)

        gate_s[...] = jnp.dot(block, dt_w[...], preferred_element_type=f32)

        def body(span):
            step = gate_s[span, :] + dt_bias_ref[...]
            delta = jnp.maximum(step, 0.0) + jnp.log1p(jnp.exp(-jnp.abs(step)))
            for b in range(blocks):
                there = pl.ds(p + span.start * size, 64, stride=size)
                delta_s[b, there, :] = delta[:, b * LANES : (b + 1) * LANES]

        by_tiles(tt, 64, body)

    def between():
        swap(1, wg, wg_send, wg_recv)
        for k in range(cot_rows.steps):
            cot_rows.step(k)

    exchange_sums(size, near, total, mail, far, out, sems, use, between)
    for j in range(half):
        pltpu.make_async_remote_copy(
            src_ref=part.at[j], dst_ref=near.at[j], send_sem=sems.at[0, j], recv_sem=sems.at[1, j],
            device_id=(place, partner), device_id_type=MESH,
        ).wait_send()
    put(delta_s, delta_out)
    put(wc, w_out.at[:, :, pl.ds(0, el)])

    count = tt // ct
    ends[0] = jnp.zeros((NS, nr, el), f32)
    ends[2] = jnp.zeros((NS, nr, el), f32)
    ends[3] = jnp.ones((NS, nr, el), f32)
    delta_sum[...] = jnp.zeros_like(delta_sum)

    def spread_chunk(c, first, last):
        rows = pl.multiple_of(c * (ct * nr), ct * nr)
        lanes = slice(first * LANES, last * LANES)
        bc[:, lanes] = spread(proj_ref[pl.ds(rows, ct * nr), :], sel.at[:, lanes])

    def token(c, at):
        return pl.ds(pl.multiple_of((c * ct + at) * nr, nr), nr), pl.ds(pl.multiple_of(at * nr, nr), nr)

    def rates(ns, lanes):
        return [jnp.broadcast_to(a_ref[n : n + 1, lanes], (nr, LANES)) for n in ns]

    def ends_forward(c, none):
        @pl.when(c == count // 2)
        def _():
            swap_on(wg, wg_send, wg_recv)

        spread_chunk(c, 0, NS)
        for b in range(blocks):
            lanes = slice(b * LANES, (b + 1) * LANES)
            rate = rates(range(NS), lanes)

            def steps(s, carried):
                state, so_far = list(carried[:-1]), carried[-1]
                for u in range(uu):
                    here, close = token(c, s * uu + u)
                    delta = delta_s[b, here, :]
                    du = delta * x_s[b, here, :]
                    so_far = so_far + delta
                    for n in range(NS):
                        b_at = n * LANES
                        state[n] = jnp.exp2(delta * rate[n]) * state[n] + du * bc[close, b_at : b_at + LANES]
                return tuple(state) + (so_far,)

            start = tuple(ends[0, n, :, lanes] for n in range(NS)) + (delta_sum[b],)
            last = lax.fori_loop(0, ct // uu, steps, start)
            for n in range(NS):
                ends[0, n, :, lanes] = last[n]
            delta_sum[b] = last[NS]
        return none

    lax.fori_loop(0, count, ends_forward, 0)
    for b in range(blocks):
        lanes = slice(b * LANES, (b + 1) * LANES)
        for n in range(NS):
            ends[1, n, :, lanes] = jnp.exp2(delta_sum[b] * a_ref[n : n + 1, lanes])
    carry.turn(0, 0)

    cot_rows.own()
    cot_rows.paired()
    swapped(wg, wg_send, wg_recv)
    put(wg, w_out.at[:, :, pl.ds(el, el)])

    def gates(p):
        weight = wg[...].reshape(size * share, el)
        gate_s[...] = jnp.dot(normed[p], weight, preferred_element_type=f32)
        gg_s[...] = lax.dot_general(
            cot_s[p], out_w[...], (((1,), (1,)), ((), ())), preferred_element_type=f32
        )

    def grad_y(p, none):
        gates(p)

        def body(span):
            gate = gate_s[span, :]
            gy = gg_s[span, :] * gate / (1.0 + jnp.exp(-gate))
            for b in range(blocks):
                there = pl.ds(p + span.start * size, tile, stride=size)
                gy_s[b, there, :] = gy[:, b * LANES : (b + 1) * LANES]

        by_tiles(tt, tile, body)
        return none

    lax.fori_loop(0, size, grad_y, 0)
    put(gy_s, gy_out)
    carry.turn(0, 1)

    def hops(way, c, first):
        @pl.when(lax.rem(c, 2) == 1)
        def _():
            carry.turn(way, lax.div(c, 2) + first)

    def ends_back(c, none):
        spread_chunk(c, NS, 2 * NS)
        for b in range(blocks):
            lanes = slice(b * LANES, (b + 1) * LANES)
            for n0 in (0, NS // 2):
                ns = range(n0, n0 + NS // 2)
                rate = rates(ns, lanes)

                def steps(s, carried):
                    through, back = (list(v) for v in carried)
                    for u in range(uu):
                        here, close = token(c, s * uu + u)
                        delta = delta_s[b, here, :]
                        gy = gy_s[b, here, :]
                        for i, n in enumerate(ns):
                            c_at = (NS + n) * LANES
                            through[i] = through[i] * jnp.exp2(delta * rate[i])
                            back[i] = back[i] + through[i] * (gy * bc[close, c_at : c_at + LANES])
                    return tuple(through), tuple(back)

                start = tuple(tuple(ends[k, n, :, lanes] for n in ns) for k in (3, 2))
                last = lax.fori_loop(0, ct // uu, steps, start)
                for i, n in enumerate(ns):
                    ends[3, n, :, lanes] = last[0][i]
                    ends[2, n, :, lanes] = last[1][i]
        hops(0, c, 2)
        return none

    lax.fori_loop(0, count, ends_back, 0)
    for t in range(count // 2 + 2, seq):
        carry.turn(0, t)
    carry.turn(1, 0)
    last_ref[...] = entered[0]

    def store_hist(c):
        slot = lax.rem(c, 2)
        return pltpu.make_async_copy(hist.at[slot], hist_out.at[pl.ds(c * ct, ct)], hist_sems.at[slot])

    def forward(c, none):
        slot = lax.rem(c, 2)

        @pl.when(c >= 2)
        def _():
            store_hist(c - 2).wait()

        spread_chunk(c, 0, 2 * NS)
        for b in range(blocks):
            lanes = slice(b * LANES, (b + 1) * LANES)
            rate = rates(range(NS), lanes)

            def steps(s, carried):
                state = list(carried)
                for u in range(uu):
                    at = s * uu + u
                    here, close = token(c, at)
                    delta = delta_s[b, here, :]
                    du = delta * x_s[b, here, :]
                    y = None
                    for n in range(NS):
                        if n % 2 == 0:
                            both = jnp.concatenate([state[n], state[n + 1]], axis=0)
                            hist[slot, at, b, pl.ds(n * nr, 2 * nr), :] = both.astype(bf16)
                        b_at, c_at = n * LANES, (NS + n) * LANES
                        decay = jnp.exp2(delta * rate[n])
                        state[n] = decay * state[n] + du * bc[close, b_at : b_at + LANES]
                        term = state[n] * bc[close, c_at : c_at + LANES]
                        y = term if y is None else y + term
                    y_s[b, here, :] = y
                return tuple(state)

            last = lax.fori_loop(0, ct // uu, steps, tuple(last_ref[n, :, lanes] for n in range(NS)))
            for n in range(NS):
                last_ref[n, :, lanes] = last[n]
        store_hist(c).start()
        hops(1, c, 1)
        return none

    lax.fori_loop(0, count, forward, 0)
    for t in range(count // 2 + 1, seq):
        carry.turn(1, t)
    leaving_ref[...] = entered[1]

    def store_branch(i):
        slot = lax.rem(i, 2)
        return pltpu.make_async_copy(branch_s.at[slot], branch_out.at[i], branch_sems.at[slot])

    def turn(value, p):
        columns = pl.ds(pl.multiple_of(p * tt, tt), tt)
        turned[:, columns] = jnp.transpose(value.astype(f32)).astype(bf16)

    def products(p, none):
        gates(p)

        def body(span):
            there = pl.ds(p + span.start * size, tile, stride=size)
            y = jnp.concatenate([y_s[b, there, :] for b in range(blocks)], axis=1)
            gate = gate_s[span, :]
            sig = 1.0 / (1.0 + jnp.exp(-gate))
            gated[span, :] = (y * gate * sig).astype(bf16)
            ggp[p, span, :] = (gg_s[span, :] * y * sig * (1.0 + gate * (1.0 - sig))).astype(bf16)

        by_tiles(tt, tile, body)

        @pl.when(p >= 2)
        def _():
            store_branch(p - 2).wait()

        branch = jnp.dot(gated[...], out_w[...], preferred_element_type=f32)
        branch_s[lax.rem(p, 2)] = branch.astype(bf16)
        store_branch(p).start()
        turn(gated[...], p)
        return none

    lax.fori_loop(0, size, products, 0)
    put(ggp, ggp_out)
    wide = 384
    group = wide // share

    def out_weights(j, none):
        columns = pl.ds(pl.multiple_of(j * wide, wide), wide)
        right = cot_s[:, :, columns].reshape(size * tt, wide)
        d_stage[:, columns] = jnp.dot(turned[...], right, preferred_element_type=f32).astype(bf16)
        return none

    lax.fori_loop(0, width // wide, out_weights, 0)
    put(d_stage, dout_out)

    def turn_gate(p, none):
        turn(ggp[p], p)
        return none

    lax.fori_loop(0, size, turn_gate, 0)

    def gate_weights(j, none):
        columns = pl.ds(pl.multiple_of(j * wide, wide), wide)
        right = normed[:, :, columns].reshape(size * tt, wide)
        value = jnp.transpose(jnp.dot(turned[...], right, preferred_element_type=f32)).astype(bf16)
        for g in range(group):
            w_stage[j * group + g] = value[g * share : (g + 1) * share, :]
        return none

    lax.fori_loop(0, width // wide, gate_weights, 0)
    put(w_stage, dwg_out)
    for c in range(max(0, count - 2), count):
        store_hist(c).wait()
    for p in range(size - 2, size):
        store_branch(p).wait()
    carry.drain()

    for i in range(size):

        @pl.when(place < seq - 1)
        def _(i=i):
            halo(i, i).wait_send()

    cot_rows.drain()
    swap_drain(wc, wc_send)
    swap_drain(wg, wg_send)
    for copy in sent:
        copy.wait_send()
    for copy in stores:
        copy.wait()


def front(tokens, cot, notes, w_local, out_w, x_w, dt_w, taps, bias, dt_bias, rate, size, seq, direct):
    tt, width = tokens.shape
    el = out_w.shape[0]
    share = width // size
    blocks = el // LANES
    ct = math.gcd(tt, 32)
    away = pl.BlockSpec(memory_space=pl.ANY)
    here = pl.BlockSpec(memory_space=pltpu.VMEM)
    f32, bf16 = jnp.float32, jnp.bfloat16
    rows, scan, states = (size, tt, width), (blocks, tt * size, LANES), (NS, size, el)
    channels, ext = (size, tt, el), (size, tt + 16, el)
    weights = (size, share, el)
    shapes = [
        (rows, bf16), ((size, share, 2 * el), bf16), (scan, f32), (scan, f32), (scan, f32), (ext, bf16),
        ((tt, blocks, NS * size, LANES), bf16), (rows, bf16), ((el, width), bf16), (weights, bf16), (channels, bf16),
        ((tt * size, LANES), f32), ((size, tt, LANES), bf16), ((size,) + notes.shape, bf16), (states, f32),
        (states, f32),
    ]
    scratch = [
        (rows, bf16), (rows, bf16), (weights, bf16), (weights, bf16), (ext, bf16), ((tt, el), bf16), (scan, f32),
        (scan, f32), (scan, f32), ((tt, el), f32), ((tt, el), f32), ((1, width), f32), ((size, LANES), f32),
        ((LANES, 2 * NS * LANES), bf16), ((ct * size, 2 * NS * LANES), f32), ((4,) + states, f32), ((2,) + states, f32),
        ((blocks, size, LANES), f32), ((2, ct, blocks, NS * size, LANES), bf16), (scan, f32), ((tt, el), bf16), (channels, bf16),
        ((2, tt, width), bf16), ((el, size * tt), bf16), ((el, width), bf16), (weights, bf16),
    ]
    one = pltpu.SemaphoreType.DMA((size,))
    return pl.pallas_call(
        functools.partial(front_kernel, size, seq, direct, ct, ct),
        in_specs=[away] * 4 + [here] * 7,
        out_specs=[away] * 11 + [here] * 5,
        out_shape=[jax.ShapeDtypeStruct(*v) for v in shapes],
        scratch_shapes=[pltpu.VMEM(*v) for v in scratch]
        + RowGather.sems(size) * 2
        + sum_scratch(size, tt)
        + Carry.scratch(states)
        + [one] * 2
        + [pltpu.SemaphoreType.DMA((2, size))] * 4
        + [one] * 2
        + [
            pltpu.SemaphoreType.DMA((size + 9,)),
            pltpu.SemaphoreType.DMA((2,)),
            pltpu.SemaphoreType.DMA((2,)),
        ],
        compiler_params=pltpu.CompilerParams(
            vmem_limit_bytes=63 * MIB, collective_id=0, has_side_effects=True
        ),
        name="front",
    )(tokens, cot, notes, w_local, out_w, x_w, dt_w, taps, bias, dt_bias, rate)


class RowScatter:
    def __init__(self, size, part, keep, land, mail, keep_sem, send, recv):
        self.size, self.part, self.keep, self.land, self.mail = size, part, keep, land, mail
        self.keep_sem, self.send, self.recv = keep_sem, send, recv
        self.me, self.place = lax.axis_index("rows"), lax.axis_index("seq")
        self.tt, self.width = keep.shape[1], keep.shape[2] // 2
        self.orders = bit_orders(size)
        self.steps = len(self.orders[0])

    @staticmethod
    def scratch(size, tt, width):
        return [
            pltpu.VMEM((size // 2, tt, width), jnp.bfloat16),
            pltpu.VMEM((size - 1, tt, width), jnp.bfloat16),
            pltpu.VMEM((size // 2 - 1, tt, width), jnp.bfloat16),
            pltpu.SemaphoreType.DMA((size // 2,)),
            pltpu.SemaphoreType.DMA((2, size - 1)),
            pltpu.SemaphoreType.DMA((2, size - 1)),
        ]

    def free(self, h, k):
        return masks_of(self.orders[h][k + 1 :])

    def at(self, h, k, m):
        if k == 0:
            return m >> 1
        return sum(len(self.free(h, j)) for j in range(k)) + self.free(h, k).index(m)

    def cols(self, h):
        return pl.ds(h * self.width, self.width)

    def receive(self, h, k, m):
        slot = self.at(h, k, m)
        wait_for(self.land.at[slot, :, self.cols(h)], self.recv.at[h, slot])

    def partial_sum(self, h, k, m, rows):
        value = self.keep[m >> 1, rows, self.cols(h)].astype(jnp.float32)
        for j in range(k):
            value = value + self.land[self.at(h, j, m), rows, self.cols(h)].astype(jnp.float32)
        return value

    def staged(self, i, stage):
        for h in range(2):
            remote(
                stage.at[i, :, self.cols(h)], self.land.at[i, :, self.cols(h)], self.send.at[h, i],
                self.recv.at[h, i], (self.place, flip(self.me, 1)),
            )

    def start(self):
        for h in range(2):
            self.scatter(h, 0)
        for m in self.free(0, 0):
            pltpu.make_async_copy(
                self.part.at[flip(self.me, m)], self.keep.at[m >> 1], self.keep_sem.at[m >> 1]
            ).start()

    def step(self, k):
        if k == 1 and self.part is not None:
            for j in range(self.size // 2):
                wait_for(self.keep.at[j], self.keep_sem.at[j])
        for h in range(2):
            self.scatter(h, k)

    def scatter(self, h, k):
        bit = self.orders[h][k]
        for m in self.free(h, k):
            slot = self.at(h, k, m)
            if k == 0:
                source = self.part.at[flip(self.me, m | bit), :, self.cols(h)]
            else:
                for j in range(k):
                    self.receive(h, j, m | bit)
                box = slot - self.size // 2

                def fill(rows, m=m, box=box):
                    value = self.partial_sum(h, k, m | bit, rows)
                    self.mail[box, rows, self.cols(h)] = value.astype(jnp.bfloat16)

                by_tiles(self.tt, 32, fill)
                source = self.mail.at[box, :, self.cols(h)]
            remote(
                source, self.land.at[slot, :, self.cols(h)], self.send.at[h, slot], self.recv.at[h, slot],
                (self.place, flip(self.me, bit)),
            )

    def later(self, first):
        for k in range(first, self.steps):
            self.step(k)

    def finish(self, own):
        for h in range(2):
            for j in range(self.steps):
                self.receive(h, j, 0)

            def fill(rows, h=h):
                own[rows, self.cols(h)] = self.partial_sum(h, self.steps, 0, rows).astype(jnp.bfloat16)

            by_tiles(self.tt, 32, fill)

    def drain(self):
        for h in range(2):
            for slot in range(self.size - 1):
                wait_for(self.land.at[slot, :, self.cols(h)], self.send.at[h, slot])


class SeqSum:
    def __init__(self, seq, lag, held, land, fill_sem, send, recv):
        self.seq, self.lag, self.held, self.land = seq, lag, held, land
        self.fill_sem, self.send, self.recv = fill_sem, send, recv
        self.me, self.place = lax.axis_index("rows"), lax.axis_index("seq")
        self.behind = (self.place, seq - 1 - self.place)
        self.chunks = held.shape[0]
        self.last_step = self.chunks + lag * (seq - 1)

    @staticmethod
    def scratch(chunks, block):
        return [
            pltpu.VMEM((chunks,) + block, jnp.bfloat16),
            pltpu.VMEM((2, chunks) + block, jnp.bfloat16),
            pltpu.SemaphoreType.DMA((chunks,)),
            pltpu.SemaphoreType.DMA((2, chunks)),
            pltpu.SemaphoreType.DMA((2, chunks)),
        ]

    def copy(self, n, way, source):
        target = (jnp.clip(self.place + 1 - 2 * way, 0, self.seq - 1), self.me)
        return pltpu.make_async_remote_copy(
            src_ref=source, dst_ref=self.land.at[way, n], send_sem=self.send.at[way, n],
            recv_sem=self.recv.at[way, n], device_id=target, device_id_type=MESH,
        )

    def hop(self, step, way):
        n = step - self.lag * self.behind[way]

        @pl.when((n >= 0) & (n < self.chunks))
        def _():
            @pl.when(self.behind[way] == 0)
            def _():
                self.copy(n, way, self.held.at[n]).start()

            @pl.when(self.behind[way] > 0)
            def _():
                self.copy(n, way, self.held.at[n]).wait_recv()

                @pl.when(self.behind[way] < self.seq - 1)
                def _():
                    value = self.held[n].astype(jnp.float32) + self.land[way, n].astype(jnp.float32)
                    self.land[way, n] = value.astype(jnp.bfloat16)
                    self.copy(n, way, self.land.at[way, n]).start()

    def advance(self, step, total):
        first = step - self.lag * jnp.minimum(self.behind[0], self.behind[1])

        @pl.when((first >= 0) & (first < self.chunks))
        def _():
            wait_for(self.held.at[first], self.fill_sem.at[first])

        self.hop(step, 0)
        self.hop(step, 1)
        n = step - self.lag * jnp.maximum(self.behind[0], self.behind[1])

        @pl.when((n >= 0) & (n < self.chunks))
        def _():
            for ways, there in (
                ((1,), self.behind[0] == 0),
                ((0,), self.behind[1] == 0),
                ((0, 1), (self.behind[0] > 0) & (self.behind[1] > 0)),
            ):

                @pl.when(there)
                def _(ways=ways):
                    value = self.held[n].astype(jnp.float32)
                    if len(ways) == 2:
                        value = -value
                    for way in ways:
                        value = value + self.land[way, n].astype(jnp.float32)
                    total[n] = value.astype(jnp.bfloat16)

    def run(self, first, last, total):
        def body(step, none):
            self.advance(step, total)
            return none

        lax.fori_loop(first, last, body, 0)

    def drain(self):
        for way in range(2):

            @pl.when(self.behind[way] < self.seq - 1)
            def _(way=way):
                def sent(n, none):
                    self.copy(n, way, self.held.at[n]).wait_send()
                    return none

                lax.fori_loop(0, self.chunks, sent, 0)


def fill_chunks(held, fill_sem, source, first=0):
    rows, cols = held.shape[1:]
    n = first
    if len(source.shape) == 3:
        for j in range(source.shape[0]):
            for i in range(source.shape[1] // rows):
                piece = source.at[j, pl.ds(i * rows, rows), :]
                pltpu.make_async_copy(piece, held.at[n], fill_sem.at[n]).start()
                n += 1
        return n
    for i in range(source.shape[0] // rows):
        for j in range(source.shape[1] // cols):
            piece = source.at[pl.ds(i * rows, rows), pl.ds(j * cols, cols)]
            pltpu.make_async_copy(piece, held.at[n], fill_sem.at[n]).start()
            n += 1
    return n


def early_blocks(size):
    return size // 4


def swap_blocks(size, weight, slots):
    me, place = lax.axis_index("rows"), lax.axis_index("seq")
    for m in range(size):
        q = flip(me, m)
        parts = weight.shape[1] // slots(m, 0)[0].shape[0]
        for i in range(parts):
            target, recv, send = slots(m, i)
            rows = target.shape[0]
            piece = weight.at[q, pl.ds(i * rows, rows), :]
            if m == 0:
                pltpu.make_async_copy(piece, target, recv).start()
            else:
                remote(piece, target, send, recv, (place, q))


def drain_swap(size, weight, slots):
    for m in range(1, size):
        for i in range(weight.shape[1] // slots(m, 0)[0].shape[0]):
            target, unused_recv, send = slots(m, i)
            wait_for(target, send)


def backward_kernel(size, seq, nr, tt, ct, uu, *refs):
    delta_in, x_in, gy_in, hist_in, proj_ref, a_ref, carry_ref, last_ref, branch, out_w, gate_w = refs[:11]
    gdelta_out, gx_out, gate_out, gbc_ref, grate_ref, branch_own, total = refs[11:18]
    sel, bc, hist, prod, state_ref, after_ref, fold, delta_ref, x_ref, gy_ref, gdelta_ref, gx_ref, gate_s = refs[18:31]
    sems, out_sems, hist_sems = refs[31:34]
    scatter = RowScatter(size, branch, *refs[34:40])
    chain = SeqSum(seq, 3, *refs[40:45])
    gate_send, gate_recv, gate_sem = refs[45:]
    el = a_ref.shape[1]
    blocks = el // LANES
    count = tt // ct

    def fetch(c):
        slot = lax.rem(c, 2)
        return pltpu.make_async_copy(hist_in.at[pl.ds(c * ct, ct)], hist.at[slot], hist_sems.at[slot])

    copies = copy_all((delta_in, x_in, gy_in), (delta_ref, x_ref, gy_ref), sems)
    fetch(count - 1).start()
    greet_rows_and_seq(size, seq)
    scatter.start()
    fill_chunks(chain.held, chain.fill_sem, out_w)
    early = early_blocks(size)
    halves = gate_w.shape[1] // chain.held.shape[1]
    first = chain.chunks - early * halves

    def slots(m, i):
        if m < early:
            n = first + m * halves + i
            return chain.held.at[n], chain.fill_sem.at[n], gate_send.at[m, i]
        return gate_s.at[m - early], gate_recv.at[m], gate_send.at[m, 0]

    swap_blocks(size, gate_w, slots)
    sel[...] = selector(LANES)
    fold_row = lax.broadcasted_iota(jnp.int32, fold.shape, 0) // LANES
    fold_col = lax.broadcasted_iota(jnp.int32, fold.shape, 1)
    fold[...] = (fold_row + R == fold_col).astype(jnp.bfloat16)
    state_ref[...] = carry_ref[...]
    after_ref[...] = last_ref[...]
    grate_ref[...] = jnp.zeros_like(grate_ref)
    for copy in copies:
        copy.wait()

    def backward(k, none):
        c = count - 1 - k
        slot = lax.rem(c, 2)

        @pl.when(c > 0)
        def _():
            fetch(c - 1).start()

        for at_k, job in (
            (count // 8, functools.partial(scatter.step, 1)),
            (count * 5 // 8, functools.partial(scatter.later, 2)),
            (count - 1, functools.partial(scatter.finish, branch_own)),
        ):
            pl.when(k == at_k)(job)

        rows = pl.multiple_of(c * (ct * nr), ct * nr)
        bc[...] = spread(proj_ref[pl.ds(rows, ct * nr), :], sel)
        fetch(c).wait()
        for b in range(blocks):
            lanes = slice(b * LANES, (b + 1) * LANES)
            for first in (True, False):
                ns = range(0, NS // 2) if first else range(NS // 2, NS)
                pairs = range(ns[0] // 2, ns[-1] // 2 + 1)
                rate = [jnp.broadcast_to(a_ref[n : n + 1, lanes], (nr, LANES)) for n in ns]

                def steps(s, carried):
                    grad, total_rate, after = (list(v) for v in carried)
                    for u in reversed(range(uu)):
                        at = (ct // uu - 1 - s) * uu + u
                        here = pl.ds(pl.multiple_of((c * ct + at) * nr, nr), nr)
                        delta = delta_ref[b, here, :]
                        x = x_ref[b, here, :]
                        gy = gy_ref[b, here, :]
                        du = delta * x
                        near = pl.ds(pl.multiple_of(at * nr, nr), nr)
                        along_rate = along_b = None
                        for p in pairs:
                            pair = hist[slot, at, b, pl.ds(2 * p * nr, 2 * nr), :].astype(jnp.float32)
                            for n, before in ((2 * p, pair[:nr]), (2 * p + 1, pair[nr:])):
                                i = n - ns[0]
                                to_b_at = slice(n * LANES, (n + 1) * LANES)
                                to_c_at = slice((NS + n) * LANES, (NS + n + 1) * LANES)
                                decay = jnp.exp2(delta * rate[i])
                                grad[i] = grad[i] + gy * bc[near, to_c_at]
                                to_c = after[i] * gy
                                to_b = grad[i] * du
                                if b > 0:
                                    to_c = to_c + prod[near, to_c_at]
                                    to_b = to_b + prod[near, to_b_at]
                                prod[near, to_c_at] = to_c
                                prod[near, to_b_at] = to_b
                                term_b = grad[i] * bc[near, to_b_at]
                                along_b = term_b if along_b is None else along_b + term_b
                                grad[i] = grad[i] * decay
                                weighted = grad[i] * before
                                total_rate[i] = total_rate[i] + weighted * delta
                                term = weighted * rate[i]
                                along_rate = term if along_rate is None else along_rate + term
                                after[i] = before
                        gdelta = along_rate * LN2 + along_b * x
                        gx = along_b * delta
                        if not first:
                            gdelta = gdelta + gdelta_ref[b, here, :]
                            gx = gx + gx_ref[b, here, :]
                        gdelta_ref[b, here, :] = gdelta
                        gx_ref[b, here, :] = gx
                    return tuple(grad), tuple(total_rate), tuple(after)

                start = tuple(tuple(ref[n, :, lanes] for n in ns) for ref in (state_ref, grate_ref, after_ref))
                ends = lax.fori_loop(0, ct // uu, steps, start)
                for i, n in enumerate(ns):
                    for ref, end in zip((state_ref, grate_ref, after_ref), ends):
                        ref[n, :, lanes] = end[i]
            chain.advance(blocks * k + b, total)
        gbc_ref[pl.ds(rows, ct * nr), :] = jnp.dot(
            prod[...].astype(jnp.bfloat16), fold[...], preferred_element_type=jnp.float32
        )
        return none

    lax.fori_loop(0, count, backward, 0)
    late = copy_all((gdelta_ref, gx_ref), (gdelta_out, gx_out), out_sems)
    for m in range(early, size):
        wait_for(gate_s.at[m - early], gate_recv.at[m])
    late += copy_all((gate_s,), (gate_out,), gate_sem)
    chain.run(blocks * count, max(blocks * count, chain.last_step), total)
    scatter.drain()
    chain.drain()
    drain_swap(size, gate_w, slots)
    for copy in late:
        copy.wait()


def scan_backward(delta, x, gy, hist, proj, rate, carry, last, branch, out_w, gate_w, size, seq):
    nr, tt, width = branch.shape
    el = rate.shape[1]
    blocks = el // LANES
    ct = math.gcd(tt, 32)
    here = pl.BlockSpec(memory_space=pltpu.VMEM)
    away = pl.BlockSpec(memory_space=pl.ANY)
    f32, bf16 = jnp.float32, jnp.bfloat16
    scan = (blocks, nr * tt, LANES)
    piece = (gate_w.shape[1] // 2, gate_w.shape[2])
    early = early_blocks(size)
    chunks = out_w.size // math.prod(piece) + 2 * early
    return pl.pallas_call(
        functools.partial(backward_kernel, size, seq, nr, tt, ct, ct),
        in_specs=[away] * 4 + [here] * 4 + [away] * 3,
        out_specs=[away] * 3 + [here] * 4,
        out_shape=[
            jax.ShapeDtypeStruct(scan, f32),
            jax.ShapeDtypeStruct(scan, f32),
            jax.ShapeDtypeStruct((size - early,) + gate_w.shape[1:], bf16),
            jax.ShapeDtypeStruct((tt * nr, LANES), f32),
            jax.ShapeDtypeStruct((NS, nr, el), f32),
            jax.ShapeDtypeStruct((tt, width), bf16),
            jax.ShapeDtypeStruct((chunks,) + piece, bf16),
        ],
        scratch_shapes=[
            pltpu.VMEM((LANES, 2 * NS * LANES), bf16),
            pltpu.VMEM((ct * nr, 2 * NS * LANES), f32),
            pltpu.VMEM((2, ct, blocks, NS * nr, LANES), bf16),
            pltpu.VMEM((ct * nr, 2 * NS * LANES), f32),
            pltpu.VMEM((NS, nr, el), f32),
            pltpu.VMEM((NS, nr, el), f32),
            pltpu.VMEM((2 * NS * LANES, LANES), bf16),
        ]
        + [pltpu.VMEM(scan, f32)] * 5
        + [
            pltpu.VMEM((size - early,) + gate_w.shape[1:], bf16),
            pltpu.SemaphoreType.DMA((3,)),
            pltpu.SemaphoreType.DMA((2,)),
            pltpu.SemaphoreType.DMA((2,)),
        ]
        + RowScatter.scratch(size, tt, width)
        + SeqSum.scratch(chunks, piece)
        + [pltpu.SemaphoreType.DMA((size, 2)), pltpu.SemaphoreType.DMA((size,)), pltpu.SemaphoreType.DMA((1,))],
        compiler_params=pltpu.CompilerParams(
            vmem_limit_bytes=62 * MIB, collective_id=3, has_side_effects=True
        ),
        name="scan_backward",
    )(delta, x, gy, hist, proj, rate, carry, last, branch, out_w, gate_w)


def small_rows(piece_rows):
    rows = 2 * LANES + 32
    return rows + -rows % piece_rows


def back_kernel(size, seq, *refs):
    gdelta_in, gx_in, delta_in, normed_in, w_in, cext_in, ggp_in, gbc_in, gate_w = refs[:9]
    rank_ref, dt_w, x_w, taps_ref, bias_ref, rate_ref, grate_ref = refs[9:16]
    own, sums = refs[16:18]
    (
        gdelta, gx, delta, normed, wv, cext, gmix, gbc, low, gcp, turned, w_stage, acc_x, acc_dt, acc,
        small, hmail, hland, stage, gco,
    ) = refs[18:38]
    part, near, total, mail, far, out, sems = refs[38:45]
    scatter = RowScatter(size, None, *refs[45:51])
    chain = SeqSum(seq, 4, *refs[51:56])
    held, fill_sem = chain.held, chain.fill_sem
    swap_send, in_sems, halo_send, halo_recv = refs[56:]
    me, parity, partner, others = row_peers(size)
    place = lax.axis_index("seq")
    share, el = w_stage.shape[1:]
    tt = low.shape[0]
    width = normed.shape[1]
    blocks = el // LANES
    half = size // 2
    f32, bf16 = jnp.float32, jnp.bfloat16
    nt = (((1,), (1,)), ((), ()))
    tn = (((0,), (0,)), ((), ()))
    copies = copy_all(
        (gdelta_in, delta_in, gbc_in, cext_in, gx_in, ggp_in, w_in, normed_in),
        (gdelta, delta, gbc, cext, gx, gmix.at[:, :, pl.ds(el, el)], wv, normed),
        in_sems,
    )
    early = fill_chunks(held, fill_sem, gate_w)
    greet_rows_and_seq(size, seq)
    for ref in (acc_x, acc_dt, acc, small):
        ref[...] = jnp.zeros_like(ref)
    for copy in copies[:3]:
        copy.wait()

    def fold8(value):
        return jnp.sum(value.reshape(value.shape[0] // 8, 8, value.shape[1]), axis=0)

    def block_at(i):
        return 2 * lax.rem(me // 2 + lax.rem(i, half), half) + lax.rem(parity + 1 + lax.div(i, half), 2)

    def steps_back(i, none):
        p = block_at(i)

        def body(span):
            for b in range(blocks):
                lanes = slice(b * LANES, (b + 1) * LANES)
                there = pl.ds(p + span.start * size, 32, stride=size)
                dl = delta[b, there, :]
                near_zero = dl * (1.0 - dl * (0.5 - dl * (1.0 / 6.0)))
                value = gdelta[b, there, :] * jnp.where(dl < 0.01, near_zero, 1.0 - jnp.exp(-dl))
                low[span, lanes] = value.astype(bf16)
                acc[KC + 1, :, lanes] = acc[KC + 1, :, lanes] + fold8(value)

        by_tiles(tt, 32, body)
        value = lax.dot_general(low[...], dt_w[...], nt, preferred_element_type=f32)
        value = value + gbc[pl.ds(p, tt, stride=size), :]
        acc_dt[...] += lax.dot_general(rank_ref[p], low[...], tn, preferred_element_type=f32)

        @pl.when(i < half)
        def _():
            part[p] = value.astype(bf16)
            remote(
                part.at[p], near.at[lax.div(p, 2)], sems.at[0, lax.div(p, 2)], sems.at[1, lax.div(p, 2)],
                (place, partner),
            )

        @pl.when(i >= half)
        def _():
            total[lax.div(p, 2)] = value

        return none

    lax.fori_loop(0, size, steps_back, 0)
    for copy in copies[3:]:
        copy.wait()
    exchange_sums(size, near, total, mail, far, out, sems, lambda p: None)
    for j in range(half):
        wait_for(near.at[j], sems.at[0, j])

    def halo(p):
        return pltpu.make_async_remote_copy(
            src_ref=hmail.at[p], dst_ref=hland.at[p], send_sem=halo_send.at[p], recv_sem=halo_recv.at[p],
            device_id=(jnp.maximum(place - 1, 0), me), device_id_type=MESH,
        )

    def conv_back(p, none):
        gco[...] = lax.dot_general(out[p], x_w[...], nt, preferred_element_type=f32)

        def body(span):
            value = gco[span, :]
            there = pl.ds(p + span.start * size, 32, stride=size)
            value = value + jnp.concatenate([gx[b, there, :] for b in range(blocks)], axis=1)
            ext = cext[p, pl.ds(span.start, 48), :].astype(f32)
            here = bias_ref[...]
            for k in range(KC):
                here = here + taps_ref[k : k + 1, :] * ext[16 - KC + 1 + k : 16 - KC + 1 + k + 32]
            sig = 1.0 / (1.0 + jnp.exp(-here))
            low[span, :] = (here * sig).astype(bf16)
            value = value * sig * (1.0 + here * (1.0 - sig))
            gcp[p, span, :] = value
            acc[KC] = acc[KC] + fold8(value)
            for k in range(KC):
                acc[k] = acc[k] + fold8(value * ext[16 - KC + 1 + k : 16 - KC + 1 + k + 32])

        by_tiles(tt, 32, body)
        acc_x[...] += lax.dot_general(out[p], low[...], tn, preferred_element_type=f32)
        hmail[p] = gcp[p, 0:16, :].astype(bf16)

        @pl.when(place > 0)
        def _():
            halo(p).start()

        @pl.when(p < early)
        def _():
            chain.advance(p, sums)

        return none

    lax.fori_loop(0, size, conv_back, 0)

    def turn(p, none):
        @pl.when(place < seq - 1)
        def _():
            halo(p).wait_recv()
            gcp[p, tt : tt + 8, :] = hland[p, 0:8, :].astype(f32)

        @pl.when(place == seq - 1)
        def _():
            gcp[p, tt : tt + 8, :] = jnp.zeros((8, el), f32)

        def body(span):
            ext = gcp[p, pl.ds(span.start, 40), :]
            value = taps_ref[KC - 1 : KC, :] * ext[0:32]
            for k in range(KC - 1):
                value = value + taps_ref[k : k + 1, :] * ext[KC - 1 - k : KC - 1 - k + 32]
            gmix[p, span, 0:el] = value.astype(bf16)

        by_tiles(tt, 32, body)
        columns = pl.ds(pl.multiple_of(p * tt, tt), tt)
        turned[:, columns] = jnp.transpose(gmix[p, :, 0:el].astype(f32)).astype(bf16)

        @pl.when(size + p < early)
        def _():
            chain.advance(size + p, sums)

        return none

    lax.fori_loop(0, size, turn, 0)
    chain.run(2 * size, max(2 * size, early), sums)

    group = 384 // share

    def weights(j, none):
        columns = pl.ds(pl.multiple_of(j * 384, 384), 384)
        value = jnp.dot(turned[...], normed[:, columns], preferred_element_type=f32)
        value = jnp.transpose(value).astype(bf16)
        for g in range(group):
            w_stage[j * group + g] = value[g * share : (g + 1) * share, :]
        return none

    lax.fori_loop(0, width // 384, weights, 0)
    rows = 2 * LANES
    small[0:LANES, :] = acc_x[...].astype(bf16)
    small[LANES:rows, :] = acc_dt[...].astype(bf16)
    rate_sum = jnp.sum(grate_ref[...], axis=1) * rate_ref[...]
    last = [rate_sum] + [jnp.sum(acc[k], axis=0, keepdims=True) for k in range(KC + 2)]
    last.append(jnp.zeros((16 - KC - 2, el), f32))
    small[rows : rows + 32, :] = jnp.concatenate(last, axis=0).astype(bf16)
    late = fill_chunks(held, fill_sem, small, early)
    halves = share // held.shape[1]

    def slots(m, i):
        n = late + m * halves + i
        return held.at[n], fill_sem.at[n], swap_send.at[n]

    swap_blocks(size, w_stage, slots)

    def spread_back(i, none):
        p = crossed(me, jnp.where(i < half, 2 * i + 1, 2 * (i - half)), size)
        weight = wv[...].reshape(width, 2 * el)
        value = lax.dot_general(gmix[p], weight, nt, preferred_element_type=f32).astype(bf16)

        @pl.when(i < half)
        def _():
            stage[i] = value
            scatter.staged(i, stage)

        @pl.when(i >= half)
        def _():
            scatter.keep[i - half] = value

        chain.advance(early + i, sums)
        return none

    lax.fori_loop(0, size, spread_back, 0)
    done = early + size
    jobs = [functools.partial(scatter.step, k) for k in range(1, scatter.steps)]
    jobs.append(functools.partial(scatter.finish, own))
    for k, job in enumerate(jobs):
        job()
        upto = min(chain.last_step, done + (chain.last_step - done) * (2 if k else 3) // 4)
        chain.run(done, upto, sums)
        done = upto
    chain.run(done, chain.last_step, sums)
    scatter.drain()
    chain.drain()
    drain_swap(size, w_stage, slots)

    def halo_sent(p, none):
        halo(p).wait_send()
        return none

    @pl.when(place > 0)
    def _():
        lax.fori_loop(0, size, halo_sent, 0)


def back(
    gdelta, gx, delta, normed, w_in, cext, ggp, gbc, rank, dt_w, x_w, taps, bias, rate, grate, gate_w, size, seq
):
    away = pl.BlockSpec(memory_space=pl.ANY)
    here = pl.BlockSpec(memory_space=pltpu.VMEM)
    f32, bf16 = jnp.float32, jnp.bfloat16
    unused_size, tt, el = ggp.shape
    share = w_in.shape[1]
    width = normed.shape[1]
    piece = (share // 2, el)
    low = small_rows(piece[0])
    chunks = 4 * size - 2 * early_blocks(size) + low // piece[0]
    scratch = [
        (gdelta.shape, f32), (gx.shape, f32), (delta.shape, f32), (normed.shape, bf16), (w_in.shape, bf16),
        (cext.shape, bf16), ((size, tt, 2 * el), bf16), (gbc.shape, f32), ((tt, el), bf16),
        ((size, tt + 8, el), f32), ((el, size * tt), bf16), ((size, share, el), bf16), ((LANES, el), f32),
        ((LANES, el), f32), ((KC + 2, 8, el), f32), ((low, el), bf16), ((size, 16, el), bf16),
        ((size, 16, el), bf16), ((size // 2, tt, width), bf16), ((tt, el), f32),
    ]
    return pl.pallas_call(
        functools.partial(back_kernel, size, seq),
        in_specs=[away] * 9 + [here] * 7,
        out_specs=[here] * 2,
        out_shape=[
            jax.ShapeDtypeStruct((tt, width), bf16),
            jax.ShapeDtypeStruct((chunks,) + piece, bf16),
        ],
        scratch_shapes=[pltpu.VMEM(*v) for v in scratch]
        + sum_scratch(size, tt)
        + RowScatter.scratch(size, tt, width)
        + SeqSum.scratch(chunks, piece)
        + [
            pltpu.SemaphoreType.DMA((chunks,)),
            pltpu.SemaphoreType.DMA((8,)),
            pltpu.SemaphoreType.DMA((size,)),
            pltpu.SemaphoreType.DMA((size,)),
        ],
        compiler_params=pltpu.CompilerParams(
            vmem_limit_bytes=63 * MIB, collective_id=4, has_side_effects=True
        ),
        name="back",
    )(gdelta, gx, delta, normed, w_in, cext, ggp, gbc, gate_w, rank, dt_w, x_w, taps, bias, rate, grate)


def local(
    tokens, resets, norm_gain, in_proj, x_proj, dt_proj, conv_weight, conv_bias, dt_bias, a_log, out_proj,
    cotangent,
):
    size = lax.axis_size("rows")
    seq = lax.axis_size("seq")
    rd, tt, unused_d = tokens.shape
    nr = rd * size
    el = E // size
    count = nr * tt
    assert rd == 1 and ITEM % tt == 0 and nr % 8 == 0

    elp = pad_lanes(el)
    share = D // size
    direct = elp == el
    f32, bf16 = jnp.float32, jnp.bfloat16

    def widen(value, axis):
        pad = [(0, 0)] * value.ndim
        pad[axis] = (0, elp - el)
        return jnp.pad(value, pad)

    if direct:
        w_local = in_proj
    else:
        w_local = jnp.moveaxis(in_proj.reshape(share, 2, size, el), 2, 0)
        w_local = widen(w_local, 3).reshape(size, share, 2 * elp)
    out_proj, x_proj = widen(out_proj, 0), widen(x_proj, 0)
    dt_pad = widen(jnp.pad(dt_proj, ((0, LANES - R), (0, 0))), 1)
    taps = widen(conv_weight.astype(f32), 1)
    bias = widen(conv_bias.astype(f32), 0)[None]
    rate = widen(-jnp.exp(a_log.astype(f32)), 1)
    notes = jnp.zeros((16, -(-share // 256) * 256), bf16)
    notes = notes.at[0, :share].set(norm_gain).at[1].set(1.0 - resets[0, 0].astype(bf16))
    (
        normed, w_in, x_t, delta_t, gy_t, conv_ext, hist, branch, grad_out_proj, grad_in_gate, grad_gate_pre, proj_t,
        rank_all, all_notes, last, carry_back,
    ) = front(
        tokens[0], cotangent[0], notes, w_local, out_proj, x_proj, dt_pad, taps, bias,
        widen(dt_bias.astype(f32), 0)[None], rate * LOG2E, size, seq, direct,
    )
    gain = all_notes[:, 0, :share].reshape(D).astype(f32)
    grad_delta, grad_input, gate_blocks, grad_bc, grate, branch_own, summed_out = scan_backward(
        delta_t, x_t, gy_t, hist, proj_t, rate * LOG2E, carry_back, last, branch,
        grad_out_proj[:el], grad_in_gate, size, seq,
    )
    grad_normed, summed = back(
        grad_delta, grad_input, delta_t, normed.reshape(count, D), w_in, conv_ext, grad_gate_pre, grad_bc, rank_all,
        dt_pad, x_proj, taps, bias, rate, grate, gate_blocks, size, seq,
    )
    block = (share, elp)
    early = 2 * early_blocks(size)
    out_rows, out_cols = 2 * el // share, D // elp
    sum_out = summed_out[:-early].reshape(out_rows, out_cols, share // 2, elp)
    sum_out = jnp.swapaxes(sum_out, 1, 2).reshape(el, D).astype(f32)
    rest = 2 * size - early
    small = summed[rest : -2 * size].reshape(-1, elp)[:, :el].astype(f32)
    order = jnp.array(range(size)) ^ lax.axis_index("rows")
    sum_gate = jnp.concatenate([summed_out[-early:], summed[:rest]])
    sum_in = [part.reshape((size,) + block)[order] for part in (summed[-2 * size :], sum_gate)]
    sum_in = jnp.transpose(jnp.stack(sum_in)[..., :el].astype(f32), (2, 0, 1, 3)).reshape(share, 2 * E)
    block_out = (tokens.astype(jnp.float32) + branch_own[None].astype(jnp.float32)).astype(jnp.bfloat16)
    grad_normed = grad_normed[None].astype(jnp.float32)

    own = tokens.astype(jnp.float32)
    inv = lax.rsqrt(jnp.mean(own * own, axis=2, keepdims=True) + epsilon)
    gain_own = jnp.sum(in_proj.astype(jnp.float32) * sum_in, axis=1) / norm_gain.astype(jnp.float32)
    grad_hat = grad_normed * gain
    grad_norm_in = inv * (
        grad_hat - own * (inv * inv) * jnp.mean(grad_hat * own, axis=2, keepdims=True)
    )
    d_tokens = (cotangent.astype(jnp.float32) + grad_norm_in).astype(jnp.bfloat16)

    more = small[2 * LANES :]
    return (
        block_out,
        d_tokens,
        gain_own,
        sum_in,
        small[:LANES].T,
        small[LANES : LANES + R],
        more[NS : NS + KC],
        more[NS + KC],
        more[NS + KC + 1],
        more[:NS],
        sum_out,
    )


def solution(mesh):
    in_specs = (
        P("rows", "seq", None),
        P("rows", "seq"),
        P("rows"),
        P("rows", None),
        P("rows", None),
        P(None, "rows"),
        P(None, "rows"),
        P("rows"),
        P("rows"),
        P(None, "rows"),
        P("rows", None),
        P("rows", "seq", None),
    )
    out_specs = (
        P("rows", "seq", None),
        P("rows", "seq", None),
        P("rows"),
        P("rows", None),
        P("rows", None),
        P(None, "rows"),
        P(None, "rows"),
        P("rows"),
        P("rows"),
        P(None, "rows"),
        P("rows", None),
    )
    return jax.shard_map(local, mesh=mesh, in_specs=in_specs, out_specs=out_specs, check_vma=False)
```

```python
import functools
import math

import jax
import jax.numpy as jnp
from jax import lax
from jax.experimental import pallas as pl
from jax.experimental.pallas import tpu as pltpu
from jax.sharding import PartitionSpec as P

D = 1536
E = 3072
R = 96
NS = 16
KC = 4
ITEM = 256

epsilon = 1e-05
LOG2E = 1.4426950408889634
LN2 = 0.6931471805599453
MIB = 2**20


LANES = 128


def pad_lanes(lanes):
    return -(-lanes // LANES) * LANES


def selector(wide):
    row = lax.broadcasted_iota(jnp.int32, (LANES, 2 * NS * wide), 0)
    col = lax.broadcasted_iota(jnp.int32, (LANES, 2 * NS * wide), 1) // wide
    return (row == col + R).astype(jnp.bfloat16)


def decay_rates(params):
    return -jnp.exp(params[8 : 8 + NS, :])


def spread(proj, sel_ref):
    return jnp.dot(proj.astype(jnp.bfloat16), sel_ref[...], preferred_element_type=jnp.float32)


def copy_all(sources, targets, sems):
    copies = []
    for i, (source, target) in enumerate(zip(sources, targets)):
        copies.append(pltpu.make_async_copy(source, target, sems.at[i]))
        copies[-1].start()
    return copies


MESH = pl.DeviceIdType.MESH


def greet(devices):
    barrier = pltpu.get_barrier_semaphore()
    for device in devices:
        pl.semaphore_signal(barrier, inc=1, device_id=device, device_id_type=MESH)
    pl.semaphore_wait(barrier, len(devices))


def remote(source, target, send, recv, device):
    copy = pltpu.make_async_remote_copy(
        src_ref=source, dst_ref=target, send_sem=send, recv_sem=recv, device_id=device, device_id_type=MESH
    )
    copy.start()
    return copy


def row_peers(size):
    me = lax.axis_index("rows")
    half = size // 2
    mine = me // 2
    return me, me % 2, me + 1 - 2 * (me % 2), [lax.rem(mine + k, half) for k in range(half)]


def exchange_sums(size, near, total, mail, far, out, sems, use, between=None):
    me, parity, partner, others = row_peers(size)
    place = lax.axis_index("seq")
    half = size // 2
    second = []
    for k in list(range(1, half)) + [0]:
        j = others[k]
        wait_for(near.at[j], sems.at[1, j])
        total[j] = total[j] + near[j].astype(jnp.float32)
        if k:
            mail[j] = total[j].astype(jnp.bfloat16)
            target = (place, 2 * j + parity)
            second.append(remote(mail.at[j], far.at[k], sems.at[2, k], sems.at[3, k], target))
    mine = others[0]
    done = total[mine]
    for k in range(1, half):
        wait_for(far.at[k], sems.at[3, k])
        done = done + far[k].astype(jnp.float32)
    out[me] = done.astype(jnp.bfloat16)
    third = []
    for k in range(1, half):
        target = (place, 2 * others[k] + parity)
        third.append(remote(out.at[me], out.at[me], sems.at[4, k], sems.at[5, k], target))
    fourth = [remote(out.at[me], out.at[me], sems.at[6, 0], sems.at[7, 0], (place, partner))]
    use(me)
    for k in range(1, half):
        block = 2 * others[half - k] + parity
        wait_for(out.at[block], sems.at[5, k])
        fourth.append(
            remote(out.at[block], out.at[block], sems.at[6, k], sems.at[7, k], (place, partner))
        )
        use(block)
    for k in range(half):
        block = 2 * others[(half - k) % half] + 1 - parity
        wait_for(out.at[block], sems.at[7, k])
        use(block)
    if between:
        between()
    for copy in second + third + fourth:
        copy.wait_send()


def sum_scratch(size, tt):
    half = size // 2
    return [
        pltpu.VMEM((size, tt, LANES), jnp.bfloat16),
        pltpu.VMEM((half, tt, LANES), jnp.bfloat16),
        pltpu.VMEM((half, tt, LANES), jnp.float32),
        pltpu.VMEM((half, tt, LANES), jnp.bfloat16),
        pltpu.VMEM((half, tt, LANES), jnp.bfloat16),
        pltpu.VMEM((size, tt, LANES), jnp.bfloat16),
        pltpu.SemaphoreType.DMA((8, half)),
    ]


class Carry:
    def __init__(self, seq, ends, alive, out, mail, land, sems):
        self.seq, self.ends, self.alive, self.out = seq, ends, alive, out
        self.mail, self.land, self.sems = mail, land, sems
        self.me, self.place = lax.axis_index("rows"), lax.axis_index("seq")

    @staticmethod
    def scratch(shape):
        return [
            pltpu.VMEM((2,) + shape, jnp.bfloat16),
            pltpu.VMEM((2,) + shape, jnp.bfloat16),
            pltpu.SemaphoreType.DMA((2, 2, shape[-1] // LANES)),
        ]

    def copy(self, way, b):
        lanes = pl.ds(b * LANES, LANES)
        target = (jnp.clip(self.place + 1 - 2 * way, 0, self.seq - 1), self.me)
        return pltpu.make_async_remote_copy(
            src_ref=self.mail.at[way, :, :, lanes], dst_ref=self.land.at[way, :, :, lanes],
            send_sem=self.sems.at[way, 0, b], recv_sem=self.sems.at[way, 1, b], device_id=target,
            device_id_type=MESH,
        )

    def hop(self, way):
        first, last = ((0, self.seq - 1), (self.seq - 1, 0))[way]
        alive = self.alive[:, 0:1][None]

        for b in range(self.mail.shape[-1] // LANES):
            lanes = slice(b * LANES, (b + 1) * LANES)

            @pl.when(self.place == first)
            def _(lanes=lanes):
                self.out[way, :, :, lanes] = jnp.zeros(self.out.shape[1:3] + (LANES,), jnp.float32)

            @pl.when(self.place != first)
            def _(b=b, lanes=lanes):
                self.copy(way, b).wait_recv()
                entering = self.land[way, :, :, lanes].astype(jnp.float32)
                self.out[way, :, :, lanes] = entering * alive if way == 0 else entering

            @pl.when(self.place != last)
            def _(b=b, lanes=lanes):
                passed = self.ends[1, :, :, lanes] * self.out[way, :, :, lanes]
                if way == 0:
                    leaving = self.ends[0, :, :, lanes] + passed
                else:
                    leaving = (self.ends[2, :, :, lanes] + passed) * alive
                self.mail[way, :, :, lanes] = leaving.astype(jnp.bfloat16)
                self.copy(way, b).start()

    def turn(self, way, t):
        behind = (self.place, self.seq - 1 - self.place)[way]
        pl.when(behind == t)(functools.partial(self.hop, way))

    def drain(self):
        for way, last in ((0, self.seq - 1), (1, 0)):

            @pl.when(self.place != last)
            def _(way=way):
                for b in range(self.mail.shape[-1] // LANES):
                    self.copy(way, b).wait_send()


def flip(place, mask):
    for k in range(mask.bit_length()):
        bit = 1 << k
        if mask & bit:
            place = place + bit * (1 - 2 * (lax.div(place, bit) % 2))
    return place


def bit_orders(size):
    rest = [1 << k for k in range(1, size.bit_length() - 1)]
    cut = max(1, len(rest) // 2)
    return [1] + rest, [1] + rest[cut:] + rest[:cut]


def masks_of(bits):
    masks = [0]
    for bit in bits:
        masks = masks + [m | bit for m in masks]
    return masks


def by_tiles(rows, tile, body):
    def step(i, none):
        body(pl.ds(pl.multiple_of(i * tile, tile), tile))
        return none

    lax.fori_loop(0, rows // tile, step, 0)


def wait_for(ref, sem):
    pltpu.make_async_copy(ref, ref, sem).wait()


def greet_seq(seq):
    me, place = lax.axis_index("rows"), lax.axis_index("seq")
    barrier = pltpu.get_barrier_semaphore()
    for step, there in ((-1, place > 0), (1, place < seq - 1)):

        @pl.when(there)
        def _(step=step):
            pl.semaphore_signal(barrier, inc=1, device_id=(place + step, me), device_id_type=MESH)

    pl.semaphore_wait(barrier, (place > 0).astype(jnp.int32) + (place < seq - 1).astype(jnp.int32))


def greet_rows_and_seq(size, seq):
    me, place = lax.axis_index("rows"), lax.axis_index("seq")
    barrier = pltpu.get_barrier_semaphore()
    for mask in range(1, size):
        pl.semaphore_signal(barrier, inc=1, device_id=(place, flip(me, mask)), device_id_type=MESH)
    for step, there in ((-1, place > 0), (1, place < seq - 1)):

        @pl.when(there)
        def _(step=step):
            pl.semaphore_signal(barrier, inc=1, device_id=(place + step, me), device_id_type=MESH)

    near = (place > 0).astype(jnp.int32) + (place < seq - 1).astype(jnp.int32)
    pl.semaphore_wait(barrier, near + size - 1)


def crossed(place, mask, size):
    out = 0
    for k in range(size.bit_length() - 1):
        bit = 1 << k
        out = out + bit * lax.rem(lax.div(place, bit) + lax.div(mask, bit), 2)
    return out


class RowGather:
    def __init__(self, size, source, out, own_sem, send, recv):
        self.size, self.source, self.out, self.own_sem, self.send, self.recv = size, source, out, own_sem, send, recv
        self.me, self.place = lax.axis_index("rows"), lax.axis_index("seq")
        self.rows = source.shape[0] // 2
        self.orders = [order[1:] for order in bit_orders(size)]
        self.steps = len(self.orders[0])

    @staticmethod
    def sems(size):
        return [pltpu.SemaphoreType.DMA((1,))] + [pltpu.SemaphoreType.DMA((2, size))] * 2

    def half(self, h, m, ref=None):
        ref = self.out.at[flip(self.me, m)] if ref is None else ref
        return ref.at[pl.ds(h * self.rows, self.rows), :]

    def push(self, h, m, bit):
        source = self.half(h, m, self.source if m == 0 else None)
        key = (h, m | bit)
        remote(
            source, self.half(h, m), self.send.at[key], self.recv.at[key], (self.place, flip(self.me, bit))
        )

    def arrived(self, h, m):
        wait_for(self.half(h, m), self.recv.at[h, m])

    def start(self):
        pltpu.make_async_copy(self.source, self.out.at[self.me], self.own_sem.at[0]).start()
        for h in range(2):
            self.push(h, 0, self.orders[h][0])
        for h in range(2):
            self.push(h, 0, 1)

    def own(self):
        wait_for(self.out.at[self.me], self.own_sem.at[0])

    def step(self, k, use=None):
        for h in range(2):
            order = self.orders[h]
            old = masks_of(order[:k])
            if k + 1 < self.steps:
                for m in old:
                    self.push(h, m, order[k + 1])
            for m in old:
                fresh = m | order[k]
                self.arrived(h, fresh)
                if k + 1 < self.steps:
                    self.push(h, fresh, order[k + 1])
                self.push(h, fresh, 1)
                if use:
                    use(h, fresh)

    def paired(self, use=None):
        for m in masks_of(self.orders[0]):
            for h in range(2):
                self.arrived(h, m | 1)
                if use:
                    use(h, m | 1)

    def drain(self):
        for h in range(2):
            for m in range(1, self.size):
                wait_for(self.half(h, 0), self.send.at[h, m])


def front_kernel(size, seq, direct, ct, uu, *refs):
    (tokens, cot, notes, w_local, out_w, x_w, dt_in, params) = refs[:8]
    (
        normed_out, w_out, x_out, delta_out, gy_out, cext_out, hist_out, branch_out, dout_out, dwg_out, ggp_out,
        proj_ref, rank_ref, all_notes, last_ref, leaving_ref,
    ) = refs[8:24]
    (
        tok, cot_s, wc, wg, cext, xb, x_s, delta_s, gy_s, gate_s, gg_s, gain_ref, alive_ref, sel, bc, ends, entered,
        delta_sum, hist, y_s, gated, ggp, branch_s, turned, d_stage, w_stage, gate_b, dt_w, a_ref,
    ) = refs[24:53]
    token_sems, cot_sems = refs[53:56], refs[56:59]
    part, near, total, mail, far, out, sems = refs[59:66]
    carry = Carry(seq, ends, alive_ref, entered, *refs[66:69])
    taps_ref, bias_ref, dt_bias_ref = params.at[0:KC], params.at[KC : KC + 1], params.at[KC + 1 : KC + 2]
    (
        note_send, note_recv, wc_send, wc_recv, wg_send, wg_recv, halo_send, halo_recv, out_sems, hist_sems, branch_sems,
    ) = refs[69:]
    normed = tok
    me, parity, partner, others = row_peers(size)
    place = lax.axis_index("seq")
    tt, width = tokens.shape
    share, el = wc.shape[1:]
    nr = size
    blocks = el // LANES
    half = size // 2
    f32, bf16 = jnp.float32, jnp.bfloat16
    tile = 32
    stores = []

    def put(source, target):
        copy = pltpu.make_async_copy(source, target, out_sems.at[len(stores)])
        copy.start()
        stores.append(copy)

    def piece(q, gate):
        if direct:
            at = pl.multiple_of(q * el, LANES) + gate * size * el
            return w_local.at[:, pl.ds(at, el)]
        return w_local.at[q, :, pl.ds(gate * el, el)]

    cut = share // 2
    beside = (flip(place, 1), me)

    def swap(gate, target, send, recv):
        there = pl.ds(pl.multiple_of(lax.rem(place, 2) * cut, cut), cut)
        for m in range(1, size):
            q = flip(me, m)
            remote(piece(q, gate).at[there, :], target.at[me, there, :], send.at[0, m], recv.at[0, m], (place, q))
        pltpu.make_async_copy(piece(me, gate), target.at[me], recv.at[0, 0]).start()

    def swap_on(target, send, recv):
        there = pl.ds(pl.multiple_of(lax.rem(place, 2) * cut, cut), cut)
        for m in range(1, size):
            block = target.at[flip(me, m), there, :]
            wait_for(block, recv.at[0, m])
            remote(block, block, send.at[1, m], recv.at[1, m], beside)

    def swapped(target, send, recv):
        wait_for(target.at[me], recv.at[0, 0])
        for m in range(1, size):
            wait_for(target.at[flip(me, m), pl.ds(0, cut), :], recv.at[1, m])

    def swap_drain(target, send):
        for k in range(2):
            for m in range(1, size):
                wait_for(target.at[0, pl.ds(0, cut), :], send.at[k, m])

    greet_rows_and_seq(size, seq)

    sent = []
    for m in range(1, size):
        sent.append(remote(notes, all_notes.at[me], note_send.at[m], note_recv.at[m], (place, flip(me, m))))
    pltpu.make_async_copy(notes, all_notes.at[me], note_recv.at[0]).start()
    token_rows = RowGather(size, tokens, tok, *token_sems)
    cot_rows = RowGather(size, cot, cot_s, *cot_sems)
    swap(0, wc, wc_send, wc_recv)
    token_rows.start()

    for m in range(size):
        wait_for(all_notes.at[flip(me, m)], note_recv.at[m])
    for p in range(size):
        note = all_notes[p].astype(f32)
        gain_ref[:, p * share : (p + 1) * share] = note[0:1, :share]
        alive_ref[p : p + 1, :] = note[1:2, :LANES]

    def norm(p, base, rows):
        def body(span):
            there = pl.ds(base + span.start, span.size)
            x = tok[p, there, :].astype(f32)
            inv = lax.rsqrt(jnp.mean(x * x, axis=1, keepdims=True) + epsilon)
            normed[p, there, :] = (x * inv * gain_ref[...]).astype(bf16)

        by_tiles(rows, 64, body)

    def norm_half(h, m):
        norm(flip(me, m), h * (tt // 2), tt // 2)

    token_rows.own()
    norm(me, 0, tt)
    swap_on(wc, wc_send, wc_recv)
    sel[...] = selector(LANES)
    a_ref[...] = decay_rates(params) * LOG2E
    dt_w[0:R, :] = dt_in[...]
    dt_w[R:, :] = jnp.zeros((LANES - R, el), bf16)
    for k in range(token_rows.steps):
        token_rows.step(k)
    token_rows.paired(norm_half)
    token_rows.drain()
    for m in masks_of(token_rows.orders[0])[1:]:
        norm(flip(me, m), 0, tt)
    swapped(wc, wc_send, wc_recv)

    @pl.when(place == 0)
    def _():
        cext[:, 0:16, :] = jnp.zeros((size, 16, el), bf16)

    def halo(p, i):
        there = cext.at[p, pl.ds(0, 16), :]
        return pltpu.make_async_remote_copy(
            src_ref=cext.at[p, pl.ds(tt, 16), :], dst_ref=there, send_sem=halo_send.at[i],
            recv_sem=halo_recv.at[i], device_id=(jnp.minimum(place + 1, seq - 1), me), device_id_type=MESH,
        )

    def block_at(i):
        return 2 * lax.rem(me // 2 + lax.rem(i, half), half) + lax.rem(parity + 1 + lax.div(i, half), 2)

    def mix(i, none):
        p = block_at(i)
        weight = wc[...].reshape(size * share, el)
        cext[p, 16:, :] = jnp.dot(normed[p], weight, preferred_element_type=f32).astype(bf16)

        @pl.when(place < seq - 1)
        def _():
            halo(p, i).start()

        return none

    lax.fori_loop(0, size, mix, 0)
    for p in range(size):
        put(normed.at[p], normed_out.at[p])

    def conv(i, none):
        p = block_at(i)

        @pl.when(place > 0)
        def _():
            halo(p, i).wait_recv()

        def body(span):
            ext = cext[p, pl.ds(span.start, tile + 16), :].astype(f32)
            value = bias_ref[...]
            for k in range(KC):
                value = value + taps_ref[k : k + 1, :] * ext[16 - KC + 1 + k : 16 - KC + 1 + k + tile]
            x = (value / (1.0 + jnp.exp(-value))).astype(bf16)
            xb[span, :] = x
            for b in range(blocks):
                there = pl.ds(p + span.start * size, tile, stride=size)
                x_s[b, there, :] = x[:, b * LANES : (b + 1) * LANES].astype(f32)

        by_tiles(tt, tile, body)
        value = jnp.dot(xb[...], x_w[...], preferred_element_type=f32)

        @pl.when(i < half)
        def _():
            part[p] = value.astype(bf16)
            pltpu.make_async_remote_copy(
                src_ref=part.at[p], dst_ref=near.at[lax.div(p, 2)], send_sem=sems.at[0, lax.div(p, 2)],
                recv_sem=sems.at[1, lax.div(p, 2)], device_id=(place, partner), device_id_type=MESH,
            ).start()

        @pl.when(i >= half)
        def _():
            total[lax.div(p, 2)] = value

        return none

    lax.fori_loop(0, size, conv, 0)
    put(cext, cext_out)
    put(x_s, x_out)

    def use(p):
        block = out[p]
        rank_ref[p] = block
        proj_ref[pl.ds(p, tt, stride=size), :] = block.astype(f32)

        gate_s[...] = jnp.dot(block, dt_w[...], preferred_element_type=f32)

        def body(span):
            step = gate_s[span, :] + dt_bias_ref[...]
            delta = jnp.maximum(step, 0.0) + jnp.log1p(jnp.exp(-jnp.abs(step)))
            for b in range(blocks):
                there = pl.ds(p + span.start * size, 64, stride=size)
                delta_s[b, there, :] = delta[:, b * LANES : (b + 1) * LANES]

        by_tiles(tt, 64, body)

    def second_wave():
        cot_rows.start()
        swap(1, wg, wg_send, wg_recv)

    exchange_sums(size, near, total, mail, far, out, sems, use, second_wave)
    for j in range(half):
        pltpu.make_async_remote_copy(
            src_ref=part.at[j], dst_ref=near.at[j], send_sem=sems.at[0, j], recv_sem=sems.at[1, j],
            device_id=(place, partner), device_id_type=MESH,
        ).wait_send()
    put(delta_s, delta_out)
    put(wc, w_out.at[:, :, pl.ds(0, el)])

    count = tt // ct
    ends[0] = jnp.zeros((NS, nr, el), f32)
    ends[2] = jnp.zeros((NS, nr, el), f32)
    ends[3] = jnp.ones((NS, nr, el), f32)
    delta_sum[...] = jnp.zeros_like(delta_sum)

    def spread_chunk(c, first, last):
        rows = pl.multiple_of(c * (ct * nr), ct * nr)
        lanes = slice(first * LANES, last * LANES)
        bc[:, lanes] = spread(proj_ref[pl.ds(rows, ct * nr), :], sel.at[:, lanes])

    def token(c, at):
        return pl.ds(pl.multiple_of((c * ct + at) * nr, nr), nr), pl.ds(pl.multiple_of(at * nr, nr), nr)

    def rates(ns, lanes):
        return [jnp.broadcast_to(a_ref[n : n + 1, lanes], (nr, LANES)) for n in ns]

    def ends_forward(c, none):
        pl.when(c == count // 2)(functools.partial(cot_rows.step, 0))
        spread_chunk(c, 0, NS)
        for b in range(blocks):
            lanes = slice(b * LANES, (b + 1) * LANES)
            rate = rates(range(NS), lanes)

            def steps(s, carried):
                state, so_far = list(carried[:-1]), carried[-1]
                for u in range(uu):
                    here, close = token(c, s * uu + u)
                    delta = delta_s[b, here, :]
                    du = delta * x_s[b, here, :]
                    so_far = so_far + delta
                    for n in range(NS):
                        b_at = n * LANES
                        state[n] = jnp.exp2(delta * rate[n]) * state[n] + du * bc[close, b_at : b_at + LANES]
                return tuple(state) + (so_far,)

            start = tuple(ends[0, n, :, lanes] for n in range(NS)) + (delta_sum[b],)
            last = lax.fori_loop(0, ct // uu, steps, start)
            for n in range(NS):
                ends[0, n, :, lanes] = last[n]
            delta_sum[b] = last[NS]
        return none

    lax.fori_loop(0, count, ends_forward, 0)
    for b in range(blocks):
        lanes = slice(b * LANES, (b + 1) * LANES)
        for n in range(NS):
            ends[1, n, :, lanes] = jnp.exp2(delta_sum[b] * a_ref[n : n + 1, lanes])
    carry.turn(0, 0)

    for t in range(1, seq):
        carry.turn(0, t)
    swap_on(wg, wg_send, wg_recv)
    last_ref[...] = entered[0]

    def store_hist(c):
        slot = lax.rem(c, 2)
        return pltpu.make_async_copy(hist.at[slot], hist_out.at[pl.ds(c * ct, ct)], hist_sems.at[slot])

    def forward(c, none):
        slot = lax.rem(c, 2)

        @pl.when(c >= 2)
        def _():
            store_hist(c - 2).wait()

        for k in range(1, cot_rows.steps):
            pl.when(c == min(count // 2 + k - 1, count - 1))(functools.partial(cot_rows.step, k))
        spread_chunk(c, 0, 2 * NS)
        for b in range(blocks):
            lanes = slice(b * LANES, (b + 1) * LANES)
            rate = rates(range(NS), lanes)

            def steps(s, carried):
                state = list(carried)
                for u in range(uu):
                    at = s * uu + u
                    here, close = token(c, at)
                    delta = delta_s[b, here, :]
                    du = delta * x_s[b, here, :]
                    y = None
                    for n in range(NS):
                        if n % 2 == 0:
                            both = jnp.concatenate([state[n], state[n + 1]], axis=0)
                            hist[slot, at, b, pl.ds(n * nr, 2 * nr), :] = both.astype(bf16)
                        b_at, c_at = n * LANES, (NS + n) * LANES
                        decay = jnp.exp2(delta * rate[n])
                        state[n] = decay * state[n] + du * bc[close, b_at : b_at + LANES]
                        term = state[n] * bc[close, c_at : c_at + LANES]
                        y = term if y is None else y + term
                    y_s[b, here, :] = y
                return tuple(state)

            last = lax.fori_loop(0, ct // uu, steps, tuple(last_ref[n, :, lanes] for n in range(NS)))
            for n in range(NS):
                last_ref[n, :, lanes] = last[n]
        store_hist(c).start()
        return none

    lax.fori_loop(0, count, forward, 0)
    cot_rows.own()
    cot_rows.paired()
    swapped(wg, wg_send, wg_recv)
    put(wg, w_out.at[:, :, pl.ds(el, el)])

    def gates(p):
        weight = wg[...].reshape(size * share, el)
        gate_s[...] = jnp.dot(normed[p], weight, preferred_element_type=f32)
        gg_s[...] = lax.dot_general(
            cot_s[p], out_w[...], (((1,), (1,)), ((), ())), preferred_element_type=f32
        )

    def grad_y(p, none):
        gates(p)

        def body(span):
            gate, gg = gate_s[span, :], gg_s[span, :]
            gate_b[p, span, :] = gate.astype(bf16)
            ggp[p, span, :] = gg.astype(bf16)
            gy = gg * gate / (1.0 + jnp.exp(-gate))
            for b in range(blocks):
                there = pl.ds(p + span.start * size, tile, stride=size)
                gy_s[b, there, :] = gy[:, b * LANES : (b + 1) * LANES]

        by_tiles(tt, tile, body)
        return none

    lax.fori_loop(0, size, grad_y, 0)
    put(gy_s, gy_out)

    def ends_back(c, none):
        spread_chunk(c, NS, 2 * NS)
        for b in range(blocks):
            lanes = slice(b * LANES, (b + 1) * LANES)
            for n0 in (0, NS // 2):
                ns = range(n0, n0 + NS // 2)
                rate = rates(ns, lanes)

                def steps(s, carried):
                    through, back = (list(v) for v in carried)
                    for u in range(uu):
                        here, close = token(c, s * uu + u)
                        delta = delta_s[b, here, :]
                        gy = gy_s[b, here, :]
                        for i, n in enumerate(ns):
                            c_at = (NS + n) * LANES
                            through[i] = through[i] * jnp.exp2(delta * rate[i])
                            back[i] = back[i] + through[i] * (gy * bc[close, c_at : c_at + LANES])
                    return tuple(through), tuple(back)

                start = tuple(tuple(ends[k, n, :, lanes] for n in ns) for k in (3, 2))
                last = lax.fori_loop(0, ct // uu, steps, start)
                for i, n in enumerate(ns):
                    ends[3, n, :, lanes] = last[0][i]
                    ends[2, n, :, lanes] = last[1][i]
        return none

    lax.fori_loop(0, count, ends_back, 0)
    carry.turn(1, 0)

    def store_branch(i):
        slot = lax.rem(i, 2)
        return pltpu.make_async_copy(branch_s.at[slot], branch_out.at[i], branch_sems.at[slot])

    def turn(value, p):
        columns = pl.ds(pl.multiple_of(p * tt, tt), tt)
        turned[:, columns] = jnp.transpose(value.astype(f32)).astype(bf16)

    def products(p, none):
        def body(span):
            there = pl.ds(p + span.start * size, tile, stride=size)
            y = jnp.concatenate([y_s[b, there, :] for b in range(blocks)], axis=1)
            gate = gate_b[p, span, :].astype(f32)
            sig = 1.0 / (1.0 + jnp.exp(-gate))
            gated[span, :] = (y * gate * sig).astype(bf16)
            ggp[p, span, :] = (ggp[p, span, :].astype(f32) * y * sig * (1.0 + gate * (1.0 - sig))).astype(bf16)

        by_tiles(tt, tile, body)

        @pl.when(p >= 2)
        def _():
            store_branch(p - 2).wait()

        branch = jnp.dot(gated[...], out_w[...], preferred_element_type=f32)
        branch_s[lax.rem(p, 2)] = branch.astype(bf16)
        store_branch(p).start()
        turn(gated[...], p)

        @pl.when(lax.rem(p, 2) == 1)
        def _():
            carry.turn(1, lax.div(p, 2) + 1)

        return none

    lax.fori_loop(0, size, products, 0)
    for t in range(half + 1, seq):
        carry.turn(1, t)
    put(ggp, ggp_out)
    wide = 384
    group = wide // share

    def out_weights(j, none):
        columns = pl.ds(pl.multiple_of(j * wide, wide), wide)
        right = cot_s[:, :, columns].reshape(size * tt, wide)
        d_stage[:, columns] = jnp.dot(turned[...], right, preferred_element_type=f32).astype(bf16)
        return none

    lax.fori_loop(0, width // wide, out_weights, 0)
    put(d_stage, dout_out)

    def turn_gate(p, none):
        turn(ggp[p], p)
        return none

    lax.fori_loop(0, size, turn_gate, 0)

    def gate_weights(j, none):
        columns = pl.ds(pl.multiple_of(j * wide, wide), wide)
        right = normed[:, :, columns].reshape(size * tt, wide)
        value = jnp.transpose(jnp.dot(turned[...], right, preferred_element_type=f32)).astype(bf16)
        for g in range(group):
            w_stage[j * group + g] = value[g * share : (g + 1) * share, :]
        return none

    lax.fori_loop(0, width // wide, gate_weights, 0)
    put(w_stage, dwg_out)
    for c in range(max(0, count - 2), count):
        store_hist(c).wait()
    for p in range(size - 2, size):
        store_branch(p).wait()
    leaving_ref[...] = entered[1]
    carry.drain()

    for i in range(size):

        @pl.when(place < seq - 1)
        def _(i=i):
            halo(i, i).wait_send()

    cot_rows.drain()
    swap_drain(wc, wc_send)
    swap_drain(wg, wg_send)
    for copy in sent:
        copy.wait_send()
    for copy in stores:
        copy.wait()


def front(tokens, cot, notes, w_local, out_w, x_w, dt_w, params, size, seq, direct):
    tt, width = tokens.shape
    el = out_w.shape[0]
    share = width // size
    blocks = el // LANES
    ct = math.gcd(tt, 32)
    away = pl.BlockSpec(memory_space=pl.ANY)
    here = pl.BlockSpec(memory_space=pltpu.VMEM)
    f32, bf16 = jnp.float32, jnp.bfloat16
    rows, scan, states = (size, tt, width), (blocks, tt * size, LANES), (NS, size, el)
    channels, ext = (size, tt, el), (size, tt + 16, el)
    weights = (size, share, el)
    shapes = [
        (rows, bf16), ((size, share, 2 * el), bf16), (scan, f32), (scan, f32), (scan, f32), (ext, bf16),
        ((tt, blocks, NS * size, LANES), bf16), (rows, bf16), ((el, width), bf16), (weights, bf16), (channels, bf16),
        ((tt * size, LANES), f32), ((size, tt, LANES), bf16), ((size,) + notes.shape, bf16), (states, f32),
        (states, f32),
    ]
    scratch = [
        (rows, bf16), (rows, bf16), (weights, bf16), (weights, bf16), (ext, bf16), ((tt, el), bf16), (scan, f32),
        (scan, f32), (scan, f32), ((tt, el), f32), ((tt, el), f32), ((1, width), f32), ((size, LANES), f32),
        ((LANES, 2 * NS * LANES), bf16), ((ct * size, 2 * NS * LANES), f32), ((4,) + states, f32), ((2,) + states, f32),
        ((blocks, size, LANES), f32), ((2, ct, blocks, NS * size, LANES), bf16), (scan, f32), ((tt, el), bf16), (channels, bf16),
        ((2, tt, width), bf16), ((el, size * tt), bf16), ((el, width), bf16), (weights, bf16),
        (channels, bf16), ((LANES, el), bf16), ((NS, el), f32),
    ]
    one = pltpu.SemaphoreType.DMA((size,))
    return pl.pallas_call(
        functools.partial(front_kernel, size, seq, direct, ct, max(1, ct * 8 // size)),
        in_specs=[away] * 4 + [here] * 4,
        out_specs=[away] * 11 + [here] * 5,
        out_shape=[jax.ShapeDtypeStruct(*v) for v in shapes],
        scratch_shapes=[pltpu.VMEM(*v) for v in scratch]
        + RowGather.sems(size) * 2
        + sum_scratch(size, tt)
        + Carry.scratch(states)
        + [one] * 2
        + [pltpu.SemaphoreType.DMA((2, size))] * 4
        + [one] * 2
        + [
            pltpu.SemaphoreType.DMA((size + 9,)),
            pltpu.SemaphoreType.DMA((2,)),
            pltpu.SemaphoreType.DMA((2,)),
        ],
        compiler_params=pltpu.CompilerParams(
            vmem_limit_bytes=63 * MIB, collective_id=0, has_side_effects=True
        ),
        name="front",
    )(tokens, cot, notes, w_local, out_w, x_w, dt_w, params)


class RowScatter:
    def __init__(self, size, part, keep, land, mail, keep_sem, send, recv):
        self.size, self.part, self.keep, self.land, self.mail = size, part, keep, land, mail
        self.keep_sem, self.send, self.recv = keep_sem, send, recv
        self.me, self.place = lax.axis_index("rows"), lax.axis_index("seq")
        self.tt, self.width = keep.shape[1], keep.shape[2] // 2
        self.orders = bit_orders(size)
        self.steps = len(self.orders[0])

    @staticmethod
    def scratch(size, tt, width):
        return [
            pltpu.VMEM((size // 2, tt, width), jnp.bfloat16),
            pltpu.VMEM((size - 1, tt, width), jnp.bfloat16),
            pltpu.VMEM((size // 2 - 1, tt, width), jnp.bfloat16),
            pltpu.SemaphoreType.DMA((size // 2,)),
            pltpu.SemaphoreType.DMA((2, size - 1)),
            pltpu.SemaphoreType.DMA((2, size - 1)),
        ]

    def free(self, h, k):
        return masks_of(self.orders[h][k + 1 :])

    def at(self, h, k, m):
        if k == 0:
            return m >> 1
        return sum(len(self.free(h, j)) for j in range(k)) + self.free(h, k).index(m)

    def cols(self, h):
        return pl.ds(h * self.width, self.width)

    def receive(self, h, k, m):
        slot = self.at(h, k, m)
        wait_for(self.land.at[slot, :, self.cols(h)], self.recv.at[h, slot])

    def partial_sum(self, h, k, m, rows):
        value = self.keep[m >> 1, rows, self.cols(h)].astype(jnp.float32)
        for j in range(k):
            value = value + self.land[self.at(h, j, m), rows, self.cols(h)].astype(jnp.float32)
        return value

    def staged(self, i, stage):
        for h in range(2):
            remote(
                stage.at[i, :, self.cols(h)], self.land.at[i, :, self.cols(h)], self.send.at[h, i],
                self.recv.at[h, i], (self.place, flip(self.me, 1)),
            )

    def start(self):
        for h in range(2):
            self.scatter(h, 0)
        for m in self.free(0, 0):
            pltpu.make_async_copy(
                self.part.at[flip(self.me, m)], self.keep.at[m >> 1], self.keep_sem.at[m >> 1]
            ).start()

    def step(self, k):
        if k == 1 and self.part is not None:
            for j in range(self.size // 2):
                wait_for(self.keep.at[j], self.keep_sem.at[j])
        for h in range(2):
            self.scatter(h, k)

    def scatter(self, h, k):
        bit = self.orders[h][k]
        for m in self.free(h, k):
            slot = self.at(h, k, m)
            if k == 0:
                source = self.part.at[flip(self.me, m | bit), :, self.cols(h)]
            else:
                for j in range(k):
                    self.receive(h, j, m | bit)
                box = slot - self.size // 2

                def fill(rows, m=m, box=box):
                    value = self.partial_sum(h, k, m | bit, rows)
                    self.mail[box, rows, self.cols(h)] = value.astype(jnp.bfloat16)

                by_tiles(self.tt, 32, fill)
                source = self.mail.at[box, :, self.cols(h)]
            remote(
                source, self.land.at[slot, :, self.cols(h)], self.send.at[h, slot], self.recv.at[h, slot],
                (self.place, flip(self.me, bit)),
            )

    def later(self, first):
        for k in range(first, self.steps):
            self.step(k)

    def finish(self, own):
        for h in range(2):
            for j in range(self.steps):
                self.receive(h, j, 0)

            def fill(rows, h=h):
                own[rows, self.cols(h)] = self.partial_sum(h, self.steps, 0, rows).astype(jnp.bfloat16)

            by_tiles(self.tt, 32, fill)

    def drain(self):
        for h in range(2):
            for slot in range(self.size - 1):
                wait_for(self.land.at[slot, :, self.cols(h)], self.send.at[h, slot])


class SeqSum:
    def __init__(self, seq, lag, held, land, fill_sem, send, recv):
        self.seq, self.lag, self.held, self.land = seq, lag, held, land
        self.fill_sem, self.send, self.recv = fill_sem, send, recv
        self.me, self.place = lax.axis_index("rows"), lax.axis_index("seq")
        self.behind = (self.place, seq - 1 - self.place)
        self.chunks = held.shape[0]
        self.last_step = self.chunks + lag * (seq - 1)

    @staticmethod
    def scratch(chunks, block):
        return [
            pltpu.VMEM((chunks,) + block, jnp.bfloat16),
            pltpu.VMEM((2, chunks) + block, jnp.bfloat16),
            pltpu.SemaphoreType.DMA((chunks,)),
            pltpu.SemaphoreType.DMA((2, chunks)),
            pltpu.SemaphoreType.DMA((2, chunks)),
        ]

    def copy(self, n, way, source):
        target = (jnp.clip(self.place + 1 - 2 * way, 0, self.seq - 1), self.me)
        return pltpu.make_async_remote_copy(
            src_ref=source, dst_ref=self.land.at[way, n], send_sem=self.send.at[way, n],
            recv_sem=self.recv.at[way, n], device_id=target, device_id_type=MESH,
        )

    def hop(self, step, way):
        n = step - self.lag * self.behind[way]

        @pl.when((n >= 0) & (n < self.chunks))
        def _():
            @pl.when(self.behind[way] == 0)
            def _():
                self.copy(n, way, self.held.at[n]).start()

            @pl.when(self.behind[way] > 0)
            def _():
                self.copy(n, way, self.held.at[n]).wait_recv()

                @pl.when(self.behind[way] < self.seq - 1)
                def _():
                    value = self.held[n].astype(jnp.float32) + self.land[way, n].astype(jnp.float32)
                    self.land[way, n] = value.astype(jnp.bfloat16)
                    self.copy(n, way, self.land.at[way, n]).start()

    def advance(self, step, total):
        first = step - self.lag * jnp.minimum(self.behind[0], self.behind[1])

        @pl.when((first >= 0) & (first < self.chunks))
        def _():
            wait_for(self.held.at[first], self.fill_sem.at[first])

        self.hop(step, 0)
        self.hop(step, 1)
        n = step - self.lag * jnp.maximum(self.behind[0], self.behind[1])

        @pl.when((n >= 0) & (n < self.chunks))
        def _():
            for ways, there in (
                ((1,), self.behind[0] == 0),
                ((0,), self.behind[1] == 0),
                ((0, 1), (self.behind[0] > 0) & (self.behind[1] > 0)),
            ):

                @pl.when(there)
                def _(ways=ways):
                    value = self.held[n].astype(jnp.float32)
                    if len(ways) == 2:
                        value = -value
                    for way in ways:
                        value = value + self.land[way, n].astype(jnp.float32)
                    total(n, value.astype(jnp.bfloat16))

    def run(self, first, last, total):
        def body(step, none):
            self.advance(step, total)
            return none

        lax.fori_loop(first, last, body, 0)

    def drain(self):
        for way in range(2):

            @pl.when(self.behind[way] < self.seq - 1)
            def _(way=way):
                def sent(n, none):
                    self.copy(n, way, self.held.at[n]).wait_send()
                    return none

                lax.fori_loop(0, self.chunks, sent, 0)


def fill_chunks(held, fill_sem, source, first=0):
    rows, cols = held.shape[1:]
    n = first
    if len(source.shape) == 3:
        for j in range(source.shape[0]):
            for i in range(source.shape[1] // rows):
                piece = source.at[j, pl.ds(i * rows, rows), :]
                pltpu.make_async_copy(piece, held.at[n], fill_sem.at[n]).start()
                n += 1
        return n
    for i in range(source.shape[0] // rows):
        for j in range(source.shape[1] // cols):
            piece = source.at[pl.ds(i * rows, rows), pl.ds(j * cols, cols)]
            pltpu.make_async_copy(piece, held.at[n], fill_sem.at[n]).start()
            n += 1
    return n


def early_blocks(size):
    return size // 4


def swap_blocks(size, weight, slots):
    me, place = lax.axis_index("rows"), lax.axis_index("seq")
    for m in range(size):
        q = flip(me, m)
        parts = weight.shape[1] // slots(m, 0)[0].shape[0]
        for i in range(parts):
            target, recv, send = slots(m, i)
            rows = target.shape[0]
            piece = weight.at[q, pl.ds(i * rows, rows), :]
            if m == 0:
                pltpu.make_async_copy(piece, target, recv).start()
            else:
                remote(piece, target, send, recv, (place, q))


def drain_swap(size, weight, slots):
    for m in range(1, size):
        for i in range(weight.shape[1] // slots(m, 0)[0].shape[0]):
            target, unused_recv, send = slots(m, i)
            wait_for(target, send)


def backward_kernel(size, seq, nr, tt, ct, uu, *refs):
    delta_in, x_in, gy_in, hist_in, proj_ref, params, carry_ref, last_ref, branch, out_w, gate_w = refs[:11]
    gdelta_out, gx_out, gate_out, gbc_ref, grate_ref, branch_own, out_sum, gate_sum = refs[11:19]
    sel, bc, hist, prod, state_ref, after_ref, fold, delta_ref, x_ref, gy_ref, gdelta_ref, gx_ref, gate_s, a_ref = refs[19:33]
    sems, out_sems, hist_sems = refs[33:36]
    scatter = RowScatter(size, branch, *refs[36:42])
    chain = SeqSum(seq, 3, *refs[42:47])
    gate_send, gate_recv, gate_sem = refs[47:]
    el = a_ref.shape[1]
    blocks = el // LANES
    count = tt // ct

    def fetch(c):
        slot = lax.rem(c, 2)
        return pltpu.make_async_copy(hist_in.at[pl.ds(c * ct, ct)], hist.at[slot], hist_sems.at[slot])

    copies = copy_all((delta_in, x_in, gy_in), (delta_ref, x_ref, gy_ref), sems)
    fetch(count - 1).start()
    greet_rows_and_seq(size, seq)
    scatter.start()
    fill_chunks(chain.held, chain.fill_sem, out_w)
    early = early_blocks(size)
    halves = gate_w.shape[1] // chain.held.shape[1]
    first = chain.chunks - early * halves

    def slots(m, i):
        if m < early:
            n = first + m * halves + i
            return chain.held.at[n], chain.fill_sem.at[n], gate_send.at[m, i]
        return gate_s.at[m - early], gate_recv.at[m], gate_send.at[m, 0]

    swap_blocks(size, gate_w, slots)
    a_ref[...] = decay_rates(params) * LOG2E
    piece = chain.held.shape[1:]

    def total(n, value):
        @pl.when(n < first)
        def _():
            across = out_sum.shape[1] // piece[1]
            down = pl.multiple_of(lax.div(n, across) * piece[0], piece[0])
            along = pl.multiple_of(lax.rem(n, across) * piece[1], LANES)
            out_sum[pl.ds(down, piece[0]), pl.ds(along, piece[1])] = value

        @pl.when(n >= first)
        def _():
            gate_sum[n - first] = value

    sel[...] = selector(LANES)
    fold_row = lax.broadcasted_iota(jnp.int32, fold.shape, 0) // LANES
    fold_col = lax.broadcasted_iota(jnp.int32, fold.shape, 1)
    fold[...] = (fold_row + R == fold_col).astype(jnp.bfloat16)
    state_ref[...] = carry_ref[...]
    after_ref[...] = last_ref[...]
    grate_ref[...] = jnp.zeros_like(grate_ref)
    for copy in copies:
        copy.wait()

    def backward(k, none):
        c = count - 1 - k
        slot = lax.rem(c, 2)

        @pl.when(c > 0)
        def _():
            fetch(c - 1).start()

        for at_k, job in (
            (count // 8, functools.partial(scatter.step, 1)),
            (count * 5 // 8, functools.partial(scatter.later, 2)),
            (count - 1, functools.partial(scatter.finish, branch_own)),
        ):
            pl.when(k == at_k)(job)

        rows = pl.multiple_of(c * (ct * nr), ct * nr)
        bc[...] = spread(proj_ref[pl.ds(rows, ct * nr), :], sel)
        fetch(c).wait()
        for b in range(blocks):
            lanes = slice(b * LANES, (b + 1) * LANES)
            for first in (True, False):
                ns = range(0, NS // 2) if first else range(NS // 2, NS)
                pairs = range(ns[0] // 2, ns[-1] // 2 + 1)
                rate = [jnp.broadcast_to(a_ref[n : n + 1, lanes], (nr, LANES)) for n in ns]

                def steps(s, carried):
                    grad, total_rate, after = (list(v) for v in carried)
                    for u in reversed(range(uu)):
                        at = (ct // uu - 1 - s) * uu + u
                        here = pl.ds(pl.multiple_of((c * ct + at) * nr, nr), nr)
                        delta = delta_ref[b, here, :]
                        x = x_ref[b, here, :]
                        gy = gy_ref[b, here, :]
                        du = delta * x
                        near = pl.ds(pl.multiple_of(at * nr, nr), nr)
                        along_rate = along_b = None
                        for p in pairs:
                            pair = hist[slot, at, b, pl.ds(2 * p * nr, 2 * nr), :].astype(jnp.float32)
                            for n, before in ((2 * p, pair[:nr]), (2 * p + 1, pair[nr:])):
                                i = n - ns[0]
                                to_b_at = slice(n * LANES, (n + 1) * LANES)
                                to_c_at = slice((NS + n) * LANES, (NS + n + 1) * LANES)
                                decay = jnp.exp2(delta * rate[i])
                                grad[i] = grad[i] + gy * bc[near, to_c_at]
                                to_c = after[i] * gy
                                to_b = grad[i] * du
                                if b > 0:
                                    to_c = to_c + prod[near, to_c_at]
                                    to_b = to_b + prod[near, to_b_at]
                                prod[near, to_c_at] = to_c
                                prod[near, to_b_at] = to_b
                                term_b = grad[i] * bc[near, to_b_at]
                                along_b = term_b if along_b is None else along_b + term_b
                                grad[i] = grad[i] * decay
                                weighted = grad[i] * before
                                total_rate[i] = total_rate[i] + weighted * delta
                                term = weighted * rate[i]
                                along_rate = term if along_rate is None else along_rate + term
                                after[i] = before
                        gdelta = along_rate * LN2 + along_b * x
                        gx = along_b * delta
                        if not first:
                            gdelta = gdelta + gdelta_ref[b, here, :]
                            gx = gx + gx_ref[b, here, :]
                        gdelta_ref[b, here, :] = gdelta
                        gx_ref[b, here, :] = gx
                    return tuple(grad), tuple(total_rate), tuple(after)

                start = tuple(tuple(ref[n, :, lanes] for n in ns) for ref in (state_ref, grate_ref, after_ref))
                ends = lax.fori_loop(0, ct // uu, steps, start)
                for i, n in enumerate(ns):
                    for ref, end in zip((state_ref, grate_ref, after_ref), ends):
                        ref[n, :, lanes] = end[i]
            chain.advance(blocks * k + b, total)
        gbc_ref[pl.ds(rows, ct * nr), :] = jnp.dot(
            prod[...].astype(jnp.bfloat16), fold[...], preferred_element_type=jnp.float32
        )
        return none

    lax.fori_loop(0, count, backward, 0)
    late = copy_all((gdelta_ref, gx_ref), (gdelta_out, gx_out), out_sems)
    for m in range(early, size):
        wait_for(gate_s.at[m - early], gate_recv.at[m])
    late += copy_all((gate_s,), (gate_out,), gate_sem)
    chain.run(blocks * count, max(blocks * count, chain.last_step), total)
    scatter.drain()
    chain.drain()
    drain_swap(size, gate_w, slots)
    for copy in late:
        copy.wait()


def scan_backward(delta, x, gy, hist, proj, params, carry, last, branch, out_w, gate_w, size, seq):
    nr, tt, width = branch.shape
    el = params.shape[1]
    blocks = el // LANES
    ct = math.gcd(tt, 32)
    here = pl.BlockSpec(memory_space=pltpu.VMEM)
    away = pl.BlockSpec(memory_space=pl.ANY)
    f32, bf16 = jnp.float32, jnp.bfloat16
    scan = (blocks, nr * tt, LANES)
    piece = (gate_w.shape[1] // 2, gate_w.shape[2])
    early = early_blocks(size)
    chunks = out_w.size // math.prod(piece) + 2 * early
    return pl.pallas_call(
        functools.partial(backward_kernel, size, seq, nr, tt, ct, max(1, ct * 8 // size)),
        in_specs=[away] * 4 + [here] * 4 + [away] * 3,
        out_specs=[away] * 3 + [here] * 5,
        out_shape=[
            jax.ShapeDtypeStruct(scan, f32),
            jax.ShapeDtypeStruct(scan, f32),
            jax.ShapeDtypeStruct((size - early,) + gate_w.shape[1:], bf16),
            jax.ShapeDtypeStruct((tt * nr, LANES), f32),
            jax.ShapeDtypeStruct((NS, nr, el), f32),
            jax.ShapeDtypeStruct((tt, width), bf16),
            jax.ShapeDtypeStruct(out_w.shape, bf16),
            jax.ShapeDtypeStruct((2 * early,) + piece, bf16),
        ],
        scratch_shapes=[
            pltpu.VMEM((LANES, 2 * NS * LANES), bf16),
            pltpu.VMEM((ct * nr, 2 * NS * LANES), f32),
            pltpu.VMEM((2, ct, blocks, NS * nr, LANES), bf16),
            pltpu.VMEM((ct * nr, 2 * NS * LANES), f32),
            pltpu.VMEM((NS, nr, el), f32),
            pltpu.VMEM((NS, nr, el), f32),
            pltpu.VMEM((2 * NS * LANES, LANES), bf16),
        ]
        + [pltpu.VMEM(scan, f32)] * 5
        + [
            pltpu.VMEM((size - early,) + gate_w.shape[1:], bf16),
            pltpu.VMEM((NS, el), f32),
            pltpu.SemaphoreType.DMA((3,)),
            pltpu.SemaphoreType.DMA((2,)),
            pltpu.SemaphoreType.DMA((2,)),
        ]
        + RowScatter.scratch(size, tt, width)
        + SeqSum.scratch(chunks, piece)
        + [pltpu.SemaphoreType.DMA((size, 2)), pltpu.SemaphoreType.DMA((size,)), pltpu.SemaphoreType.DMA((1,))],
        compiler_params=pltpu.CompilerParams(
            vmem_limit_bytes=62 * MIB, collective_id=3, has_side_effects=True
        ),
        name="scan_backward",
    )(delta, x, gy, hist, proj, params, carry, last, branch, out_w, gate_w)


def small_rows(piece_rows):
    rows = 2 * LANES + 32
    return rows + -rows % piece_rows


def back_kernel(size, seq, *refs):
    gdelta_in, gx_in, delta_in, normed_in, w_in, cext_in, ggp_in, gbc_in, gate_w = refs[:9]
    rank_ref, dt_in, x_w, params, grate_ref, gate_sum = refs[9:15]
    own, in_sum, small_sum = refs[15:18]
    taps_ref, bias_ref = params.at[0:KC], params.at[KC : KC + 1]
    (
        gdelta, gx, delta, normed, wv, cext, gmix, gbc, low, gcp, turned, w_stage, acc_x, acc_dt, acc,
        small, hmail, hland, stage, gco, dt_w,
    ) = refs[18:39]
    part, near, total, mail, far, out, sems = refs[39:46]
    scatter = RowScatter(size, None, *refs[46:52])
    chain = SeqSum(seq, 4, *refs[52:57])
    held, fill_sem = chain.held, chain.fill_sem
    swap_send, in_sems, halo_send, halo_recv = refs[57:]
    me, parity, partner, others = row_peers(size)
    place = lax.axis_index("seq")
    share, el = w_stage.shape[1:]
    tt = low.shape[0]
    width = normed.shape[1]
    blocks = el // LANES
    half = size // 2
    f32, bf16 = jnp.float32, jnp.bfloat16
    nt = (((1,), (1,)), ((), ()))
    tn = (((0,), (0,)), ((), ()))
    copies = copy_all(
        (gdelta_in, delta_in, gbc_in, cext_in, gx_in, ggp_in, w_in, normed_in),
        (gdelta, delta, gbc, cext, gx, gmix.at[:, :, pl.ds(el, el)], wv, normed),
        in_sems,
    )
    early = fill_chunks(held, fill_sem, gate_w)
    greet_rows_and_seq(size, seq)
    for ref in (acc_x, acc_dt, acc, small):
        ref[...] = jnp.zeros_like(ref)
    for copy in copies[:3]:
        copy.wait()

    dt_w[0:R, :] = dt_in[...]
    dt_w[R:, :] = jnp.zeros((LANES - R, el), bf16)
    rows = held.shape[1]
    halves = share // rows
    first = small_rows(rows) // rows
    before = early_blocks(size)

    def place_in(m, i, gate, value):
        along = pl.multiple_of((gate * size + crossed(me, m, size)) * el, LANES)
        in_sum[pl.ds(pl.multiple_of(i * rows, rows), rows), pl.ds(along, el)] = value

    def sums(n, value):
        @pl.when(n < early)
        def _():
            place_in(before + lax.div(n, halves), lax.rem(n, halves), 1, value)

        @pl.when((n >= early) & (n < early + first))
        def _():
            small_sum[pl.ds(pl.multiple_of((n - early) * rows, rows), rows), :] = value

        @pl.when(n >= early + first)
        def _():
            k = n - early - first
            place_in(lax.div(k, halves), lax.rem(k, halves), 0, value)

    for n in range(before * halves):
        place_in(n // halves, n % halves, 1, gate_sum[n])

    def fold8(value):
        return jnp.sum(value.reshape(value.shape[0] // 8, 8, value.shape[1]), axis=0)

    def block_at(i):
        return 2 * lax.rem(me // 2 + lax.rem(i, half), half) + lax.rem(parity + 1 + lax.div(i, half), 2)

    def steps_back(i, none):
        p = block_at(i)

        def body(span):
            for b in range(blocks):
                lanes = slice(b * LANES, (b + 1) * LANES)
                there = pl.ds(p + span.start * size, 32, stride=size)
                dl = delta[b, there, :]
                near_zero = dl * (1.0 - dl * (0.5 - dl * (1.0 / 6.0)))
                value = gdelta[b, there, :] * jnp.where(dl < 0.01, near_zero, 1.0 - jnp.exp(-dl))
                low[span, lanes] = value.astype(bf16)
                acc[KC + 1, :, lanes] = acc[KC + 1, :, lanes] + fold8(value)

        by_tiles(tt, 32, body)
        value = lax.dot_general(low[...], dt_w[...], nt, preferred_element_type=f32)
        value = value + gbc[pl.ds(p, tt, stride=size), :]
        acc_dt[...] += lax.dot_general(rank_ref[p], low[...], tn, preferred_element_type=f32)

        @pl.when(i < half)
        def _():
            part[p] = value.astype(bf16)
            remote(
                part.at[p], near.at[lax.div(p, 2)], sems.at[0, lax.div(p, 2)], sems.at[1, lax.div(p, 2)],
                (place, partner),
            )

        @pl.when(i >= half)
        def _():
            total[lax.div(p, 2)] = value

        return none

    lax.fori_loop(0, size, steps_back, 0)
    for copy in copies[3:]:
        copy.wait()
    exchange_sums(size, near, total, mail, far, out, sems, lambda p: None)
    for j in range(half):
        wait_for(near.at[j], sems.at[0, j])

    def halo(p):
        return pltpu.make_async_remote_copy(
            src_ref=hmail.at[p], dst_ref=hland.at[p], send_sem=halo_send.at[p], recv_sem=halo_recv.at[p],
            device_id=(jnp.maximum(place - 1, 0), me), device_id_type=MESH,
        )

    def conv_back(p, none):
        gco[...] = lax.dot_general(out[p], x_w[...], nt, preferred_element_type=f32)

        def body(span):
            value = gco[span, :]
            there = pl.ds(p + span.start * size, 32, stride=size)
            value = value + jnp.concatenate([gx[b, there, :] for b in range(blocks)], axis=1)
            ext = cext[p, pl.ds(span.start, 48), :].astype(f32)
            here = bias_ref[...]
            for k in range(KC):
                here = here + taps_ref[k : k + 1, :] * ext[16 - KC + 1 + k : 16 - KC + 1 + k + 32]
            sig = 1.0 / (1.0 + jnp.exp(-here))
            low[span, :] = (here * sig).astype(bf16)
            value = value * sig * (1.0 + here * (1.0 - sig))
            gcp[p, span, :] = value
            acc[KC] = acc[KC] + fold8(value)
            for k in range(KC):
                acc[k] = acc[k] + fold8(value * ext[16 - KC + 1 + k : 16 - KC + 1 + k + 32])

        by_tiles(tt, 32, body)
        acc_x[...] += lax.dot_general(out[p], low[...], tn, preferred_element_type=f32)
        hmail[p] = gcp[p, 0:16, :].astype(bf16)

        @pl.when(place > 0)
        def _():
            halo(p).start()

        @pl.when(p < early)
        def _():
            chain.advance(p, sums)

        return none

    lax.fori_loop(0, size, conv_back, 0)

    def turn(p, none):
        @pl.when(place < seq - 1)
        def _():
            halo(p).wait_recv()
            gcp[p, tt : tt + 8, :] = hland[p, 0:8, :].astype(f32)

        @pl.when(place == seq - 1)
        def _():
            gcp[p, tt : tt + 8, :] = jnp.zeros((8, el), f32)

        def body(span):
            ext = gcp[p, pl.ds(span.start, 40), :]
            value = taps_ref[KC - 1 : KC, :] * ext[0:32]
            for k in range(KC - 1):
                value = value + taps_ref[k : k + 1, :] * ext[KC - 1 - k : KC - 1 - k + 32]
            gmix[p, span, 0:el] = value.astype(bf16)

        by_tiles(tt, 32, body)
        columns = pl.ds(pl.multiple_of(p * tt, tt), tt)
        turned[:, columns] = jnp.transpose(gmix[p, :, 0:el].astype(f32)).astype(bf16)

        @pl.when(size + p < early)
        def _():
            chain.advance(size + p, sums)

        return none

    lax.fori_loop(0, size, turn, 0)
    chain.run(2 * size, max(2 * size, early), sums)

    group = 384 // share

    def weights(j, none):
        columns = pl.ds(pl.multiple_of(j * 384, 384), 384)
        value = jnp.dot(turned[...], normed[:, columns], preferred_element_type=f32)
        value = jnp.transpose(value).astype(bf16)
        for g in range(group):
            w_stage[j * group + g] = value[g * share : (g + 1) * share, :]
        return none

    lax.fori_loop(0, width // 384, weights, 0)
    top = 2 * LANES
    small[0:LANES, :] = acc_x[...].astype(bf16)
    small[LANES:top, :] = acc_dt[...].astype(bf16)
    rate_sum = jnp.sum(grate_ref[...], axis=1) * decay_rates(params)
    last = [rate_sum] + [jnp.sum(acc[k], axis=0, keepdims=True) for k in range(KC + 2)]
    last.append(jnp.zeros((16 - KC - 2, el), f32))
    small[top : top + 32, :] = jnp.concatenate(last, axis=0).astype(bf16)
    late = fill_chunks(held, fill_sem, small, early)

    def slots(m, i):
        n = late + m * halves + i
        return held.at[n], fill_sem.at[n], swap_send.at[n]

    swap_blocks(size, w_stage, slots)

    def spread_back(i, none):
        p = crossed(me, jnp.where(i < half, 2 * i + 1, 2 * (i - half)), size)
        weight = wv[...].reshape(width, 2 * el)
        value = lax.dot_general(gmix[p], weight, nt, preferred_element_type=f32).astype(bf16)

        @pl.when(i < half)
        def _():
            stage[i] = value
            scatter.staged(i, stage)

        @pl.when(i >= half)
        def _():
            scatter.keep[i - half] = value

        chain.advance(early + i, sums)
        return none

    lax.fori_loop(0, size, spread_back, 0)
    done = early + size
    jobs = [functools.partial(scatter.step, k) for k in range(1, scatter.steps)]
    jobs.append(functools.partial(scatter.finish, own))
    for k, job in enumerate(jobs):
        job()
        upto = min(chain.last_step, done + (chain.last_step - done) * (2 if k else 3) // 4)
        chain.run(done, upto, sums)
        done = upto
    chain.run(done, chain.last_step, sums)
    scatter.drain()
    chain.drain()
    drain_swap(size, w_stage, slots)

    def halo_sent(p, none):
        halo(p).wait_send()
        return none

    @pl.when(place > 0)
    def _():
        lax.fori_loop(0, size, halo_sent, 0)


def back(
    gdelta, gx, delta, normed, w_in, cext, ggp, gbc, gate_w, rank, dt_w, x_w, params, grate, gate_sum, size, seq
):
    away = pl.BlockSpec(memory_space=pl.ANY)
    here = pl.BlockSpec(memory_space=pltpu.VMEM)
    f32, bf16 = jnp.float32, jnp.bfloat16
    unused_size, tt, el = ggp.shape
    share = w_in.shape[1]
    width = normed.shape[1]
    piece = (share // 2, el)
    low = small_rows(piece[0])
    chunks = 4 * size - 2 * early_blocks(size) + low // piece[0]
    scratch = [
        (gdelta.shape, f32), (gx.shape, f32), (delta.shape, f32), (normed.shape, bf16), (w_in.shape, bf16),
        (cext.shape, bf16), ((size, tt, 2 * el), bf16), (gbc.shape, f32), ((tt, el), bf16),
        ((size, tt + 8, el), f32), ((el, size * tt), bf16), ((size, share, el), bf16), ((LANES, el), f32),
        ((LANES, el), f32), ((KC + 2, 8, el), f32), ((low, el), bf16), ((size, 16, el), bf16),
        ((size, 16, el), bf16), ((size // 2, tt, width), bf16), ((tt, el), f32),
        ((LANES, el), bf16),
    ]
    return pl.pallas_call(
        functools.partial(back_kernel, size, seq),
        in_specs=[away] * 9 + [here] * 6,
        out_specs=[here] * 3,
        out_shape=[
            jax.ShapeDtypeStruct((tt, width), bf16),
            jax.ShapeDtypeStruct((share, 2 * size * el), bf16),
            jax.ShapeDtypeStruct((low, el), bf16),
        ],
        scratch_shapes=[pltpu.VMEM(*v) for v in scratch]
        + sum_scratch(size, tt)
        + RowScatter.scratch(size, tt, width)
        + SeqSum.scratch(chunks, piece)
        + [
            pltpu.SemaphoreType.DMA((chunks,)),
            pltpu.SemaphoreType.DMA((8,)),
            pltpu.SemaphoreType.DMA((size,)),
            pltpu.SemaphoreType.DMA((size,)),
        ],
        compiler_params=pltpu.CompilerParams(
            vmem_limit_bytes=63 * MIB, collective_id=4, has_side_effects=True
        ),
        name="back",
    )(gdelta, gx, delta, normed, w_in, cext, ggp, gbc, gate_w, rank, dt_w, x_w, params, grate, gate_sum)


def local(
    tokens, resets, norm_gain, in_proj, x_proj, dt_proj, conv_weight, conv_bias, dt_bias, a_log, out_proj,
    cotangent,
):
    size = lax.axis_size("rows")
    seq = lax.axis_size("seq")
    rd, tt, unused_d = tokens.shape
    nr = rd * size
    el = E // size
    count = nr * tt
    assert rd == 1 and ITEM % tt == 0 and nr % 8 == 0

    elp = pad_lanes(el)
    share = D // size
    direct = elp == el
    f32, bf16 = jnp.float32, jnp.bfloat16

    def widen(value, axis):
        pad = [(0, 0)] * value.ndim
        pad[axis] = (0, elp - el)
        return jnp.pad(value, pad)

    if direct:
        w_local = in_proj
    else:
        w_local = jnp.moveaxis(in_proj.reshape(share, 2, size, el), 2, 0)
        w_local = widen(w_local, 3).reshape(size, share, 2 * elp)
    out_proj, x_proj = widen(out_proj, 0), widen(x_proj, 0)
    dt_proj = widen(dt_proj, 1)
    params = [conv_weight, conv_bias[None], dt_bias[None], jnp.zeros((8 - KC - 2, el), bf16), a_log]
    params = widen(jnp.concatenate(params, axis=0).astype(f32), 1)
    notes = jnp.zeros((16, -(-share // 256) * 256), bf16)
    notes = notes.at[0, :share].set(norm_gain).at[1].set(1.0 - resets[0, 0].astype(bf16))
    (
        normed, w_in, x_t, delta_t, gy_t, conv_ext, hist, branch, grad_out_proj, grad_in_gate, grad_gate_pre, proj_t,
        rank_all, all_notes, last, carry_back,
    ) = front(
        tokens[0], cotangent[0], notes, w_local, out_proj, x_proj, dt_proj, params, size, seq, direct
    )
    gain = all_notes[:, 0, :share].reshape(D).astype(f32)
    grad_delta, grad_input, gate_blocks, grad_bc, grate, branch_own, sum_out, gate_sum = scan_backward(
        delta_t, x_t, gy_t, hist, proj_t, params, carry_back, last, branch, grad_out_proj[:el], grad_in_gate, size, seq
    )
    grad_normed, sum_in, small = back(
        grad_delta, grad_input, delta_t, normed.reshape(count, D), w_in, conv_ext, grad_gate_pre, grad_bc, gate_blocks,
        rank_all, dt_proj, x_proj, params, grate, gate_sum, size, seq,
    )
    sum_in = sum_in.reshape(share, 2, size, elp)[..., :el].reshape(share, 2 * E).astype(f32)
    sum_out = sum_out.astype(f32)
    small = small[:, :el].astype(f32)
    block_out = (tokens.astype(jnp.float32) + branch_own[None].astype(jnp.float32)).astype(jnp.bfloat16)
    grad_normed = grad_normed[None].astype(jnp.float32)

    own = tokens.astype(jnp.float32)
    inv = lax.rsqrt(jnp.mean(own * own, axis=2, keepdims=True) + epsilon)
    gain_own = jnp.sum(in_proj.astype(jnp.float32) * sum_in, axis=1) / norm_gain.astype(jnp.float32)
    grad_hat = grad_normed * gain
    grad_norm_in = inv * (
        grad_hat - own * (inv * inv) * jnp.mean(grad_hat * own, axis=2, keepdims=True)
    )
    d_tokens = (cotangent.astype(jnp.float32) + grad_norm_in).astype(jnp.bfloat16)

    more = small[2 * LANES :]
    return (
        block_out,
        d_tokens,
        gain_own,
        sum_in,
        small[:LANES].T,
        small[LANES : LANES + R],
        more[NS : NS + KC],
        more[NS + KC],
        more[NS + KC + 1],
        more[:NS],
        sum_out,
    )


def solution(mesh):
    in_specs = (
        P("rows", "seq", None),
        P("rows", "seq"),
        P("rows"),
        P("rows", None),
        P("rows", None),
        P(None, "rows"),
        P(None, "rows"),
        P("rows"),
        P("rows"),
        P(None, "rows"),
        P("rows", None),
        P("rows", "seq", None),
    )
    out_specs = (
        P("rows", "seq", None),
        P("rows", "seq", None),
        P("rows"),
        P("rows", None),
        P("rows", None),
        P(None, "rows"),
        P(None, "rows"),
        P("rows"),
        P("rows"),
        P(None, "rows"),
        P("rows", None),
    )
    return jax.shard_map(local, mesh=mesh, in_specs=in_specs, out_specs=out_specs, check_vma=False)
```

```python
import functools
import math

import jax
import jax.numpy as jnp
from jax import lax
from jax.experimental import pallas as pl
from jax.experimental.pallas import tpu as pltpu
from jax.sharding import PartitionSpec as P

D = 1536
E = 3072
R = 96
NS = 16
KC = 4
ITEM = 256

epsilon = 1e-05
LOG2E = 1.4426950408889634
LN2 = 0.6931471805599453
MIB = 2**20


LANES = 128


def pad_lanes(lanes):
    return -(-lanes // LANES) * LANES


def selector(wide):
    row = lax.broadcasted_iota(jnp.int32, (LANES, 2 * NS * wide), 0)
    col = lax.broadcasted_iota(jnp.int32, (LANES, 2 * NS * wide), 1) // wide
    return (row == col + R).astype(jnp.bfloat16)


def decay_rates(params):
    return -jnp.exp(params[8 : 8 + NS, :])


def spread(proj, sel_ref):
    return jnp.dot(proj.astype(jnp.bfloat16), sel_ref[...], preferred_element_type=jnp.float32)


def copy_all(sources, targets, sems):
    copies = []
    for i, (source, target) in enumerate(zip(sources, targets)):
        copies.append(pltpu.make_async_copy(source, target, sems.at[i]))
        copies[-1].start()
    return copies


MESH = pl.DeviceIdType.MESH


def greet(devices):
    barrier = pltpu.get_barrier_semaphore()
    for device in devices:
        pl.semaphore_signal(barrier, inc=1, device_id=device, device_id_type=MESH)
    pl.semaphore_wait(barrier, len(devices))


def remote(source, target, send, recv, device):
    copy = pltpu.make_async_remote_copy(
        src_ref=source, dst_ref=target, send_sem=send, recv_sem=recv, device_id=device, device_id_type=MESH
    )
    copy.start()
    return copy


def row_peers(size):
    me = lax.axis_index("rows")
    half = size // 2
    mine = me // 2
    return me, me % 2, me + 1 - 2 * (me % 2), [lax.rem(mine + k, half) for k in range(half)]


def exchange_sums(size, near, total, mail, far, out, sems, use, between=None):
    me, parity, partner, others = row_peers(size)
    place = lax.axis_index("seq")
    half = size // 2
    second = []
    for k in list(range(1, half)) + [0]:
        j = others[k]
        wait_for(near.at[j], sems.at[1, j])
        total[j] = total[j] + near[j].astype(jnp.float32)
        if k:
            mail[j] = total[j].astype(jnp.bfloat16)
            target = (place, 2 * j + parity)
            second.append(remote(mail.at[j], far.at[k], sems.at[2, k], sems.at[3, k], target))
    mine = others[0]
    done = total[mine]
    for k in range(1, half):
        wait_for(far.at[k], sems.at[3, k])
        done = done + far[k].astype(jnp.float32)
    out[me] = done.astype(jnp.bfloat16)
    third = []
    for k in range(1, half):
        target = (place, 2 * others[k] + parity)
        third.append(remote(out.at[me], out.at[me], sems.at[4, k], sems.at[5, k], target))
    fourth = [remote(out.at[me], out.at[me], sems.at[6, 0], sems.at[7, 0], (place, partner))]
    use(me)
    for k in range(1, half):
        block = 2 * others[half - k] + parity
        wait_for(out.at[block], sems.at[5, k])
        fourth.append(
            remote(out.at[block], out.at[block], sems.at[6, k], sems.at[7, k], (place, partner))
        )
        use(block)
    for k in range(half):
        block = 2 * others[(half - k) % half] + 1 - parity
        wait_for(out.at[block], sems.at[7, k])
        use(block)
    if between:
        between()
    for copy in second + third + fourth:
        copy.wait_send()


def sum_scratch(size, tt):
    half = size // 2
    return [
        pltpu.VMEM((size, tt, LANES), jnp.bfloat16),
        pltpu.VMEM((half, tt, LANES), jnp.bfloat16),
        pltpu.VMEM((half, tt, LANES), jnp.float32),
        pltpu.VMEM((half, tt, LANES), jnp.bfloat16),
        pltpu.VMEM((half, tt, LANES), jnp.bfloat16),
        pltpu.VMEM((size, tt, LANES), jnp.bfloat16),
        pltpu.SemaphoreType.DMA((8, half)),
    ]


class Carry:
    def __init__(self, seq, ends, alive, out, mail, land, sems):
        self.seq, self.ends, self.alive, self.out = seq, ends, alive, out
        self.mail, self.land, self.sems = mail, land, sems
        self.me, self.place = lax.axis_index("rows"), lax.axis_index("seq")

    @staticmethod
    def scratch(shape):
        return [
            pltpu.VMEM((2,) + shape, jnp.bfloat16),
            pltpu.VMEM((2,) + shape, jnp.bfloat16),
            pltpu.SemaphoreType.DMA((2, 2, shape[-1] // LANES)),
        ]

    def copy(self, way, b):
        lanes = pl.ds(b * LANES, LANES)
        target = (jnp.clip(self.place + 1 - 2 * way, 0, self.seq - 1), self.me)
        return pltpu.make_async_remote_copy(
            src_ref=self.mail.at[way, :, :, lanes], dst_ref=self.land.at[way, :, :, lanes],
            send_sem=self.sems.at[way, 0, b], recv_sem=self.sems.at[way, 1, b], device_id=target,
            device_id_type=MESH,
        )

    def hop(self, way):
        first, last = ((0, self.seq - 1), (self.seq - 1, 0))[way]
        alive = self.alive[:, 0:1][None]

        for b in range(self.mail.shape[-1] // LANES):
            lanes = slice(b * LANES, (b + 1) * LANES)

            @pl.when(self.place == first)
            def _(lanes=lanes):
                self.out[way, :, :, lanes] = jnp.zeros(self.out.shape[1:3] + (LANES,), jnp.float32)

            @pl.when(self.place != first)
            def _(b=b, lanes=lanes):
                self.copy(way, b).wait_recv()
                entering = self.land[way, :, :, lanes].astype(jnp.float32)
                self.out[way, :, :, lanes] = entering * alive if way == 0 else entering

            @pl.when(self.place != last)
            def _(b=b, lanes=lanes):
                passed = self.ends[1, :, :, lanes] * self.out[way, :, :, lanes]
                if way == 0:
                    leaving = self.ends[0, :, :, lanes] + passed
                else:
                    leaving = (self.ends[2, :, :, lanes] + passed) * alive
                self.mail[way, :, :, lanes] = leaving.astype(jnp.bfloat16)
                self.copy(way, b).start()

    def turn(self, way, t):
        behind = (self.place, self.seq - 1 - self.place)[way]
        pl.when(behind == t)(functools.partial(self.hop, way))

    def drain(self):
        for way, last in ((0, self.seq - 1), (1, 0)):

            @pl.when(self.place != last)
            def _(way=way):
                for b in range(self.mail.shape[-1] // LANES):
                    self.copy(way, b).wait_send()


def flip(place, mask):
    for k in range(mask.bit_length()):
        bit = 1 << k
        if mask & bit:
            place = place + bit * (1 - 2 * (lax.div(place, bit) % 2))
    return place


def bit_orders(size):
    rest = [1 << k for k in range(1, size.bit_length() - 1)]
    cut = max(1, len(rest) // 2)
    return [1] + rest, [1] + rest[cut:] + rest[:cut]


def masks_of(bits):
    masks = [0]
    for bit in bits:
        masks = masks + [m | bit for m in masks]
    return masks


def by_tiles(rows, tile, body):
    def step(i, none):
        body(pl.ds(pl.multiple_of(i * tile, tile), tile))
        return none

    lax.fori_loop(0, rows // tile, step, 0)


def wait_for(ref, sem):
    pltpu.make_async_copy(ref, ref, sem).wait()


def greet_seq(seq):
    me, place = lax.axis_index("rows"), lax.axis_index("seq")
    barrier = pltpu.get_barrier_semaphore()
    for step, there in ((-1, place > 0), (1, place < seq - 1)):

        @pl.when(there)
        def _(step=step):
            pl.semaphore_signal(barrier, inc=1, device_id=(place + step, me), device_id_type=MESH)

    pl.semaphore_wait(barrier, (place > 0).astype(jnp.int32) + (place < seq - 1).astype(jnp.int32))


def greet_rows_and_seq(size, seq):
    me, place = lax.axis_index("rows"), lax.axis_index("seq")
    barrier = pltpu.get_barrier_semaphore()
    for mask in range(1, size):
        pl.semaphore_signal(barrier, inc=1, device_id=(place, flip(me, mask)), device_id_type=MESH)
    for step, there in ((-1, place > 0), (1, place < seq - 1)):

        @pl.when(there)
        def _(step=step):
            pl.semaphore_signal(barrier, inc=1, device_id=(place + step, me), device_id_type=MESH)

    near = (place > 0).astype(jnp.int32) + (place < seq - 1).astype(jnp.int32)
    pl.semaphore_wait(barrier, near + size - 1)


def crossed(place, mask, size):
    out = 0
    for k in range(size.bit_length() - 1):
        bit = 1 << k
        out = out + bit * lax.rem(lax.div(place, bit) + lax.div(mask, bit), 2)
    return out


class RowGather:
    def __init__(self, size, source, out, own_sem, send, recv):
        self.size, self.source, self.out, self.own_sem, self.send, self.recv = size, source, out, own_sem, send, recv
        self.me, self.place = lax.axis_index("rows"), lax.axis_index("seq")
        self.rows = source.shape[0] // 2
        self.orders = [order[1:] for order in bit_orders(size)]
        self.steps = len(self.orders[0])

    @staticmethod
    def sems(size):
        return [pltpu.SemaphoreType.DMA((1,))] + [pltpu.SemaphoreType.DMA((2, size))] * 2

    def half(self, h, m, ref=None):
        ref = self.out.at[flip(self.me, m)] if ref is None else ref
        return ref.at[pl.ds(h * self.rows, self.rows), :]

    def push(self, h, m, bit):
        source = self.half(h, m, self.source if m == 0 else None)
        key = (h, m | bit)
        remote(
            source, self.half(h, m), self.send.at[key], self.recv.at[key], (self.place, flip(self.me, bit))
        )

    def arrived(self, h, m):
        wait_for(self.half(h, m), self.recv.at[h, m])

    def start(self):
        pltpu.make_async_copy(self.source, self.out.at[self.me], self.own_sem.at[0]).start()
        for h in range(2):
            self.push(h, 0, self.orders[h][0])
        for h in range(2):
            self.push(h, 0, 1)

    def own(self):
        wait_for(self.out.at[self.me], self.own_sem.at[0])

    def step(self, k, use=None):
        for h in range(2):
            order = self.orders[h]
            old = masks_of(order[:k])
            if k + 1 < self.steps:
                for m in old:
                    self.push(h, m, order[k + 1])
            for m in old:
                fresh = m | order[k]
                self.arrived(h, fresh)
                if k + 1 < self.steps:
                    self.push(h, fresh, order[k + 1])
                self.push(h, fresh, 1)
                if use:
                    use(h, fresh)

    def paired(self, use=None):
        for m in masks_of(self.orders[0]):
            for h in range(2):
                self.arrived(h, m | 1)
                if use:
                    use(h, m | 1)

    def drain(self):
        for h in range(2):
            for m in range(1, self.size):
                wait_for(self.half(h, 0), self.send.at[h, m])


def front_kernel(size, seq, direct, ct, uu, *refs):
    (tokens, cot, notes, w_local, out_w, x_w, dt_in, params) = refs[:8]
    (
        normed_out, w_out, x_out, delta_out, gy_out, cext_out, hist_out, branch_out, dout_out, dwg_out, ggp_out,
        proj_ref, rank_ref, last_ref, leaving_ref, gain_ref,
    ) = refs[8:24]
    (
        tok, cot_s, wc, wg, cext, xb, x_s, delta_s, gy_s, gate_s, gg_s, all_notes, alive_ref, sel, bc, ends, entered,
        delta_sum, hist, y_s, gated, ggp, branch_s, turned, d_stage, w_stage, gate_b, dt_w, a_ref,
    ) = refs[24:53]
    token_sems, cot_sems = refs[53:56], refs[56:59]
    part, near, total, mail, far, out, sems = refs[59:66]
    carry = Carry(seq, ends, alive_ref, entered, *refs[66:69])
    taps_ref, bias_ref, dt_bias_ref = params.at[0:KC], params.at[KC : KC + 1], params.at[KC + 1 : KC + 2]
    (
        note_send, note_recv, wc_send, wc_recv, wg_send, wg_recv, halo_send, halo_recv, out_sems, hist_sems, branch_sems,
    ) = refs[69:]
    normed = tok
    me, parity, partner, others = row_peers(size)
    place = lax.axis_index("seq")
    tt, width = tokens.shape
    share, el = wc.shape[1:]
    nr = size
    blocks = el // LANES
    half = size // 2
    f32, bf16 = jnp.float32, jnp.bfloat16
    tile = 64
    stores = []

    def put(source, target):
        copy = pltpu.make_async_copy(source, target, out_sems.at[len(stores)])
        copy.start()
        stores.append(copy)

    def piece(q, gate):
        if direct:
            at = pl.multiple_of(q * el, LANES) + gate * size * el
            return w_local.at[:, pl.ds(at, el)]
        return w_local.at[q, :, pl.ds(gate * el, el)]

    cut = share // 2
    beside = (flip(place, 1), me)

    def swap(gate, target, send, recv):
        there = pl.ds(pl.multiple_of(lax.rem(place, 2) * cut, cut), cut)
        for m in range(1, size):
            q = flip(me, m)
            remote(piece(q, gate).at[there, :], target.at[me, there, :], send.at[0, m], recv.at[0, m], (place, q))
        pltpu.make_async_copy(piece(me, gate), target.at[me], recv.at[0, 0]).start()

    def swap_on(target, send, recv):
        there = pl.ds(pl.multiple_of(lax.rem(place, 2) * cut, cut), cut)
        for m in range(1, size):
            block = target.at[flip(me, m), there, :]
            wait_for(block, recv.at[0, m])
            remote(block, block, send.at[1, m], recv.at[1, m], beside)

    def swapped(target, send, recv):
        wait_for(target.at[me], recv.at[0, 0])
        for m in range(1, size):
            wait_for(target.at[flip(me, m), pl.ds(0, cut), :], recv.at[1, m])

    def swap_drain(target, send):
        for k in range(2):
            for m in range(1, size):
                wait_for(target.at[0, pl.ds(0, cut), :], send.at[k, m])

    greet_rows_and_seq(size, seq)

    sent = []
    for m in range(1, size):
        sent.append(remote(notes, all_notes.at[me], note_send.at[m], note_recv.at[m], (place, flip(me, m))))
    pltpu.make_async_copy(notes, all_notes.at[me], note_recv.at[0]).start()
    token_rows = RowGather(size, tokens, tok, *token_sems)
    cot_rows = RowGather(size, cot, cot_s, *cot_sems)
    swap(0, wc, wc_send, wc_recv)
    token_rows.start()

    for m in range(size):
        wait_for(all_notes.at[flip(me, m)], note_recv.at[m])
    for p in range(size):
        note = all_notes[p].astype(f32)
        gain_ref[:, p * share : (p + 1) * share] = note[0:1, :share]
        alive_ref[p : p + 1, :] = note[1:2, :LANES]

    def norm(p, base, rows):
        def body(span):
            there = pl.ds(base + span.start, span.size)
            x = tok[p, there, :].astype(f32)
            inv = lax.rsqrt(jnp.mean(x * x, axis=1, keepdims=True) + epsilon)
            normed[p, there, :] = (x * inv * gain_ref[...]).astype(bf16)

        by_tiles(rows, 64, body)

    def norm_half(h, m):
        norm(flip(me, m), h * (tt // 2), tt // 2)

    token_rows.own()
    norm(me, 0, tt)
    swap_on(wc, wc_send, wc_recv)
    sel[...] = selector(LANES)
    a_ref[...] = decay_rates(params) * LOG2E
    dt_w[0:R, :] = dt_in[...]
    dt_w[R:, :] = jnp.zeros((LANES - R, el), bf16)
    for k in range(token_rows.steps):
        token_rows.step(k)
    token_rows.paired(norm_half)
    token_rows.drain()
    for m in masks_of(token_rows.orders[0])[1:]:
        norm(flip(me, m), 0, tt)
    swapped(wc, wc_send, wc_recv)

    @pl.when(place == 0)
    def _():
        cext[:, 0:16, :] = jnp.zeros((size, 16, el), bf16)

    def halo(p, i):
        there = cext.at[p, pl.ds(0, 16), :]
        return pltpu.make_async_remote_copy(
            src_ref=cext.at[p, pl.ds(tt, 16), :], dst_ref=there, send_sem=halo_send.at[i],
            recv_sem=halo_recv.at[i], device_id=(jnp.minimum(place + 1, seq - 1), me), device_id_type=MESH,
        )

    def block_at(i):
        return 2 * lax.rem(me // 2 + lax.rem(i, half), half) + lax.rem(parity + 1 + lax.div(i, half), 2)

    def mix(i, none):
        p = block_at(i)
        weight = wc[...].reshape(size * share, el)
        cext[p, 16:, :] = jnp.dot(normed[p], weight, preferred_element_type=f32).astype(bf16)

        @pl.when(place < seq - 1)
        def _():
            halo(p, i).start()

        return none

    lax.fori_loop(0, size, mix, 0)
    for p in range(size):
        put(normed.at[p], normed_out.at[p])

    def conv(i, none):
        p = block_at(i)

        @pl.when(place > 0)
        def _():
            halo(p, i).wait_recv()

        def body(span):
            ext = cext[p, pl.ds(span.start, tile + 16), :].astype(f32)
            value = bias_ref[...]
            for k in range(KC):
                value = value + taps_ref[k : k + 1, :] * ext[16 - KC + 1 + k : 16 - KC + 1 + k + tile]
            x = (value / (1.0 + jnp.exp(-value))).astype(bf16)
            xb[span, :] = x
            for b in range(blocks):
                there = pl.ds(p + span.start * size, tile, stride=size)
                x_s[b, there, :] = x[:, b * LANES : (b + 1) * LANES].astype(f32)

        by_tiles(tt, tile, body)
        value = jnp.dot(xb[...], x_w[...], preferred_element_type=f32)

        @pl.when(i < half)
        def _():
            part[p] = value.astype(bf16)
            pltpu.make_async_remote_copy(
                src_ref=part.at[p], dst_ref=near.at[lax.div(p, 2)], send_sem=sems.at[0, lax.div(p, 2)],
                recv_sem=sems.at[1, lax.div(p, 2)], device_id=(place, partner), device_id_type=MESH,
            ).start()

        @pl.when(i >= half)
        def _():
            total[lax.div(p, 2)] = value

        return none

    lax.fori_loop(0, size, conv, 0)
    put(cext, cext_out)
    put(x_s, x_out)

    def use(p):
        block = out[p]
        rank_ref[p] = block
        proj_ref[pl.ds(p, tt, stride=size), :] = block.astype(f32)

        gate_s[...] = jnp.dot(block, dt_w[...], preferred_element_type=f32)

        def body(span):
            step = gate_s[span, :] + dt_bias_ref[...]
            delta = jnp.maximum(step, 0.0) + jnp.log1p(jnp.exp(-jnp.abs(step)))
            for b in range(blocks):
                there = pl.ds(p + span.start * size, 64, stride=size)
                delta_s[b, there, :] = delta[:, b * LANES : (b + 1) * LANES]

        by_tiles(tt, 64, body)

    def second_wave():
        cot_rows.start()
        swap(1, wg, wg_send, wg_recv)

    exchange_sums(size, near, total, mail, far, out, sems, use, second_wave)
    for j in range(half):
        pltpu.make_async_remote_copy(
            src_ref=part.at[j], dst_ref=near.at[j], send_sem=sems.at[0, j], recv_sem=sems.at[1, j],
            device_id=(place, partner), device_id_type=MESH,
        ).wait_send()
    put(delta_s, delta_out)
    put(wc, w_out.at[:, :, pl.ds(0, el)])

    count = tt // ct
    ends[0] = jnp.zeros((NS, nr, el), f32)
    ends[2] = jnp.zeros((NS, nr, el), f32)
    ends[3] = jnp.ones((NS, nr, el), f32)
    delta_sum[...] = jnp.zeros_like(delta_sum)

    def spread_chunk(c, first, last):
        rows = pl.multiple_of(c * (ct * nr), ct * nr)
        lanes = slice(first * LANES, last * LANES)
        bc[:, lanes] = spread(proj_ref[pl.ds(rows, ct * nr), :], sel.at[:, lanes])

    def token(c, at):
        return pl.ds(pl.multiple_of((c * ct + at) * nr, nr), nr), pl.ds(pl.multiple_of(at * nr, nr), nr)

    def rates(ns, lanes):
        return [jnp.broadcast_to(a_ref[n : n + 1, lanes], (nr, LANES)) for n in ns]

    def ends_forward(c, none):
        pl.when(c == count // 2)(functools.partial(cot_rows.step, 0))
        spread_chunk(c, 0, NS)
        for b in range(blocks):
            lanes = slice(b * LANES, (b + 1) * LANES)
            rate = rates(range(NS), lanes)

            def steps(s, carried):
                state, so_far = list(carried[:-1]), carried[-1]
                for u in range(uu):
                    here, close = token(c, s * uu + u)
                    delta = delta_s[b, here, :]
                    du = delta * x_s[b, here, :]
                    so_far = so_far + delta
                    for n in range(NS):
                        b_at = n * LANES
                        state[n] = jnp.exp2(delta * rate[n]) * state[n] + du * bc[close, b_at : b_at + LANES]
                return tuple(state) + (so_far,)

            start = tuple(ends[0, n, :, lanes] for n in range(NS)) + (delta_sum[b],)
            last = lax.fori_loop(0, ct // uu, steps, start)
            for n in range(NS):
                ends[0, n, :, lanes] = last[n]
            delta_sum[b] = last[NS]
        return none

    lax.fori_loop(0, count, ends_forward, 0)
    for b in range(blocks):
        lanes = slice(b * LANES, (b + 1) * LANES)
        for n in range(NS):
            ends[1, n, :, lanes] = jnp.exp2(delta_sum[b] * a_ref[n : n + 1, lanes])
    carry.turn(0, 0)

    for t in range(1, seq):
        carry.turn(0, t)
    swap_on(wg, wg_send, wg_recv)
    last_ref[...] = entered[0]

    def store_hist(c):
        slot = lax.rem(c, 2)
        return pltpu.make_async_copy(hist.at[slot], hist_out.at[pl.ds(c * ct, ct)], hist_sems.at[slot])

    def forward(c, none):
        slot = lax.rem(c, 2)

        @pl.when(c >= 2)
        def _():
            store_hist(c - 2).wait()

        for k in range(1, cot_rows.steps):
            pl.when(c == min(count // 2 + k - 1, count - 1))(functools.partial(cot_rows.step, k))
        spread_chunk(c, 0, 2 * NS)
        for b in range(blocks):
            lanes = slice(b * LANES, (b + 1) * LANES)
            rate = rates(range(NS), lanes)

            def steps(s, carried):
                state = list(carried)
                for u in range(uu):
                    at = s * uu + u
                    here, close = token(c, at)
                    delta = delta_s[b, here, :]
                    du = delta * x_s[b, here, :]
                    y = None
                    for n in range(NS):
                        if n % 2 == 0:
                            both = jnp.concatenate([state[n], state[n + 1]], axis=0)
                            hist[slot, at, b, pl.ds(n * nr, 2 * nr), :] = both.astype(bf16)
                        b_at, c_at = n * LANES, (NS + n) * LANES
                        decay = jnp.exp2(delta * rate[n])
                        state[n] = decay * state[n] + du * bc[close, b_at : b_at + LANES]
                        term = state[n] * bc[close, c_at : c_at + LANES]
                        y = term if y is None else y + term
                    y_s[b, here, :] = y
                return tuple(state)

            last = lax.fori_loop(0, ct // uu, steps, tuple(last_ref[n, :, lanes] for n in range(NS)))
            for n in range(NS):
                last_ref[n, :, lanes] = last[n]
        store_hist(c).start()
        return none

    lax.fori_loop(0, count, forward, 0)
    cot_rows.own()
    cot_rows.paired()
    swapped(wg, wg_send, wg_recv)
    put(wg, w_out.at[:, :, pl.ds(el, el)])

    def gates(p):
        weight = wg[...].reshape(size * share, el)
        gate_s[...] = jnp.dot(normed[p], weight, preferred_element_type=f32)
        gg_s[...] = lax.dot_general(
            cot_s[p], out_w[...], (((1,), (1,)), ((), ())), preferred_element_type=f32
        )

    def grad_y(p, none):
        gates(p)

        def body(span):
            gate, gg = gate_s[span, :], gg_s[span, :]
            gate_b[p, span, :] = gate.astype(bf16)
            ggp[p, span, :] = gg.astype(bf16)
            gy = gg * gate / (1.0 + jnp.exp(-gate))
            for b in range(blocks):
                there = pl.ds(p + span.start * size, tile, stride=size)
                gy_s[b, there, :] = gy[:, b * LANES : (b + 1) * LANES]

        by_tiles(tt, tile, body)
        return none

    lax.fori_loop(0, size, grad_y, 0)
    put(gy_s, gy_out)

    def ends_back(c, none):
        spread_chunk(c, NS, 2 * NS)
        for b in range(blocks):
            lanes = slice(b * LANES, (b + 1) * LANES)
            for n0 in (0, NS // 2):
                ns = range(n0, n0 + NS // 2)
                rate = rates(ns, lanes)

                def steps(s, carried):
                    through, back = (list(v) for v in carried)
                    for u in range(uu):
                        here, close = token(c, s * uu + u)
                        delta = delta_s[b, here, :]
                        gy = gy_s[b, here, :]
                        for i, n in enumerate(ns):
                            c_at = (NS + n) * LANES
                            through[i] = through[i] * jnp.exp2(delta * rate[i])
                            back[i] = back[i] + through[i] * (gy * bc[close, c_at : c_at + LANES])
                    return tuple(through), tuple(back)

                start = tuple(tuple(ends[k, n, :, lanes] for n in ns) for k in (3, 2))
                last = lax.fori_loop(0, ct // uu, steps, start)
                for i, n in enumerate(ns):
                    ends[3, n, :, lanes] = last[0][i]
                    ends[2, n, :, lanes] = last[1][i]
        return none

    lax.fori_loop(0, count, ends_back, 0)
    carry.turn(1, 0)

    def store_branch(i):
        slot = lax.rem(i, 2)
        return pltpu.make_async_copy(branch_s.at[slot], branch_out.at[i], branch_sems.at[slot])

    def turn(value, p):
        columns = pl.ds(pl.multiple_of(p * tt, tt), tt)
        turned[:, columns] = jnp.transpose(value.astype(f32)).astype(bf16)

    def products(p, none):
        def body(span):
            there = pl.ds(p + span.start * size, tile, stride=size)
            y = jnp.concatenate([y_s[b, there, :] for b in range(blocks)], axis=1)
            gate = gate_b[p, span, :].astype(f32)
            sig = 1.0 / (1.0 + jnp.exp(-gate))
            gated[span, :] = (y * gate * sig).astype(bf16)
            ggp[p, span, :] = (ggp[p, span, :].astype(f32) * y * sig * (1.0 + gate * (1.0 - sig))).astype(bf16)

        by_tiles(tt, tile, body)

        @pl.when(p >= 2)
        def _():
            store_branch(p - 2).wait()

        branch = jnp.dot(gated[...], out_w[...], preferred_element_type=f32)
        branch_s[lax.rem(p, 2)] = branch.astype(bf16)
        store_branch(p).start()
        turn(gated[...], p)

        @pl.when(lax.rem(p, 2) == 1)
        def _():
            carry.turn(1, lax.div(p, 2) + 1)

        return none

    lax.fori_loop(0, size, products, 0)
    for t in range(half + 1, seq):
        carry.turn(1, t)
    put(ggp, ggp_out)
    wide = 384
    group = wide // share

    def out_weights(j, none):
        columns = pl.ds(pl.multiple_of(j * wide, wide), wide)
        right = cot_s[:, :, columns].reshape(size * tt, wide)
        d_stage[:, columns] = jnp.dot(turned[...], right, preferred_element_type=f32).astype(bf16)
        return none

    lax.fori_loop(0, width // wide, out_weights, 0)
    put(d_stage, dout_out)

    def turn_gate(p, none):
        turn(ggp[p], p)
        return none

    lax.fori_loop(0, size, turn_gate, 0)

    def gate_weights(j, none):
        columns = pl.ds(pl.multiple_of(j * wide, wide), wide)
        right = normed[:, :, columns].reshape(size * tt, wide)
        value = jnp.transpose(jnp.dot(turned[...], right, preferred_element_type=f32)).astype(bf16)
        for g in range(group):
            w_stage[j * group + g] = value[g * share : (g + 1) * share, :]
        return none

    lax.fori_loop(0, width // wide, gate_weights, 0)
    put(w_stage, dwg_out)
    for c in range(max(0, count - 2), count):
        store_hist(c).wait()
    for p in range(size - 2, size):
        store_branch(p).wait()
    leaving_ref[...] = entered[1]
    carry.drain()

    for i in range(size):

        @pl.when(place < seq - 1)
        def _(i=i):
            halo(i, i).wait_send()

    cot_rows.drain()
    swap_drain(wc, wc_send)
    swap_drain(wg, wg_send)
    for copy in sent:
        copy.wait_send()
    for copy in stores:
        copy.wait()


def front(tokens, cot, notes, w_local, out_w, x_w, dt_w, params, size, seq, direct):
    tt, width = tokens.shape
    el = out_w.shape[0]
    share = width // size
    blocks = el // LANES
    ct = math.gcd(tt, 32)
    away = pl.BlockSpec(memory_space=pl.ANY)
    here = pl.BlockSpec(memory_space=pltpu.VMEM)
    f32, bf16 = jnp.float32, jnp.bfloat16
    rows, scan, states = (size, tt, width), (blocks, tt * size, LANES), (NS, size, el)
    channels, ext = (size, tt, el), (size, tt + 16, el)
    weights = (size, share, el)
    shapes = [
        (rows, bf16), ((size, share, 2 * el), bf16), (scan, f32), (scan, f32), (scan, f32), (ext, bf16),
        ((tt, blocks, NS * size, LANES), bf16), (rows, bf16), ((el, width), bf16), (weights, bf16), (channels, bf16),
        ((tt * size, LANES), f32), ((size, tt, LANES), bf16), (states, f32), (states, f32),
        ((1, width), f32),
    ]
    scratch = [
        (rows, bf16), (rows, bf16), (weights, bf16), (weights, bf16), (ext, bf16), ((tt, el), bf16), (scan, f32),
        (scan, f32), (scan, f32), ((tt, el), f32), ((tt, el), f32), ((size,) + notes.shape, bf16), ((size, LANES), f32),
        ((LANES, 2 * NS * LANES), bf16), ((ct * size, 2 * NS * LANES), f32), ((4,) + states, f32), ((2,) + states, f32),
        ((blocks, size, LANES), f32), ((2, ct, blocks, NS * size, LANES), bf16), (scan, f32), ((tt, el), bf16), (channels, bf16),
        ((2, tt, width), bf16), ((el, size * tt), bf16), ((el, width), bf16), (weights, bf16),
        (channels, bf16), ((LANES, el), bf16), ((NS, el), f32),
    ]
    one = pltpu.SemaphoreType.DMA((size,))
    return pl.pallas_call(
        functools.partial(front_kernel, size, seq, direct, ct, max(1, ct * 8 // size)),
        in_specs=[away] * 4 + [here] * 4,
        out_specs=[away] * 11 + [here] * 5,
        out_shape=[jax.ShapeDtypeStruct(*v) for v in shapes],
        scratch_shapes=[pltpu.VMEM(*v) for v in scratch]
        + RowGather.sems(size) * 2
        + sum_scratch(size, tt)
        + Carry.scratch(states)
        + [one] * 2
        + [pltpu.SemaphoreType.DMA((2, size))] * 4
        + [one] * 2
        + [
            pltpu.SemaphoreType.DMA((size + 9,)),
            pltpu.SemaphoreType.DMA((2,)),
            pltpu.SemaphoreType.DMA((2,)),
        ],
        compiler_params=pltpu.CompilerParams(
            vmem_limit_bytes=63 * MIB, collective_id=0, has_side_effects=True
        ),
        name="front",
    )(tokens, cot, notes, w_local, out_w, x_w, dt_w, params)


class RowScatter:
    def __init__(self, size, part, keep, land, mail, keep_sem, send, recv):
        self.size, self.part, self.keep, self.land, self.mail = size, part, keep, land, mail
        self.keep_sem, self.send, self.recv = keep_sem, send, recv
        self.me, self.place = lax.axis_index("rows"), lax.axis_index("seq")
        self.tt, self.width = keep.shape[1], keep.shape[2] // 2
        self.orders = bit_orders(size)
        self.steps = len(self.orders[0])

    @staticmethod
    def scratch(size, tt, width):
        return [
            pltpu.VMEM((size // 2, tt, width), jnp.bfloat16),
            pltpu.VMEM((size - 1, tt, width), jnp.bfloat16),
            pltpu.VMEM((size // 2 - 1, tt, width), jnp.bfloat16),
            pltpu.SemaphoreType.DMA((size // 2,)),
            pltpu.SemaphoreType.DMA((2, size - 1)),
            pltpu.SemaphoreType.DMA((2, size - 1)),
        ]

    def free(self, h, k):
        return masks_of(self.orders[h][k + 1 :])

    def at(self, h, k, m):
        if k == 0:
            return m >> 1
        return sum(len(self.free(h, j)) for j in range(k)) + self.free(h, k).index(m)

    def cols(self, h):
        return pl.ds(h * self.width, self.width)

    def receive(self, h, k, m):
        slot = self.at(h, k, m)
        wait_for(self.land.at[slot, :, self.cols(h)], self.recv.at[h, slot])

    def partial_sum(self, h, k, m, rows):
        value = self.keep[m >> 1, rows, self.cols(h)].astype(jnp.float32)
        for j in range(k):
            value = value + self.land[self.at(h, j, m), rows, self.cols(h)].astype(jnp.float32)
        return value

    def staged(self, i, stage):
        for h in range(2):
            remote(
                stage.at[i, :, self.cols(h)], self.land.at[i, :, self.cols(h)], self.send.at[h, i],
                self.recv.at[h, i], (self.place, flip(self.me, 1)),
            )

    def start(self):
        for h in range(2):
            self.scatter(h, 0)
        for m in self.free(0, 0):
            pltpu.make_async_copy(
                self.part.at[flip(self.me, m)], self.keep.at[m >> 1], self.keep_sem.at[m >> 1]
            ).start()

    def step(self, k):
        if k == 1 and self.part is not None:
            for j in range(self.size // 2):
                wait_for(self.keep.at[j], self.keep_sem.at[j])
        for h in range(2):
            self.scatter(h, k)

    def scatter(self, h, k):
        bit = self.orders[h][k]
        for m in self.free(h, k):
            slot = self.at(h, k, m)
            if k == 0:
                source = self.part.at[flip(self.me, m | bit), :, self.cols(h)]
            else:
                for j in range(k):
                    self.receive(h, j, m | bit)
                box = slot - self.size // 2

                def fill(rows, m=m, box=box):
                    value = self.partial_sum(h, k, m | bit, rows)
                    self.mail[box, rows, self.cols(h)] = value.astype(jnp.bfloat16)

                by_tiles(self.tt, 32, fill)
                source = self.mail.at[box, :, self.cols(h)]
            remote(
                source, self.land.at[slot, :, self.cols(h)], self.send.at[h, slot], self.recv.at[h, slot],
                (self.place, flip(self.me, bit)),
            )

    def later(self, first):
        for k in range(first, self.steps):
            self.step(k)

    def finish(self, own):
        for h in range(2):
            for j in range(self.steps):
                self.receive(h, j, 0)

            def fill(rows, h=h):
                own[rows, self.cols(h)] = self.partial_sum(h, self.steps, 0, rows).astype(jnp.bfloat16)

            by_tiles(self.tt, 32, fill)

    def drain(self):
        for h in range(2):
            for slot in range(self.size - 1):
                wait_for(self.land.at[slot, :, self.cols(h)], self.send.at[h, slot])


class SeqSum:
    def __init__(self, seq, lag, held, land, fill_sem, send, recv):
        self.seq, self.lag, self.held, self.land = seq, lag, held, land
        self.fill_sem, self.send, self.recv = fill_sem, send, recv
        self.me, self.place = lax.axis_index("rows"), lax.axis_index("seq")
        self.behind = (self.place, seq - 1 - self.place)
        self.chunks = held.shape[0]
        self.last_step = self.chunks + lag * (seq - 1)

    @staticmethod
    def scratch(chunks, block):
        return [
            pltpu.VMEM((chunks,) + block, jnp.bfloat16),
            pltpu.VMEM((2, chunks) + block, jnp.bfloat16),
            pltpu.SemaphoreType.DMA((chunks,)),
            pltpu.SemaphoreType.DMA((2, chunks)),
            pltpu.SemaphoreType.DMA((2, chunks)),
        ]

    def copy(self, n, way, source):
        target = (jnp.clip(self.place + 1 - 2 * way, 0, self.seq - 1), self.me)
        return pltpu.make_async_remote_copy(
            src_ref=source, dst_ref=self.land.at[way, n], send_sem=self.send.at[way, n],
            recv_sem=self.recv.at[way, n], device_id=target, device_id_type=MESH,
        )

    def hop(self, step, way):
        n = step - self.lag * self.behind[way]

        @pl.when((n >= 0) & (n < self.chunks))
        def _():
            @pl.when(self.behind[way] == 0)
            def _():
                self.copy(n, way, self.held.at[n]).start()

            @pl.when(self.behind[way] > 0)
            def _():
                self.copy(n, way, self.held.at[n]).wait_recv()

                @pl.when(self.behind[way] < self.seq - 1)
                def _():
                    value = self.held[n].astype(jnp.float32) + self.land[way, n].astype(jnp.float32)
                    self.land[way, n] = value.astype(jnp.bfloat16)
                    self.copy(n, way, self.land.at[way, n]).start()

    def advance(self, step, total):
        first = step - self.lag * jnp.minimum(self.behind[0], self.behind[1])

        @pl.when((first >= 0) & (first < self.chunks))
        def _():
            wait_for(self.held.at[first], self.fill_sem.at[first])

        self.hop(step, 0)
        self.hop(step, 1)
        n = step - self.lag * jnp.maximum(self.behind[0], self.behind[1])

        @pl.when((n >= 0) & (n < self.chunks))
        def _():
            for ways, there in (
                ((1,), self.behind[0] == 0),
                ((0,), self.behind[1] == 0),
                ((0, 1), (self.behind[0] > 0) & (self.behind[1] > 0)),
            ):

                @pl.when(there)
                def _(ways=ways):
                    value = self.held[n].astype(jnp.float32)
                    if len(ways) == 2:
                        value = -value
                    for way in ways:
                        value = value + self.land[way, n].astype(jnp.float32)
                    total(n, value.astype(jnp.bfloat16))

    def run(self, first, last, total):
        def body(step, none):
            self.advance(step, total)
            return none

        lax.fori_loop(first, last, body, 0)

    def drain(self):
        for way in range(2):

            @pl.when(self.behind[way] < self.seq - 1)
            def _(way=way):
                def sent(n, none):
                    self.copy(n, way, self.held.at[n]).wait_send()
                    return none

                lax.fori_loop(0, self.chunks, sent, 0)


def fill_chunks(held, fill_sem, source, first=0):
    rows, cols = held.shape[1:]
    n = first
    if len(source.shape) == 3:
        for j in range(source.shape[0]):
            for i in range(source.shape[1] // rows):
                piece = source.at[j, pl.ds(i * rows, rows), :]
                pltpu.make_async_copy(piece, held.at[n], fill_sem.at[n]).start()
                n += 1
        return n
    for i in range(source.shape[0] // rows):
        for j in range(source.shape[1] // cols):
            piece = source.at[pl.ds(i * rows, rows), pl.ds(j * cols, cols)]
            pltpu.make_async_copy(piece, held.at[n], fill_sem.at[n]).start()
            n += 1
    return n


def early_blocks(size):
    return size // 4


def swap_blocks(size, weight, slots):
    me, place = lax.axis_index("rows"), lax.axis_index("seq")
    for m in range(size):
        q = flip(me, m)
        parts = weight.shape[1] // slots(m, 0)[0].shape[0]
        for i in range(parts):
            target, recv, send = slots(m, i)
            rows = target.shape[0]
            piece = weight.at[q, pl.ds(i * rows, rows), :]
            if m == 0:
                pltpu.make_async_copy(piece, target, recv).start()
            else:
                remote(piece, target, send, recv, (place, q))


def drain_swap(size, weight, slots):
    for m in range(1, size):
        for i in range(weight.shape[1] // slots(m, 0)[0].shape[0]):
            target, unused_recv, send = slots(m, i)
            wait_for(target, send)


def backward_kernel(size, seq, nr, tt, ct, uu, *refs):
    delta_in, x_in, gy_in, hist_in, proj_ref, params, carry_ref, last_ref, branch, out_w, gate_w = refs[:11]
    gdelta_out, gx_out, gate_out, gbc_ref, grate_ref, branch_own, out_sum, gate_sum = refs[11:19]
    sel, bc, hist, prod, state_ref, after_ref, fold, delta_ref, x_ref, gy_ref, gdelta_ref, gx_ref, gate_s, a_ref = refs[19:33]
    sems, out_sems, hist_sems = refs[33:36]
    scatter = RowScatter(size, branch, *refs[36:42])
    chain = SeqSum(seq, 3, *refs[42:47])
    gate_send, gate_recv, gate_sem = refs[47:]
    el = a_ref.shape[1]
    blocks = el // LANES
    count = tt // ct

    def fetch(c):
        slot = lax.rem(c, 2)
        return pltpu.make_async_copy(hist_in.at[pl.ds(c * ct, ct)], hist.at[slot], hist_sems.at[slot])

    copies = copy_all((delta_in, x_in, gy_in), (delta_ref, x_ref, gy_ref), sems)
    fetch(count - 1).start()
    greet_rows_and_seq(size, seq)
    scatter.start()
    fill_chunks(chain.held, chain.fill_sem, out_w)
    early = early_blocks(size)
    halves = gate_w.shape[1] // chain.held.shape[1]
    first = chain.chunks - early * halves

    def slots(m, i):
        if m < early:
            n = first + m * halves + i
            return chain.held.at[n], chain.fill_sem.at[n], gate_send.at[m, i]
        return gate_s.at[m - early], gate_recv.at[m], gate_send.at[m, 0]

    swap_blocks(size, gate_w, slots)
    a_ref[...] = decay_rates(params) * LOG2E
    piece = chain.held.shape[1:]

    def total(n, value):
        @pl.when(n < first)
        def _():
            across = out_sum.shape[1] // piece[1]
            down = pl.multiple_of(lax.div(n, across) * piece[0], piece[0])
            along = pl.multiple_of(lax.rem(n, across) * piece[1], LANES)
            out_sum[pl.ds(down, piece[0]), pl.ds(along, piece[1])] = value

        @pl.when(n >= first)
        def _():
            gate_sum[n - first] = value

    sel[...] = selector(LANES)
    fold_row = lax.broadcasted_iota(jnp.int32, fold.shape, 0) // LANES
    fold_col = lax.broadcasted_iota(jnp.int32, fold.shape, 1)
    fold[...] = (fold_row + R == fold_col).astype(jnp.bfloat16)
    state_ref[...] = carry_ref[...]
    after_ref[...] = last_ref[...]
    grate_ref[...] = jnp.zeros_like(grate_ref)
    for copy in copies:
        copy.wait()

    def backward(k, none):
        c = count - 1 - k
        slot = lax.rem(c, 2)

        @pl.when(c > 0)
        def _():
            fetch(c - 1).start()

        for at_k, job in (
            (count // 8, functools.partial(scatter.step, 1)),
            (count * 5 // 8, functools.partial(scatter.later, 2)),
            (count - 1, functools.partial(scatter.finish, branch_own)),
        ):
            pl.when(k == at_k)(job)

        rows = pl.multiple_of(c * (ct * nr), ct * nr)
        bc[...] = spread(proj_ref[pl.ds(rows, ct * nr), :], sel)
        fetch(c).wait()
        for b in range(blocks):
            lanes = slice(b * LANES, (b + 1) * LANES)
            for first in (True, False):
                ns = range(0, NS // 2) if first else range(NS // 2, NS)
                pairs = range(ns[0] // 2, ns[-1] // 2 + 1)
                rate = [jnp.broadcast_to(a_ref[n : n + 1, lanes], (nr, LANES)) for n in ns]

                def steps(s, carried):
                    grad, total_rate, after = (list(v) for v in carried)
                    for u in reversed(range(uu)):
                        at = (ct // uu - 1 - s) * uu + u
                        here = pl.ds(pl.multiple_of((c * ct + at) * nr, nr), nr)
                        delta = delta_ref[b, here, :]
                        x = x_ref[b, here, :]
                        gy = gy_ref[b, here, :]
                        du = delta * x
                        near = pl.ds(pl.multiple_of(at * nr, nr), nr)
                        along_rate = along_b = None
                        for p in pairs:
                            pair = hist[slot, at, b, pl.ds(2 * p * nr, 2 * nr), :].astype(jnp.float32)
                            for n, before in ((2 * p, pair[:nr]), (2 * p + 1, pair[nr:])):
                                i = n - ns[0]
                                to_b_at = slice(n * LANES, (n + 1) * LANES)
                                to_c_at = slice((NS + n) * LANES, (NS + n + 1) * LANES)
                                decay = jnp.exp2(delta * rate[i])
                                grad[i] = grad[i] + gy * bc[near, to_c_at]
                                to_c = after[i] * gy
                                to_b = grad[i] * du
                                if b > 0:
                                    to_c = to_c + prod[near, to_c_at]
                                    to_b = to_b + prod[near, to_b_at]
                                prod[near, to_c_at] = to_c
                                prod[near, to_b_at] = to_b
                                term_b = grad[i] * bc[near, to_b_at]
                                along_b = term_b if along_b is None else along_b + term_b
                                grad[i] = grad[i] * decay
                                weighted = grad[i] * before
                                total_rate[i] = total_rate[i] + weighted * delta
                                term = weighted * rate[i]
                                along_rate = term if along_rate is None else along_rate + term
                                after[i] = before
                        gdelta = along_rate * LN2 + along_b * x
                        gx = along_b * delta
                        if not first:
                            gdelta = gdelta + gdelta_ref[b, here, :]
                            gx = gx + gx_ref[b, here, :]
                        gdelta_ref[b, here, :] = gdelta
                        gx_ref[b, here, :] = gx
                    return tuple(grad), tuple(total_rate), tuple(after)

                start = tuple(tuple(ref[n, :, lanes] for n in ns) for ref in (state_ref, grate_ref, after_ref))
                ends = lax.fori_loop(0, ct // uu, steps, start)
                for i, n in enumerate(ns):
                    for ref, end in zip((state_ref, grate_ref, after_ref), ends):
                        ref[n, :, lanes] = end[i]
            chain.advance(blocks * k + b, total)
        gbc_ref[pl.ds(rows, ct * nr), :] = jnp.dot(
            prod[...].astype(jnp.bfloat16), fold[...], preferred_element_type=jnp.float32
        )
        return none

    lax.fori_loop(0, count, backward, 0)
    late = copy_all((gdelta_ref, gx_ref), (gdelta_out, gx_out), out_sems)
    for m in range(early, size):
        wait_for(gate_s.at[m - early], gate_recv.at[m])
    late += copy_all((gate_s,), (gate_out,), gate_sem)
    chain.run(blocks * count, max(blocks * count, chain.last_step), total)
    scatter.drain()
    chain.drain()
    drain_swap(size, gate_w, slots)
    for copy in late:
        copy.wait()


def scan_backward(delta, x, gy, hist, proj, params, carry, last, branch, out_w, gate_w, size, seq):
    nr, tt, width = branch.shape
    el = params.shape[1]
    blocks = el // LANES
    ct = math.gcd(tt, 32)
    here = pl.BlockSpec(memory_space=pltpu.VMEM)
    away = pl.BlockSpec(memory_space=pl.ANY)
    f32, bf16 = jnp.float32, jnp.bfloat16
    scan = (blocks, nr * tt, LANES)
    piece = (gate_w.shape[1] // 2, gate_w.shape[2])
    early = early_blocks(size)
    chunks = out_w.size // math.prod(piece) + 2 * early
    return pl.pallas_call(
        functools.partial(backward_kernel, size, seq, nr, tt, ct, max(1, ct * 8 // size)),
        in_specs=[away] * 4 + [here] * 4 + [away] * 3,
        out_specs=[away] * 3 + [here] * 5,
        out_shape=[
            jax.ShapeDtypeStruct(scan, f32),
            jax.ShapeDtypeStruct(scan, f32),
            jax.ShapeDtypeStruct((size - early,) + gate_w.shape[1:], bf16),
            jax.ShapeDtypeStruct((tt * nr, LANES), f32),
            jax.ShapeDtypeStruct((NS, nr, el), f32),
            jax.ShapeDtypeStruct((tt, width), bf16),
            jax.ShapeDtypeStruct(out_w.shape, bf16),
            jax.ShapeDtypeStruct((2 * early,) + piece, bf16),
        ],
        scratch_shapes=[
            pltpu.VMEM((LANES, 2 * NS * LANES), bf16),
            pltpu.VMEM((ct * nr, 2 * NS * LANES), f32),
            pltpu.VMEM((2, ct, blocks, NS * nr, LANES), bf16),
            pltpu.VMEM((ct * nr, 2 * NS * LANES), f32),
            pltpu.VMEM((NS, nr, el), f32),
            pltpu.VMEM((NS, nr, el), f32),
            pltpu.VMEM((2 * NS * LANES, LANES), bf16),
        ]
        + [pltpu.VMEM(scan, f32)] * 5
        + [
            pltpu.VMEM((size - early,) + gate_w.shape[1:], bf16),
            pltpu.VMEM((NS, el), f32),
            pltpu.SemaphoreType.DMA((3,)),
            pltpu.SemaphoreType.DMA((2,)),
            pltpu.SemaphoreType.DMA((2,)),
        ]
        + RowScatter.scratch(size, tt, width)
        + SeqSum.scratch(chunks, piece)
        + [pltpu.SemaphoreType.DMA((size, 2)), pltpu.SemaphoreType.DMA((size,)), pltpu.SemaphoreType.DMA((1,))],
        compiler_params=pltpu.CompilerParams(
            vmem_limit_bytes=62 * MIB, collective_id=3, has_side_effects=True
        ),
        name="scan_backward",
    )(delta, x, gy, hist, proj, params, carry, last, branch, out_w, gate_w)


def small_rows(piece_rows):
    rows = 2 * LANES + 32
    return rows + -rows % piece_rows


def back_kernel(size, seq, *refs):
    gdelta_in, gx_in, delta_in, normed_in, w_in, cext_in, ggp_in, gbc_in, gate_w = refs[:9]
    rank_ref, dt_in, x_w, params, grate_ref, gate_sum = refs[9:15]
    own, in_sum, small_sum = refs[15:18]
    taps_ref, bias_ref = params.at[0:KC], params.at[KC : KC + 1]
    (
        gdelta, gx, delta, normed, wv, cext, gmix, gbc, low, gcp, turned, w_stage, acc_x, acc_dt, acc,
        small, hmail, hland, stage, gco, dt_w,
    ) = refs[18:39]
    part, near, total, mail, far, out, sems = refs[39:46]
    scatter = RowScatter(size, None, *refs[46:52])
    chain = SeqSum(seq, 4, *refs[52:57])
    held, fill_sem = chain.held, chain.fill_sem
    swap_send, in_sems, halo_send, halo_recv = refs[57:]
    me, parity, partner, others = row_peers(size)
    place = lax.axis_index("seq")
    share, el = w_stage.shape[1:]
    tt = low.shape[0]
    width = normed.shape[1]
    blocks = el // LANES
    half = size // 2
    f32, bf16 = jnp.float32, jnp.bfloat16
    nt = (((1,), (1,)), ((), ()))
    tn = (((0,), (0,)), ((), ()))
    copies = copy_all(
        (gdelta_in, delta_in, gbc_in, cext_in, gx_in, ggp_in, w_in, normed_in),
        (gdelta, delta, gbc, cext, gx, gmix.at[:, :, pl.ds(el, el)], wv, normed),
        in_sems,
    )
    early = fill_chunks(held, fill_sem, gate_w)
    greet_rows_and_seq(size, seq)
    for ref in (acc_x, acc_dt, acc, small):
        ref[...] = jnp.zeros_like(ref)
    for copy in copies[:3]:
        copy.wait()

    dt_w[0:R, :] = dt_in[...]
    dt_w[R:, :] = jnp.zeros((LANES - R, el), bf16)
    rows = held.shape[1]
    halves = share // rows
    first = small_rows(rows) // rows
    before = early_blocks(size)

    def place_in(m, i, gate, value):
        along = pl.multiple_of((gate * size + crossed(me, m, size)) * el, LANES)
        in_sum[pl.ds(pl.multiple_of(i * rows, rows), rows), pl.ds(along, el)] = value

    def sums(n, value):
        @pl.when(n < early)
        def _():
            place_in(before + lax.div(n, halves), lax.rem(n, halves), 1, value)

        @pl.when((n >= early) & (n < early + first))
        def _():
            small_sum[pl.ds(pl.multiple_of((n - early) * rows, rows), rows), :] = value

        @pl.when(n >= early + first)
        def _():
            k = n - early - first
            place_in(lax.div(k, halves), lax.rem(k, halves), 0, value)

    for n in range(before * halves):
        place_in(n // halves, n % halves, 1, gate_sum[n])

    def fold8(value):
        return jnp.sum(value.reshape(value.shape[0] // 8, 8, value.shape[1]), axis=0)

    def block_at(i):
        return 2 * lax.rem(me // 2 + lax.rem(i, half), half) + lax.rem(parity + 1 + lax.div(i, half), 2)

    def steps_back(i, none):
        p = block_at(i)

        def body(span):
            for b in range(blocks):
                lanes = slice(b * LANES, (b + 1) * LANES)
                there = pl.ds(p + span.start * size, 64, stride=size)
                dl = delta[b, there, :]
                near_zero = dl * (1.0 - dl * (0.5 - dl * (1.0 / 6.0)))
                value = gdelta[b, there, :] * jnp.where(dl < 0.01, near_zero, 1.0 - jnp.exp(-dl))
                low[span, lanes] = value.astype(bf16)
                acc[KC + 1, :, lanes] = acc[KC + 1, :, lanes] + fold8(value)

        by_tiles(tt, 64, body)
        value = lax.dot_general(low[...], dt_w[...], nt, preferred_element_type=f32)
        value = value + gbc[pl.ds(p, tt, stride=size), :]
        acc_dt[...] += lax.dot_general(rank_ref[p], low[...], tn, preferred_element_type=f32)

        @pl.when(i < half)
        def _():
            part[p] = value.astype(bf16)
            remote(
                part.at[p], near.at[lax.div(p, 2)], sems.at[0, lax.div(p, 2)], sems.at[1, lax.div(p, 2)],
                (place, partner),
            )

        @pl.when(i >= half)
        def _():
            total[lax.div(p, 2)] = value

        return none

    lax.fori_loop(0, size, steps_back, 0)
    for copy in copies[3:]:
        copy.wait()
    def halo(p):
        return pltpu.make_async_remote_copy(
            src_ref=hmail.at[p], dst_ref=hland.at[p], send_sem=halo_send.at[p], recv_sem=halo_recv.at[p],
            device_id=(jnp.maximum(place - 1, 0), me), device_id_type=MESH,
        )

    def conv_back(p, step):
        gco[...] = lax.dot_general(out[p], x_w[...], nt, preferred_element_type=f32)

        def body(span):
            value = gco[span, :]
            there = pl.ds(p + span.start * size, 64, stride=size)
            value = value + jnp.concatenate([gx[b, there, :] for b in range(blocks)], axis=1)
            ext = cext[p, pl.ds(span.start, 80), :].astype(f32)
            here = bias_ref[...]
            for k in range(KC):
                here = here + taps_ref[k : k + 1, :] * ext[16 - KC + 1 + k : 16 - KC + 1 + k + 64]
            sig = 1.0 / (1.0 + jnp.exp(-here))
            low[span, :] = (here * sig).astype(bf16)
            value = value * sig * (1.0 + here * (1.0 - sig))
            gcp[p, span, :] = value
            acc[KC] = acc[KC] + fold8(value)
            for k in range(KC):
                acc[k] = acc[k] + fold8(value * ext[16 - KC + 1 + k : 16 - KC + 1 + k + 64])

        by_tiles(tt, 64, body)
        acc_x[...] += lax.dot_general(out[p], low[...], tn, preferred_element_type=f32)
        hmail[p] = gcp[p, 0:16, :].astype(bf16)

        @pl.when(place > 0)
        def _():
            halo(p).start()

        if step < early:
            chain.advance(step, sums)

    steps_done = iter(range(size))
    exchange_sums(size, near, total, mail, far, out, sems, lambda p: conv_back(p, next(steps_done)))
    for j in range(half):
        wait_for(near.at[j], sems.at[0, j])

    def turn(p, none):
        @pl.when(place < seq - 1)
        def _():
            halo(p).wait_recv()
            gcp[p, tt : tt + 8, :] = hland[p, 0:8, :].astype(f32)

        @pl.when(place == seq - 1)
        def _():
            gcp[p, tt : tt + 8, :] = jnp.zeros((8, el), f32)

        def body(span):
            ext = gcp[p, pl.ds(span.start, 72), :]
            value = taps_ref[KC - 1 : KC, :] * ext[0:64]
            for k in range(KC - 1):
                value = value + taps_ref[k : k + 1, :] * ext[KC - 1 - k : KC - 1 - k + 64]
            gmix[p, span, 0:el] = value.astype(bf16)

        by_tiles(tt, 64, body)
        columns = pl.ds(pl.multiple_of(p * tt, tt), tt)
        turned[:, columns] = jnp.transpose(gmix[p, :, 0:el].astype(f32)).astype(bf16)

        @pl.when(size + p < early)
        def _():
            chain.advance(size + p, sums)

        return none

    lax.fori_loop(0, size, turn, 0)
    chain.run(2 * size, max(2 * size, early), sums)

    group = 384 // share

    def weights(j, none):
        columns = pl.ds(pl.multiple_of(j * 384, 384), 384)
        value = jnp.dot(turned[...], normed[:, columns], preferred_element_type=f32)
        value = jnp.transpose(value).astype(bf16)
        for g in range(group):
            w_stage[j * group + g] = value[g * share : (g + 1) * share, :]
        return none

    lax.fori_loop(0, width // 384, weights, 0)
    top = 2 * LANES
    small[0:LANES, :] = acc_x[...].astype(bf16)
    small[LANES:top, :] = acc_dt[...].astype(bf16)
    rate_sum = jnp.sum(grate_ref[...], axis=1) * decay_rates(params)
    last = [rate_sum] + [jnp.sum(acc[k], axis=0, keepdims=True) for k in range(KC + 2)]
    last.append(jnp.zeros((16 - KC - 2, el), f32))
    small[top : top + 32, :] = jnp.concatenate(last, axis=0).astype(bf16)
    late = fill_chunks(held, fill_sem, small, early)

    def slots(m, i):
        n = late + m * halves + i
        return held.at[n], fill_sem.at[n], swap_send.at[n]

    swap_blocks(size, w_stage, slots)

    def spread_back(i, none):
        p = crossed(me, jnp.where(i < half, 2 * i + 1, 2 * (i - half)), size)
        weight = wv[...].reshape(width, 2 * el)
        value = lax.dot_general(gmix[p], weight, nt, preferred_element_type=f32).astype(bf16)

        @pl.when(i < half)
        def _():
            stage[i] = value
            scatter.staged(i, stage)

        @pl.when(i >= half)
        def _():
            scatter.keep[i - half] = value

        chain.advance(early + i, sums)
        return none

    lax.fori_loop(0, size, spread_back, 0)
    done = early + size
    jobs = [functools.partial(scatter.step, k) for k in range(1, scatter.steps)]
    jobs.append(functools.partial(scatter.finish, own))
    for k, job in enumerate(jobs):
        job()
        upto = min(chain.last_step, done + (chain.last_step - done) * (2 if k else 3) // 4)
        chain.run(done, upto, sums)
        done = upto
    chain.run(done, chain.last_step, sums)
    scatter.drain()
    chain.drain()
    drain_swap(size, w_stage, slots)

    def halo_sent(p, none):
        halo(p).wait_send()
        return none

    @pl.when(place > 0)
    def _():
        lax.fori_loop(0, size, halo_sent, 0)


def back(
    gdelta, gx, delta, normed, w_in, cext, ggp, gbc, gate_w, rank, dt_w, x_w, params, grate, gate_sum, size, seq
):
    away = pl.BlockSpec(memory_space=pl.ANY)
    here = pl.BlockSpec(memory_space=pltpu.VMEM)
    f32, bf16 = jnp.float32, jnp.bfloat16
    unused_size, tt, el = ggp.shape
    share = w_in.shape[1]
    width = normed.shape[1]
    piece = (share // 2, el)
    low = small_rows(piece[0])
    chunks = 4 * size - 2 * early_blocks(size) + low // piece[0]
    scratch = [
        (gdelta.shape, f32), (gx.shape, f32), (delta.shape, f32), (normed.shape, bf16), (w_in.shape, bf16),
        (cext.shape, bf16), ((size, tt, 2 * el), bf16), (gbc.shape, f32), ((tt, el), bf16),
        ((size, tt + 8, el), f32), ((el, size * tt), bf16), ((size, share, el), bf16), ((LANES, el), f32),
        ((LANES, el), f32), ((KC + 2, 8, el), f32), ((low, el), bf16), ((size, 16, el), bf16),
        ((size, 16, el), bf16), ((size // 2, tt, width), bf16), ((tt, el), f32),
        ((LANES, el), bf16),
    ]
    return pl.pallas_call(
        functools.partial(back_kernel, size, seq),
        in_specs=[away] * 9 + [here] * 6,
        out_specs=[here] * 3,
        out_shape=[
            jax.ShapeDtypeStruct((tt, width), bf16),
            jax.ShapeDtypeStruct((share, 2 * size * el), bf16),
            jax.ShapeDtypeStruct((low, el), bf16),
        ],
        scratch_shapes=[pltpu.VMEM(*v) for v in scratch]
        + sum_scratch(size, tt)
        + RowScatter.scratch(size, tt, width)
        + SeqSum.scratch(chunks, piece)
        + [
            pltpu.SemaphoreType.DMA((chunks,)),
            pltpu.SemaphoreType.DMA((8,)),
            pltpu.SemaphoreType.DMA((size,)),
            pltpu.SemaphoreType.DMA((size,)),
        ],
        compiler_params=pltpu.CompilerParams(
            vmem_limit_bytes=63 * MIB, collective_id=4, has_side_effects=True
        ),
        name="back",
    )(gdelta, gx, delta, normed, w_in, cext, ggp, gbc, gate_w, rank, dt_w, x_w, params, grate, gate_sum)


def local(
    tokens, resets, norm_gain, in_proj, x_proj, dt_proj, conv_weight, conv_bias, dt_bias, a_log, out_proj,
    cotangent,
):
    size = lax.axis_size("rows")
    seq = lax.axis_size("seq")
    rd, tt, unused_d = tokens.shape
    nr = rd * size
    el = E // size
    count = nr * tt
    assert rd == 1 and ITEM % tt == 0 and nr % 8 == 0

    elp = pad_lanes(el)
    share = D // size
    direct = elp == el
    f32, bf16 = jnp.float32, jnp.bfloat16

    def widen(value, axis):
        pad = [(0, 0)] * value.ndim
        pad[axis] = (0, elp - el)
        return jnp.pad(value, pad)

    if direct:
        w_local = in_proj
    else:
        w_local = jnp.moveaxis(in_proj.reshape(share, 2, size, el), 2, 0)
        w_local = widen(w_local, 3).reshape(size, share, 2 * elp)
    out_proj, x_proj = widen(out_proj, 0), widen(x_proj, 0)
    dt_proj = widen(dt_proj, 1)
    params = [conv_weight, conv_bias[None], dt_bias[None], jnp.zeros((8 - KC - 2, el), bf16), a_log]
    params = widen(jnp.concatenate(params, axis=0).astype(f32), 1)
    notes = jnp.zeros((16, -(-share // 256) * 256), bf16)
    notes = notes.at[0, :share].set(norm_gain).at[1].set(1.0 - resets[0, 0].astype(bf16))
    (
        normed, w_in, x_t, delta_t, gy_t, conv_ext, hist, branch, grad_out_proj, grad_in_gate, grad_gate_pre, proj_t,
        rank_all, last, carry_back, gain,
    ) = front(
        tokens[0], cotangent[0], notes, w_local, out_proj, x_proj, dt_proj, params, size, seq, direct
    )
    grad_delta, grad_input, gate_blocks, grad_bc, grate, branch_own, sum_out, gate_sum = scan_backward(
        delta_t, x_t, gy_t, hist, proj_t, params, carry_back, last, branch, grad_out_proj[:el], grad_in_gate, size, seq
    )
    grad_normed, sum_in, small = back(
        grad_delta, grad_input, delta_t, normed.reshape(count, D), w_in, conv_ext, grad_gate_pre, grad_bc, gate_blocks,
        rank_all, dt_proj, x_proj, params, grate, gate_sum, size, seq,
    )
    sum_in = sum_in.reshape(share, 2, size, elp)[..., :el].reshape(share, 2 * E)
    sum_out = sum_out.astype(f32)
    small = small[:, :el].astype(f32)
    block_out = (tokens.astype(jnp.float32) + branch_own[None].astype(jnp.float32)).astype(jnp.bfloat16)
    grad_normed = grad_normed[None].astype(jnp.float32)

    own = tokens.astype(jnp.float32)
    inv = lax.rsqrt(jnp.mean(own * own, axis=2, keepdims=True) + epsilon)
    gain_own = jnp.sum(in_proj.astype(f32) * sum_in.astype(f32), axis=1) / norm_gain.astype(jnp.float32)
    grad_hat = grad_normed * gain
    grad_norm_in = inv * (
        grad_hat - own * (inv * inv) * jnp.mean(grad_hat * own, axis=2, keepdims=True)
    )
    d_tokens = (cotangent.astype(jnp.float32) + grad_norm_in).astype(jnp.bfloat16)

    more = small[2 * LANES :]
    return (
        block_out,
        d_tokens,
        gain_own,
        sum_in.astype(f32),
        small[:LANES].T,
        small[LANES : LANES + R],
        more[NS : NS + KC],
        more[NS + KC],
        more[NS + KC + 1],
        more[:NS],
        sum_out,
    )


def solution(mesh):
    in_specs = (
        P("rows", "seq", None),
        P("rows", "seq"),
        P("rows"),
        P("rows", None),
        P("rows", None),
        P(None, "rows"),
        P(None, "rows"),
        P("rows"),
        P("rows"),
        P(None, "rows"),
        P("rows", None),
        P("rows", "seq", None),
    )
    out_specs = (
        P("rows", "seq", None),
        P("rows", "seq", None),
        P("rows"),
        P("rows", None),
        P("rows", None),
        P(None, "rows"),
        P(None, "rows"),
        P("rows"),
        P("rows"),
        P(None, "rows"),
        P("rows", None),
    )
    return jax.shard_map(local, mesh=mesh, in_specs=in_specs, out_specs=out_specs, check_vma=False)
```

```python
import functools
import math

import jax
import jax.numpy as jnp
from jax import lax
from jax.experimental import pallas as pl
from jax.experimental.pallas import tpu as pltpu
from jax.sharding import PartitionSpec as P

D = 1536
E = 3072
R = 96
NS = 16
KC = 4
ITEM = 256

epsilon = 1e-05
LOG2E = 1.4426950408889634
LN2 = 0.6931471805599453
MIB = 2**20


LANES = 128


def pad_lanes(lanes):
    return -(-lanes // LANES) * LANES


def selector(wide):
    row = lax.broadcasted_iota(jnp.int32, (LANES, 2 * NS * wide), 0)
    col = lax.broadcasted_iota(jnp.int32, (LANES, 2 * NS * wide), 1) // wide
    return (row == col + R).astype(jnp.bfloat16)


def decay_rates(params):
    return -jnp.exp(params[8 : 8 + NS, :])


def spread(proj, sel_ref):
    return jnp.dot(proj.astype(jnp.bfloat16), sel_ref[...], preferred_element_type=jnp.float32)


def copy_all(sources, targets, sems):
    copies = []
    for i, (source, target) in enumerate(zip(sources, targets)):
        copies.append(pltpu.make_async_copy(source, target, sems.at[i]))
        copies[-1].start()
    return copies


MESH = pl.DeviceIdType.MESH


def greet(devices):
    barrier = pltpu.get_barrier_semaphore()
    for device in devices:
        pl.semaphore_signal(barrier, inc=1, device_id=device, device_id_type=MESH)
    pl.semaphore_wait(barrier, len(devices))


def remote(source, target, send, recv, device):
    copy = pltpu.make_async_remote_copy(
        src_ref=source, dst_ref=target, send_sem=send, recv_sem=recv, device_id=device, device_id_type=MESH
    )
    copy.start()
    return copy


def row_peers(size):
    me = lax.axis_index("rows")
    half = size // 2
    mine = me // 2
    return me, me % 2, me + 1 - 2 * (me % 2), [lax.rem(mine + k, half) for k in range(half)]


def exchange_sums(size, near, total, mail, far, out, sems, use, between=None):
    me, parity, partner, others = row_peers(size)
    place = lax.axis_index("seq")
    half = size // 2
    second = []
    for k in list(range(1, half)) + [0]:
        j = others[k]
        wait_for(near.at[j], sems.at[1, j])
        total[j] = total[j] + near[j].astype(jnp.float32)
        if k:
            mail[j] = total[j].astype(jnp.bfloat16)
            target = (place, 2 * j + parity)
            second.append(remote(mail.at[j], far.at[k], sems.at[2, k], sems.at[3, k], target))
    mine = others[0]
    done = total[mine]
    for k in range(1, half):
        wait_for(far.at[k], sems.at[3, k])
        done = done + far[k].astype(jnp.float32)
    out[me] = done.astype(jnp.bfloat16)
    third = []
    for k in range(1, half):
        target = (place, 2 * others[k] + parity)
        third.append(remote(out.at[me], out.at[me], sems.at[4, k], sems.at[5, k], target))
    fourth = [remote(out.at[me], out.at[me], sems.at[6, 0], sems.at[7, 0], (place, partner))]
    use(me)
    for k in range(1, half):
        block = 2 * others[half - k] + parity
        wait_for(out.at[block], sems.at[5, k])
        fourth.append(
            remote(out.at[block], out.at[block], sems.at[6, k], sems.at[7, k], (place, partner))
        )
        use(block)
    for k in range(half):
        block = 2 * others[(half - k) % half] + 1 - parity
        wait_for(out.at[block], sems.at[7, k])
        use(block)
    if between:
        between()
    for copy in second + third + fourth:
        copy.wait_send()


def sum_scratch(size, tt):
    half = size // 2
    return [
        pltpu.VMEM((size, tt, LANES), jnp.bfloat16),
        pltpu.VMEM((half, tt, LANES), jnp.bfloat16),
        pltpu.VMEM((half, tt, LANES), jnp.float32),
        pltpu.VMEM((half, tt, LANES), jnp.bfloat16),
        pltpu.VMEM((half, tt, LANES), jnp.bfloat16),
        pltpu.VMEM((size, tt, LANES), jnp.bfloat16),
        pltpu.SemaphoreType.DMA((8, half)),
    ]


class Carry:
    def __init__(self, seq, ends, alive, out, mail, land, sems):
        self.seq, self.ends, self.alive, self.out = seq, ends, alive, out
        self.mail, self.land, self.sems = mail, land, sems
        self.me, self.place = lax.axis_index("rows"), lax.axis_index("seq")

    @staticmethod
    def scratch(shape):
        return [
            pltpu.VMEM((2,) + shape, jnp.bfloat16),
            pltpu.VMEM((2,) + shape, jnp.bfloat16),
            pltpu.SemaphoreType.DMA((2, 2, shape[-1] // LANES)),
        ]

    def copy(self, way, b):
        lanes = pl.ds(b * LANES, LANES)
        target = (jnp.clip(self.place + 1 - 2 * way, 0, self.seq - 1), self.me)
        return pltpu.make_async_remote_copy(
            src_ref=self.mail.at[way, :, :, lanes], dst_ref=self.land.at[way, :, :, lanes],
            send_sem=self.sems.at[way, 0, b], recv_sem=self.sems.at[way, 1, b], device_id=target,
            device_id_type=MESH,
        )

    def hop(self, way):
        first, last = ((0, self.seq - 1), (self.seq - 1, 0))[way]
        alive = self.alive[:, 0:1][None]

        for b in range(self.mail.shape[-1] // LANES):
            lanes = slice(b * LANES, (b + 1) * LANES)

            @pl.when(self.place == first)
            def _(lanes=lanes):
                self.out[way, :, :, lanes] = jnp.zeros(self.out.shape[1:3] + (LANES,), jnp.float32)

            @pl.when(self.place != first)
            def _(b=b, lanes=lanes):
                self.copy(way, b).wait_recv()
                entering = self.land[way, :, :, lanes].astype(jnp.float32)
                self.out[way, :, :, lanes] = entering * alive if way == 0 else entering

            @pl.when(self.place != last)
            def _(b=b, lanes=lanes):
                passed = self.ends[1, :, :, lanes] * self.out[way, :, :, lanes]
                if way == 0:
                    leaving = self.ends[0, :, :, lanes] + passed
                else:
                    leaving = (self.ends[2, :, :, lanes] + passed) * alive
                self.mail[way, :, :, lanes] = leaving.astype(jnp.bfloat16)
                self.copy(way, b).start()

    def turn(self, way, t):
        behind = (self.place, self.seq - 1 - self.place)[way]
        pl.when(behind == t)(functools.partial(self.hop, way))

    def drain(self):
        for way, last in ((0, self.seq - 1), (1, 0)):

            @pl.when(self.place != last)
            def _(way=way):
                for b in range(self.mail.shape[-1] // LANES):
                    self.copy(way, b).wait_send()


def flip(place, mask):
    for k in range(mask.bit_length()):
        bit = 1 << k
        if mask & bit:
            place = place + bit * (1 - 2 * (lax.div(place, bit) % 2))
    return place


def bit_orders(size):
    rest = [1 << k for k in range(1, size.bit_length() - 1)]
    cut = max(1, len(rest) // 2)
    return [1] + rest, [1] + rest[cut:] + rest[:cut]


def masks_of(bits):
    masks = [0]
    for bit in bits:
        masks = masks + [m | bit for m in masks]
    return masks


def by_tiles(rows, tile, body):
    def step(i, none):
        body(pl.ds(pl.multiple_of(i * tile, tile), tile))
        return none

    lax.fori_loop(0, rows // tile, step, 0)


def wait_for(ref, sem):
    pltpu.make_async_copy(ref, ref, sem).wait()


def greet_seq(seq):
    me, place = lax.axis_index("rows"), lax.axis_index("seq")
    barrier = pltpu.get_barrier_semaphore()
    for step, there in ((-1, place > 0), (1, place < seq - 1)):

        @pl.when(there)
        def _(step=step):
            pl.semaphore_signal(barrier, inc=1, device_id=(place + step, me), device_id_type=MESH)

    pl.semaphore_wait(barrier, (place > 0).astype(jnp.int32) + (place < seq - 1).astype(jnp.int32))


def greet_rows_and_seq(size, seq):
    me, place = lax.axis_index("rows"), lax.axis_index("seq")
    barrier = pltpu.get_barrier_semaphore()
    for mask in range(1, size):
        pl.semaphore_signal(barrier, inc=1, device_id=(place, flip(me, mask)), device_id_type=MESH)
    for step, there in ((-1, place > 0), (1, place < seq - 1)):

        @pl.when(there)
        def _(step=step):
            pl.semaphore_signal(barrier, inc=1, device_id=(place + step, me), device_id_type=MESH)

    near = (place > 0).astype(jnp.int32) + (place < seq - 1).astype(jnp.int32)
    pl.semaphore_wait(barrier, near + size - 1)


def crossed(place, mask, size):
    out = 0
    for k in range(size.bit_length() - 1):
        bit = 1 << k
        out = out + bit * lax.rem(lax.div(place, bit) + lax.div(mask, bit), 2)
    return out


class RowGather:
    def __init__(self, size, source, out, own_sem, send, recv):
        self.size, self.source, self.out, self.own_sem, self.send, self.recv = size, source, out, own_sem, send, recv
        self.me, self.place = lax.axis_index("rows"), lax.axis_index("seq")
        self.rows = source.shape[0] // 2
        self.orders = [order[1:] for order in bit_orders(size)]
        self.steps = len(self.orders[0])

    @staticmethod
    def sems(size):
        return [pltpu.SemaphoreType.DMA((1,))] + [pltpu.SemaphoreType.DMA((2, size))] * 2

    def half(self, h, m, ref=None):
        ref = self.out.at[flip(self.me, m)] if ref is None else ref
        return ref.at[pl.ds(h * self.rows, self.rows), :]

    def push(self, h, m, bit):
        source = self.half(h, m, self.source if m == 0 else None)
        key = (h, m | bit)
        remote(
            source, self.half(h, m), self.send.at[key], self.recv.at[key], (self.place, flip(self.me, bit))
        )

    def arrived(self, h, m):
        wait_for(self.half(h, m), self.recv.at[h, m])

    def start(self):
        pltpu.make_async_copy(self.source, self.out.at[self.me], self.own_sem.at[0]).start()
        for h in range(2):
            self.push(h, 0, self.orders[h][0])
        for h in range(2):
            self.push(h, 0, 1)

    def own(self):
        wait_for(self.out.at[self.me], self.own_sem.at[0])

    def step(self, k, use=None):
        for h in range(2):
            order = self.orders[h]
            old = masks_of(order[:k])
            if k + 1 < self.steps:
                for m in old:
                    self.push(h, m, order[k + 1])
            for m in old:
                fresh = m | order[k]
                self.arrived(h, fresh)
                if k + 1 < self.steps:
                    self.push(h, fresh, order[k + 1])
                self.push(h, fresh, 1)
                if use:
                    use(h, fresh)

    def paired(self, use=None):
        for m in masks_of(self.orders[0]):
            for h in range(2):
                self.arrived(h, m | 1)
                if use:
                    use(h, m | 1)

    def drain(self):
        for h in range(2):
            for m in range(1, self.size):
                wait_for(self.half(h, 0), self.send.at[h, m])


def front_kernel(size, seq, direct, ct, uu, *refs):
    (tokens, cot, notes, w_local, out_w, x_w, dt_in, params) = refs[:8]
    (
        normed_out, w_out, x_out, delta_out, gy_out, cext_out, hist_out, branch_out, dout_out, dwg_out, ggp_out,
        proj_ref, rank_ref, last_ref, leaving_ref, gain_ref,
    ) = refs[8:24]
    (
        tok, cot_s, wc, wg, cext, xb, x_s, delta_s, gy_s, gate_s, gg_s, all_notes, alive_ref, sel, bc, ends, entered,
        delta_sum, hist, y_s, gated, ggp, branch_s, turned, d_stage, w_stage, gate_b, dt_w, a_ref,
    ) = refs[24:53]
    token_sems, cot_sems = refs[53:56], refs[56:59]
    part, near, total, mail, far, out, sems = refs[59:66]
    carry = Carry(seq, ends, alive_ref, entered, *refs[66:69])
    taps_ref, bias_ref, dt_bias_ref = params.at[0:KC], params.at[KC : KC + 1], params.at[KC + 1 : KC + 2]
    (
        note_send, note_recv, wc_send, wc_recv, wg_send, wg_recv, halo_send, halo_recv, out_sems, hist_sems, branch_sems,
    ) = refs[69:]
    normed = tok
    me, parity, partner, others = row_peers(size)
    place = lax.axis_index("seq")
    tt, width = tokens.shape
    share, el = wc.shape[1:]
    nr = size
    blocks = el // LANES
    half = size // 2
    f32, bf16 = jnp.float32, jnp.bfloat16
    tile = 64
    stores = []

    def put(source, target):
        copy = pltpu.make_async_copy(source, target, out_sems.at[len(stores)])
        copy.start()
        stores.append(copy)

    def piece(q, gate):
        if direct:
            at = pl.multiple_of(q * el, LANES) + gate * size * el
            return w_local.at[:, pl.ds(at, el)]
        return w_local.at[q, :, pl.ds(gate * el, el)]

    cut = share // 2
    beside = (flip(place, 1), me)

    def swap(gate, target, send, recv):
        there = pl.ds(pl.multiple_of(lax.rem(place, 2) * cut, cut), cut)
        for m in range(1, size):
            q = flip(me, m)
            remote(piece(q, gate).at[there, :], target.at[me, there, :], send.at[0, m], recv.at[0, m], (place, q))
        pltpu.make_async_copy(piece(me, gate), target.at[me], recv.at[0, 0]).start()

    def swap_on(target, send, recv):
        there = pl.ds(pl.multiple_of(lax.rem(place, 2) * cut, cut), cut)
        for m in range(1, size):
            block = target.at[flip(me, m), there, :]
            wait_for(block, recv.at[0, m])
            remote(block, block, send.at[1, m], recv.at[1, m], beside)

    def swapped(target, send, recv):
        wait_for(target.at[me], recv.at[0, 0])
        for m in range(1, size):
            wait_for(target.at[flip(me, m), pl.ds(0, cut), :], recv.at[1, m])

    def swap_drain(target, send):
        for k in range(2):
            for m in range(1, size):
                wait_for(target.at[0, pl.ds(0, cut), :], send.at[k, m])

    greet_rows_and_seq(size, seq)

    sent = []
    for m in range(1, size):
        sent.append(remote(notes, all_notes.at[me], note_send.at[m], note_recv.at[m], (place, flip(me, m))))
    pltpu.make_async_copy(notes, all_notes.at[me], note_recv.at[0]).start()
    token_rows = RowGather(size, tokens, tok, *token_sems)
    cot_rows = RowGather(size, cot, cot_s, *cot_sems)
    swap(0, wc, wc_send, wc_recv)
    token_rows.start()

    for m in range(size):
        wait_for(all_notes.at[flip(me, m)], note_recv.at[m])
    for p in range(size):
        note = all_notes[p].astype(f32)
        gain_ref[:, p * share : (p + 1) * share] = note[0:1, :share]
        alive_ref[p : p + 1, :] = note[1:2, :LANES]

    def norm(p, base, rows):
        def body(span):
            there = pl.ds(base + span.start, span.size)
            x = tok[p, there, :].astype(f32)
            inv = lax.rsqrt(jnp.mean(x * x, axis=1, keepdims=True) + epsilon)
            normed[p, there, :] = (x * inv * gain_ref[...]).astype(bf16)

        by_tiles(rows, 64, body)

    def norm_half(h, m):
        norm(flip(me, m), h * (tt // 2), tt // 2)

    token_rows.own()
    norm(me, 0, tt)
    swap_on(wc, wc_send, wc_recv)
    sel[...] = selector(LANES)
    a_ref[...] = decay_rates(params) * LOG2E
    dt_w[0:R, :] = dt_in[...]
    dt_w[R:, :] = jnp.zeros((LANES - R, el), bf16)
    for k in range(token_rows.steps):
        token_rows.step(k)
    token_rows.paired(norm_half)
    token_rows.drain()
    for m in masks_of(token_rows.orders[0])[1:]:
        norm(flip(me, m), 0, tt)
    swapped(wc, wc_send, wc_recv)

    @pl.when(place == 0)
    def _():
        cext[:, 0:16, :] = jnp.zeros((size, 16, el), bf16)

    def halo(p, i):
        there = cext.at[p, pl.ds(0, 16), :]
        return pltpu.make_async_remote_copy(
            src_ref=cext.at[p, pl.ds(tt, 16), :], dst_ref=there, send_sem=halo_send.at[i],
            recv_sem=halo_recv.at[i], device_id=(jnp.minimum(place + 1, seq - 1), me), device_id_type=MESH,
        )

    def block_at(i):
        return 2 * lax.rem(me // 2 + lax.rem(i, half), half) + lax.rem(parity + 1 + lax.div(i, half), 2)

    def mix(i, none):
        p = block_at(i)
        weight = wc[...].reshape(size * share, el)
        cext[p, 16:, :] = jnp.dot(normed[p], weight, preferred_element_type=f32).astype(bf16)

        @pl.when(place < seq - 1)
        def _():
            halo(p, i).start()

        return none

    lax.fori_loop(0, size, mix, 0)
    for p in range(size):
        put(normed.at[p], normed_out.at[p])

    def conv(i, none):
        p = block_at(i)

        @pl.when(place > 0)
        def _():
            halo(p, i).wait_recv()

        def body(span):
            ext = cext[p, pl.ds(span.start, tile + 16), :].astype(f32)
            value = bias_ref[...]
            for k in range(KC):
                value = value + taps_ref[k : k + 1, :] * ext[16 - KC + 1 + k : 16 - KC + 1 + k + tile]
            x = (value / (1.0 + jnp.exp(-value))).astype(bf16)
            xb[span, :] = x
            for b in range(blocks):
                there = pl.ds(p + span.start * size, tile, stride=size)
                x_s[b, there, :] = x[:, b * LANES : (b + 1) * LANES].astype(f32)

        by_tiles(tt, tile, body)
        value = jnp.dot(xb[...], x_w[...], preferred_element_type=f32)

        @pl.when(i < half)
        def _():
            part[p] = value.astype(bf16)
            pltpu.make_async_remote_copy(
                src_ref=part.at[p], dst_ref=near.at[lax.div(p, 2)], send_sem=sems.at[0, lax.div(p, 2)],
                recv_sem=sems.at[1, lax.div(p, 2)], device_id=(place, partner), device_id_type=MESH,
            ).start()

        @pl.when(i >= half)
        def _():
            total[lax.div(p, 2)] = value

        return none

    lax.fori_loop(0, size, conv, 0)
    put(cext, cext_out)
    put(x_s, x_out)

    def use(p):
        block = out[p]
        rank_ref[p] = block
        proj_ref[pl.ds(p, tt, stride=size), :] = block.astype(f32)

        gate_s[...] = jnp.dot(block, dt_w[...], preferred_element_type=f32)

        def body(span):
            step = gate_s[span, :] + dt_bias_ref[...]
            delta = jnp.maximum(step, 0.0) + jnp.log1p(jnp.exp(-jnp.abs(step)))
            for b in range(blocks):
                there = pl.ds(p + span.start * size, 64, stride=size)
                delta_s[b, there, :] = delta[:, b * LANES : (b + 1) * LANES]

        by_tiles(tt, 64, body)

    def second_wave():
        cot_rows.start()
        swap(1, wg, wg_send, wg_recv)

    exchange_sums(size, near, total, mail, far, out, sems, use, second_wave)
    for j in range(half):
        pltpu.make_async_remote_copy(
            src_ref=part.at[j], dst_ref=near.at[j], send_sem=sems.at[0, j], recv_sem=sems.at[1, j],
            device_id=(place, partner), device_id_type=MESH,
        ).wait_send()
    put(delta_s, delta_out)
    put(wc, w_out.at[:, :, pl.ds(0, el)])

    count = tt // ct
    ends[0] = jnp.zeros((NS, nr, el), f32)
    ends[2] = jnp.zeros((NS, nr, el), f32)
    ends[3] = jnp.ones((NS, nr, el), f32)
    delta_sum[...] = jnp.zeros_like(delta_sum)

    def spread_chunk(c, first, last):
        rows = pl.multiple_of(c * (ct * nr), ct * nr)
        lanes = slice(first * LANES, last * LANES)
        bc[:, lanes] = spread(proj_ref[pl.ds(rows, ct * nr), :], sel.at[:, lanes])

    def token(c, at):
        return pl.ds(pl.multiple_of((c * ct + at) * nr, nr), nr), pl.ds(pl.multiple_of(at * nr, nr), nr)

    def rates(ns, lanes):
        return [jnp.broadcast_to(a_ref[n : n + 1, lanes], (nr, LANES)) for n in ns]

    def ends_forward(c, none):
        pl.when(c == count // 2)(functools.partial(cot_rows.step, 0))
        spread_chunk(c, 0, NS)
        for b in range(blocks):
            lanes = slice(b * LANES, (b + 1) * LANES)
            rate = rates(range(NS), lanes)

            def steps(s, carried):
                state, so_far = list(carried[:-1]), carried[-1]
                for u in range(uu):
                    here, close = token(c, s * uu + u)
                    delta = delta_s[b, here, :]
                    du = delta * x_s[b, here, :]
                    so_far = so_far + delta
                    for n in range(NS):
                        b_at = n * LANES
                        state[n] = jnp.exp2(delta * rate[n]) * state[n] + du * bc[close, b_at : b_at + LANES]
                return tuple(state) + (so_far,)

            start = tuple(ends[0, n, :, lanes] for n in range(NS)) + (delta_sum[b],)
            last = lax.fori_loop(0, ct // uu, steps, start)
            for n in range(NS):
                ends[0, n, :, lanes] = last[n]
            delta_sum[b] = last[NS]
        return none

    lax.fori_loop(0, count, ends_forward, 0)
    for b in range(blocks):
        lanes = slice(b * LANES, (b + 1) * LANES)
        for n in range(NS):
            ends[1, n, :, lanes] = jnp.exp2(delta_sum[b] * a_ref[n : n + 1, lanes])
    carry.turn(0, 0)

    for t in range(1, seq):
        carry.turn(0, t)
    swap_on(wg, wg_send, wg_recv)
    last_ref[...] = entered[0]

    def store_hist(c):
        slot = lax.rem(c, 2)
        return pltpu.make_async_copy(hist.at[slot], hist_out.at[pl.ds(c * ct, ct)], hist_sems.at[slot])

    def forward(c, none):
        slot = lax.rem(c, 2)

        @pl.when(c >= 2)
        def _():
            store_hist(c - 2).wait()

        for k in range(1, cot_rows.steps):
            pl.when(c == min(count // 2 + k - 1, count - 1))(functools.partial(cot_rows.step, k))
        spread_chunk(c, 0, 2 * NS)
        for b in range(blocks):
            lanes = slice(b * LANES, (b + 1) * LANES)
            rate = rates(range(NS), lanes)

            def steps(s, carried):
                state = list(carried)
                for u in range(uu):
                    at = s * uu + u
                    here, close = token(c, at)
                    delta = delta_s[b, here, :]
                    du = delta * x_s[b, here, :]
                    y = None
                    for n in range(NS):
                        if n % 2 == 0:
                            both = jnp.concatenate([state[n], state[n + 1]], axis=0)
                            hist[slot, at, b, pl.ds(n * nr, 2 * nr), :] = both.astype(bf16)
                        b_at, c_at = n * LANES, (NS + n) * LANES
                        decay = jnp.exp2(delta * rate[n])
                        state[n] = decay * state[n] + du * bc[close, b_at : b_at + LANES]
                        term = state[n] * bc[close, c_at : c_at + LANES]
                        y = term if y is None else y + term
                    y_s[b, here, :] = y
                return tuple(state)

            last = lax.fori_loop(0, ct // uu, steps, tuple(last_ref[n, :, lanes] for n in range(NS)))
            for n in range(NS):
                last_ref[n, :, lanes] = last[n]
        store_hist(c).start()
        return none

    lax.fori_loop(0, count, forward, 0)
    cot_rows.own()
    cot_rows.paired()
    swapped(wg, wg_send, wg_recv)
    put(wg, w_out.at[:, :, pl.ds(el, el)])

    def gates(p):
        weight = wg[...].reshape(size * share, el)
        gate_s[...] = jnp.dot(normed[p], weight, preferred_element_type=f32)
        gg_s[...] = lax.dot_general(
            cot_s[p], out_w[...], (((1,), (1,)), ((), ())), preferred_element_type=f32
        )

    def grad_y(p, none):
        gates(p)

        def body(span):
            gate, gg = gate_s[span, :], gg_s[span, :]
            gate_b[p, span, :] = gate.astype(bf16)
            ggp[p, span, :] = gg.astype(bf16)
            gy = gg * gate / (1.0 + jnp.exp(-gate))
            for b in range(blocks):
                there = pl.ds(p + span.start * size, tile, stride=size)
                gy_s[b, there, :] = gy[:, b * LANES : (b + 1) * LANES]

        by_tiles(tt, tile, body)
        return none

    lax.fori_loop(0, size, grad_y, 0)
    put(gy_s, gy_out)

    def ends_back(c, none):
        spread_chunk(c, NS, 2 * NS)
        for b in range(blocks):
            lanes = slice(b * LANES, (b + 1) * LANES)
            for n0 in (0, NS // 2):
                ns = range(n0, n0 + NS // 2)
                rate = rates(ns, lanes)

                def steps(s, carried):
                    through, back = (list(v) for v in carried)
                    for u in range(uu):
                        here, close = token(c, s * uu + u)
                        delta = delta_s[b, here, :]
                        gy = gy_s[b, here, :]
                        for i, n in enumerate(ns):
                            c_at = (NS + n) * LANES
                            through[i] = through[i] * jnp.exp2(delta * rate[i])
                            back[i] = back[i] + through[i] * (gy * bc[close, c_at : c_at + LANES])
                    return tuple(through), tuple(back)

                start = tuple(tuple(ends[k, n, :, lanes] for n in ns) for k in (3, 2))
                last = lax.fori_loop(0, ct // uu, steps, start)
                for i, n in enumerate(ns):
                    ends[3, n, :, lanes] = last[0][i]
                    ends[2, n, :, lanes] = last[1][i]
        return none

    lax.fori_loop(0, count, ends_back, 0)
    carry.turn(1, 0)

    def store_branch(i):
        slot = lax.rem(i, 2)
        return pltpu.make_async_copy(branch_s.at[slot], branch_out.at[i], branch_sems.at[slot])

    def turn(value, p):
        columns = pl.ds(pl.multiple_of(p * tt, tt), tt)
        turned[:, columns] = jnp.transpose(value.astype(f32)).astype(bf16)

    def products(p, none):
        def body(span):
            there = pl.ds(p + span.start * size, tile, stride=size)
            y = jnp.concatenate([y_s[b, there, :] for b in range(blocks)], axis=1)
            gate = gate_b[p, span, :].astype(f32)
            sig = 1.0 / (1.0 + jnp.exp(-gate))
            gated[span, :] = (y * gate * sig).astype(bf16)
            ggp[p, span, :] = (ggp[p, span, :].astype(f32) * y * sig * (1.0 + gate * (1.0 - sig))).astype(bf16)

        by_tiles(tt, tile, body)

        @pl.when(p >= 2)
        def _():
            store_branch(p - 2).wait()

        branch = jnp.dot(gated[...], out_w[...], preferred_element_type=f32)
        branch_s[lax.rem(p, 2)] = branch.astype(bf16)
        store_branch(p).start()
        turn(gated[...], p)

        @pl.when(lax.rem(p, 2) == 1)
        def _():
            carry.turn(1, lax.div(p, 2) + 1)

        return none

    lax.fori_loop(0, size, products, 0)
    for t in range(half + 1, seq):
        carry.turn(1, t)
    put(ggp, ggp_out)
    wide = 384
    group = wide // share

    def out_weights(j, none):
        columns = pl.ds(pl.multiple_of(j * wide, wide), wide)
        right = cot_s[:, :, columns].reshape(size * tt, wide)
        d_stage[:, columns] = jnp.dot(turned[...], right, preferred_element_type=f32).astype(bf16)
        return none

    lax.fori_loop(0, width // wide, out_weights, 0)
    put(d_stage, dout_out)

    def turn_gate(p, none):
        turn(ggp[p], p)
        return none

    lax.fori_loop(0, size, turn_gate, 0)

    def gate_weights(j, none):
        columns = pl.ds(pl.multiple_of(j * wide, wide), wide)
        right = normed[:, :, columns].reshape(size * tt, wide)
        value = jnp.transpose(jnp.dot(turned[...], right, preferred_element_type=f32)).astype(bf16)
        for g in range(group):
            w_stage[j * group + g] = value[g * share : (g + 1) * share, :]
        return none

    lax.fori_loop(0, width // wide, gate_weights, 0)
    put(w_stage, dwg_out)
    for c in range(max(0, count - 2), count):
        store_hist(c).wait()
    for p in range(size - 2, size):
        store_branch(p).wait()
    leaving_ref[...] = entered[1]
    carry.drain()

    for i in range(size):

        @pl.when(place < seq - 1)
        def _(i=i):
            halo(i, i).wait_send()

    cot_rows.drain()
    swap_drain(wc, wc_send)
    swap_drain(wg, wg_send)
    for copy in sent:
        copy.wait_send()
    for copy in stores:
        copy.wait()


def front(tokens, cot, notes, w_local, out_w, x_w, dt_w, params, size, seq, direct):
    tt, width = tokens.shape
    el = out_w.shape[0]
    share = width // size
    blocks = el // LANES
    ct = math.gcd(tt, 32)
    away = pl.BlockSpec(memory_space=pl.ANY)
    here = pl.BlockSpec(memory_space=pltpu.VMEM)
    f32, bf16 = jnp.float32, jnp.bfloat16
    rows, scan, states = (size, tt, width), (blocks, tt * size, LANES), (NS, size, el)
    channels, ext = (size, tt, el), (size, tt + 16, el)
    weights = (size, share, el)
    shapes = [
        (rows, bf16), ((size, share, 2 * el), bf16), (scan, f32), (scan, f32), (scan, f32), (ext, bf16),
        ((tt, blocks, NS * size, LANES), bf16), (rows, bf16), ((el, width), bf16), (weights, bf16), (channels, bf16),
        ((tt * size, LANES), f32), ((size, tt, LANES), bf16), (states, f32), (states, f32),
        ((1, width), f32),
    ]
    scratch = [
        (rows, bf16), (rows, bf16), (weights, bf16), (weights, bf16), (ext, bf16), ((tt, el), bf16), (scan, f32),
        (scan, f32), (scan, f32), ((tt, el), f32), ((tt, el), f32), ((size,) + notes.shape, bf16), ((size, LANES), f32),
        ((LANES, 2 * NS * LANES), bf16), ((ct * size, 2 * NS * LANES), f32), ((4,) + states, f32), ((2,) + states, f32),
        ((blocks, size, LANES), f32), ((2, ct, blocks, NS * size, LANES), bf16), (scan, f32), ((tt, el), bf16), (channels, bf16),
        ((2, tt, width), bf16), ((el, size * tt), bf16), ((el, width), bf16), (weights, bf16),
        (channels, bf16), ((LANES, el), bf16), ((NS, el), f32),
    ]
    one = pltpu.SemaphoreType.DMA((size,))
    return pl.pallas_call(
        functools.partial(front_kernel, size, seq, direct, ct, max(1, ct * 8 // size)),
        in_specs=[away] * 4 + [here] * 4,
        out_specs=[away] * 11 + [here] * 5,
        out_shape=[jax.ShapeDtypeStruct(*v) for v in shapes],
        scratch_shapes=[pltpu.VMEM(*v) for v in scratch]
        + RowGather.sems(size) * 2
        + sum_scratch(size, tt)
        + Carry.scratch(states)
        + [one] * 2
        + [pltpu.SemaphoreType.DMA((2, size))] * 4
        + [one] * 2
        + [
            pltpu.SemaphoreType.DMA((size + 9,)),
            pltpu.SemaphoreType.DMA((2,)),
            pltpu.SemaphoreType.DMA((2,)),
        ],
        compiler_params=pltpu.CompilerParams(
            vmem_limit_bytes=63 * MIB, collective_id=0, has_side_effects=True
        ),
        name="front",
    )(tokens, cot, notes, w_local, out_w, x_w, dt_w, params)


class RowScatter:
    def __init__(self, size, part, keep, land, mail, keep_sem, send, recv):
        self.size, self.part, self.keep, self.land, self.mail = size, part, keep, land, mail
        self.keep_sem, self.send, self.recv = keep_sem, send, recv
        self.me, self.place = lax.axis_index("rows"), lax.axis_index("seq")
        self.tt, self.width = keep.shape[1], keep.shape[2] // 2
        self.orders = bit_orders(size)
        self.steps = len(self.orders[0])

    @staticmethod
    def scratch(size, tt, width):
        return [
            pltpu.VMEM((size // 2, tt, width), jnp.bfloat16),
            pltpu.VMEM((size - 1, tt, width), jnp.bfloat16),
            pltpu.VMEM((size // 2 - 1, tt, width), jnp.bfloat16),
            pltpu.SemaphoreType.DMA((size // 2,)),
            pltpu.SemaphoreType.DMA((2, size - 1)),
            pltpu.SemaphoreType.DMA((2, size - 1)),
        ]

    def free(self, h, k):
        return masks_of(self.orders[h][k + 1 :])

    def at(self, h, k, m):
        if k == 0:
            return m >> 1
        return sum(len(self.free(h, j)) for j in range(k)) + self.free(h, k).index(m)

    def cols(self, h):
        return pl.ds(h * self.width, self.width)

    def receive(self, h, k, m):
        slot = self.at(h, k, m)
        wait_for(self.land.at[slot, :, self.cols(h)], self.recv.at[h, slot])

    def partial_sum(self, h, k, m, rows):
        value = self.keep[m >> 1, rows, self.cols(h)].astype(jnp.float32)
        for j in range(k):
            value = value + self.land[self.at(h, j, m), rows, self.cols(h)].astype(jnp.float32)
        return value

    def staged(self, i, stage):
        for h in range(2):
            remote(
                stage.at[i, :, self.cols(h)], self.land.at[i, :, self.cols(h)], self.send.at[h, i],
                self.recv.at[h, i], (self.place, flip(self.me, 1)),
            )

    def start(self):
        for h in range(2):
            self.scatter(h, 0)
        for m in self.free(0, 0):
            pltpu.make_async_copy(
                self.part.at[flip(self.me, m)], self.keep.at[m >> 1], self.keep_sem.at[m >> 1]
            ).start()

    def step(self, k):
        if k == 1 and self.part is not None:
            for j in range(self.size // 2):
                wait_for(self.keep.at[j], self.keep_sem.at[j])
        for h in range(2):
            self.scatter(h, k)

    def scatter(self, h, k):
        bit = self.orders[h][k]
        for m in self.free(h, k):
            slot = self.at(h, k, m)
            if k == 0:
                source = self.part.at[flip(self.me, m | bit), :, self.cols(h)]
            else:
                for j in range(k):
                    self.receive(h, j, m | bit)
                box = slot - self.size // 2

                def fill(rows, m=m, box=box):
                    value = self.partial_sum(h, k, m | bit, rows)
                    self.mail[box, rows, self.cols(h)] = value.astype(jnp.bfloat16)

                by_tiles(self.tt, 32, fill)
                source = self.mail.at[box, :, self.cols(h)]
            remote(
                source, self.land.at[slot, :, self.cols(h)], self.send.at[h, slot], self.recv.at[h, slot],
                (self.place, flip(self.me, bit)),
            )

    def later(self, first):
        for k in range(first, self.steps):
            self.step(k)

    def finish(self, own):
        for h in range(2):
            for j in range(self.steps):
                self.receive(h, j, 0)

            def fill(rows, h=h):
                own[rows, self.cols(h)] = self.partial_sum(h, self.steps, 0, rows).astype(jnp.bfloat16)

            by_tiles(self.tt, 32, fill)

    def drain(self):
        for h in range(2):
            for slot in range(self.size - 1):
                wait_for(self.land.at[slot, :, self.cols(h)], self.send.at[h, slot])


class SeqSum:
    def __init__(self, seq, lag, held, land, fill_sem, send, recv):
        self.seq, self.lag, self.held, self.land = seq, lag, held, land
        self.fill_sem, self.send, self.recv = fill_sem, send, recv
        self.me, self.place = lax.axis_index("rows"), lax.axis_index("seq")
        self.behind = (self.place, seq - 1 - self.place)
        self.chunks = held.shape[0]
        self.last_step = self.chunks + lag * (seq - 1)

    @staticmethod
    def scratch(chunks, block):
        return [
            pltpu.VMEM((chunks,) + block, jnp.bfloat16),
            pltpu.VMEM((2, chunks) + block, jnp.bfloat16),
            pltpu.SemaphoreType.DMA((chunks,)),
            pltpu.SemaphoreType.DMA((2, chunks)),
            pltpu.SemaphoreType.DMA((2, chunks)),
        ]

    def copy(self, n, way, source):
        target = (jnp.clip(self.place + 1 - 2 * way, 0, self.seq - 1), self.me)
        return pltpu.make_async_remote_copy(
            src_ref=source, dst_ref=self.land.at[way, n], send_sem=self.send.at[way, n],
            recv_sem=self.recv.at[way, n], device_id=target, device_id_type=MESH,
        )

    def hop(self, step, way):
        n = step - self.lag * self.behind[way]

        @pl.when((n >= 0) & (n < self.chunks))
        def _():
            @pl.when(self.behind[way] == 0)
            def _():
                self.copy(n, way, self.held.at[n]).start()

            @pl.when(self.behind[way] > 0)
            def _():
                self.copy(n, way, self.held.at[n]).wait_recv()

                @pl.when(self.behind[way] < self.seq - 1)
                def _():
                    value = self.held[n].astype(jnp.float32) + self.land[way, n].astype(jnp.float32)
                    self.land[way, n] = value.astype(jnp.bfloat16)
                    self.copy(n, way, self.land.at[way, n]).start()

    def advance(self, step, total):
        first = step - self.lag * jnp.minimum(self.behind[0], self.behind[1])

        @pl.when((first >= 0) & (first < self.chunks))
        def _():
            wait_for(self.held.at[first], self.fill_sem.at[first])

        self.hop(step, 0)
        self.hop(step, 1)
        n = step - self.lag * jnp.maximum(self.behind[0], self.behind[1])

        @pl.when((n >= 0) & (n < self.chunks))
        def _():
            for ways, there in (
                ((1,), self.behind[0] == 0),
                ((0,), self.behind[1] == 0),
                ((0, 1), (self.behind[0] > 0) & (self.behind[1] > 0)),
            ):

                @pl.when(there)
                def _(ways=ways):
                    value = self.held[n].astype(jnp.float32)
                    if len(ways) == 2:
                        value = -value
                    for way in ways:
                        value = value + self.land[way, n].astype(jnp.float32)
                    total(n, value.astype(jnp.bfloat16))

    def run(self, first, last, total):
        def body(step, none):
            self.advance(step, total)
            return none

        lax.fori_loop(first, last, body, 0)

    def drain(self):
        for way in range(2):

            @pl.when(self.behind[way] < self.seq - 1)
            def _(way=way):
                def sent(n, none):
                    self.copy(n, way, self.held.at[n]).wait_send()
                    return none

                lax.fori_loop(0, self.chunks, sent, 0)


def fill_chunks(held, fill_sem, source, first=0):
    rows, cols = held.shape[1:]
    n = first
    if len(source.shape) == 3:
        for j in range(source.shape[0]):
            for i in range(source.shape[1] // rows):
                piece = source.at[j, pl.ds(i * rows, rows), :]
                pltpu.make_async_copy(piece, held.at[n], fill_sem.at[n]).start()
                n += 1
        return n
    for i in range(source.shape[0] // rows):
        for j in range(source.shape[1] // cols):
            piece = source.at[pl.ds(i * rows, rows), pl.ds(j * cols, cols)]
            pltpu.make_async_copy(piece, held.at[n], fill_sem.at[n]).start()
            n += 1
    return n


def early_blocks(size):
    return size // 4


def swap_blocks(size, weight, slots):
    me, place = lax.axis_index("rows"), lax.axis_index("seq")
    for m in range(size):
        q = flip(me, m)
        parts = weight.shape[1] // slots(m, 0)[0].shape[0]
        for i in range(parts):
            target, recv, send = slots(m, i)
            rows = target.shape[0]
            piece = weight.at[q, pl.ds(i * rows, rows), :]
            if m == 0:
                pltpu.make_async_copy(piece, target, recv).start()
            else:
                remote(piece, target, send, recv, (place, q))


def drain_swap(size, weight, slots):
    for m in range(1, size):
        for i in range(weight.shape[1] // slots(m, 0)[0].shape[0]):
            target, unused_recv, send = slots(m, i)
            wait_for(target, send)


def backward_kernel(size, seq, nr, tt, ct, uu, *refs):
    delta_in, x_in, gy_in, hist_in, proj_ref, params, carry_ref, last_ref, branch, out_w, gate_w = refs[:11]
    gdelta_out, gx_out, gate_out, gbc_ref, grate_ref, branch_own, out_sum, gate_sum = refs[11:19]
    sel, bc, hist, prod, state_ref, after_ref, fold, delta_ref, x_ref, gy_ref, gdelta_ref, gx_ref, gate_s, a_ref = refs[19:33]
    sems, out_sems, hist_sems = refs[33:36]
    scatter = RowScatter(size, branch, *refs[36:42])
    chain = SeqSum(seq, 3, *refs[42:47])
    gate_send, gate_recv, gate_sem = refs[47:]
    el = a_ref.shape[1]
    blocks = el // LANES
    count = tt // ct

    def fetch(c):
        slot = lax.rem(c, 2)
        return pltpu.make_async_copy(hist_in.at[pl.ds(c * ct, ct)], hist.at[slot], hist_sems.at[slot])

    copies = copy_all((delta_in, x_in, gy_in), (delta_ref, x_ref, gy_ref), sems)
    fetch(count - 1).start()
    greet_rows_and_seq(size, seq)
    scatter.start()
    fill_chunks(chain.held, chain.fill_sem, out_w)
    early = early_blocks(size)
    halves = gate_w.shape[1] // chain.held.shape[1]
    first = chain.chunks - early * halves

    def slots(m, i):
        if m < early:
            n = first + m * halves + i
            return chain.held.at[n], chain.fill_sem.at[n], gate_send.at[m, i]
        return gate_s.at[m - early], gate_recv.at[m], gate_send.at[m, 0]

    swap_blocks(size, gate_w, slots)
    a_ref[...] = decay_rates(params) * LOG2E
    piece = chain.held.shape[1:]

    def total(n, value):
        @pl.when(n < first)
        def _():
            across = out_sum.shape[1] // piece[1]
            down = pl.multiple_of(lax.div(n, across) * piece[0], piece[0])
            along = pl.multiple_of(lax.rem(n, across) * piece[1], LANES)
            out_sum[pl.ds(down, piece[0]), pl.ds(along, piece[1])] = value

        @pl.when(n >= first)
        def _():
            gate_sum[n - first] = value

    sel[...] = selector(LANES)
    fold_row = lax.broadcasted_iota(jnp.int32, fold.shape, 0) // LANES
    fold_col = lax.broadcasted_iota(jnp.int32, fold.shape, 1)
    fold[...] = (fold_row + R == fold_col).astype(jnp.bfloat16)
    state_ref[...] = carry_ref[...]
    after_ref[...] = last_ref[...]
    grate_ref[...] = jnp.zeros_like(grate_ref)
    for copy in copies:
        copy.wait()

    def backward(k, none):
        c = count - 1 - k
        slot = lax.rem(c, 2)

        @pl.when(c > 0)
        def _():
            fetch(c - 1).start()

        for at_k, job in (
            (count // 8, functools.partial(scatter.step, 1)),
            (count * 5 // 8, functools.partial(scatter.later, 2)),
            (count - 1, functools.partial(scatter.finish, branch_own)),
        ):
            pl.when(k == at_k)(job)

        rows = pl.multiple_of(c * (ct * nr), ct * nr)
        bc[...] = spread(proj_ref[pl.ds(rows, ct * nr), :], sel)
        fetch(c).wait()
        for b in range(blocks):
            lanes = slice(b * LANES, (b + 1) * LANES)
            for first in (True, False):
                ns = range(0, NS // 2) if first else range(NS // 2, NS)
                pairs = range(ns[0] // 2, ns[-1] // 2 + 1)
                rate = [jnp.broadcast_to(a_ref[n : n + 1, lanes], (nr, LANES)) for n in ns]

                def steps(s, carried):
                    grad, total_rate, after = (list(v) for v in carried)
                    for u in reversed(range(uu)):
                        at = (ct // uu - 1 - s) * uu + u
                        here = pl.ds(pl.multiple_of((c * ct + at) * nr, nr), nr)
                        delta = delta_ref[b, here, :]
                        x = x_ref[b, here, :]
                        gy = gy_ref[b, here, :]
                        du = delta * x
                        near = pl.ds(pl.multiple_of(at * nr, nr), nr)
                        along_rate = along_b = None
                        for p in pairs:
                            pair = hist[slot, at, b, pl.ds(2 * p * nr, 2 * nr), :].astype(jnp.float32)
                            for n, before in ((2 * p, pair[:nr]), (2 * p + 1, pair[nr:])):
                                i = n - ns[0]
                                to_b_at = slice(n * LANES, (n + 1) * LANES)
                                to_c_at = slice((NS + n) * LANES, (NS + n + 1) * LANES)
                                decay = jnp.exp2(delta * rate[i])
                                grad[i] = grad[i] + gy * bc[near, to_c_at]
                                to_c = after[i] * gy
                                to_b = grad[i] * du
                                if b > 0:
                                    to_c = to_c + prod[near, to_c_at]
                                    to_b = to_b + prod[near, to_b_at]
                                prod[near, to_c_at] = to_c
                                prod[near, to_b_at] = to_b
                                term_b = grad[i] * bc[near, to_b_at]
                                along_b = term_b if along_b is None else along_b + term_b
                                grad[i] = grad[i] * decay
                                weighted = grad[i] * before
                                total_rate[i] = total_rate[i] + weighted * delta
                                term = weighted * rate[i]
                                along_rate = term if along_rate is None else along_rate + term
                                after[i] = before
                        gdelta = along_rate * LN2 + along_b * x
                        gx = along_b * delta
                        if not first:
                            gdelta = gdelta + gdelta_ref[b, here, :]
                            gx = gx + gx_ref[b, here, :]
                        gdelta_ref[b, here, :] = gdelta
                        gx_ref[b, here, :] = gx
                    return tuple(grad), tuple(total_rate), tuple(after)

                start = tuple(tuple(ref[n, :, lanes] for n in ns) for ref in (state_ref, grate_ref, after_ref))
                ends = lax.fori_loop(0, ct // uu, steps, start)
                for i, n in enumerate(ns):
                    for ref, end in zip((state_ref, grate_ref, after_ref), ends):
                        ref[n, :, lanes] = end[i]
            chain.advance(blocks * k + b, total)
        gbc_ref[pl.ds(rows, ct * nr), :] = jnp.dot(
            prod[...].astype(jnp.bfloat16), fold[...], preferred_element_type=jnp.float32
        )
        return none

    lax.fori_loop(0, count, backward, 0)
    late = copy_all((gdelta_ref, gx_ref), (gdelta_out, gx_out), out_sems)
    for m in range(early, size):
        wait_for(gate_s.at[m - early], gate_recv.at[m])
    late += copy_all((gate_s,), (gate_out,), gate_sem)
    chain.run(blocks * count, max(blocks * count, chain.last_step), total)
    scatter.drain()
    chain.drain()
    drain_swap(size, gate_w, slots)
    for copy in late:
        copy.wait()


def scan_backward(delta, x, gy, hist, proj, params, carry, last, branch, out_w, gate_w, size, seq):
    nr, tt, width = branch.shape
    el = params.shape[1]
    blocks = el // LANES
    ct = math.gcd(tt, 32)
    here = pl.BlockSpec(memory_space=pltpu.VMEM)
    away = pl.BlockSpec(memory_space=pl.ANY)
    f32, bf16 = jnp.float32, jnp.bfloat16
    scan = (blocks, nr * tt, LANES)
    piece = (gate_w.shape[1] // 2, gate_w.shape[2])
    early = early_blocks(size)
    chunks = out_w.size // math.prod(piece) + 2 * early
    return pl.pallas_call(
        functools.partial(backward_kernel, size, seq, nr, tt, ct, max(1, ct * 8 // size)),
        in_specs=[away] * 4 + [here] * 4 + [away] * 3,
        out_specs=[away] * 3 + [here] * 5,
        out_shape=[
            jax.ShapeDtypeStruct(scan, f32),
            jax.ShapeDtypeStruct(scan, f32),
            jax.ShapeDtypeStruct((size - early,) + gate_w.shape[1:], bf16),
            jax.ShapeDtypeStruct((tt * nr, LANES), f32),
            jax.ShapeDtypeStruct((NS, nr, el), f32),
            jax.ShapeDtypeStruct((tt, width), bf16),
            jax.ShapeDtypeStruct(out_w.shape, bf16),
            jax.ShapeDtypeStruct((2 * early,) + piece, bf16),
        ],
        scratch_shapes=[
            pltpu.VMEM((LANES, 2 * NS * LANES), bf16),
            pltpu.VMEM((ct * nr, 2 * NS * LANES), f32),
            pltpu.VMEM((2, ct, blocks, NS * nr, LANES), bf16),
            pltpu.VMEM((ct * nr, 2 * NS * LANES), f32),
            pltpu.VMEM((NS, nr, el), f32),
            pltpu.VMEM((NS, nr, el), f32),
            pltpu.VMEM((2 * NS * LANES, LANES), bf16),
        ]
        + [pltpu.VMEM(scan, f32)] * 5
        + [
            pltpu.VMEM((size - early,) + gate_w.shape[1:], bf16),
            pltpu.VMEM((NS, el), f32),
            pltpu.SemaphoreType.DMA((3,)),
            pltpu.SemaphoreType.DMA((2,)),
            pltpu.SemaphoreType.DMA((2,)),
        ]
        + RowScatter.scratch(size, tt, width)
        + SeqSum.scratch(chunks, piece)
        + [pltpu.SemaphoreType.DMA((size, 2)), pltpu.SemaphoreType.DMA((size,)), pltpu.SemaphoreType.DMA((1,))],
        compiler_params=pltpu.CompilerParams(
            vmem_limit_bytes=62 * MIB, collective_id=3, has_side_effects=True
        ),
        name="scan_backward",
    )(delta, x, gy, hist, proj, params, carry, last, branch, out_w, gate_w)


def small_rows(piece_rows):
    rows = 2 * LANES + 32
    return rows + -rows % piece_rows


def back_kernel(size, seq, *refs):
    gdelta_in, gx_in, delta_in, normed_in, w_in, cext_in, ggp_in, gbc_in, gate_w = refs[:9]
    rank_ref, dt_in, x_w, params, grate_ref, gate_sum = refs[9:15]
    own, in_sum, small_sum = refs[15:18]
    taps_ref, bias_ref = params.at[0:KC], params.at[KC : KC + 1]
    (
        gdelta, gx, delta, normed, wv, cext, gmix, gbc, low, gcp, turned, w_stage, acc_x, acc_dt, acc,
        small, hmail, hland, stage, gco, dt_w,
    ) = refs[18:39]
    part, near, total, mail, far, out, sems = refs[39:46]
    scatter = RowScatter(size, None, *refs[46:52])
    chain = SeqSum(seq, 4, *refs[52:57])
    held, fill_sem = chain.held, chain.fill_sem
    swap_send, in_sems, halo_send, halo_recv = refs[57:]
    me, parity, partner, others = row_peers(size)
    place = lax.axis_index("seq")
    share, el = w_stage.shape[1:]
    tt = low.shape[0]
    width = normed.shape[1]
    blocks = el // LANES
    half = size // 2
    f32, bf16 = jnp.float32, jnp.bfloat16
    nt = (((1,), (1,)), ((), ()))
    tn = (((0,), (0,)), ((), ()))
    copies = copy_all(
        (gdelta_in, delta_in, gbc_in, cext_in, gx_in, ggp_in, w_in, normed_in),
        (gdelta, delta, gbc, cext, gx, gmix.at[:, :, pl.ds(el, el)], wv, normed),
        in_sems,
    )
    early = fill_chunks(held, fill_sem, gate_w)
    greet_rows_and_seq(size, seq)
    for ref in (acc_x, acc_dt, acc, small):
        ref[...] = jnp.zeros_like(ref)
    for copy in copies[:3]:
        copy.wait()

    dt_w[0:R, :] = dt_in[...]
    dt_w[R:, :] = jnp.zeros((LANES - R, el), bf16)
    rows = held.shape[1]
    halves = share // rows
    first = small_rows(rows) // rows
    before = early_blocks(size)

    def place_in(m, i, gate, value):
        along = pl.multiple_of((gate * size + crossed(me, m, size)) * el, LANES)
        in_sum[pl.ds(pl.multiple_of(i * rows, rows), rows), pl.ds(along, el)] = value

    def sums(n, value):
        @pl.when(n < early)
        def _():
            place_in(before + lax.div(n, halves), lax.rem(n, halves), 1, value)

        @pl.when((n >= early) & (n < early + first))
        def _():
            small_sum[pl.ds(pl.multiple_of((n - early) * rows, rows), rows), :] = value

        @pl.when(n >= early + first)
        def _():
            k = n - early - first
            place_in(lax.div(k, halves), lax.rem(k, halves), 0, value)

    for n in range(before * halves):
        place_in(n // halves, n % halves, 1, gate_sum[n])

    def fold8(value):
        return jnp.sum(value.reshape(value.shape[0] // 8, 8, value.shape[1]), axis=0)

    def block_at(i):
        return 2 * lax.rem(me // 2 + lax.rem(i, half), half) + lax.rem(parity + 1 + lax.div(i, half), 2)

    def steps_back(i, none):
        p = block_at(i)

        def body(span):
            for b in range(blocks):
                lanes = slice(b * LANES, (b + 1) * LANES)
                there = pl.ds(p + span.start * size, 64, stride=size)
                dl = delta[b, there, :]
                near_zero = dl * (1.0 - dl * (0.5 - dl * (1.0 / 6.0)))
                value = gdelta[b, there, :] * jnp.where(dl < 0.01, near_zero, 1.0 - jnp.exp(-dl))
                low[span, lanes] = value.astype(bf16)
                acc[KC + 1, :, lanes] = acc[KC + 1, :, lanes] + fold8(value)

        by_tiles(tt, 64, body)
        value = lax.dot_general(low[...], dt_w[...], nt, preferred_element_type=f32)
        value = value + gbc[pl.ds(p, tt, stride=size), :]
        acc_dt[...] += lax.dot_general(rank_ref[p], low[...], tn, preferred_element_type=f32)

        @pl.when(i < half)
        def _():
            part[p] = value.astype(bf16)
            remote(
                part.at[p], near.at[lax.div(p, 2)], sems.at[0, lax.div(p, 2)], sems.at[1, lax.div(p, 2)],
                (place, partner),
            )

        @pl.when(i >= half)
        def _():
            total[lax.div(p, 2)] = value

        return none

    lax.fori_loop(0, size, steps_back, 0)
    for copy in copies[3:]:
        copy.wait()
    def halo(p):
        return pltpu.make_async_remote_copy(
            src_ref=hmail.at[p], dst_ref=hland.at[p], send_sem=halo_send.at[p], recv_sem=halo_recv.at[p],
            device_id=(jnp.maximum(place - 1, 0), me), device_id_type=MESH,
        )

    def conv_back(p, step):
        gco[...] = lax.dot_general(out[p], x_w[...], nt, preferred_element_type=f32)

        def body(span):
            value = gco[span, :]
            there = pl.ds(p + span.start * size, 64, stride=size)
            value = value + jnp.concatenate([gx[b, there, :] for b in range(blocks)], axis=1)
            ext = cext[p, pl.ds(span.start, 80), :].astype(f32)
            here = bias_ref[...]
            for k in range(KC):
                here = here + taps_ref[k : k + 1, :] * ext[16 - KC + 1 + k : 16 - KC + 1 + k + 64]
            sig = 1.0 / (1.0 + jnp.exp(-here))
            low[span, :] = (here * sig).astype(bf16)
            value = value * sig * (1.0 + here * (1.0 - sig))
            gcp[p, span, :] = value
            acc[KC] = acc[KC] + fold8(value)
            for k in range(KC):
                acc[k] = acc[k] + fold8(value * ext[16 - KC + 1 + k : 16 - KC + 1 + k + 64])

        by_tiles(tt, 64, body)
        acc_x[...] += lax.dot_general(out[p], low[...], tn, preferred_element_type=f32)
        hmail[p] = gcp[p, 0:16, :].astype(bf16)

        @pl.when(place > 0)
        def _():
            halo(p).start()

        if step < early:
            chain.advance(step, sums)

    steps_done = iter(range(size))
    exchange_sums(size, near, total, mail, far, out, sems, lambda p: conv_back(p, next(steps_done)))
    for j in range(half):
        wait_for(near.at[j], sems.at[0, j])

    def turn(p, none):
        @pl.when(place < seq - 1)
        def _():
            halo(p).wait_recv()
            gcp[p, tt : tt + 8, :] = hland[p, 0:8, :].astype(f32)

        @pl.when(place == seq - 1)
        def _():
            gcp[p, tt : tt + 8, :] = jnp.zeros((8, el), f32)

        def body(span):
            ext = gcp[p, pl.ds(span.start, 72), :]
            value = taps_ref[KC - 1 : KC, :] * ext[0:64]
            for k in range(KC - 1):
                value = value + taps_ref[k : k + 1, :] * ext[KC - 1 - k : KC - 1 - k + 64]
            gmix[p, span, 0:el] = value.astype(bf16)

        by_tiles(tt, 64, body)
        columns = pl.ds(pl.multiple_of(p * tt, tt), tt)
        turned[:, columns] = jnp.transpose(gmix[p, :, 0:el].astype(f32)).astype(bf16)

        @pl.when(size + p < early)
        def _():
            chain.advance(size + p, sums)

        return none

    lax.fori_loop(0, size, turn, 0)
    chain.run(2 * size, max(2 * size, early), sums)

    group = 384 // share

    def weights(j, none):
        columns = pl.ds(pl.multiple_of(j * 384, 384), 384)
        value = jnp.dot(turned[...], normed[:, columns], preferred_element_type=f32)
        value = jnp.transpose(value).astype(bf16)
        for g in range(group):
            w_stage[j * group + g] = value[g * share : (g + 1) * share, :]
        return none

    lax.fori_loop(0, width // 384, weights, 0)
    top = 2 * LANES
    small[0:LANES, :] = acc_x[...].astype(bf16)
    small[LANES:top, :] = acc_dt[...].astype(bf16)
    rate_sum = jnp.sum(grate_ref[...], axis=1) * decay_rates(params)
    last = [rate_sum] + [jnp.sum(acc[k], axis=0, keepdims=True) for k in range(KC + 2)]
    last.append(jnp.zeros((16 - KC - 2, el), f32))
    small[top : top + 32, :] = jnp.concatenate(last, axis=0).astype(bf16)
    late = fill_chunks(held, fill_sem, small, early)

    def slots(m, i):
        n = late + m * halves + i
        return held.at[n], fill_sem.at[n], swap_send.at[n]

    swap_blocks(size, w_stage, slots)

    def spread_back(i, none):
        p = crossed(me, jnp.where(i < half, 2 * i + 1, 2 * (i - half)), size)
        weight = wv[...].reshape(width, 2 * el)
        value = lax.dot_general(gmix[p], weight, nt, preferred_element_type=f32).astype(bf16)

        @pl.when(i < half)
        def _():
            stage[i] = value
            scatter.staged(i, stage)

        @pl.when(i >= half)
        def _():
            scatter.keep[i - half] = value

        chain.advance(early + i, sums)
        return none

    lax.fori_loop(0, size, spread_back, 0)
    done = early + size
    jobs = [functools.partial(scatter.step, k) for k in range(1, scatter.steps)]
    jobs.append(functools.partial(scatter.finish, own))
    for k, job in enumerate(jobs):
        job()
        upto = min(chain.last_step, done + (chain.last_step - done) * (2 if k else 3) // 4)
        chain.run(done, upto, sums)
        done = upto
    chain.run(done, chain.last_step, sums)
    scatter.drain()
    chain.drain()
    drain_swap(size, w_stage, slots)

    def halo_sent(p, none):
        halo(p).wait_send()
        return none

    @pl.when(place > 0)
    def _():
        lax.fori_loop(0, size, halo_sent, 0)


def back(
    gdelta, gx, delta, normed, w_in, cext, ggp, gbc, gate_w, rank, dt_w, x_w, params, grate, gate_sum, size, seq
):
    away = pl.BlockSpec(memory_space=pl.ANY)
    here = pl.BlockSpec(memory_space=pltpu.VMEM)
    f32, bf16 = jnp.float32, jnp.bfloat16
    unused_size, tt, el = ggp.shape
    share = w_in.shape[1]
    width = normed.shape[1]
    piece = (share // 2, el)
    low = small_rows(piece[0])
    chunks = 4 * size - 2 * early_blocks(size) + low // piece[0]
    scratch = [
        (gdelta.shape, f32), (gx.shape, f32), (delta.shape, f32), (normed.shape, bf16), (w_in.shape, bf16),
        (cext.shape, bf16), ((size, tt, 2 * el), bf16), (gbc.shape, f32), ((tt, el), bf16),
        ((size, tt + 8, el), f32), ((el, size * tt), bf16), ((size, share, el), bf16), ((LANES, el), f32),
        ((LANES, el), f32), ((KC + 2, 8, el), f32), ((low, el), bf16), ((size, 16, el), bf16),
        ((size, 16, el), bf16), ((size // 2, tt, width), bf16), ((tt, el), f32),
        ((LANES, el), bf16),
    ]
    return pl.pallas_call(
        functools.partial(back_kernel, size, seq),
        in_specs=[away] * 9 + [here] * 6,
        out_specs=[here] * 3,
        out_shape=[
            jax.ShapeDtypeStruct((tt, width), bf16),
            jax.ShapeDtypeStruct((share, 2 * size * el), bf16),
            jax.ShapeDtypeStruct((low, el), bf16),
        ],
        scratch_shapes=[pltpu.VMEM(*v) for v in scratch]
        + sum_scratch(size, tt)
        + RowScatter.scratch(size, tt, width)
        + SeqSum.scratch(chunks, piece)
        + [
            pltpu.SemaphoreType.DMA((chunks,)),
            pltpu.SemaphoreType.DMA((8,)),
            pltpu.SemaphoreType.DMA((size,)),
            pltpu.SemaphoreType.DMA((size,)),
        ],
        compiler_params=pltpu.CompilerParams(
            vmem_limit_bytes=63 * MIB, collective_id=4, has_side_effects=True
        ),
        name="back",
    )(gdelta, gx, delta, normed, w_in, cext, ggp, gbc, gate_w, rank, dt_w, x_w, params, grate, gate_sum)


def local(
    tokens, resets, norm_gain, in_proj, x_proj, dt_proj, conv_weight, conv_bias, dt_bias, a_log, out_proj,
    cotangent,
):
    size = lax.axis_size("rows")
    seq = lax.axis_size("seq")
    rd, tt, unused_d = tokens.shape
    nr = rd * size
    el = E // size
    count = nr * tt
    assert rd == 1 and ITEM % tt == 0 and nr % 8 == 0

    elp = pad_lanes(el)
    share = D // size
    direct = elp == el
    f32, bf16 = jnp.float32, jnp.bfloat16

    def widen(value, axis):
        pad = [(0, 0)] * value.ndim
        pad[axis] = (0, elp - el)
        return jnp.pad(value, pad)

    if direct:
        w_local = in_proj
    else:
        w_local = jnp.moveaxis(in_proj.reshape(share, 2, size, el), 2, 0)
        w_local = widen(w_local, 3).reshape(size, share, 2 * elp)
    out_proj, x_proj = widen(out_proj, 0), widen(x_proj, 0)
    dt_proj = widen(dt_proj, 1)
    params = [conv_weight, conv_bias[None], dt_bias[None], jnp.zeros((8 - KC - 2, el), bf16), a_log]
    params = widen(jnp.concatenate(params, axis=0).astype(f32), 1)
    across = -(-share // 256) * 256
    line = lax.broadcasted_iota(jnp.int32, (16, across), 0)
    fresh = 1.0 - resets[:, :1].astype(bf16)
    notes = jnp.where(line == 0, jnp.pad(norm_gain, (0, across - share))[None], jnp.where(line == 1, fresh, 0.0))
    notes = notes.astype(bf16)
    (
        normed, w_in, x_t, delta_t, gy_t, conv_ext, hist, branch, grad_out_proj, grad_in_gate, grad_gate_pre, proj_t,
        rank_all, last, carry_back, gain,
    ) = front(
        tokens[0], cotangent[0], notes, w_local, out_proj, x_proj, dt_proj, params, size, seq, direct
    )
    grad_delta, grad_input, gate_blocks, grad_bc, grate, branch_own, sum_out, gate_sum = scan_backward(
        delta_t, x_t, gy_t, hist, proj_t, params, carry_back, last, branch, grad_out_proj[:el], grad_in_gate, size, seq
    )
    grad_normed, sum_in, small = back(
        grad_delta, grad_input, delta_t, normed.reshape(count, D), w_in, conv_ext, grad_gate_pre, grad_bc, gate_blocks,
        rank_all, dt_proj, x_proj, params, grate, gate_sum, size, seq,
    )
    sum_in = sum_in.reshape(share, 2, size, elp)[..., :el].reshape(share, 2 * E)
    sum_out = sum_out.astype(f32)
    block_out = (tokens.astype(jnp.float32) + branch_own[None].astype(jnp.float32)).astype(jnp.bfloat16)
    grad_normed = grad_normed[None].astype(jnp.float32)

    own = tokens.astype(jnp.float32)
    inv = lax.rsqrt(jnp.mean(own * own, axis=2, keepdims=True) + epsilon)
    gain_own = jnp.sum(in_proj.astype(f32) * sum_in.astype(f32), axis=1) / norm_gain.astype(jnp.float32)
    grad_hat = grad_normed * gain
    grad_norm_in = inv * (
        grad_hat - own * (inv * inv) * jnp.mean(grad_hat * own, axis=2, keepdims=True)
    )
    d_tokens = (cotangent.astype(jnp.float32) + grad_norm_in).astype(jnp.bfloat16)


    def rows(first, last):
        return small[first:last, :el].astype(f32)

    top = 2 * LANES + NS
    return (
        block_out,
        d_tokens,
        gain_own,
        sum_in.astype(f32),
        rows(0, LANES).T,
        rows(LANES, LANES + R),
        rows(top, top + KC),
        rows(top + KC, top + KC + 1)[0],
        rows(top + KC + 1, top + KC + 2)[0],
        rows(2 * LANES, top),
        sum_out,
    )


def solution(mesh):
    in_specs = (
        P("rows", "seq", None),
        P("rows", "seq"),
        P("rows"),
        P("rows", None),
        P("rows", None),
        P(None, "rows"),
        P(None, "rows"),
        P("rows"),
        P("rows"),
        P(None, "rows"),
        P("rows", None),
        P("rows", "seq", None),
    )
    out_specs = (
        P("rows", "seq", None),
        P("rows", "seq", None),
        P("rows"),
        P("rows", None),
        P("rows", None),
        P(None, "rows"),
        P(None, "rows"),
        P("rows"),
        P("rows"),
        P(None, "rows"),
        P("rows", None),
    )
    return jax.shard_map(local, mesh=mesh, in_specs=in_specs, out_specs=out_specs, check_vma=False)
```
